32 devices in a mesh: seq: 8 (over z, y), chan: 2 (over core), dp: 2 (over x).
Axes of the slice: x: 2, y: 2, z: 4, core: 2. Of those that a mesh axis runs over, the one named last changes fastest.
Arguments:
- tokens: bfloat16 [2, 2, 1024, 768], P(None, 'dp', 'seq', 'chan'), may hold values from -6 to 6
- lengths: int32 [2, 2], P(None, 'dp'), may hold values from 128 to 1024, as said below
- cotangent: bfloat16 [2, 2, 1024, 768], P(None, 'dp', 'seq', 'chan'), may hold values from -6 to 6
- norm_gain: float32 [2, 2, 768], P(None, None, 'chan'), may hold values from 0.5 to 1.5
- norm_bias: float32 [2, 2, 768], P(None, None, 'chan'), may hold values from -1.25 to 1.25
- in_weight: bfloat16 [2, 3, 768, 768], P(None, None, None, 'chan'), may hold values from -0.21875 to 0.21875
- in_bias: float32 [2, 3, 768], P(None, None, 'chan'), may hold values from -1.25 to 1.25
- short_taps: float32 [2, 3, 3, 768], P(None, None, None, 'chan'), may hold values from -3.5 to 3.5
- short_bias: float32 [2, 3, 768], P(None, None, 'chan'), may hold values from -1.25 to 1.25
- skip_gain: float32 [2, 768], P(None, 'chan'), may hold values from -6 to 6
- out_weight: bfloat16 [2, 768, 768], P(None, 'chan'), may hold values from -0.21875 to 0.21875
- out_bias: float32 [2, 768], P(None, 'chan'), may hold values from -1.25 to 1.25
- up_weight: bfloat16 [2, 768, 3072], P(None, None, 'chan'), may hold values from -0.21875 to 0.21875
- up_bias: float32 [2, 3072], P(None, 'chan'), may hold values from -1.25 to 1.25
- down_weight: bfloat16 [2, 3072, 768], P(None, 'chan'), may hold values from -0.109375 to 0.109375
- down_bias: float32 [2, 768], P(None, 'chan'), may hold values from -1.25 to 1.25
- filter_in: float32 [2, 33, 64], replicated, may hold values from -1 to 1
- filter_bias: float32 [2, 64], replicated, may hold values from -1 to 1
- filter_freq: float32 [2, 64], replicated, may hold values from 0.5 to 2
- filter_out: float32 [2, 64, 768], P(None, None, 'chan'), may hold values from -0.046875 to 0.046875
- decay_rate: float32 [2, 768], P(None, 'chan'), may hold values from 0.25 to 16
Outputs:
- out_act: float32 [2, 2, 1024, 768], P(None, 'dp', 'seq', 'chan')
- grad_tokens: float32 [2, 2, 1024, 768], P(None, 'dp', 'seq', 'chan')
- grad_in_weight: float32 [2, 3, 768, 768], P(None, None, ('seq', 'dp'), 'chan')
- grad_out_weight: float32 [2, 768, 768], P(None, 'chan', ('seq', 'dp'))
- grad_up_weight: float32 [2, 768, 3072], P(None, ('seq', 'dp'), 'chan')
- grad_down_weight: float32 [2, 3072, 768], P(None, 'chan', ('seq', 'dp'))
- grad_norm_gain: float32 [2, 2, 768], replicated
- grad_norm_bias: float32 [2, 2, 768], replicated
- grad_in_bias: float32 [2, 3, 768], replicated
- grad_short_taps: float32 [2, 3, 3, 768], replicated
- grad_short_bias: float32 [2, 3, 768], replicated
- grad_skip_gain: float32 [2, 768], replicated
- grad_out_bias: float32 [2, 768], replicated
- grad_up_bias: float32 [2, 3072], replicated
- grad_down_bias: float32 [2, 768], replicated
- grad_filter_in: float32 [2, 33, 64], replicated
- grad_filter_bias: float32 [2, 64], replicated
- grad_filter_freq: float32 [2, 64], replicated
- grad_filter_out: float32 [2, 64, 768], replicated
The draws below stay inside these ranges and needn't reach their ends.
Inputs may be any that keep to these rules, and one draw needn't show every extreme that they name: `lengths`: in every column b one of the 2 sequences, a different one from seed to seed, has the full length 1024.
All inputs are finite; a program needn't handle non-finite values.
Results may differ from the reference program's by a relative error of at most 0.028.
Values may be sent and summed in bfloat16 or wider, within the bound.
A program may use at most 256 MiB of HBM per device.

```python
import math
import jax
import jax.numpy as jnp
from jax import lax

D = 768
FF = 3072
EMB = 33
FILT = 64
LAYERS = 2
SEQ_DEV = 128
MICRO = 2
MIN_LEN = 128
SEQ_LEN = 1024
BATCH = 2
N_SEQ = 8


def draw_lengths(key, part):
    key = jax.random.fold_in(key, 11)
    key_levels, key_full = jax.random.split(key)
    full_length = SEQ_DEV * N_SEQ
    levels = jax.random.randint(key_levels, (MICRO, BATCH), 0, 64)
    drawn_len = MIN_LEN + (full_length - MIN_LEN) * levels * levels // 4096
    longest = jax.random.randint(key_full, (BATCH,), 0, MICRO)
    row_ids = jnp.arange(MICRO, dtype=jnp.int32)[:, None]
    return jnp.where(row_ids == longest[None, :], full_length, drawn_len).astype(jnp.int32)


def steps_of(own_key, shape, pieces, smallest, top_value):
    def one(dim, parts):
        steps = jax.random.uniform(jax.random.fold_in(jax.random.fold_in(own_key, 6), dim), (parts,), jnp.float32, smallest / len(pieces), top_value / len(pieces))
        return jnp.repeat(jnp.exp(steps), shape[dim] // parts).reshape((-1,) + (1,) * (len(shape) - dim - 1))

    loudness = one(*pieces[0])
    for cut in pieces[1:]:
        loudness = loudness * one(*cut)
    return loudness


def noise(stream_key, dims, scale, most, cuts=(), kind=jnp.bfloat16):
    values = jax.random.normal(stream_key, dims, jnp.float32) * scale
    if len(cuts) > 0:
        values = steps_of(stream_key, dims, cuts, -0.22, 0.18) * values
    return jnp.clip(values, min=-most, max=most).astype(kind)


def setup_inputs(seed: int = 0) -> dict:
    keys = jax.random.split(jax.random.key(seed), 22)
    return {
        "tokens": noise(keys[0], (MICRO, BATCH, SEQ_LEN, D), 1.0, 6.0, ((1, 2), (2, 8), (3, 2))),
        "lengths": draw_lengths(jax.random.fold_in(keys[21], 71), 0),
        "cotangent": noise(keys[2], (MICRO, BATCH, SEQ_LEN, D), 1.0, 6.0, ((1, 2), (2, 8), (3, 2))),
        "norm_gain": jnp.clip(1.0 + 0.1 * jax.random.normal(keys[3], (LAYERS, 2, D), jnp.float32), 0.5, 1.5),
        "norm_bias": noise(keys[4], (LAYERS, 2, D), 0.2, 1.25, ((2, 2),), jnp.float32),
        "in_weight": noise(keys[5], (LAYERS, 3, D, D), D ** -0.5, 0.21875, ((3, 2),)),
        "in_bias": noise(keys[6], (LAYERS, 3, D), 0.2, 1.25, ((2, 2),), jnp.float32),
        "short_taps": noise(keys[7], (LAYERS, 3, 3, D), 3 ** -0.5, 3.5, ((3, 2),), jnp.float32),
        "short_bias": noise(keys[8], (LAYERS, 3, D), 0.2, 1.25, ((2, 2),), jnp.float32),
        "skip_gain": noise(keys[9], (LAYERS, D), 1.0, 6.0, ((1, 2),), jnp.float32),
        "out_weight": noise(keys[10], (LAYERS, D, D), D ** -0.5, 0.21875, ((1, 2),)),
        "out_bias": noise(keys[11], (LAYERS, D), 0.2, 1.25, ((1, 2),), jnp.float32),
        "up_weight": noise(keys[12], (LAYERS, D, FF), D ** -0.5, 0.21875, ((2, 2),)),
        "up_bias": noise(keys[13], (LAYERS, FF), 0.2, 1.25, ((1, 2),), jnp.float32),
        "down_weight": noise(keys[14], (LAYERS, FF, D), FF ** -0.5, 0.109375, ((1, 2),)),
        "down_bias": noise(keys[15], (LAYERS, D), 0.2, 1.25, ((1, 2),), jnp.float32),
        "filter_in": noise(keys[16], (LAYERS, EMB, FILT), EMB ** -0.5, 1.0, (), jnp.float32),
        "filter_bias": jnp.clip(jax.random.uniform(keys[17], (LAYERS, FILT), jnp.float32, -1.0, 1.0), -1.0, 1.0),
        "filter_freq": jnp.clip(jax.random.uniform(keys[18], (LAYERS, FILT), jnp.float32, 0.5, 2.0), 0.5, 2.0),
        "filter_out": noise(keys[19], (LAYERS, FILT, D), (FILT * SEQ_LEN // 4) ** -0.5, 0.046875, ((2, 2),), jnp.float32),
        "decay_rate": jnp.clip(jnp.exp(math.log(16.0) - 4.158883 * jax.random.uniform(keys[20], (LAYERS, D), jnp.float32) ** steps_of(keys[20], (LAYERS, D), ((1, 2),), -0.2, 0.2)), 0.25, 16.0),
    }


@jax.custom_vjp
def low(v):
    return lax.optimization_barrier(v.astype(jnp.bfloat16)).astype(jnp.float32)

@jax.custom_vjp
def low_back(v):
    return v

def low_keep(v):
    return (low(v), None)

def low_pass(kept, grad):
    return (grad,)

def back_keep(v):
    return (v, None)

def back_low(kept, grad):
    return (low(grad),)
low.defvjp(low_keep, low_pass)
low_back.defvjp(back_keep, back_low)
HIGH = lax.Precision.HIGHEST
EPS = 1e-05

def positions(seq_length, emb_width):
    band_count = (emb_width - 1) // 2
    step_ids = jnp.arange(seq_length, dtype=jnp.float32)
    steps_norm = step_ids / seq_length
    band_freq = jnp.linspace(0.0001, band_count - 1, band_count).astype(jnp.float32)
    phases = 2.0 * math.pi * steps_norm[:, None] * band_freq[None, :]
    table = jnp.concatenate([steps_norm[:, None], jnp.cos(phases), -jnp.sin(phases)], axis=1)
    return (table, steps_norm)

def layer_norm(values, gain_row, bias_row):
    mean_row = lax.optimization_barrier(jnp.mean(values, axis=-1, keepdims=True))
    centred = values - mean_row
    variance = lax.optimization_barrier(jnp.mean(centred * centred, axis=-1, keepdims=True))
    return centred * lax.rsqrt(variance + EPS) * gain_row + bias_row

def short_conv(streams, taps, short_b):
    count = streams.shape[1]
    padded = jnp.pad(streams, ((0, 0), (2, 0), (0, 0)))
    return taps[:, 0][:, None, :] * padded[:, 2:] + taps[:, 1][:, None, :] * padded[:, 1:count + 1] + taps[:, 2][:, None, :] * padded[:, :count] + short_b[:, None, :]

def long_conv(signal, long_filter, skip_row):
    count = signal.shape[0]
    spectrum = jnp.fft.rfft(signal, n=2 * count, axis=0) * jnp.fft.rfft(long_filter, n=2 * count, axis=0)
    return jnp.fft.irfft(spectrum, n=2 * count, axis=0)[:count] + skip_row * signal

def hyena_stack(params, sequence, pad_mask):
    norm_gain, norm_bias, in_weight, in_bias, short_taps, short_bias, skip_gain, out_weight, out_bias, up_weight, up_bias, down_weight, down_bias, filter_in, filter_bias, filter_freq, filter_out, decay_rate = params
    seq_length = sequence.shape[0]
    table, steps_norm = positions(seq_length, filter_in.shape[1])
    resid = sequence
    for layer_index in range(norm_gain.shape[0]):
        hidden = jnp.sin(filter_freq[layer_index] * (jnp.dot(table, filter_in[layer_index], precision=HIGH) + filter_bias[layer_index]))
        long_filter = jnp.dot(hidden, filter_out[layer_index], precision=HIGH) * jnp.exp(-steps_norm[:, None] * decay_rate[layer_index][None, :])
        normed = low(layer_norm(resid, norm_gain[layer_index, 0], norm_bias[layer_index, 0]))
        streams = low_back(jnp.einsum('ld,kdc->klc', normed, in_weight[layer_index], precision=HIGH)) + in_bias[layer_index][:, None, :]
        short_out = short_conv(streams, short_taps[layer_index], short_bias[layer_index])
        product = short_out[1] * short_out[2]
        long_out = long_conv(product, long_filter, skip_gain[layer_index])
        mixed = low(short_out[0] * long_out)
        branch = low_back(jnp.dot(mixed, out_weight[layer_index], precision=HIGH)) + out_bias[layer_index]
        resid = resid + pad_mask[:, None] * branch
        normed = low(layer_norm(resid, norm_gain[layer_index, 1], norm_bias[layer_index, 1]))
        pre_act = low_back(jnp.dot(normed, up_weight[layer_index], precision=HIGH)) + up_bias[layer_index]
        activated = low(jax.nn.gelu(pre_act, approximate=False))
        branch = low_back(jnp.dot(activated, down_weight[layer_index], precision=HIGH)) + down_bias[layer_index]
        resid = resid + pad_mask[:, None] * branch
    return resid

def reference(tokens, lengths, cotangent, norm_gain, norm_bias, in_weight, in_bias, short_taps, short_bias, skip_gain, out_weight, out_bias, up_weight, up_bias, down_weight, down_bias, filter_in, filter_bias, filter_freq, filter_out, decay_rate):
    params = tuple((item.astype(jnp.float32) for item in (norm_gain, norm_bias, in_weight, in_bias, short_taps, short_bias, skip_gain, out_weight, out_bias, up_weight, up_bias, down_weight, down_bias, filter_in, filter_bias, filter_freq, filter_out, decay_rate)))
    micro_count, batch_count, seq_length, width = tokens.shape
    flat_tokens = tokens.reshape(micro_count * batch_count, seq_length, width).astype(jnp.float32)
    flat_cot = cotangent.reshape(micro_count * batch_count, seq_length, width).astype(jnp.float32)
    flat_len = lengths.reshape(micro_count * batch_count).astype(jnp.int32)
    zeros = jax.tree.map(jnp.zeros_like, params)

    def one_sequence(carry, item):
        sequence, cot_seq, seq_len = item
        pad_mask = (jnp.arange(seq_length, dtype=jnp.int32) < seq_len).astype(jnp.float32)

        def forward(param_set, inputs):
            return hyena_stack(param_set, inputs, pad_mask)
        result, pull = jax.vjp(forward, params, sequence)
        grad_params, grad_input = pull(cot_seq)
        return (jax.tree.map(jnp.add, carry, grad_params), (result, grad_input))
    totals, (results, grad_inputs) = lax.scan(one_sequence, zeros, (flat_tokens, flat_cot, flat_len))
    shape_out = (micro_count, batch_count, seq_length, width)
    g_norm_gain, g_norm_bias, g_in_weight, g_in_bias, g_short_taps, g_short_bias, g_skip, g_out_weight, g_out_bias, g_up_weight, g_up_bias, g_down_weight, g_down_bias, g_filter_in, g_filter_bias, g_filter_freq, g_filter_out, g_decay = totals
    return (results.reshape(shape_out), grad_inputs.reshape(shape_out), g_in_weight, g_out_weight, g_up_weight, g_down_weight, g_norm_gain, g_norm_bias, g_in_bias, g_short_taps, g_short_bias, g_skip, g_out_bias, g_up_bias, g_down_bias, g_filter_in, g_filter_bias, g_filter_freq, g_filter_out)
```

```python
import functools
import math

import jax
import jax.numpy as jnp
import numpy as np
from jax import lax
from jax.experimental import pallas as pl
from jax.experimental.pallas import tpu as pltpu
from jax.sharding import PartitionSpec as P

EPS = 1e-05
HIGH = lax.Precision.HIGHEST


def shifted(value, axis, steps):
    count = lax.axis_size(axis)
    initial, last = (max(0, -steps), min(count, count - steps))
    return lax.ppermute(value, axis, [(source, source + steps) for source in range(initial, last)])


def positions(seq_length, emb_width):
    band_count = (emb_width - 1) // 2
    step_ids = jnp.arange(seq_length, dtype=jnp.float32)
    steps_norm = step_ids / seq_length
    band_freq = jnp.linspace(0.0001, band_count - 1, band_count).astype(jnp.float32)
    phases = 2.0 * math.pi * steps_norm[:, None] * band_freq[None, :]
    table = jnp.concatenate([steps_norm[:, None], jnp.cos(phases), -jnp.sin(phases)], axis=1)
    return (table, steps_norm)


def angle_table(row_count, col_count, modulus):
    product = (
        jnp.arange(row_count, dtype=jnp.int32)[:, None]
        * jnp.arange(col_count, dtype=jnp.int32)[None, :]
        % modulus
    )
    theta = product.astype(jnp.float32) * (2.0 * math.pi / modulus)
    return (jnp.cos(theta), jnp.sin(theta))


def split_length(total_length):
    lesser = 2
    for candidate in range(2, math.isqrt(total_length) + 1, 2):
        if total_length % candidate == 0:
            lesser = candidate
    return (lesser, total_length // lesser)


def dft_basis(seq_length):
    padded_len = 2 * seq_length
    lesser, greater = split_length(padded_len)
    cos_p, sin_p = angle_table(lesser, lesser, lesser)
    cos_q, sin_q = angle_table(greater, greater, greater)
    twist_c, twist_s = angle_table(lesser, greater, padded_len)
    return (cos_p, sin_p, cos_q, sin_q, twist_c, twist_s)


def right_mul(left, table):
    return jnp.einsum("ckb,bj->ckj", left, table, precision=HIGH)


def to_spectrum(signal, basis):
    cos_p, sin_p, cos_q, sin_q, twist_c, twist_s = basis
    half = cos_p.shape[0] // 2
    blocks = signal.reshape(signal.shape[0], half, cos_q.shape[0])
    first_re = jnp.einsum("ka,cab->ckb", cos_p[:, :half], blocks, precision=HIGH)
    first_im = -jnp.einsum("ka,cab->ckb", sin_p[:, :half], blocks, precision=HIGH)
    turned_re = first_re * twist_c + first_im * twist_s
    turned_im = first_im * twist_c - first_re * twist_s
    spec_re = right_mul(turned_re, cos_q) + right_mul(turned_im, sin_q)
    spec_im = right_mul(turned_im, cos_q) - right_mul(turned_re, sin_q)
    return (spec_re, spec_im)


def from_spectrum(spec_re, spec_im, basis):
    cos_p, sin_p, cos_q, sin_q, twist_c, twist_s = basis
    half = cos_p.shape[0] // 2
    back_re = right_mul(spec_re, cos_q) - right_mul(spec_im, sin_q)
    back_im = right_mul(spec_im, cos_q) + right_mul(spec_re, sin_q)
    turned_re = back_re * twist_c - back_im * twist_s
    turned_im = back_im * twist_c + back_re * twist_s
    signal = jnp.einsum("ak,ckb->cab", cos_p[:half], turned_re, precision=HIGH) - jnp.einsum(
        "ak,ckb->cab", sin_p[:half], turned_im, precision=HIGH
    )
    return signal.reshape(signal.shape[0], half * cos_q.shape[0]) / (
        cos_p.shape[0] * cos_q.shape[0]
    )


def complex_mul(left_re, left_im, right_re, right_im):
    return (left_re * right_re - left_im * right_im, left_re * right_im + left_im * right_re)


def filter_block(table, steps_norm, weight_in, bias_in, freq_in, cols_in, decay_cols):
    hidden = jnp.sin(freq_in * (jnp.dot(table, weight_in, precision=HIGH) + bias_in))
    raw = jnp.einsum("lf,fc->cl", hidden, cols_in, precision=HIGH)
    return raw * jnp.exp(-decay_cols[:, None] * steps_norm[None, :])


def to_channels(block):
    parts = lax.axis_size("seq")
    shaped = block.reshape(parts, block.shape[0] // parts, block.shape[1])
    moved = lax.all_to_all(
        shaped.astype(jnp.bfloat16), "seq", split_axis=0, concat_axis=2, tiled=True
    ).astype(shaped.dtype)
    return moved.reshape(moved.shape[1], moved.shape[2])


def to_positions(block):
    shaped = block.reshape(1, block.shape[0], block.shape[1])
    moved = lax.all_to_all(
        shaped.astype(jnp.bfloat16), "seq", split_axis=2, concat_axis=0, tiled=True
    ).astype(shaped.dtype)
    return moved.reshape(moved.shape[0] * moved.shape[1], moved.shape[2])


def branch_sum(partial_value):
    return lax.psum_scatter(
        partial_value.astype(jnp.bfloat16), "chan", scatter_dimension=1, tiled=True
    ).astype(jnp.float32)


def branch_grad(grad_low):
    return lax.all_gather(grad_low, "chan", axis=1, tiled=True)


def place(values, start, full_width, axis):
    full_shape = list(values.shape)
    full_shape[axis] = full_width
    return lax.dynamic_update_slice_in_dim(jnp.zeros(full_shape, jnp.float32), values, start, axis)


def local(
    tokens,
    lengths,
    cotangent,
    norm_gain,
    norm_bias,
    in_weight,
    in_bias,
    short_taps,
    short_bias,
    skip_gain,
    out_weight,
    out_bias,
    up_weight,
    up_bias,
    down_weight,
    down_bias,
    filter_in,
    filter_bias,
    filter_freq,
    filter_out,
    decay_rate,
):
    micro_count = tokens.shape[0]
    rows_dev = tokens.shape[2]
    chan_width = tokens.shape[3]
    layer_count = norm_gain.shape[0]
    hidden_width = up_weight.shape[2]
    seq_parts = lax.axis_size("seq")
    chan_parts = lax.axis_size("chan")
    full_width = chan_width * chan_parts
    seq_length = rows_dev * seq_parts
    seq_index = lax.axis_index("seq")
    chan_index = lax.axis_index("chan")
    block_width = chan_width // seq_parts
    col_start = seq_index * block_width
    chan_start = chan_index * chan_width
    basis = dft_basis(seq_length)
    table, steps_norm = positions(seq_length, filter_in.shape[1])
    positions_dev = seq_index * rows_dev + jnp.arange(rows_dev, dtype=jnp.int32)
    filters = []
    for layer_index in range(layer_count):
        filter_cols = lax.dynamic_slice_in_dim(filter_out[layer_index], col_start, block_width, 1)
        decay_cols = lax.dynamic_slice_in_dim(decay_rate[layer_index], col_start, block_width, 0)
        skip_cols = lax.dynamic_slice_in_dim(skip_gain[layer_index], col_start, block_width, 0)

        def make_one(weight_in, bias_in, freq_in, cols_in, decay_cols=decay_cols):
            return filter_block(table, steps_norm, weight_in, bias_in, freq_in, cols_in, decay_cols)

        long_filter, filter_pull = jax.vjp(
            make_one,
            filter_in[layer_index],
            filter_bias[layer_index],
            filter_freq[layer_index],
            filter_cols,
        )
        filt_re, filt_im = to_spectrum(long_filter, basis)
        filters.append((filt_re, filt_im, filter_pull, skip_cols))

    def norm_forward(resid, gain_bias):
        full_rows, full_gb = (
            lax.all_gather(resid, "chan", axis=1, tiled=True),
            lax.all_gather(gain_bias, "chan", axis=1, tiled=True),
        )
        mean_row = jnp.mean(full_rows, axis=1, keepdims=True)
        centred = full_rows - mean_row
        rstd = lax.rsqrt(jnp.mean(centred * centred, axis=1, keepdims=True) + EPS)
        scaled = centred * rstd
        normed = (scaled * full_gb[0] + full_gb[1]).astype(jnp.bfloat16)
        return (normed, (scaled, rstd, full_gb[0]))

    def norm_backward(grad_partial, norm_saved):
        scaled, rstd, gain_row = norm_saved
        grad_rows = lax.psum(grad_partial.astype(jnp.bfloat16), "chan").astype(jnp.float32)
        grad_scaled = grad_rows * gain_row
        grad_full = rstd * (
            grad_scaled
            - jnp.mean(grad_scaled, axis=1, keepdims=True)
            - scaled * jnp.mean(grad_scaled * scaled, axis=1, keepdims=True)
        )
        grad_own = lax.dynamic_slice_in_dim(grad_full, chan_start, chan_width, 1)
        rows_own = lax.dynamic_slice_in_dim(grad_rows, chan_start, chan_width, 1)
        scaled_own = lax.dynamic_slice_in_dim(scaled, chan_start, chan_width, 1)
        return (grad_own, jnp.sum(rows_own * scaled_own, axis=0), jnp.sum(rows_own, axis=0))

    def mixer_forward(resid, pad_mask, layer_index):
        normed, norm_saved = norm_forward(
            resid, jnp.stack([norm_gain[layer_index, 0], norm_bias[layer_index, 0]])
        )
        streams = (
            jnp.einsum(
                "sd,kdc->kcs", normed, in_weight[layer_index], preferred_element_type=jnp.float32
            )
            + in_bias[layer_index][:, :, None]
        )
        rim = shifted(streams[:, :, rows_dev - 2 :], "seq", 1)
        padded = jnp.concatenate([rim, streams], axis=2)
        taps = short_taps[layer_index]
        short_out = (
            taps[:, 0][:, :, None] * padded[:, :, 2:]
            + taps[:, 1][:, :, None] * padded[:, :, 1 : rows_dev + 1]
            + taps[:, 2][:, :, None] * padded[:, :, :rows_dev]
            + short_bias[layer_index][:, :, None]
        )
        product = short_out[1] * short_out[2]
        chan_prod = to_channels(product)
        filt_re, filt_im, filter_pull, skip_cols = filters[layer_index]
        prod_re, prod_im = to_spectrum(chan_prod, basis)
        conv_re, conv_im = complex_mul(prod_re, prod_im, filt_re, filt_im)
        chan_out = from_spectrum(conv_re, conv_im, basis) + skip_cols[:, None] * chan_prod
        long_out = to_positions(chan_out)
        mixed = (short_out[0] * long_out).astype(jnp.bfloat16)
        partial_value = jnp.einsum(
            "cs,cd->sd", mixed, out_weight[layer_index], preferred_element_type=jnp.float32
        )
        branch = branch_sum(partial_value) + out_bias[layer_index]
        saved = (
            normed,
            norm_saved,
            padded,
            short_out,
            chan_prod,
            prod_re,
            prod_im,
            long_out,
            mixed,
        )
        return (resid + pad_mask[:, None] * branch, saved)

    def mlp_forward(resid, pad_mask, layer_index):
        normed, norm_saved = norm_forward(
            resid, jnp.stack([norm_gain[layer_index, 1], norm_bias[layer_index, 1]])
        )
        pre_act = (
            jnp.dot(normed, up_weight[layer_index], preferred_element_type=jnp.float32)
            + up_bias[layer_index]
        )
        activated = jax.nn.gelu(pre_act, approximate=False).astype(jnp.bfloat16)
        partial_value = jnp.dot(
            activated, down_weight[layer_index], preferred_element_type=jnp.float32
        )
        branch = branch_sum(partial_value) + down_bias[layer_index]
        return (resid + pad_mask[:, None] * branch, (normed, norm_saved, pre_act, activated))

    def mlp_backward(grad_resid, pad_mask, layer_index, saved):
        normed, norm_saved, pre_act, activated = saved
        grad_branch = pad_mask[:, None] * grad_resid
        g_down_bias = jnp.sum(grad_branch, axis=0)
        grad_full = branch_grad(grad_branch.astype(jnp.bfloat16))
        g_down_weight = jnp.einsum(
            "sf,sd->fd", activated, grad_full, preferred_element_type=jnp.float32
        )
        grad_act = jnp.einsum(
            "sd,fd->sf", grad_full, down_weight[layer_index], preferred_element_type=jnp.float32
        )
        unused_value, gelu_pull = jax.vjp(
            lambda inner: jax.nn.gelu(inner, approximate=False), pre_act
        )
        grad_pre = gelu_pull(grad_act)[0]
        g_up_bias = jnp.sum(grad_pre, axis=0)
        pre_low = grad_pre.astype(jnp.bfloat16)
        g_up_weight = jnp.einsum("sd,sf->df", normed, pre_low, preferred_element_type=jnp.float32)
        grad_normed = jnp.einsum(
            "sf,df->sd", pre_low, up_weight[layer_index], preferred_element_type=jnp.float32
        )
        grad_own, g_gain, g_bias = norm_backward(grad_normed, norm_saved)
        return (
            grad_resid + grad_own,
            (g_up_weight, g_down_weight, g_gain, g_bias, g_up_bias, g_down_bias),
        )

    mixer_acc = [None] * layer_count
    mlp_acc = [None] * layer_count
    outputs = []
    input_grads = []
    for micro_index in range(micro_count):
        pad_mask = (positions_dev < lengths[micro_index, 0]).astype(jnp.float32)
        resid = tokens[micro_index, 0].astype(jnp.float32)
        layer_inputs = []
        layer_saved = []
        for layer_index in range(layer_count):
            layer_inputs.append(resid)
            resid, mix_saved = mixer_forward(resid, pad_mask, layer_index)
            layer_inputs.append(resid)
            resid, mlp_saved = mlp_forward(resid, pad_mask, layer_index)
            layer_saved.append((mix_saved, mlp_saved))
        outputs.append(resid)
        grad_resid = cotangent[micro_index, 0].astype(jnp.float32)
        for layer_index in reversed(range(layer_count)):
            mlp_saved = mlp_forward(layer_inputs[2 * layer_index + 1], pad_mask, layer_index)[1]
            grad_resid, mlp_grads = mlp_backward(grad_resid, pad_mask, layer_index, mlp_saved)
            mix_saved = mixer_forward(layer_inputs[2 * layer_index], pad_mask, layer_index)[1]
            (
                mixer_normed,
                mixer_norm_saved,
                mixer_padded,
                mixer_short_out,
                mixer_chan_prod,
                mixer_prod_re,
                mixer_prod_im,
                mixer_long_out,
                mixer_mixed,
            ) = mix_saved
            mixer_filt_re, mixer_filt_im, mixer_filter_pull, mixer_skip_cols = filters[layer_index]
            mixer_grad_branch = pad_mask[:, None] * grad_resid
            g_out_bias = jnp.sum(mixer_grad_branch, axis=0)
            mixer_grad_full = branch_grad(mixer_grad_branch.astype(jnp.bfloat16))
            g_out_weight = jnp.einsum(
                "cs,sd->cd", mixer_mixed, mixer_grad_full, preferred_element_type=jnp.float32
            )
            grad_mixed = jnp.einsum(
                "sd,cd->cs",
                mixer_grad_full,
                out_weight[layer_index],
                preferred_element_type=jnp.float32,
            )
            grad_long = grad_mixed * mixer_short_out[0]
            grad_gate = grad_mixed * mixer_long_out
            chan_grad = to_channels(grad_long)
            grad_re, grad_im = to_spectrum(chan_grad, basis)
            back_re, back_im = complex_mul(grad_re, grad_im, mixer_filt_re, -mixer_filt_im)
            chan_dprod = (
                from_spectrum(back_re, back_im, basis) + mixer_skip_cols[:, None] * chan_grad
            )
            corr_re, corr_im = complex_mul(grad_re, grad_im, mixer_prod_re, -mixer_prod_im)
            grad_filter = from_spectrum(corr_re, corr_im, basis)
            g_skip = jnp.sum(chan_grad * mixer_chan_prod, axis=1)
            grad_product = to_positions(chan_dprod)
            grad_short = jnp.stack(
                [grad_gate, grad_product * mixer_short_out[2], grad_product * mixer_short_out[1]]
            )
            g_short_bias = jnp.sum(grad_short, axis=2)
            g_taps = jnp.stack(
                [
                    jnp.sum(grad_short * mixer_padded[:, :, 2:], axis=2),
                    jnp.sum(grad_short * mixer_padded[:, :, 1 : rows_dev + 1], axis=2),
                    jnp.sum(grad_short * mixer_padded[:, :, :rows_dev], axis=2),
                ],
                axis=1,
            )
            next_rim = shifted(grad_short[:, :, :2], "seq", -1)
            extended = jnp.concatenate([grad_short, next_rim], axis=2)
            mixer_taps = short_taps[layer_index]
            grad_streams = (
                mixer_taps[:, 0][:, :, None] * extended[:, :, :rows_dev]
                + mixer_taps[:, 1][:, :, None] * extended[:, :, 1 : rows_dev + 1]
                + mixer_taps[:, 2][:, :, None] * extended[:, :, 2:]
            )
            g_in_bias = jnp.sum(grad_streams, axis=2)
            streams_low = grad_streams.astype(jnp.bfloat16)
            g_in_weight = jnp.einsum(
                "sd,kcs->kdc", mixer_normed, streams_low, preferred_element_type=jnp.float32
            )
            mixer_grad_normed = jnp.einsum(
                "kcs,kdc->sd",
                streams_low,
                in_weight[layer_index],
                preferred_element_type=jnp.float32,
            )
            mixer_grad_own, mixer_g_gain, mixer_g_bias = norm_backward(
                mixer_grad_normed, mixer_norm_saved
            )
            grads = (
                g_in_weight,
                g_out_weight,
                mixer_g_gain,
                mixer_g_bias,
                g_in_bias,
                g_taps,
                g_short_bias,
                g_skip,
                g_out_bias,
                grad_filter,
            )
            grad_resid, mix_grads = (grad_resid + mixer_grad_own, grads)
            if mixer_acc[layer_index] is None:
                mixer_acc[layer_index] = mix_grads
                mlp_acc[layer_index] = mlp_grads
            else:
                mixer_acc[layer_index] = jax.tree.map(jnp.add, mixer_acc[layer_index], mix_grads)
                mlp_acc[layer_index] = jax.tree.map(jnp.add, mlp_acc[layer_index], mlp_grads)
        input_grads.append(grad_resid)
    filter_grads = [
        filters[layer_index][2](mixer_acc[layer_index][9]) for layer_index in range(layer_count)
    ]
    skip_start = chan_start + col_start

    def stack_mix(member):
        return jnp.stack([mixer_acc[layer_index][member] for layer_index in range(layer_count)])

    def stack_mlp(member):
        return jnp.stack([mlp_acc[layer_index][member] for layer_index in range(layer_count)])

    def stack_filter(member):
        return jnp.stack([filter_grads[layer_index][member] for layer_index in range(layer_count)])

    big_grads = (
        lax.psum_scatter(stack_mix(0), ("seq", "dp"), scatter_dimension=2, tiled=True),
        lax.psum_scatter(stack_mix(1), ("seq", "dp"), scatter_dimension=2, tiled=True),
        lax.psum_scatter(stack_mlp(0), ("seq", "dp"), scatter_dimension=1, tiled=True),
        lax.psum_scatter(stack_mlp(1), ("seq", "dp"), scatter_dimension=2, tiled=True),
    )
    gain_grads = jnp.stack([stack_mix(2), stack_mlp(2)], axis=1)
    bias_grads = jnp.stack([stack_mix(3), stack_mlp(3)], axis=1)
    small = lax.psum(
        (
            place(gain_grads, chan_start, full_width, 2),
            place(bias_grads, chan_start, full_width, 2),
            place(stack_mix(4), chan_start, full_width, 2),
            place(stack_mix(5), chan_start, full_width, 3),
            place(stack_mix(6), chan_start, full_width, 2),
            place(stack_mix(7), skip_start, full_width, 1),
            place(stack_mix(8), chan_start, full_width, 1),
            place(stack_mlp(4), chan_index * hidden_width, hidden_width * chan_parts, 1),
            place(stack_mlp(5), chan_start, full_width, 1),
            stack_filter(0),
            stack_filter(1),
            stack_filter(2),
            place(stack_filter(3), skip_start, full_width, 2),
        ),
        ("seq", "chan", "dp"),
    )
    out_act = jnp.stack(outputs)[:, None]
    grad_tokens = jnp.stack(input_grads)[:, None]
    return (
        out_act,
        grad_tokens,
        big_grads[0],
        big_grads[1],
        big_grads[2],
        big_grads[3],
        small[0],
        small[1],
        small[2],
        small[3],
        small[4],
        small[5],
        small[6],
        small[7],
        small[8],
        small[9],
        small[10],
        small[11],
        small[12],
    )


F32 = jnp.float32
BF16 = jnp.bfloat16
MESH = pl.DeviceIdType.MESH
ORDERS = (("x", "y", "l", "h"), ("y", "l", "x", "h"), ("l", "x", "y", "h"))


def half_tables(count):
    odd = 2 * np.arange(count, dtype=np.int64) + 1
    angle = np.outer(odd, odd) % (8 * count) * (math.pi / (4 * count))
    twist = odd * (math.pi / (4 * count))
    return np.cos(angle), np.sin(angle), np.cos(twist)[:, None], np.sin(twist)[:, None]


def mesh_bits():
    seq, dp = lax.axis_index("seq"), lax.axis_index("dp")
    return {"x": dp, "y": lax.rem(seq, 2), "l": lax.rem(seq // 2, 2), "h": seq // 4}


def mesh_peers():
    seq, dp = lax.axis_index("seq"), lax.axis_index("dp")
    bits = mesh_bits()
    return {
        "x": {"dp": 1 - dp},
        "y": {"seq": seq + 1 - 2 * bits["y"]},
        "l": {"seq": seq + 2 - 4 * bits["l"]},
        "h": {"seq": seq + 4 - 8 * bits["h"]},
    }


def greet(devices):
    barrier = pltpu.get_barrier_semaphore()
    for device in devices:
        pl.semaphore_signal(barrier, inc=1, device_id=device, device_id_type=MESH)
    pl.semaphore_wait(barrier, len(devices))


def scatter_kernel(chunk_width, parts_ref, out_ref, recv1, recv2, recv3, recv4, send_sem, recv_sem):
    layers, rows, columns = parts_ref.shape[0], parts_ref.shape[5], parts_ref.shape[6]
    per_layer = columns // chunk_width
    bits, peers = mesh_bits(), mesh_peers()
    greet([peers[axis] for axis in "xylh"])
    received = (recv1, recv2, recv3, recv4)
    chunks = [(layer, part) for layer in range(layers) for part in range(per_layer)]

    def axes_left(chunk, stage):
        order = ORDERS[chunk % len(ORDERS)]
        return [axis for axis in "hlyx" if axis not in order[:stage]]

    def held(chunk, stage, index):
        layer, part = chunks[chunk]
        if stage == 0:
            return parts_ref.at[
                (layer, *index, slice(None), pl.ds(part * chunk_width, chunk_width))
            ]
        return received[stage - 1].at[(chunk, *index)]

    def copies(chunk, stage):
        axis = ORDERS[chunk % len(ORDERS)][stage]
        left = axes_left(chunk, stage)
        index = tuple(1 - bits[axis] if name == axis else slice(None) for name in left)
        return pltpu.make_async_remote_copy(
            src_ref=held(chunk, stage, index),
            dst_ref=received[stage].at[chunk],
            send_sem=send_sem.at[chunk, stage],
            recv_sem=recv_sem.at[chunk, stage],
            device_id=peers[axis],
            device_id_type=MESH,
        )

    def combine(chunk, stage):
        axis = ORDERS[chunk % len(ORDERS)][stage]
        left = axes_left(chunk, stage)
        place = left.index(axis)
        layer, part = chunks[chunk]
        for flat in range(2 ** (len(left) - 1)):
            kept = [flat >> shift & 1 for shift in reversed(range(len(left) - 1))]
            mine = tuple(kept[:place] + [bits[axis]] + kept[place:])
            own = held(chunk, stage, mine)[...].astype(F32)
            total = own + received[stage].at[(chunk, *kept)][...].astype(F32)
            if stage == 3:
                out_ref[layer, :, pl.ds(part * chunk_width, chunk_width)] = total
            else:
                received[stage].at[(chunk, *kept)][...] = total.astype(BF16)

    slots = sorted(
        ((chunk // 3 + (1.0, 1.5, 1.75, 1.875)[stage], chunk, stage))
        for chunk in range(len(chunks))
        for stage in range(4)
    )
    for chunk in range(len(chunks)):
        copies(chunk, 0).start()
    for _, chunk, stage in slots:
        copies(chunk, stage).wait_recv()
        combine(chunk, stage)
        if stage < 3:
            copies(chunk, stage + 1).start()
    for _, chunk, stage in slots:
        copies(chunk, stage).wait_send()


def scatter_sum(parts):
    layers, rows, columns = parts.shape[0], parts.shape[5], parts.shape[6]
    chunk_width = columns // 6
    count = layers * 6
    return pl.pallas_call(
        functools.partial(scatter_kernel, chunk_width),
        out_shape=jax.ShapeDtypeStruct((layers, rows, columns), F32),
        in_specs=[pl.BlockSpec(memory_space=pltpu.VMEM)],
        out_specs=pl.BlockSpec(memory_space=pltpu.VMEM),
        scratch_shapes=[
            pltpu.VMEM((count, *[2] * (3 - stage), rows, chunk_width), BF16) for stage in range(4)
        ]
        + [pltpu.SemaphoreType.DMA((count, 4)), pltpu.SemaphoreType.DMA((count, 4))],
        compiler_params=pltpu.CompilerParams(
            collective_id=1, has_side_effects=True, vmem_limit_bytes=58 << 20
        ),
        name="scatter_sum",
    )(parts)


def small_kernel(parts_ref, out_ref, recv, send_sem, recv_sem, core_sem):
    seq, dp, chan = lax.axis_index("seq"), lax.axis_index("dp"), lax.axis_index("chan")
    count = parts_ref.shape[0]
    me = seq * 2 + dp
    others = [lax.rem(me + step, count) for step in range(1, count)]
    devices = [{"seq": other // 2, "dp": lax.rem(other, 2)} for other in others]
    greet(devices + [{"chan": 1 - chan}])
    first = []
    for step in range(count - 1):
        first.append(
            pltpu.make_async_remote_copy(
                src_ref=parts_ref.at[others[step]],
                dst_ref=recv.at[step],
                send_sem=send_sem.at[0, step],
                recv_sem=recv_sem.at[0, step],
                device_id=devices[step],
                device_id_type=MESH,
            )
        )
        first[-1].start()
    total = parts_ref[me]
    for step in range(count - 1):
        first[step].wait()
        total = total + recv[step]
    out_ref[chan, me] = total
    second = []
    for step in range(count - 1):
        second.append(
            pltpu.make_async_remote_copy(
                src_ref=out_ref.at[chan, me],
                dst_ref=out_ref.at[chan, me],
                send_sem=send_sem.at[1, step],
                recv_sem=recv_sem.at[1, step],
                device_id=devices[step],
                device_id_type=MESH,
            )
        )
        second[-1].start()
    for copy in second:
        copy.wait()
    last = pltpu.make_async_remote_copy(
        src_ref=out_ref.at[chan],
        dst_ref=out_ref.at[chan],
        send_sem=core_sem.at[0],
        recv_sem=core_sem.at[1],
        device_id={"chan": 1 - chan},
        device_id_type=MESH,
    )
    last.start()
    last.wait()


def small_sum(parts):
    count, rows, lanes = parts.shape
    return pl.pallas_call(
        small_kernel,
        out_shape=jax.ShapeDtypeStruct((2, count, rows, lanes), F32),
        in_specs=[pl.BlockSpec(memory_space=pltpu.VMEM)],
        out_specs=pl.BlockSpec(memory_space=pltpu.VMEM),
        scratch_shapes=[
            pltpu.VMEM((count - 1, rows, lanes), F32),
            pltpu.SemaphoreType.DMA((2, count - 1)),
            pltpu.SemaphoreType.DMA((2, count - 1)),
            pltpu.SemaphoreType.DMA((2,)),
        ],
        compiler_params=pltpu.CompilerParams(collective_id=2, has_side_effects=True),
        name="small_sum",
    )(parts)


def local_fast(
    tokens,
    lengths,
    cotangent,
    norm_gain,
    norm_bias,
    in_weight,
    in_bias,
    short_taps,
    short_bias,
    skip_gain,
    out_weight,
    out_bias,
    up_weight,
    up_bias,
    down_weight,
    down_bias,
    filter_in,
    filter_bias,
    filter_freq,
    filter_out,
    decay_rate,
):
    micro, rows_dev, half = tokens.shape[0], tokens.shape[2], tokens.shape[3]
    layers = norm_gain.shape[0]
    hidden = up_weight.shape[2]
    seq_parts = lax.axis_size("seq")
    seq_index, chan_index = lax.axis_index("seq"), lax.axis_index("chan")
    width = 2 * half
    rows = micro * rows_dev
    length = rows_dev * seq_parts
    block = half // seq_parts
    col_start, chan_start = seq_index * block, chan_index * half

    def both(value):
        return lax.all_gather(value, "chan", axis=value.ndim - 1, tiled=True)

    def pair_sum(value):
        return value + lax.ppermute(value.astype(BF16), "chan", [(0, 1), (1, 0)]).astype(F32)

    def own_half(value):
        return lax.dynamic_slice_in_dim(value, chan_start, half, value.ndim - 1)

    def mm(spec, left, right):
        return jnp.einsum(spec, left, right, preferred_element_type=F32)

    streams_in = both(jnp.stack([tokens, cotangent]))
    resid = streams_in[0, :, 0].reshape(rows, width).astype(F32)
    grad = streams_in[1, :, 0].reshape(rows, width).astype(F32)
    rows_full = both(
        jnp.concatenate(
            [
                norm_gain.reshape(-1, half),
                norm_bias.reshape(-1, half),
                out_bias,
                down_bias,
            ],
            axis=0,
        )
    )
    gains = rows_full[: 2 * layers].reshape(layers, 2, width)
    biases = rows_full[2 * layers : 4 * layers].reshape(layers, 2, width)
    out_b, down_b = rows_full[4 * layers : 5 * layers], rows_full[5 * layers :]
    ids = seq_index * rows_dev + jnp.arange(rows_dev, dtype=jnp.int32)
    mask = (ids[None, :] < lengths[:, :1]).astype(F32).reshape(rows, 1)

    cos_np, sin_np, turn_c, turn_s = half_tables(length)
    cos_t, sin_t = jnp.asarray(cos_np, BF16), jnp.asarray(sin_np, BF16)
    turn_c, turn_s = jnp.asarray(turn_c, F32), jnp.asarray(turn_s, F32)
    table, steps_norm = positions(length, filter_in.shape[1])

    def split(value):
        high = value.astype(BF16)
        return high, (value - high.astype(F32)).astype(BF16)

    def transform(value):
        return mm("kt,tc->kc", cos_t, value), mm("kt,tc->kc", sin_t, value)

    def transform_fine(value):
        high, low = split(value)
        pair_c, pair_s = transform(jnp.concatenate([high, low], axis=1))
        n = value.shape[1]
        return pair_c[:, :n] + pair_c[:, n:], pair_s[:, :n] + pair_s[:, n:]

    def make_filter(w_in, w_bias, w_freq, w_out, decay):
        wave = jnp.sin(w_freq * (jnp.dot(table, w_in, precision=HIGH) + w_bias))
        return jnp.dot(wave, w_out, precision=HIGH) * jnp.exp(-steps_norm[:, None] * decay[None, :])

    filters = []
    for layer in range(layers):
        w_out = lax.dynamic_slice_in_dim(filter_out[layer], col_start, block, 1)
        decay = lax.dynamic_slice_in_dim(decay_rate[layer], col_start, block, 0)
        skip = lax.dynamic_slice_in_dim(skip_gain[layer], col_start, block, 0)
        long_filter, pull = jax.vjp(
            lambda *leaves, decay=decay: make_filter(*leaves, decay),
            filter_in[layer],
            filter_bias[layer],
            filter_freq[layer],
            w_out,
        )
        filt_c, filt_s = transform_fine(long_filter)
        filt_re = (filt_c * turn_c + filt_s * turn_s) / length
        filt_im = (filt_c * turn_s - filt_s * turn_c) / length
        filters.append(
            (jnp.tile(filt_re, (1, micro)), jnp.tile(filt_im, (1, micro)), pull, jnp.tile(skip, micro))
        )

    def to_channels(value):
        shaped = value.astype(BF16).reshape(micro, rows_dev, seq_parts, block)
        shaped = shaped.transpose(2, 1, 0, 3).reshape(seq_parts, rows_dev, micro * block)
        return lax.all_to_all(shaped, "seq", 0, 0, tiled=True).reshape(length, micro * block)

    def to_positions(value):
        shaped = value.astype(BF16).reshape(seq_parts, rows_dev, micro * block)
        moved = lax.all_to_all(shaped, "seq", 0, 0, tiled=True)
        moved = moved.reshape(seq_parts, rows_dev, micro, block).transpose(2, 1, 0, 3)
        return moved.reshape(micro, rows_dev, half).astype(F32)

    def norm_forward(value, gain, bias):
        centred = value - jnp.mean(value, axis=1, keepdims=True)
        rstd = lax.rsqrt(jnp.mean(centred * centred, axis=1, keepdims=True) + EPS)
        scaled = centred * rstd
        return (scaled * gain + bias).astype(BF16), scaled, rstd

    def norm_backward(grad_value, scaled, rstd, gain):
        weighted = grad_value * gain
        back = rstd * (
            weighted
            - jnp.mean(weighted, axis=1, keepdims=True)
            - scaled * jnp.mean(weighted * scaled, axis=1, keepdims=True)
        )
        return back, own_half(jnp.sum(grad_value * scaled, axis=0)), own_half(jnp.sum(grad_value, axis=0))

    def three(value):
        return value.reshape(micro, rows_dev, 3, half)

    saved = []
    for layer in range(layers):
        normed, scaled, rstd = norm_forward(resid, gains[layer, 0], biases[layer, 0])
        streams = three(mm("sd,kdc->skc", normed, in_weight[layer])) + in_bias[layer]
        rim = shifted(streams[:, rows_dev - 2 :], "seq", 1)
        padded = jnp.concatenate([rim, streams], axis=1)
        taps = short_taps[layer]
        short = (
            taps[:, 0] * padded[:, 2:]
            + taps[:, 1] * padded[:, 1:-1]
            + taps[:, 2] * padded[:, :-2]
            + short_bias[layer]
        )
        signal = to_channels(short[:, :, 1] * short[:, :, 2])
        filt_re, filt_im, pull, skip = filters[layer]
        prod_c, prod_s = transform(signal)
        conv = mm("tk,kc->tc", cos_t, (prod_c * filt_re + prod_s * filt_im).astype(BF16)) + mm(
            "tk,kc->tc", sin_t, (prod_s * filt_re - prod_c * filt_im).astype(BF16)
        )
        long_out = to_positions(conv + skip * signal.astype(F32))
        mixed = (short[:, :, 0] * long_out).astype(BF16).reshape(rows, half)
        resid = resid + mask * (pair_sum(mm("sc,cd->sd", mixed, out_weight[layer])) + out_b[layer])
        mix_saved = (normed, scaled, rstd, padded, short, signal, prod_c, prod_s, long_out, mixed)
        normed, scaled, rstd = norm_forward(resid, gains[layer, 1], biases[layer, 1])
        pre_act = mm("sd,df->sf", normed, up_weight[layer]) + up_bias[layer]
        activated = jax.nn.gelu(pre_act, approximate=False).astype(BF16)
        resid = resid + mask * (pair_sum(mm("sf,fd->sd", activated, down_weight[layer])) + down_b[layer])
        saved.append((mix_saved, (normed, scaled, rstd, pre_act, activated)))
    out_act = own_half(resid)

    big, small = [None] * layers, [None] * layers
    for layer in reversed(range(layers)):
        mix_saved, (normed, scaled, rstd, pre_act, activated) = saved[layer]
        branch = mask * grad
        g_down_bias = own_half(jnp.sum(branch, axis=0))
        low = branch.astype(BF16)
        g_down = mm("sd,sf->df", low, activated).astype(BF16)
        grad_act = mm("sd,fd->sf", low, down_weight[layer])
        cdf = 0.5 * (1.0 + lax.erf(pre_act * math.sqrt(0.5)))
        slope = cdf + pre_act * jnp.exp(-0.5 * pre_act * pre_act) * (1.0 / math.sqrt(2.0 * math.pi))
        grad_pre = grad_act * slope
        g_up_bias = jnp.sum(grad_pre, axis=0)
        pre_low = grad_pre.astype(BF16)
        g_up = mm("sd,sf->df", normed, pre_low).astype(BF16)
        grad_normed = pair_sum(mm("sf,df->sd", pre_low, up_weight[layer]))
        back, g_gain1, g_bias1 = norm_backward(grad_normed, scaled, rstd, gains[layer, 1])
        grad = grad + back

        normed, scaled, rstd, padded, short, signal, prod_c, prod_s, long_out, mixed = mix_saved
        filt_re, filt_im, pull, skip = filters[layer]
        branch = mask * grad
        g_out_bias = own_half(jnp.sum(branch, axis=0))
        low = branch.astype(BF16)
        g_out = mm("sd,sc->dc", low, mixed).astype(BF16)
        grad_mixed = mm("sd,cd->sc", low, out_weight[layer]).reshape(micro, rows_dev, half)
        grad_gate = grad_mixed * long_out
        chan_grad = to_channels(grad_mixed * short[:, :, 0])
        grad_c, grad_s = transform(chan_grad)
        chan_dprod = mm(
            "tk,kc->tc", cos_t, (grad_c * filt_re - grad_s * filt_im).astype(BF16)
        ) + mm("tk,kc->tc", sin_t, (grad_s * filt_re + grad_c * filt_im).astype(BF16))
        wide_grad = chan_grad.astype(F32)
        g_skip = jnp.sum((wide_grad * signal.astype(F32)).reshape(length, micro, block), axis=(0, 1))
        grad_product = to_positions(chan_dprod + skip * wide_grad)

        def over_micro(value):
            return jnp.sum(value.reshape(length, micro, block), axis=1)

        corr_re = over_micro(grad_c * prod_c + grad_s * prod_s) / length
        corr_im = over_micro(grad_c * prod_s - grad_s * prod_c) / length
        corr_c = split(corr_re * turn_c + corr_im * turn_s)
        corr_s = split(corr_re * turn_s - corr_im * turn_c)
        grad_filter = mm("tk,kc->tc", cos_t, jnp.concatenate(corr_c, axis=1)) + mm(
            "tk,kc->tc", sin_t, jnp.concatenate(corr_s, axis=1)
        )
        grad_filter = grad_filter[:, :block] + grad_filter[:, block:]
        g_fin, g_fbias, g_ffreq, g_fout = pull(grad_filter)

        grad_short = jnp.stack(
            [grad_gate, grad_product * short[:, :, 2], grad_product * short[:, :, 1]], axis=2
        )
        g_short_bias = jnp.sum(grad_short, axis=(0, 1))
        g_taps = jnp.stack(
            [
                jnp.sum(grad_short * padded[:, 2:], axis=(0, 1)),
                jnp.sum(grad_short * padded[:, 1:-1], axis=(0, 1)),
                jnp.sum(grad_short * padded[:, :-2], axis=(0, 1)),
            ],
            axis=1,
        )
        extended = jnp.concatenate([grad_short, shifted(grad_short[:, :2], "seq", -1)], axis=1)
        taps = short_taps[layer]
        grad_streams = (
            taps[:, 0] * extended[:, :-2] + taps[:, 1] * extended[:, 1:-1] + taps[:, 2] * extended[:, 2:]
        )
        g_in_bias = jnp.sum(grad_streams, axis=(0, 1))
        streams_low = grad_streams.astype(BF16).reshape(rows, 3 * half)
        g_in = mm("sd,sc->dc", normed, streams_low).astype(BF16)
        grad_normed = pair_sum(
            mm("skc,kdc->sd", streams_low.reshape(rows, 3, half), in_weight[layer])
        )
        back, g_gain0, g_bias0 = norm_backward(grad_normed, scaled, rstd, gains[layer, 0])
        grad = grad + back
        big[layer] = jnp.concatenate([g_in, g_out, g_up, g_down], axis=1)
        placed = place(jnp.concatenate([g_skip[None], g_fout], axis=0), col_start, half, 1)
        spread = jnp.concatenate([g_fin.reshape(-1), g_fbias, g_ffreq])
        spread_rows = -(-spread.shape[0] // half)
        spread = jnp.pad(spread, (0, spread_rows * half - spread.shape[0]))
        small[layer] = jnp.concatenate(
            [
                jnp.stack([g_gain0, g_gain1, g_bias0, g_bias1]),
                g_in_bias,
                g_taps.reshape(-1, half),
                g_short_bias,
                g_out_bias[None],
                g_down_bias[None],
                g_up_bias.reshape(-1, half),
                placed,
                spread.reshape(spread_rows, half),
            ],
            axis=0,
        )
    grad_tokens = own_half(grad)

    parts = jnp.stack(big).reshape(layers, 2, 2, 2, 2, width // 16, -1)
    scattered = scatter_sum(parts)
    flat = jnp.concatenate(small, axis=0).reshape(-1)
    lanes = 128
    piece = -(-flat.shape[0] // (16 * lanes * 8)) * 8
    flat_parts = jnp.pad(flat, (0, 16 * piece * lanes - flat.shape[0])).reshape(16, piece, lanes)
    summed = small_sum(flat_parts).reshape(2, -1)[:, : flat.shape[0]].reshape(2, layers, -1, half)

    def joined(start, stop, shape):
        value = summed[:, :, start:stop]
        value = value.transpose(1, 2, 0, 3).reshape(layers, stop - start, width)
        return value.reshape((layers, *shape, width))

    hid_rows = hidden // half
    up_value = summed[:, :, 21 : 21 + hid_rows].transpose(1, 0, 2, 3).reshape(layers, 2 * hidden)
    after = 21 + hid_rows
    bands, feat = filter_in.shape[1], filter_in.shape[2]
    spread = jnp.sum(summed[:, :, after + 1 + feat :], axis=0).reshape(layers, -1)
    in_cols, out_cols = 3 * half, 4 * half
    g_in = scattered[:, :, :in_cols].reshape(layers, width // 16, 3, half).transpose(0, 2, 1, 3)
    g_out = scattered[:, :, in_cols:out_cols].transpose(0, 2, 1)
    g_up = scattered[:, :, out_cols : out_cols + hidden]
    g_down = scattered[:, :, out_cols + hidden :].transpose(0, 2, 1)
    return (
        out_act.reshape(micro, 1, rows_dev, half),
        grad_tokens.reshape(micro, 1, rows_dev, half),
        g_in,
        g_out,
        g_up,
        g_down,
        joined(0, 2, (2,)),
        joined(2, 4, (2,)),
        joined(4, 7, (3,)),
        joined(7, 16, (3, 3)),
        joined(16, 19, (3,)),
        joined(after, after + 1, ()),
        joined(19, 20, ()),
        up_value,
        joined(20, 21, ()),
        spread[:, : bands * feat].reshape(layers, bands, feat),
        spread[:, bands * feat : bands * feat + feat],
        spread[:, bands * feat + feat : bands * feat + 2 * feat],
        joined(after + 1, after + 1 + feat, (feat,)),
    )


def solution(mesh):
    in_specs = (
        P(None, "dp", "seq", "chan"),
        P(None, "dp"),
        P(None, "dp", "seq", "chan"),
        P(None, None, "chan"),
        P(None, None, "chan"),
        P(None, None, None, "chan"),
        P(None, None, "chan"),
        P(None, None, None, "chan"),
        P(None, None, "chan"),
        P(None, "chan"),
        P(None, "chan", None),
        P(None, "chan"),
        P(None, None, "chan"),
        P(None, "chan"),
        P(None, "chan", None),
        P(None, "chan"),
        P(),
        P(),
        P(),
        P(None, None, "chan"),
        P(None, "chan"),
    )
    out_specs = (
        P(None, "dp", "seq", "chan"),
        P(None, "dp", "seq", "chan"),
        P(None, None, ("seq", "dp"), "chan"),
        P(None, "chan", ("seq", "dp")),
        P(None, ("seq", "dp"), "chan"),
        P(None, "chan", ("seq", "dp")),
        P(),
        P(),
        P(),
        P(),
        P(),
        P(),
        P(),
        P(),
        P(),
        P(),
        P(),
        P(),
        P(),
    )
    def entry(*args):
        fits = args[0].shape[2] * mesh.shape["seq"] <= 2048 and mesh.shape["seq"] == 8 and mesh.shape["dp"] == 2
        return (local_fast if fits else local)(*args)

    return jax.shard_map(entry, mesh=mesh, in_specs=in_specs, out_specs=out_specs, check_vma=False)
```

```python
import functools
import math
import types

import jax
import jax.numpy as jnp
import numpy as np
from jax import lax
from jax.experimental import pallas as pl
from jax.experimental.pallas import tpu as pltpu
from jax.sharding import PartitionSpec as P

EPS = 1e-05
HIGH = lax.Precision.HIGHEST


def shifted(value, axis, steps):
    count = lax.axis_size(axis)
    initial, last = (max(0, -steps), min(count, count - steps))
    return lax.ppermute(value, axis, [(source, source + steps) for source in range(initial, last)])


def positions(seq_length, emb_width):
    band_count = (emb_width - 1) // 2
    step_ids = jnp.arange(seq_length, dtype=jnp.float32)
    steps_norm = step_ids / seq_length
    band_freq = jnp.linspace(0.0001, band_count - 1, band_count).astype(jnp.float32)
    phases = 2.0 * math.pi * steps_norm[:, None] * band_freq[None, :]
    table = jnp.concatenate([steps_norm[:, None], jnp.cos(phases), -jnp.sin(phases)], axis=1)
    return (table, steps_norm)


def angle_table(row_count, col_count, modulus):
    product = (
        jnp.arange(row_count, dtype=jnp.int32)[:, None]
        * jnp.arange(col_count, dtype=jnp.int32)[None, :]
        % modulus
    )
    theta = product.astype(jnp.float32) * (2.0 * math.pi / modulus)
    return (jnp.cos(theta), jnp.sin(theta))


def split_length(total_length):
    lesser = 2
    for candidate in range(2, math.isqrt(total_length) + 1, 2):
        if total_length % candidate == 0:
            lesser = candidate
    return (lesser, total_length // lesser)


def dft_basis(seq_length):
    padded_len = 2 * seq_length
    lesser, greater = split_length(padded_len)
    cos_p, sin_p = angle_table(lesser, lesser, lesser)
    cos_q, sin_q = angle_table(greater, greater, greater)
    twist_c, twist_s = angle_table(lesser, greater, padded_len)
    return (cos_p, sin_p, cos_q, sin_q, twist_c, twist_s)


def right_mul(left, table):
    return jnp.einsum("ckb,bj->ckj", left, table, precision=HIGH)


def to_spectrum(signal, basis):
    cos_p, sin_p, cos_q, sin_q, twist_c, twist_s = basis
    half = cos_p.shape[0] // 2
    blocks = signal.reshape(signal.shape[0], half, cos_q.shape[0])
    first_re = jnp.einsum("ka,cab->ckb", cos_p[:, :half], blocks, precision=HIGH)
    first_im = -jnp.einsum("ka,cab->ckb", sin_p[:, :half], blocks, precision=HIGH)
    turned_re = first_re * twist_c + first_im * twist_s
    turned_im = first_im * twist_c - first_re * twist_s
    spec_re = right_mul(turned_re, cos_q) + right_mul(turned_im, sin_q)
    spec_im = right_mul(turned_im, cos_q) - right_mul(turned_re, sin_q)
    return (spec_re, spec_im)


def from_spectrum(spec_re, spec_im, basis):
    cos_p, sin_p, cos_q, sin_q, twist_c, twist_s = basis
    half = cos_p.shape[0] // 2
    back_re = right_mul(spec_re, cos_q) - right_mul(spec_im, sin_q)
    back_im = right_mul(spec_im, cos_q) + right_mul(spec_re, sin_q)
    turned_re = back_re * twist_c - back_im * twist_s
    turned_im = back_im * twist_c + back_re * twist_s
    signal = jnp.einsum("ak,ckb->cab", cos_p[:half], turned_re, precision=HIGH) - jnp.einsum(
        "ak,ckb->cab", sin_p[:half], turned_im, precision=HIGH
    )
    return signal.reshape(signal.shape[0], half * cos_q.shape[0]) / (
        cos_p.shape[0] * cos_q.shape[0]
    )


def complex_mul(left_re, left_im, right_re, right_im):
    return (left_re * right_re - left_im * right_im, left_re * right_im + left_im * right_re)


def filter_block(table, steps_norm, weight_in, bias_in, freq_in, cols_in, decay_cols):
    hidden = jnp.sin(freq_in * (jnp.dot(table, weight_in, precision=HIGH) + bias_in))
    raw = jnp.einsum("lf,fc->cl", hidden, cols_in, precision=HIGH)
    return raw * jnp.exp(-decay_cols[:, None] * steps_norm[None, :])


def to_channels(block):
    parts = lax.axis_size("seq")
    shaped = block.reshape(parts, block.shape[0] // parts, block.shape[1])
    moved = lax.all_to_all(
        shaped.astype(jnp.bfloat16), "seq", split_axis=0, concat_axis=2, tiled=True
    ).astype(shaped.dtype)
    return moved.reshape(moved.shape[1], moved.shape[2])


def to_positions(block):
    shaped = block.reshape(1, block.shape[0], block.shape[1])
    moved = lax.all_to_all(
        shaped.astype(jnp.bfloat16), "seq", split_axis=2, concat_axis=0, tiled=True
    ).astype(shaped.dtype)
    return moved.reshape(moved.shape[0] * moved.shape[1], moved.shape[2])


def branch_sum(partial_value):
    return lax.psum_scatter(
        partial_value.astype(jnp.bfloat16), "chan", scatter_dimension=1, tiled=True
    ).astype(jnp.float32)


def branch_grad(grad_low):
    return lax.all_gather(grad_low, "chan", axis=1, tiled=True)


def place(values, start, full_width, axis):
    full_shape = list(values.shape)
    full_shape[axis] = full_width
    return lax.dynamic_update_slice_in_dim(jnp.zeros(full_shape, jnp.float32), values, start, axis)


def local(
    tokens,
    lengths,
    cotangent,
    norm_gain,
    norm_bias,
    in_weight,
    in_bias,
    short_taps,
    short_bias,
    skip_gain,
    out_weight,
    out_bias,
    up_weight,
    up_bias,
    down_weight,
    down_bias,
    filter_in,
    filter_bias,
    filter_freq,
    filter_out,
    decay_rate,
):
    micro_count = tokens.shape[0]
    rows_dev = tokens.shape[2]
    chan_width = tokens.shape[3]
    layer_count = norm_gain.shape[0]
    hidden_width = up_weight.shape[2]
    seq_parts = lax.axis_size("seq")
    chan_parts = lax.axis_size("chan")
    full_width = chan_width * chan_parts
    seq_length = rows_dev * seq_parts
    seq_index = lax.axis_index("seq")
    chan_index = lax.axis_index("chan")
    block_width = chan_width // seq_parts
    col_start = seq_index * block_width
    chan_start = chan_index * chan_width
    basis = dft_basis(seq_length)
    table, steps_norm = positions(seq_length, filter_in.shape[1])
    positions_dev = seq_index * rows_dev + jnp.arange(rows_dev, dtype=jnp.int32)
    filters = []
    for layer_index in range(layer_count):
        filter_cols = lax.dynamic_slice_in_dim(filter_out[layer_index], col_start, block_width, 1)
        decay_cols = lax.dynamic_slice_in_dim(decay_rate[layer_index], col_start, block_width, 0)
        skip_cols = lax.dynamic_slice_in_dim(skip_gain[layer_index], col_start, block_width, 0)

        def make_one(weight_in, bias_in, freq_in, cols_in, decay_cols=decay_cols):
            return filter_block(table, steps_norm, weight_in, bias_in, freq_in, cols_in, decay_cols)

        long_filter, filter_pull = jax.vjp(
            make_one,
            filter_in[layer_index],
            filter_bias[layer_index],
            filter_freq[layer_index],
            filter_cols,
        )
        filt_re, filt_im = to_spectrum(long_filter, basis)
        filters.append((filt_re, filt_im, filter_pull, skip_cols))

    def norm_forward(resid, gain_bias):
        full_rows, full_gb = (
            lax.all_gather(resid, "chan", axis=1, tiled=True),
            lax.all_gather(gain_bias, "chan", axis=1, tiled=True),
        )
        mean_row = jnp.mean(full_rows, axis=1, keepdims=True)
        centred = full_rows - mean_row
        rstd = lax.rsqrt(jnp.mean(centred * centred, axis=1, keepdims=True) + EPS)
        scaled = centred * rstd
        normed = (scaled * full_gb[0] + full_gb[1]).astype(jnp.bfloat16)
        return (normed, (scaled, rstd, full_gb[0]))

    def norm_backward(grad_partial, norm_saved):
        scaled, rstd, gain_row = norm_saved
        grad_rows = lax.psum(grad_partial.astype(jnp.bfloat16), "chan").astype(jnp.float32)
        grad_scaled = grad_rows * gain_row
        grad_full = rstd * (
            grad_scaled
            - jnp.mean(grad_scaled, axis=1, keepdims=True)
            - scaled * jnp.mean(grad_scaled * scaled, axis=1, keepdims=True)
        )
        grad_own = lax.dynamic_slice_in_dim(grad_full, chan_start, chan_width, 1)
        rows_own = lax.dynamic_slice_in_dim(grad_rows, chan_start, chan_width, 1)
        scaled_own = lax.dynamic_slice_in_dim(scaled, chan_start, chan_width, 1)
        return (grad_own, jnp.sum(rows_own * scaled_own, axis=0), jnp.sum(rows_own, axis=0))

    def mixer_forward(resid, pad_mask, layer_index):
        normed, norm_saved = norm_forward(
            resid, jnp.stack([norm_gain[layer_index, 0], norm_bias[layer_index, 0]])
        )
        streams = (
            jnp.einsum(
                "sd,kdc->kcs", normed, in_weight[layer_index], preferred_element_type=jnp.float32
            )
            + in_bias[layer_index][:, :, None]
        )
        rim = shifted(streams[:, :, rows_dev - 2 :], "seq", 1)
        padded = jnp.concatenate([rim, streams], axis=2)
        taps = short_taps[layer_index]
        short_out = (
            taps[:, 0][:, :, None] * padded[:, :, 2:]
            + taps[:, 1][:, :, None] * padded[:, :, 1 : rows_dev + 1]
            + taps[:, 2][:, :, None] * padded[:, :, :rows_dev]
            + short_bias[layer_index][:, :, None]
        )
        product = short_out[1] * short_out[2]
        chan_prod = to_channels(product)
        filt_re, filt_im, filter_pull, skip_cols = filters[layer_index]
        prod_re, prod_im = to_spectrum(chan_prod, basis)
        conv_re, conv_im = complex_mul(prod_re, prod_im, filt_re, filt_im)
        chan_out = from_spectrum(conv_re, conv_im, basis) + skip_cols[:, None] * chan_prod
        long_out = to_positions(chan_out)
        mixed = (short_out[0] * long_out).astype(jnp.bfloat16)
        partial_value = jnp.einsum(
            "cs,cd->sd", mixed, out_weight[layer_index], preferred_element_type=jnp.float32
        )
        branch = branch_sum(partial_value) + out_bias[layer_index]
        saved = (
            normed,
            norm_saved,
            padded,
            short_out,
            chan_prod,
            prod_re,
            prod_im,
            long_out,
            mixed,
        )
        return (resid + pad_mask[:, None] * branch, saved)

    def mlp_forward(resid, pad_mask, layer_index):
        normed, norm_saved = norm_forward(
            resid, jnp.stack([norm_gain[layer_index, 1], norm_bias[layer_index, 1]])
        )
        pre_act = (
            jnp.dot(normed, up_weight[layer_index], preferred_element_type=jnp.float32)
            + up_bias[layer_index]
        )
        activated = jax.nn.gelu(pre_act, approximate=False).astype(jnp.bfloat16)
        partial_value = jnp.dot(
            activated, down_weight[layer_index], preferred_element_type=jnp.float32
        )
        branch = branch_sum(partial_value) + down_bias[layer_index]
        return (resid + pad_mask[:, None] * branch, (normed, norm_saved, pre_act, activated))

    def mlp_backward(grad_resid, pad_mask, layer_index, saved):
        normed, norm_saved, pre_act, activated = saved
        grad_branch = pad_mask[:, None] * grad_resid
        g_down_bias = jnp.sum(grad_branch, axis=0)
        grad_full = branch_grad(grad_branch.astype(jnp.bfloat16))
        g_down_weight = jnp.einsum(
            "sf,sd->fd", activated, grad_full, preferred_element_type=jnp.float32
        )
        grad_act = jnp.einsum(
            "sd,fd->sf", grad_full, down_weight[layer_index], preferred_element_type=jnp.float32
        )
        unused_value, gelu_pull = jax.vjp(
            lambda inner: jax.nn.gelu(inner, approximate=False), pre_act
        )
        grad_pre = gelu_pull(grad_act)[0]
        g_up_bias = jnp.sum(grad_pre, axis=0)
        pre_low = grad_pre.astype(jnp.bfloat16)
        g_up_weight = jnp.einsum("sd,sf->df", normed, pre_low, preferred_element_type=jnp.float32)
        grad_normed = jnp.einsum(
            "sf,df->sd", pre_low, up_weight[layer_index], preferred_element_type=jnp.float32
        )
        grad_own, g_gain, g_bias = norm_backward(grad_normed, norm_saved)
        return (
            grad_resid + grad_own,
            (g_up_weight, g_down_weight, g_gain, g_bias, g_up_bias, g_down_bias),
        )

    mixer_acc = [None] * layer_count
    mlp_acc = [None] * layer_count
    outputs = []
    input_grads = []
    for micro_index in range(micro_count):
        pad_mask = (positions_dev < lengths[micro_index, 0]).astype(jnp.float32)
        resid = tokens[micro_index, 0].astype(jnp.float32)
        layer_inputs = []
        layer_saved = []
        for layer_index in range(layer_count):
            layer_inputs.append(resid)
            resid, mix_saved = mixer_forward(resid, pad_mask, layer_index)
            layer_inputs.append(resid)
            resid, mlp_saved = mlp_forward(resid, pad_mask, layer_index)
            layer_saved.append((mix_saved, mlp_saved))
        outputs.append(resid)
        grad_resid = cotangent[micro_index, 0].astype(jnp.float32)
        for layer_index in reversed(range(layer_count)):
            mlp_saved = mlp_forward(layer_inputs[2 * layer_index + 1], pad_mask, layer_index)[1]
            grad_resid, mlp_grads = mlp_backward(grad_resid, pad_mask, layer_index, mlp_saved)
            mix_saved = mixer_forward(layer_inputs[2 * layer_index], pad_mask, layer_index)[1]
            (
                mixer_normed,
                mixer_norm_saved,
                mixer_padded,
                mixer_short_out,
                mixer_chan_prod,
                mixer_prod_re,
                mixer_prod_im,
                mixer_long_out,
                mixer_mixed,
            ) = mix_saved
            mixer_filt_re, mixer_filt_im, mixer_filter_pull, mixer_skip_cols = filters[layer_index]
            mixer_grad_branch = pad_mask[:, None] * grad_resid
            g_out_bias = jnp.sum(mixer_grad_branch, axis=0)
            mixer_grad_full = branch_grad(mixer_grad_branch.astype(jnp.bfloat16))
            g_out_weight = jnp.einsum(
                "cs,sd->cd", mixer_mixed, mixer_grad_full, preferred_element_type=jnp.float32
            )
            grad_mixed = jnp.einsum(
                "sd,cd->cs",
                mixer_grad_full,
                out_weight[layer_index],
                preferred_element_type=jnp.float32,
            )
            grad_long = grad_mixed * mixer_short_out[0]
            grad_gate = grad_mixed * mixer_long_out
            chan_grad = to_channels(grad_long)
            grad_re, grad_im = to_spectrum(chan_grad, basis)
            back_re, back_im = complex_mul(grad_re, grad_im, mixer_filt_re, -mixer_filt_im)
            chan_dprod = (
                from_spectrum(back_re, back_im, basis) + mixer_skip_cols[:, None] * chan_grad
            )
            corr_re, corr_im = complex_mul(grad_re, grad_im, mixer_prod_re, -mixer_prod_im)
            grad_filter = from_spectrum(corr_re, corr_im, basis)
            g_skip = jnp.sum(chan_grad * mixer_chan_prod, axis=1)
            grad_product = to_positions(chan_dprod)
            grad_short = jnp.stack(
                [grad_gate, grad_product * mixer_short_out[2], grad_product * mixer_short_out[1]]
            )
            g_short_bias = jnp.sum(grad_short, axis=2)
            g_taps = jnp.stack(
                [
                    jnp.sum(grad_short * mixer_padded[:, :, 2:], axis=2),
                    jnp.sum(grad_short * mixer_padded[:, :, 1 : rows_dev + 1], axis=2),
                    jnp.sum(grad_short * mixer_padded[:, :, :rows_dev], axis=2),
                ],
                axis=1,
            )
            next_rim = shifted(grad_short[:, :, :2], "seq", -1)
            extended = jnp.concatenate([grad_short, next_rim], axis=2)
            mixer_taps = short_taps[layer_index]
            grad_streams = (
                mixer_taps[:, 0][:, :, None] * extended[:, :, :rows_dev]
                + mixer_taps[:, 1][:, :, None] * extended[:, :, 1 : rows_dev + 1]
                + mixer_taps[:, 2][:, :, None] * extended[:, :, 2:]
            )
            g_in_bias = jnp.sum(grad_streams, axis=2)
            streams_low = grad_streams.astype(jnp.bfloat16)
            g_in_weight = jnp.einsum(
                "sd,kcs->kdc", mixer_normed, streams_low, preferred_element_type=jnp.float32
            )
            mixer_grad_normed = jnp.einsum(
                "kcs,kdc->sd",
                streams_low,
                in_weight[layer_index],
                preferred_element_type=jnp.float32,
            )
            mixer_grad_own, mixer_g_gain, mixer_g_bias = norm_backward(
                mixer_grad_normed, mixer_norm_saved
            )
            grads = (
                g_in_weight,
                g_out_weight,
                mixer_g_gain,
                mixer_g_bias,
                g_in_bias,
                g_taps,
                g_short_bias,
                g_skip,
                g_out_bias,
                grad_filter,
            )
            grad_resid, mix_grads = (grad_resid + mixer_grad_own, grads)
            if mixer_acc[layer_index] is None:
                mixer_acc[layer_index] = mix_grads
                mlp_acc[layer_index] = mlp_grads
            else:
                mixer_acc[layer_index] = jax.tree.map(jnp.add, mixer_acc[layer_index], mix_grads)
                mlp_acc[layer_index] = jax.tree.map(jnp.add, mlp_acc[layer_index], mlp_grads)
        input_grads.append(grad_resid)
    filter_grads = [
        filters[layer_index][2](mixer_acc[layer_index][9]) for layer_index in range(layer_count)
    ]
    skip_start = chan_start + col_start

    def stack_mix(member):
        return jnp.stack([mixer_acc[layer_index][member] for layer_index in range(layer_count)])

    def stack_mlp(member):
        return jnp.stack([mlp_acc[layer_index][member] for layer_index in range(layer_count)])

    def stack_filter(member):
        return jnp.stack([filter_grads[layer_index][member] for layer_index in range(layer_count)])

    big_grads = (
        lax.psum_scatter(stack_mix(0), ("seq", "dp"), scatter_dimension=2, tiled=True),
        lax.psum_scatter(stack_mix(1), ("seq", "dp"), scatter_dimension=2, tiled=True),
        lax.psum_scatter(stack_mlp(0), ("seq", "dp"), scatter_dimension=1, tiled=True),
        lax.psum_scatter(stack_mlp(1), ("seq", "dp"), scatter_dimension=2, tiled=True),
    )
    gain_grads = jnp.stack([stack_mix(2), stack_mlp(2)], axis=1)
    bias_grads = jnp.stack([stack_mix(3), stack_mlp(3)], axis=1)
    small = lax.psum(
        (
            place(gain_grads, chan_start, full_width, 2),
            place(bias_grads, chan_start, full_width, 2),
            place(stack_mix(4), chan_start, full_width, 2),
            place(stack_mix(5), chan_start, full_width, 3),
            place(stack_mix(6), chan_start, full_width, 2),
            place(stack_mix(7), skip_start, full_width, 1),
            place(stack_mix(8), chan_start, full_width, 1),
            place(stack_mlp(4), chan_index * hidden_width, hidden_width * chan_parts, 1),
            place(stack_mlp(5), chan_start, full_width, 1),
            stack_filter(0),
            stack_filter(1),
            stack_filter(2),
            place(stack_filter(3), skip_start, full_width, 2),
        ),
        ("seq", "chan", "dp"),
    )
    out_act = jnp.stack(outputs)[:, None]
    grad_tokens = jnp.stack(input_grads)[:, None]
    return (
        out_act,
        grad_tokens,
        big_grads[0],
        big_grads[1],
        big_grads[2],
        big_grads[3],
        small[0],
        small[1],
        small[2],
        small[3],
        small[4],
        small[5],
        small[6],
        small[7],
        small[8],
        small[9],
        small[10],
        small[11],
        small[12],
    )


F32 = jnp.float32
BF16 = jnp.bfloat16
MESH = pl.DeviceIdType.MESH
ORDERS = (("x", "y", "l", "h"), ("y", "l", "x", "h"), ("l", "x", "y", "h"))


def half_tables(count):
    odd = 2 * np.arange(count, dtype=np.int64) + 1
    angle = np.outer(odd, odd) % (8 * count) * (math.pi / (4 * count))
    twist = odd * (math.pi / (4 * count))
    return np.cos(angle), np.sin(angle), np.cos(twist)[:, None], np.sin(twist)[:, None]


def mesh_bits():
    seq, dp = lax.axis_index("seq"), lax.axis_index("dp")
    return {"x": dp, "y": lax.rem(seq, 2), "l": lax.rem(seq // 2, 2), "h": seq // 4}


def mesh_peers():
    seq, dp = lax.axis_index("seq"), lax.axis_index("dp")
    bits = mesh_bits()
    return {
        "x": {"dp": 1 - dp},
        "y": {"seq": seq + 1 - 2 * bits["y"]},
        "l": {"seq": seq + 2 - 4 * bits["l"]},
        "h": {"seq": seq + 4 - 8 * bits["h"]},
    }


def greet(devices):
    barrier = pltpu.get_barrier_semaphore()
    for device in devices:
        pl.semaphore_signal(barrier, inc=1, device_id=device, device_id_type=MESH)
    pl.semaphore_wait(barrier, len(devices))


def scatter_kernel(chunk_width, parts_ref, out_ref, recv1, recv2, recv3, recv4, send_sem, recv_sem):
    layers, rows, columns = parts_ref.shape[0], parts_ref.shape[5], parts_ref.shape[6]
    per_layer = columns // chunk_width
    bits, peers = mesh_bits(), mesh_peers()
    greet([peers[axis] for axis in "xylh"])
    received = (recv1, recv2, recv3, recv4)
    chunks = [(layer, part) for layer in range(layers) for part in range(per_layer)]

    def axes_left(chunk, stage):
        order = ORDERS[chunk % len(ORDERS)]
        return [axis for axis in "hlyx" if axis not in order[:stage]]

    def held(chunk, stage, index):
        layer, part = chunks[chunk]
        if stage == 0:
            return parts_ref.at[
                (layer, *index, slice(None), pl.ds(part * chunk_width, chunk_width))
            ]
        return received[stage - 1].at[(chunk, *index)]

    def copies(chunk, stage):
        axis = ORDERS[chunk % len(ORDERS)][stage]
        left = axes_left(chunk, stage)
        index = tuple(1 - bits[axis] if name == axis else slice(None) for name in left)
        return pltpu.make_async_remote_copy(
            src_ref=held(chunk, stage, index),
            dst_ref=received[stage].at[chunk],
            send_sem=send_sem.at[chunk, stage],
            recv_sem=recv_sem.at[chunk, stage],
            device_id=peers[axis],
            device_id_type=MESH,
        )

    def combine(chunk, stage):
        axis = ORDERS[chunk % len(ORDERS)][stage]
        left = axes_left(chunk, stage)
        place = left.index(axis)
        layer, part = chunks[chunk]
        for flat in range(2 ** (len(left) - 1)):
            kept = [flat >> shift & 1 for shift in reversed(range(len(left) - 1))]
            mine = tuple(kept[:place] + [bits[axis]] + kept[place:])
            own = held(chunk, stage, mine)[...].astype(F32)
            total = own + received[stage].at[(chunk, *kept)][...].astype(F32)
            if stage == 3:
                out_ref[layer, :, pl.ds(part * chunk_width, chunk_width)] = total
            else:
                received[stage].at[(chunk, *kept)][...] = total.astype(BF16)

    slots = sorted(
        ((chunk // 3 + (1.0, 1.5, 1.75, 1.875)[stage], chunk, stage))
        for chunk in range(len(chunks))
        for stage in range(4)
    )
    for chunk in range(len(chunks)):
        copies(chunk, 0).start()
    for _, chunk, stage in slots:
        copies(chunk, stage).wait_recv()
        combine(chunk, stage)
        if stage < 3:
            copies(chunk, stage + 1).start()
    for _, chunk, stage in slots:
        copies(chunk, stage).wait_send()


def scatter_sum(parts):
    layers, rows, columns = parts.shape[0], parts.shape[5], parts.shape[6]
    chunk_width = columns // 6
    count = layers * 6
    return pl.pallas_call(
        functools.partial(scatter_kernel, chunk_width),
        out_shape=jax.ShapeDtypeStruct((layers, rows, columns), F32),
        in_specs=[pl.BlockSpec(memory_space=pltpu.VMEM)],
        out_specs=pl.BlockSpec(memory_space=pltpu.VMEM),
        scratch_shapes=[
            pltpu.VMEM((count, *[2] * (3 - stage), rows, chunk_width), BF16) for stage in range(4)
        ]
        + [pltpu.SemaphoreType.DMA((count, 4)), pltpu.SemaphoreType.DMA((count, 4))],
        compiler_params=pltpu.CompilerParams(
            collective_id=1, has_side_effects=True, vmem_limit_bytes=58 << 20
        ),
        name="scatter_sum",
    )(parts)


def small_kernel(parts_ref, out_ref, recv, send_sem, recv_sem, core_sem):
    seq, dp, chan = lax.axis_index("seq"), lax.axis_index("dp"), lax.axis_index("chan")
    count = parts_ref.shape[0]
    me = seq * 2 + dp
    others = [lax.rem(me + step, count) for step in range(1, count)]
    devices = [{"seq": other // 2, "dp": lax.rem(other, 2)} for other in others]
    greet(devices + [{"chan": 1 - chan}])
    first = []
    for step in range(count - 1):
        first.append(
            pltpu.make_async_remote_copy(
                src_ref=parts_ref.at[others[step]],
                dst_ref=recv.at[step],
                send_sem=send_sem.at[0, step],
                recv_sem=recv_sem.at[0, step],
                device_id=devices[step],
                device_id_type=MESH,
            )
        )
        first[-1].start()
    total = parts_ref[me]
    for step in range(count - 1):
        first[step].wait()
        total = total + recv[step]
    out_ref[chan, me] = total
    second = []
    for step in range(count - 1):
        second.append(
            pltpu.make_async_remote_copy(
                src_ref=out_ref.at[chan, me],
                dst_ref=out_ref.at[chan, me],
                send_sem=send_sem.at[1, step],
                recv_sem=recv_sem.at[1, step],
                device_id=devices[step],
                device_id_type=MESH,
            )
        )
        second[-1].start()
    for copy in second:
        copy.wait()
    last = pltpu.make_async_remote_copy(
        src_ref=out_ref.at[chan],
        dst_ref=out_ref.at[chan],
        send_sem=core_sem.at[0],
        recv_sem=core_sem.at[1],
        device_id={"chan": 1 - chan},
        device_id_type=MESH,
    )
    last.start()
    last.wait()


def small_sum(parts):
    count, rows, lanes = parts.shape
    return pl.pallas_call(
        small_kernel,
        out_shape=jax.ShapeDtypeStruct((2, count, rows, lanes), F32),
        in_specs=[pl.BlockSpec(memory_space=pltpu.VMEM)],
        out_specs=pl.BlockSpec(memory_space=pltpu.VMEM),
        scratch_shapes=[
            pltpu.VMEM((count - 1, rows, lanes), F32),
            pltpu.SemaphoreType.DMA((2, count - 1)),
            pltpu.SemaphoreType.DMA((2, count - 1)),
            pltpu.SemaphoreType.DMA((2,)),
        ],
        compiler_params=pltpu.CompilerParams(collective_id=2, has_side_effects=True),
        name="small_sum",
    )(parts)


def mm(left, right):
    return jnp.dot(left, right, preferred_element_type=F32)


def mm_nt(left, right):
    return lax.dot_general(left, right, (((1,), (1,)), ((), ())), preferred_element_type=F32)


def chain_kernel(sizes, names, *refs):
    layers, micro, span, half, hidden = sizes
    r = types.SimpleNamespace(**dict(zip(names, refs)))
    width, rows, parts = 2 * half, micro * span, 8
    block = half // parts
    length = span * parts
    seq, chan = lax.axis_index("seq"), lax.axis_index("chan")
    pair = seq + 1 - 2 * lax.rem(seq, 2)
    step = 32

    def load(name, layer, slot):
        return pltpu.make_async_copy(getattr(r, name).at[layer], getattr(r, name + "_v").at[layer], r.w_sem.at[layer, slot])

    weights = (("win", 0), ("wout", 1), ("wup", 2), ("wdown", 3))
    table_loads = [
        pltpu.make_async_copy(r.cos, r.cos_v, r.t_sem.at[0]),
        pltpu.make_async_copy(r.sin, r.sin_v, r.t_sem.at[1]),
    ]
    load("win", 0, 0).start()
    for copy in table_loads:
        copy.start()
    for layer in range(layers):
        for name, slot in weights:
            if (layer, slot) != (0, 0):
                load(name, layer, slot).start()
    greet([{"seq": lax.rem(seq + far, parts)} for far in range(1, parts)] + [{"chan": 1 - chan}])

    def seq_copy(send, recv, sems, other, outgoing):
        slot = seq if outgoing else other
        return pltpu.make_async_remote_copy(
            src_ref=getattr(r, send).at[other],
            dst_ref=getattr(r, recv).at[slot],
            send_sem=getattr(r, sems).at[0, other],
            recv_sem=getattr(r, sems).at[1, slot],
            device_id={"seq": other},
            device_id_type=MESH,
        )

    def all_others():
        return [lax.rem(seq + far, parts) for far in (4, 3, 5, 2, 6, 1, 7)]

    def wait_all(send, recv, sems):
        for other in all_others():
            seq_copy(send, recv, sems, other, False).wait_recv()
        for other in all_others():
            seq_copy(send, recv, sems, other, True).wait_send()

    def pair_copy(slot, m):
        return pltpu.make_async_remote_copy(
            src_ref=r.pair_send.at[slot, m],
            dst_ref=r.pair_recv.at[slot, m],
            send_sem=r.pair_sem.at[0, slot, m],
            recv_sem=r.pair_sem.at[1, slot, m],
            device_id={"chan": 1 - chan},
            device_id_type=MESH,
        )

    def rim_copy(way):
        other = lax.rem(seq + (1 if way == 0 else parts - 1), parts)
        return pltpu.make_async_remote_copy(
            src_ref=r.rim_send.at[way],
            dst_ref=r.rim_recv.at[way],
            send_sem=r.rim_sem.at[0, way],
            recv_sem=r.rim_sem.at[1, way],
            device_id={"seq": other},
            device_id_type=MESH,
        )

    def paired(slot, m, base, count):
        at = (slot, m, pl.ds(base, count), slice(None))
        return r.pair_send[at].astype(F32) + r.pair_recv[at].astype(F32)

    def row(name, index):
        return getattr(r, name)[pl.ds(index, 1), :]

    gains = [[row("vec", 2 * layer + n) for n in range(2)] for layer in range(layers)]
    biases = [[row("vec", 2 * layers + 2 * layer + n) for n in range(2)] for layer in range(layers)]
    branch_bias = [[row("vec", 4 * layers + layer), row("vec", 5 * layers + layer)] for layer in range(layers)]

    def norm_rows(at, x, layer, n):
        centred = x - jnp.mean(x, axis=1, keepdims=True)
        rstd = lax.rsqrt(jnp.mean(centred * centred, axis=1, keepdims=True) + EPS)
        scaled = centred * rstd
        r.xh[layer, n, at, :] = scaled
        r.rstd[layer, n, at, :] = rstd
        r.u[layer, n, at, :] = (scaled * gains[layer][n] + biases[layer][n]).astype(BF16)

    def forward_rows(slot, bias, layer, n):
        for m in range(micro):
            pair_copy(slot, m).wait_recv()

            @pl.loop(0, span // step)
            def _(i):
                base = pl.multiple_of(i * step, step)
                at = pl.ds(m * span + base, step)
                x = r.x[at, :] + r.mask[at, :] * (paired(slot, m, base, step) + bias)
                r.x[at, :] = x
                if layer < layers:
                    norm_rows(at, x, layer, n)

        for m in range(micro):
            pair_copy(slot, m).wait_send()

    def send_partial(slot, make):
        for m in range(micro):
            r.pair_send[slot, m] = make(m).astype(BF16)
            pair_copy(slot, m).start()

    def tap(layer, k, j):
        return r.taps[layer, k, pl.ds(j, 1), :]

    def short_part(layer, k, m, low, high):
        z = r.z
        total = r.short_b[layer, pl.ds(k, 1), :]
        for j in range(3):
            total = total + tap(layer, k, j) * z[layer, k, m, pl.ds(8 + low - j, high - low), :]
        r.s[layer, k, m, pl.ds(low, high - low), :] = total

    def to_channels(m, value):
        turned = value.T.astype(BF16)
        for j in range(parts):
            r.a_send[j, pl.ds(m * block, block), :] = turned[j * block : (j + 1) * block]

    def start_channels():
        for other in all_others():
            seq_copy("a_send", "a_recv", "a_sem", other, True).start()
        r.a_recv[seq] = r.a_send[seq]

    def gathered():
        return jnp.concatenate([r.a_recv[j] for j in range(parts)], axis=1)

    def from_channels(m):
        stack = [r.b_recv[j, pl.ds(m * block, block), :].astype(F32) for j in range(parts)]
        return jnp.concatenate(stack, axis=0).T

    def inverse_and_send(signal):
        for far in (2, 1, 3, 0):
            at = lax.rem(seq // 2 + far, parts // 2)
            lanes = pl.ds(pl.multiple_of(at * 2 * span, 2 * span), 2 * span)
            out = mm(r.spec[0], r.cos_v[:, lanes]) + mm(r.spec[1], r.sin_v[:, lanes])
            out = (out + r.skip_v[...] * signal[:, lanes].astype(F32)).astype(BF16)
            for h in range(2):
                r.b_send[2 * at + h] = out[:, h * span : (h + 1) * span]
            if far:
                for h in range(2):
                    seq_copy("b_send", "b_recv", "b_sem", 2 * at + h, True).start()
            else:
                seq_copy("b_send", "b_recv", "b_sem", pair, True).start()
                r.b_recv[seq] = r.b_send[seq]

    for base in range(0, rows, step):
        at = pl.ds(base, step)
        x = r.x0[at, :].astype(F32)
        r.x[at, :] = x
        norm_rows(at, x, 0, 0)

    for layer in range(layers):
        load("win", layer, 0).wait()
        for k in range(3):
            z = mm(r.u[layer, 0], r.win_v[layer, k]) + r.in_b[layer, pl.ds(k, 1), :]
            for m in range(micro):
                r.z[layer, k, m, pl.ds(8, span), :] = z[m * span : (m + 1) * span]
                r.rim_send[0, pl.ds(k * 4 + m * 2, 2), :] = z[(m + 1) * span - 2 : (m + 1) * span]
        rim_copy(0).start()
        for k in range(3):
            for m in range(micro):
                short_part(layer, k, m, step, span)
        rim_copy(0).wait()
        inner = (seq > 0).astype(F32)
        for k in range(3):
            for m in range(micro):
                r.z[layer, k, m, pl.ds(6, 2), :] = inner * r.rim_recv[0, pl.ds(k * 4 + m * 2, 2), :]
                short_part(layer, k, m, 0, step)
        for m in range(micro):
            to_channels(m, r.s[layer, 1, m] * r.s[layer, 2, m])
        start_channels()
        if layer == 0:
            for copy in table_loads:
                copy.wait()
        wait_all("a_send", "a_recv", "a_sem")
        signal = gathered()
        r.sig[layer] = signal
        r.skip_v[...] = r.skip[layer]
        for c in range(0, length, 256):
            lanes = pl.ds(c, 256)
            pc, ps = mm(signal, r.cos_v[:, lanes]), mm(signal, r.sin_v[:, lanes])
            fr, fi = r.fr[layer, :, lanes], r.fi[layer, :, lanes]
            r.pc[layer, :, lanes], r.ps[layer, :, lanes] = pc, ps
            r.spec[0, :, lanes] = (pc * fr + ps * fi).astype(BF16)
            r.spec[1, :, lanes] = (ps * fr - pc * fi).astype(BF16)
        inverse_and_send(r.sig.at[layer])
        load("wout", layer, 1).wait()
        wait_all("b_send", "b_recv", "b_sem")
        for m in range(micro):
            y = from_channels(m)
            r.y[layer, m] = y.astype(BF16)
            r.mixed[layer, pl.ds(m * span, span), :] = (r.s[layer, 0, m] * y).astype(BF16)
        send_partial(0, lambda m: mm(r.mixed[layer, pl.ds(m * span, span), :], r.wout_v[layer]))
        forward_rows(0, branch_bias[layer][0], layer, 1)

        load("wup", layer, 2).wait()
        for c in range(0, hidden, 256):
            lanes = pl.ds(c, 256)
            for m in range(micro):
                at = pl.ds(m * span, span)
                a = mm(r.u[layer, 1, at, :], r.wup_v[layer, :, lanes]) + r.up_b[pl.ds(layer, 1), lanes]
                cdf = 0.5 + 0.5 * lax.erf(a * math.sqrt(0.5))
                pdf = jnp.exp(-0.5 * a * a) * (1.0 / math.sqrt(2.0 * math.pi))
                r.g[layer, at, lanes] = (a * cdf).astype(BF16)
                r.slope[layer, at, lanes] = (cdf + a * pdf).astype(BF16)
        load("wdown", layer, 3).wait()
        send_partial(1, lambda m: mm(r.g[layer, pl.ds(m * span, span), :], r.wdown_v[layer]))
        forward_rows(1, branch_bias[layer][1], layer + 1, 0)

    own_lanes = pl.ds(pl.multiple_of(chan * half, half), half)
    r.out_act[...] = r.x[:, own_lanes]

    def branch_rows(at, dx):
        branch = r.mask[at, :] * dx
        r.grad[at, :] = branch.astype(BF16)
        return jnp.sum(branch.reshape(step // 8, 8, width), axis=0)

    def put768(layer, index, value):
        r.o768[layer, pl.ds(index, 1), :] = jnp.sum(value, axis=0, keepdims=True)

    total = jnp.zeros((8, width), F32)
    for base in range(0, rows, step):
        at = pl.ds(base, step)
        dx = r.c0[at, :].astype(F32)
        r.x[at, :] = dx
        total = total + branch_rows(at, dx)
    put768(layers - 1, 5, total)

    def backward_rows(slot, layer, n):
        gain = gains[layer][n]
        sums = [jnp.zeros((8, width), F32)] * 3
        for m in range(micro):
            pair_copy(slot, m).wait_recv()

            def body(i, carry):
                base = pl.multiple_of(i * step, step)
                at = pl.ds(m * span + base, step)
                du = paired(slot, m, base, step)
                scaled = r.xh[layer, n, at, :]
                weighted = du * gain
                back = r.rstd[layer, n, at, :] * (
                    weighted
                    - jnp.mean(weighted, axis=1, keepdims=True)
                    - scaled * jnp.mean(weighted * scaled, axis=1, keepdims=True)
                )
                dx = r.x[at, :] + back
                r.x[at, :] = dx
                shape = (step // 8, 8, width)
                return [
                    carry[0] + jnp.sum((du * scaled).reshape(shape), axis=0),
                    carry[1] + jnp.sum(du.reshape(shape), axis=0),
                    carry[2] + branch_rows(at, dx),
                ]

            sums = lax.fori_loop(0, span // step, body, sums)
        for m in range(micro):
            pair_copy(slot, m).wait_send()
        put768(layer, n, sums[0])
        put768(layer, 2 + n, sums[1])
        if n == 1:
            put768(layer, 4, sums[2])
        elif layer > 0:
            put768(layer - 1, 5, sums[2])

    def transpose_into(name, value):
        getattr(r, name)[...] = value.astype(F32).T.astype(BF16)

    def weight_grad(layer, start, turned, value):
        columns = value.shape[1]
        piece = 384 if columns == 384 else 512
        for c in range(0, columns, piece):
            out = mm(getattr(r, turned)[...], value[:, c : c + piece]).astype(BF16)
            r.big[layer, :, :, :, :, :, pl.ds(start + c, piece)] = out.reshape(2, 2, 2, 2, width // 16, piece)

    for layer in reversed(range(layers)):
        for c in range(0, hidden, 256):
            lanes = pl.ds(c, 256)
            da = mm_nt(r.grad[...], r.wdown_v[layer, lanes, :]) * r.slope[layer, :, lanes].astype(F32)
            r.o_up[pl.ds(layer, 1), lanes] = jnp.sum(da, axis=0, keepdims=True)
            r.da[:, lanes] = da.astype(BF16)
        send_partial(0, lambda m: mm_nt(r.da[pl.ds(m * span, span), :], r.wup_v[layer]))
        transpose_into("turned", r.grad[...])
        weight_grad(layer, 4 * half + hidden, "turned", r.g.at[layer])
        transpose_into("turned", r.u[layer, 1])
        weight_grad(layer, 4 * half, "turned", r.da)
        backward_rows(0, layer, 1)

        for m in range(micro):
            dmixed = mm_nt(r.grad[pl.ds(m * span, span), :], r.wout_v[layer])
            to_channels(m, dmixed * r.s[layer, 0, m])
            r.ds[0, m, pl.ds(0, span), :] = dmixed * r.y[layer, m].astype(F32)
        start_channels()
        transpose_into("turned", r.grad[...])
        weight_grad(layer, 3 * half, "turned", r.mixed.at[layer])
        wait_all("a_send", "a_recv", "a_sem")
        signal = gathered()
        r.dsig[...] = signal
        r.skip_v[...] = r.skip[layer]
        for c in range(0, length, 256):
            lanes = pl.ds(c, 256)
            gc, gs = mm(signal, r.cos_v[:, lanes]), mm(signal, r.sin_v[:, lanes])
            fr, fi = r.fr[layer, :, lanes], r.fi[layer, :, lanes]
            r.gc[:, lanes], r.gs[:, lanes] = gc, gs
            r.spec[0, :, lanes] = (gc * fr - gs * fi).astype(BF16)
            r.spec[1, :, lanes] = (gs * fr + gc * fi).astype(BF16)
        inverse_and_send(r.dsig)
        r.o_skip[layer] = jnp.sum(r.dsig[...].astype(F32) * r.sig[layer].astype(F32), axis=1, keepdims=True)
        for c in range(0, length, 256):
            lanes = pl.ds(c, 256)
            gc, gs, pc, ps = r.gc[:, lanes], r.gs[:, lanes], r.pc[layer, :, lanes], r.ps[layer, :, lanes]
            re, im = gc * pc + gs * ps, gc * ps - gs * pc
            re = sum(re[m * block : (m + 1) * block] for m in range(micro)) * (1.0 / length)
            im = sum(im[m * block : (m + 1) * block] for m in range(micro)) * (1.0 / length)
            tc, ts = r.turn[pl.ds(0, 1), lanes], r.turn[pl.ds(1, 1), lanes]
            for which, value in enumerate((re * tc + im * ts, re * ts - im * tc)):
                high = value.astype(BF16)
                r.corr[which, pl.ds(0, block), lanes] = high
                r.corr[which, pl.ds(block, block), lanes] = (value - high.astype(F32)).astype(BF16)
        for c in range(0, length, 256):
            lanes = pl.ds(c, 256)
            out = mm(r.corr[0], r.cos_v[:, lanes]) + mm(r.corr[1], r.sin_v[:, lanes])
            r.o_filt[layer, :, lanes] = out[:block] + out[block:]
        wait_all("b_send", "b_recv", "b_sem")
        for m in range(micro):
            dp = from_channels(m)
            for k in (1, 2):
                value = dp * r.s[layer, 3 - k, m]
                r.ds[k, m, pl.ds(0, span), :] = value
            for k in range(3):
                r.rim_send[1, pl.ds(k * 4 + m * 2, 2), :] = r.ds[k, m, pl.ds(0, 2), :]
        rim_copy(1).start()
        for k in range(3):
            sums = [0.0] * 4
            for m in range(micro):
                ds = r.ds[k, m, pl.ds(0, span), :]
                sums[3] = sums[3] + jnp.sum(ds, axis=0, keepdims=True)
                for j in range(3):
                    z = r.z[layer, k, m, pl.ds(8 - j, span), :]
                    sums[j] = sums[j] + jnp.sum(ds * z, axis=0, keepdims=True)
            for j in range(3):
                r.o384[layer, pl.ds(3 + 3 * k + j, 1), :] = sums[j]
            r.o384[layer, pl.ds(12 + k, 1), :] = sums[3]
        rim_copy(1).wait()
        inner = (seq < parts - 1).astype(F32)
        for k in range(3):
            total = 0.0
            for m in range(micro):
                r.ds[k, m, pl.ds(span, 2), :] = inner * r.rim_recv[1, pl.ds(k * 4 + m * 2, 2), :]
                dz = 0.0
                for j in range(3):
                    dz = dz + tap(layer, k, j) * r.ds[k, m, pl.ds(j, span), :]
                total = total + jnp.sum(dz, axis=0, keepdims=True)
                r.gz[k, pl.ds(m * span, span), :] = dz.astype(BF16)
            r.o384[layer, pl.ds(k, 1), :] = total
        send_partial(
            1, lambda m: sum(mm_nt(r.gz[k, pl.ds(m * span, span), :], r.win_v[layer, k]) for k in range(3))
        )
        transpose_into("turned", r.u[layer, 0])
        for k in range(3):
            weight_grad(layer, k * half, "turned", r.gz.at[k])
        backward_rows(1, layer, 0)
    r.grad_tokens[...] = r.x[:, own_lanes]


def chain(inputs, sizes):
    layers, micro, span, half, hidden = sizes
    width, rows, parts = 2 * half, micro * span, 8
    block, length = half // parts, span * parts
    lanes = micro * block
    in_any = ("win", "wout", "wup", "wdown", "cos", "sin")
    outs = dict(
        out_act=((rows, half), F32),
        grad_tokens=((rows, half), F32),
        big=((layers, 2, 2, 2, 2, width // 16, 4 * half + 2 * hidden), BF16),
        o768=((layers, 8, width), F32),
        o384=((layers, 16, half), F32),
        o_up=((layers, hidden), F32),
        o_skip=((layers, lanes, 1), F32),
        o_filt=((layers, block, length), F32),
    )
    dma, vm = pltpu.SemaphoreType.DMA, pltpu.VMEM
    scratch = dict(
        win_v=vm((layers, 3, width, half), BF16),
        wout_v=vm((layers, half, width), BF16),
        wup_v=vm((layers, width, hidden), BF16),
        wdown_v=vm((layers, hidden, width), BF16),
        cos_v=vm((length, length), BF16),
        sin_v=vm((length, length), BF16),
        skip_v=vm((lanes, 1), F32),
        x=vm((rows, width), F32),
        xh=vm((layers, 2, rows, width), F32),
        rstd=vm((layers, 2, rows, 1), F32),
        u=vm((layers, 2, rows, width), BF16),
        z=vm((layers, 3, micro, span + 8, half), F32),
        s=vm((layers, 3, micro, span, half), F32),
        y=vm((layers, micro, span, half), BF16),
        mixed=vm((layers, rows, half), BF16),
        sig=vm((layers, lanes, length), BF16),
        dsig=vm((lanes, length), BF16),
        pc=vm((layers, lanes, length), F32),
        ps=vm((layers, lanes, length), F32),
        gc=vm((lanes, length), F32),
        gs=vm((lanes, length), F32),
        spec=vm((2, lanes, length), BF16),
        corr=vm((2, 2 * block, length), BF16),
        slope=vm((layers, rows, hidden), BF16),
        g=vm((layers, rows, hidden), BF16),
        da=vm((rows, hidden), BF16),
        grad=vm((rows, width), BF16),
        turned=vm((width, rows), BF16),
        ds=vm((3, micro, span + 8, half), F32),
        gz=vm((3, rows, half), BF16),
        a_send=vm((parts, lanes, span), BF16),
        a_recv=vm((parts, lanes, span), BF16),
        b_send=vm((parts, lanes, span), BF16),
        b_recv=vm((parts, lanes, span), BF16),
        pair_send=vm((2, micro, span, width), BF16),
        pair_recv=vm((2, micro, span, width), BF16),
        rim_send=vm((2, 16, half), F32),
        rim_recv=vm((2, 16, half), F32),
        w_sem=dma((layers, 4)),
        t_sem=dma((2,)),
        a_sem=dma((2, parts)),
        b_sem=dma((2, parts)),
        pair_sem=dma((2, 2, micro)),
        rim_sem=dma((2, 2)),
    )
    names = [*inputs, *outs, *scratch]
    results = pl.pallas_call(
        functools.partial(chain_kernel, sizes, names),
        out_shape=[jax.ShapeDtypeStruct(*spec) for spec in outs.values()],
        in_specs=[
            pl.BlockSpec(memory_space=pl.ANY if name in in_any else pltpu.VMEM) for name in inputs
        ],
        out_specs=[pl.BlockSpec(memory_space=pltpu.VMEM) for _ in outs],
        scratch_shapes=list(scratch.values()),
        compiler_params=pltpu.CompilerParams(
            collective_id=3, has_side_effects=True, vmem_limit_bytes=61 << 20
        ),
        name="chain",
    )(*inputs.values())
    return types.SimpleNamespace(**dict(zip(outs, results)))


def local_fast(
    tokens,
    lengths,
    cotangent,
    norm_gain,
    norm_bias,
    in_weight,
    in_bias,
    short_taps,
    short_bias,
    skip_gain,
    out_weight,
    out_bias,
    up_weight,
    up_bias,
    down_weight,
    down_bias,
    filter_in,
    filter_bias,
    filter_freq,
    filter_out,
    decay_rate,
):
    micro, rows_dev, half = tokens.shape[0], tokens.shape[2], tokens.shape[3]
    layers = norm_gain.shape[0]
    hidden = up_weight.shape[2]
    seq_parts = lax.axis_size("seq")
    seq_index, chan_index = lax.axis_index("seq"), lax.axis_index("chan")
    width = 2 * half
    rows = micro * rows_dev
    length = rows_dev * seq_parts
    block = half // seq_parts
    col_start, chan_start = seq_index * block, chan_index * half

    def both(value):
        return lax.all_gather(value, "chan", axis=value.ndim - 1, tiled=True)

    fresh = both(jnp.stack([tokens, cotangent]))[:, :, 0].reshape(2, rows, width)
    vectors = both(
        jnp.concatenate(
            [norm_gain.reshape(-1, half), norm_bias.reshape(-1, half), out_bias, down_bias], axis=0
        )
    )
    ids = seq_index * rows_dev + jnp.arange(rows_dev, dtype=jnp.int32)
    mask = (ids[None, :] < lengths[:, :1]).astype(F32).reshape(rows, 1)
    cos_np, sin_np, turn_c, turn_s = half_tables(length)
    cos_t, sin_t = jnp.asarray(cos_np, BF16), jnp.asarray(sin_np, BF16)
    turn = jnp.asarray(np.concatenate([turn_c, turn_s], axis=1).T, F32)
    table, steps_norm = positions(length, filter_in.shape[1])

    def transform_fine(value):
        high = value.astype(BF16)
        both_parts = jnp.concatenate([high, (value - high.astype(F32)).astype(BF16)], axis=0)
        pair_c, pair_s = mm(both_parts, cos_t), mm(both_parts, sin_t)
        n = value.shape[0]
        return pair_c[:n] + pair_c[n:], pair_s[:n] + pair_s[n:]

    def make_filter(w_in, w_bias, w_freq, w_out, decay):
        wave = jnp.sin(w_freq * (jnp.dot(table, w_in, precision=HIGH) + w_bias))
        raw = jnp.einsum("lf,fc->cl", wave, w_out, precision=HIGH)
        return raw * jnp.exp(-decay[:, None] * steps_norm[None, :])

    pulls, filt_re, filt_im, skips = [], [], [], []
    for layer in range(layers):
        w_out = lax.dynamic_slice_in_dim(filter_out[layer], col_start, block, 1)
        decay = lax.dynamic_slice_in_dim(decay_rate[layer], col_start, block, 0)
        skip = lax.dynamic_slice_in_dim(skip_gain[layer], col_start, block, 0)
        long_filter, pull = jax.vjp(
            lambda *leaves, decay=decay: make_filter(*leaves, decay),
            filter_in[layer],
            filter_bias[layer],
            filter_freq[layer],
            w_out,
        )
        filt_c, filt_s = transform_fine(long_filter)
        filt_re.append(jnp.tile((filt_c * turn[0] + filt_s * turn[1]) / length, (micro, 1)))
        filt_im.append(jnp.tile((filt_c * turn[1] - filt_s * turn[0]) / length, (micro, 1)))
        skips.append(jnp.tile(skip, micro)[:, None])
        pulls.append(pull)
    inputs = dict(
        x0=fresh[0],
        c0=fresh[1],
        mask=mask,
        vec=vectors,
        in_b=in_bias,
        taps=short_taps,
        short_b=short_bias,
        up_b=up_bias,
        skip=jnp.stack(skips),
        turn=turn,
        fr=jnp.stack(filt_re),
        fi=jnp.stack(filt_im),
        win=in_weight,
        wout=out_weight,
        wup=up_weight,
        wdown=down_weight,
        cos=cos_t,
        sin=sin_t,
    )
    out = chain(inputs, (layers, micro, rows_dev, half, hidden))
    out_act, grad_tokens = out.out_act, out.grad_tokens
    own768 = lax.dynamic_slice_in_dim(out.o768, chan_start, half, 2)
    small = []
    for layer in range(layers):
        g_fin, g_fbias, g_ffreq, g_fout = pulls[layer](out.o_filt[layer])
        g_skip = jnp.sum(out.o_skip[layer].reshape(micro, 1, block), axis=0)
        placed = place(jnp.concatenate([g_skip, g_fout], axis=0), col_start, half, 1)
        spread = jnp.concatenate([g_fin.reshape(-1), g_fbias, g_ffreq])
        spread_rows = -(-spread.shape[0] // half)
        spread = jnp.pad(spread, (0, spread_rows * half - spread.shape[0]))
        small.append(
            jnp.concatenate(
                [
                    own768[layer, :4],
                    out.o384[layer, :15],
                    own768[layer, 4:6],
                    out.o_up[layer].reshape(-1, half),
                    placed,
                    spread.reshape(spread_rows, half),
                ],
                axis=0,
            )
        )
    scattered = scatter_sum(out.big)
    flat = jnp.concatenate(small, axis=0).reshape(-1)
    lanes = 128
    piece = -(-flat.shape[0] // (16 * lanes * 8)) * 8
    flat_parts = jnp.pad(flat, (0, 16 * piece * lanes - flat.shape[0])).reshape(16, piece, lanes)
    summed = small_sum(flat_parts).reshape(2, -1)[:, : flat.shape[0]].reshape(2, layers, -1, half)

    def joined(start, stop, shape):
        value = summed[:, :, start:stop]
        value = value.transpose(1, 2, 0, 3).reshape(layers, stop - start, width)
        return value.reshape((layers, *shape, width))

    hid_rows = hidden // half
    up_value = summed[:, :, 21 : 21 + hid_rows].transpose(1, 0, 2, 3).reshape(layers, 2 * hidden)
    after = 21 + hid_rows
    bands, feat = filter_in.shape[1], filter_in.shape[2]
    spread = jnp.sum(summed[:, :, after + 1 + feat :], axis=0).reshape(layers, -1)
    in_cols, out_cols = 3 * half, 4 * half
    g_in = scattered[:, :, :in_cols].reshape(layers, width // 16, 3, half).transpose(0, 2, 1, 3)
    g_out = scattered[:, :, in_cols:out_cols].transpose(0, 2, 1)
    g_up = scattered[:, :, out_cols : out_cols + hidden]
    g_down = scattered[:, :, out_cols + hidden :].transpose(0, 2, 1)
    return (
        out_act.reshape(micro, 1, rows_dev, half),
        grad_tokens.reshape(micro, 1, rows_dev, half),
        g_in,
        g_out,
        g_up,
        g_down,
        joined(0, 2, (2,)),
        joined(2, 4, (2,)),
        joined(4, 7, (3,)),
        joined(7, 16, (3, 3)),
        joined(16, 19, (3,)),
        joined(after, after + 1, ()),
        joined(19, 20, ()),
        up_value,
        joined(20, 21, ()),
        spread[:, : bands * feat].reshape(layers, bands, feat),
        spread[:, bands * feat : bands * feat + feat],
        spread[:, bands * feat + feat : bands * feat + 2 * feat],
        joined(after + 1, after + 1 + feat, (feat,)),
    )


def solution(mesh):
    in_specs = (
        P(None, "dp", "seq", "chan"),
        P(None, "dp"),
        P(None, "dp", "seq", "chan"),
        P(None, None, "chan"),
        P(None, None, "chan"),
        P(None, None, None, "chan"),
        P(None, None, "chan"),
        P(None, None, None, "chan"),
        P(None, None, "chan"),
        P(None, "chan"),
        P(None, "chan", None),
        P(None, "chan"),
        P(None, None, "chan"),
        P(None, "chan"),
        P(None, "chan", None),
        P(None, "chan"),
        P(),
        P(),
        P(),
        P(None, None, "chan"),
        P(None, "chan"),
    )
    out_specs = (
        P(None, "dp", "seq", "chan"),
        P(None, "dp", "seq", "chan"),
        P(None, None, ("seq", "dp"), "chan"),
        P(None, "chan", ("seq", "dp")),
        P(None, ("seq", "dp"), "chan"),
        P(None, "chan", ("seq", "dp")),
        P(),
        P(),
        P(),
        P(),
        P(),
        P(),
        P(),
        P(),
        P(),
        P(),
        P(),
        P(),
        P(),
    )
    def entry(*args):
        fits = args[0].shape[2] * mesh.shape["seq"] <= 2048 and mesh.shape["seq"] == 8 and mesh.shape["dp"] == 2
        return (local_fast if fits else local)(*args)

    return jax.shard_map(entry, mesh=mesh, in_specs=in_specs, out_specs=out_specs, check_vma=False)
```

```python
import functools
import math
import types

import jax
import jax.numpy as jnp
import numpy as np
from jax import lax
from jax.experimental import pallas as pl
from jax.experimental.pallas import tpu as pltpu
from jax.sharding import PartitionSpec as P

EPS = 1e-05
HIGH = lax.Precision.HIGHEST


def shifted(value, axis, steps):
    count = lax.axis_size(axis)
    initial, last = (max(0, -steps), min(count, count - steps))
    return lax.ppermute(value, axis, [(source, source + steps) for source in range(initial, last)])


def positions(seq_length, emb_width):
    band_count = (emb_width - 1) // 2
    step_ids = jnp.arange(seq_length, dtype=jnp.float32)
    steps_norm = step_ids / seq_length
    band_freq = jnp.linspace(0.0001, band_count - 1, band_count).astype(jnp.float32)
    phases = 2.0 * math.pi * steps_norm[:, None] * band_freq[None, :]
    table = jnp.concatenate([steps_norm[:, None], jnp.cos(phases), -jnp.sin(phases)], axis=1)
    return (table, steps_norm)


def angle_table(row_count, col_count, modulus):
    product = (
        jnp.arange(row_count, dtype=jnp.int32)[:, None]
        * jnp.arange(col_count, dtype=jnp.int32)[None, :]
        % modulus
    )
    theta = product.astype(jnp.float32) * (2.0 * math.pi / modulus)
    return (jnp.cos(theta), jnp.sin(theta))


def split_length(total_length):
    lesser = 2
    for candidate in range(2, math.isqrt(total_length) + 1, 2):
        if total_length % candidate == 0:
            lesser = candidate
    return (lesser, total_length // lesser)


def dft_basis(seq_length):
    padded_len = 2 * seq_length
    lesser, greater = split_length(padded_len)
    cos_p, sin_p = angle_table(lesser, lesser, lesser)
    cos_q, sin_q = angle_table(greater, greater, greater)
    twist_c, twist_s = angle_table(lesser, greater, padded_len)
    return (cos_p, sin_p, cos_q, sin_q, twist_c, twist_s)


def right_mul(left, table):
    return jnp.einsum("ckb,bj->ckj", left, table, precision=HIGH)


def to_spectrum(signal, basis):
    cos_p, sin_p, cos_q, sin_q, twist_c, twist_s = basis
    half = cos_p.shape[0] // 2
    blocks = signal.reshape(signal.shape[0], half, cos_q.shape[0])
    first_re = jnp.einsum("ka,cab->ckb", cos_p[:, :half], blocks, precision=HIGH)
    first_im = -jnp.einsum("ka,cab->ckb", sin_p[:, :half], blocks, precision=HIGH)
    turned_re = first_re * twist_c + first_im * twist_s
    turned_im = first_im * twist_c - first_re * twist_s
    spec_re = right_mul(turned_re, cos_q) + right_mul(turned_im, sin_q)
    spec_im = right_mul(turned_im, cos_q) - right_mul(turned_re, sin_q)
    return (spec_re, spec_im)


def from_spectrum(spec_re, spec_im, basis):
    cos_p, sin_p, cos_q, sin_q, twist_c, twist_s = basis
    half = cos_p.shape[0] // 2
    back_re = right_mul(spec_re, cos_q) - right_mul(spec_im, sin_q)
    back_im = right_mul(spec_im, cos_q) + right_mul(spec_re, sin_q)
    turned_re = back_re * twist_c - back_im * twist_s
    turned_im = back_im * twist_c + back_re * twist_s
    signal = jnp.einsum("ak,ckb->cab", cos_p[:half], turned_re, precision=HIGH) - jnp.einsum(
        "ak,ckb->cab", sin_p[:half], turned_im, precision=HIGH
    )
    return signal.reshape(signal.shape[0], half * cos_q.shape[0]) / (
        cos_p.shape[0] * cos_q.shape[0]
    )


def complex_mul(left_re, left_im, right_re, right_im):
    return (left_re * right_re - left_im * right_im, left_re * right_im + left_im * right_re)


def filter_block(table, steps_norm, weight_in, bias_in, freq_in, cols_in, decay_cols):
    hidden = jnp.sin(freq_in * (jnp.dot(table, weight_in, precision=HIGH) + bias_in))
    raw = jnp.einsum("lf,fc->cl", hidden, cols_in, precision=HIGH)
    return raw * jnp.exp(-decay_cols[:, None] * steps_norm[None, :])


def to_channels(block):
    parts = lax.axis_size("seq")
    shaped = block.reshape(parts, block.shape[0] // parts, block.shape[1])
    moved = lax.all_to_all(
        shaped.astype(jnp.bfloat16), "seq", split_axis=0, concat_axis=2, tiled=True
    ).astype(shaped.dtype)
    return moved.reshape(moved.shape[1], moved.shape[2])


def to_positions(block):
    shaped = block.reshape(1, block.shape[0], block.shape[1])
    moved = lax.all_to_all(
        shaped.astype(jnp.bfloat16), "seq", split_axis=2, concat_axis=0, tiled=True
    ).astype(shaped.dtype)
    return moved.reshape(moved.shape[0] * moved.shape[1], moved.shape[2])


def branch_sum(partial_value):
    return lax.psum_scatter(
        partial_value.astype(jnp.bfloat16), "chan", scatter_dimension=1, tiled=True
    ).astype(jnp.float32)


def branch_grad(grad_low):
    return lax.all_gather(grad_low, "chan", axis=1, tiled=True)


def place(values, start, full_width, axis):
    full_shape = list(values.shape)
    full_shape[axis] = full_width
    return lax.dynamic_update_slice_in_dim(jnp.zeros(full_shape, jnp.float32), values, start, axis)


def local(
    tokens,
    lengths,
    cotangent,
    norm_gain,
    norm_bias,
    in_weight,
    in_bias,
    short_taps,
    short_bias,
    skip_gain,
    out_weight,
    out_bias,
    up_weight,
    up_bias,
    down_weight,
    down_bias,
    filter_in,
    filter_bias,
    filter_freq,
    filter_out,
    decay_rate,
):
    micro_count = tokens.shape[0]
    rows_dev = tokens.shape[2]
    chan_width = tokens.shape[3]
    layer_count = norm_gain.shape[0]
    hidden_width = up_weight.shape[2]
    seq_parts = lax.axis_size("seq")
    chan_parts = lax.axis_size("chan")
    full_width = chan_width * chan_parts
    seq_length = rows_dev * seq_parts
    seq_index = lax.axis_index("seq")
    chan_index = lax.axis_index("chan")
    block_width = chan_width // seq_parts
    col_start = seq_index * block_width
    chan_start = chan_index * chan_width
    basis = dft_basis(seq_length)
    table, steps_norm = positions(seq_length, filter_in.shape[1])
    positions_dev = seq_index * rows_dev + jnp.arange(rows_dev, dtype=jnp.int32)
    filters = []
    for layer_index in range(layer_count):
        filter_cols = lax.dynamic_slice_in_dim(filter_out[layer_index], col_start, block_width, 1)
        decay_cols = lax.dynamic_slice_in_dim(decay_rate[layer_index], col_start, block_width, 0)
        skip_cols = lax.dynamic_slice_in_dim(skip_gain[layer_index], col_start, block_width, 0)

        def make_one(weight_in, bias_in, freq_in, cols_in, decay_cols=decay_cols):
            return filter_block(table, steps_norm, weight_in, bias_in, freq_in, cols_in, decay_cols)

        long_filter, filter_pull = jax.vjp(
            make_one,
            filter_in[layer_index],
            filter_bias[layer_index],
            filter_freq[layer_index],
            filter_cols,
        )
        filt_re, filt_im = to_spectrum(long_filter, basis)
        filters.append((filt_re, filt_im, filter_pull, skip_cols))

    def norm_forward(resid, gain_bias):
        full_rows, full_gb = (
            lax.all_gather(resid, "chan", axis=1, tiled=True),
            lax.all_gather(gain_bias, "chan", axis=1, tiled=True),
        )
        mean_row = jnp.mean(full_rows, axis=1, keepdims=True)
        centred = full_rows - mean_row
        rstd = lax.rsqrt(jnp.mean(centred * centred, axis=1, keepdims=True) + EPS)
        scaled = centred * rstd
        normed = (scaled * full_gb[0] + full_gb[1]).astype(jnp.bfloat16)
        return (normed, (scaled, rstd, full_gb[0]))

    def norm_backward(grad_partial, norm_saved):
        scaled, rstd, gain_row = norm_saved
        grad_rows = lax.psum(grad_partial.astype(jnp.bfloat16), "chan").astype(jnp.float32)
        grad_scaled = grad_rows * gain_row
        grad_full = rstd * (
            grad_scaled
            - jnp.mean(grad_scaled, axis=1, keepdims=True)
            - scaled * jnp.mean(grad_scaled * scaled, axis=1, keepdims=True)
        )
        grad_own = lax.dynamic_slice_in_dim(grad_full, chan_start, chan_width, 1)
        rows_own = lax.dynamic_slice_in_dim(grad_rows, chan_start, chan_width, 1)
        scaled_own = lax.dynamic_slice_in_dim(scaled, chan_start, chan_width, 1)
        return (grad_own, jnp.sum(rows_own * scaled_own, axis=0), jnp.sum(rows_own, axis=0))

    def mixer_forward(resid, pad_mask, layer_index):
        normed, norm_saved = norm_forward(
            resid, jnp.stack([norm_gain[layer_index, 0], norm_bias[layer_index, 0]])
        )
        streams = (
            jnp.einsum(
                "sd,kdc->kcs", normed, in_weight[layer_index], preferred_element_type=jnp.float32
            )
            + in_bias[layer_index][:, :, None]
        )
        rim = shifted(streams[:, :, rows_dev - 2 :], "seq", 1)
        padded = jnp.concatenate([rim, streams], axis=2)
        taps = short_taps[layer_index]
        short_out = (
            taps[:, 0][:, :, None] * padded[:, :, 2:]
            + taps[:, 1][:, :, None] * padded[:, :, 1 : rows_dev + 1]
            + taps[:, 2][:, :, None] * padded[:, :, :rows_dev]
            + short_bias[layer_index][:, :, None]
        )
        product = short_out[1] * short_out[2]
        chan_prod = to_channels(product)
        filt_re, filt_im, filter_pull, skip_cols = filters[layer_index]
        prod_re, prod_im = to_spectrum(chan_prod, basis)
        conv_re, conv_im = complex_mul(prod_re, prod_im, filt_re, filt_im)
        chan_out = from_spectrum(conv_re, conv_im, basis) + skip_cols[:, None] * chan_prod
        long_out = to_positions(chan_out)
        mixed = (short_out[0] * long_out).astype(jnp.bfloat16)
        partial_value = jnp.einsum(
            "cs,cd->sd", mixed, out_weight[layer_index], preferred_element_type=jnp.float32
        )
        branch = branch_sum(partial_value) + out_bias[layer_index]
        saved = (
            normed,
            norm_saved,
            padded,
            short_out,
            chan_prod,
            prod_re,
            prod_im,
            long_out,
            mixed,
        )
        return (resid + pad_mask[:, None] * branch, saved)

    def mlp_forward(resid, pad_mask, layer_index):
        normed, norm_saved = norm_forward(
            resid, jnp.stack([norm_gain[layer_index, 1], norm_bias[layer_index, 1]])
        )
        pre_act = (
            jnp.dot(normed, up_weight[layer_index], preferred_element_type=jnp.float32)
            + up_bias[layer_index]
        )
        activated = jax.nn.gelu(pre_act, approximate=False).astype(jnp.bfloat16)
        partial_value = jnp.dot(
            activated, down_weight[layer_index], preferred_element_type=jnp.float32
        )
        branch = branch_sum(partial_value) + down_bias[layer_index]
        return (resid + pad_mask[:, None] * branch, (normed, norm_saved, pre_act, activated))

    def mlp_backward(grad_resid, pad_mask, layer_index, saved):
        normed, norm_saved, pre_act, activated = saved
        grad_branch = pad_mask[:, None] * grad_resid
        g_down_bias = jnp.sum(grad_branch, axis=0)
        grad_full = branch_grad(grad_branch.astype(jnp.bfloat16))
        g_down_weight = jnp.einsum(
            "sf,sd->fd", activated, grad_full, preferred_element_type=jnp.float32
        )
        grad_act = jnp.einsum(
            "sd,fd->sf", grad_full, down_weight[layer_index], preferred_element_type=jnp.float32
        )
        unused_value, gelu_pull = jax.vjp(
            lambda inner: jax.nn.gelu(inner, approximate=False), pre_act
        )
        grad_pre = gelu_pull(grad_act)[0]
        g_up_bias = jnp.sum(grad_pre, axis=0)
        pre_low = grad_pre.astype(jnp.bfloat16)
        g_up_weight = jnp.einsum("sd,sf->df", normed, pre_low, preferred_element_type=jnp.float32)
        grad_normed = jnp.einsum(
            "sf,df->sd", pre_low, up_weight[layer_index], preferred_element_type=jnp.float32
        )
        grad_own, g_gain, g_bias = norm_backward(grad_normed, norm_saved)
        return (
            grad_resid + grad_own,
            (g_up_weight, g_down_weight, g_gain, g_bias, g_up_bias, g_down_bias),
        )

    mixer_acc = [None] * layer_count
    mlp_acc = [None] * layer_count
    outputs = []
    input_grads = []
    for micro_index in range(micro_count):
        pad_mask = (positions_dev < lengths[micro_index, 0]).astype(jnp.float32)
        resid = tokens[micro_index, 0].astype(jnp.float32)
        layer_inputs = []
        layer_saved = []
        for layer_index in range(layer_count):
            layer_inputs.append(resid)
            resid, mix_saved = mixer_forward(resid, pad_mask, layer_index)
            layer_inputs.append(resid)
            resid, mlp_saved = mlp_forward(resid, pad_mask, layer_index)
            layer_saved.append((mix_saved, mlp_saved))
        outputs.append(resid)
        grad_resid = cotangent[micro_index, 0].astype(jnp.float32)
        for layer_index in reversed(range(layer_count)):
            mlp_saved = mlp_forward(layer_inputs[2 * layer_index + 1], pad_mask, layer_index)[1]
            grad_resid, mlp_grads = mlp_backward(grad_resid, pad_mask, layer_index, mlp_saved)
            mix_saved = mixer_forward(layer_inputs[2 * layer_index], pad_mask, layer_index)[1]
            (
                mixer_normed,
                mixer_norm_saved,
                mixer_padded,
                mixer_short_out,
                mixer_chan_prod,
                mixer_prod_re,
                mixer_prod_im,
                mixer_long_out,
                mixer_mixed,
            ) = mix_saved
            mixer_filt_re, mixer_filt_im, mixer_filter_pull, mixer_skip_cols = filters[layer_index]
            mixer_grad_branch = pad_mask[:, None] * grad_resid
            g_out_bias = jnp.sum(mixer_grad_branch, axis=0)
            mixer_grad_full = branch_grad(mixer_grad_branch.astype(jnp.bfloat16))
            g_out_weight = jnp.einsum(
                "cs,sd->cd", mixer_mixed, mixer_grad_full, preferred_element_type=jnp.float32
            )
            grad_mixed = jnp.einsum(
                "sd,cd->cs",
                mixer_grad_full,
                out_weight[layer_index],
                preferred_element_type=jnp.float32,
            )
            grad_long = grad_mixed * mixer_short_out[0]
            grad_gate = grad_mixed * mixer_long_out
            chan_grad = to_channels(grad_long)
            grad_re, grad_im = to_spectrum(chan_grad, basis)
            back_re, back_im = complex_mul(grad_re, grad_im, mixer_filt_re, -mixer_filt_im)
            chan_dprod = (
                from_spectrum(back_re, back_im, basis) + mixer_skip_cols[:, None] * chan_grad
            )
            corr_re, corr_im = complex_mul(grad_re, grad_im, mixer_prod_re, -mixer_prod_im)
            grad_filter = from_spectrum(corr_re, corr_im, basis)
            g_skip = jnp.sum(chan_grad * mixer_chan_prod, axis=1)
            grad_product = to_positions(chan_dprod)
            grad_short = jnp.stack(
                [grad_gate, grad_product * mixer_short_out[2], grad_product * mixer_short_out[1]]
            )
            g_short_bias = jnp.sum(grad_short, axis=2)
            g_taps = jnp.stack(
                [
                    jnp.sum(grad_short * mixer_padded[:, :, 2:], axis=2),
                    jnp.sum(grad_short * mixer_padded[:, :, 1 : rows_dev + 1], axis=2),
                    jnp.sum(grad_short * mixer_padded[:, :, :rows_dev], axis=2),
                ],
                axis=1,
            )
            next_rim = shifted(grad_short[:, :, :2], "seq", -1)
            extended = jnp.concatenate([grad_short, next_rim], axis=2)
            mixer_taps = short_taps[layer_index]
            grad_streams = (
                mixer_taps[:, 0][:, :, None] * extended[:, :, :rows_dev]
                + mixer_taps[:, 1][:, :, None] * extended[:, :, 1 : rows_dev + 1]
                + mixer_taps[:, 2][:, :, None] * extended[:, :, 2:]
            )
            g_in_bias = jnp.sum(grad_streams, axis=2)
            streams_low = grad_streams.astype(jnp.bfloat16)
            g_in_weight = jnp.einsum(
                "sd,kcs->kdc", mixer_normed, streams_low, preferred_element_type=jnp.float32
            )
            mixer_grad_normed = jnp.einsum(
                "kcs,kdc->sd",
                streams_low,
                in_weight[layer_index],
                preferred_element_type=jnp.float32,
            )
            mixer_grad_own, mixer_g_gain, mixer_g_bias = norm_backward(
                mixer_grad_normed, mixer_norm_saved
            )
            grads = (
                g_in_weight,
                g_out_weight,
                mixer_g_gain,
                mixer_g_bias,
                g_in_bias,
                g_taps,
                g_short_bias,
                g_skip,
                g_out_bias,
                grad_filter,
            )
            grad_resid, mix_grads = (grad_resid + mixer_grad_own, grads)
            if mixer_acc[layer_index] is None:
                mixer_acc[layer_index] = mix_grads
                mlp_acc[layer_index] = mlp_grads
            else:
                mixer_acc[layer_index] = jax.tree.map(jnp.add, mixer_acc[layer_index], mix_grads)
                mlp_acc[layer_index] = jax.tree.map(jnp.add, mlp_acc[layer_index], mlp_grads)
        input_grads.append(grad_resid)
    filter_grads = [
        filters[layer_index][2](mixer_acc[layer_index][9]) for layer_index in range(layer_count)
    ]
    skip_start = chan_start + col_start

    def stack_mix(member):
        return jnp.stack([mixer_acc[layer_index][member] for layer_index in range(layer_count)])

    def stack_mlp(member):
        return jnp.stack([mlp_acc[layer_index][member] for layer_index in range(layer_count)])

    def stack_filter(member):
        return jnp.stack([filter_grads[layer_index][member] for layer_index in range(layer_count)])

    big_grads = (
        lax.psum_scatter(stack_mix(0), ("seq", "dp"), scatter_dimension=2, tiled=True),
        lax.psum_scatter(stack_mix(1), ("seq", "dp"), scatter_dimension=2, tiled=True),
        lax.psum_scatter(stack_mlp(0), ("seq", "dp"), scatter_dimension=1, tiled=True),
        lax.psum_scatter(stack_mlp(1), ("seq", "dp"), scatter_dimension=2, tiled=True),
    )
    gain_grads = jnp.stack([stack_mix(2), stack_mlp(2)], axis=1)
    bias_grads = jnp.stack([stack_mix(3), stack_mlp(3)], axis=1)
    small = lax.psum(
        (
            place(gain_grads, chan_start, full_width, 2),
            place(bias_grads, chan_start, full_width, 2),
            place(stack_mix(4), chan_start, full_width, 2),
            place(stack_mix(5), chan_start, full_width, 3),
            place(stack_mix(6), chan_start, full_width, 2),
            place(stack_mix(7), skip_start, full_width, 1),
            place(stack_mix(8), chan_start, full_width, 1),
            place(stack_mlp(4), chan_index * hidden_width, hidden_width * chan_parts, 1),
            place(stack_mlp(5), chan_start, full_width, 1),
            stack_filter(0),
            stack_filter(1),
            stack_filter(2),
            place(stack_filter(3), skip_start, full_width, 2),
        ),
        ("seq", "chan", "dp"),
    )
    out_act = jnp.stack(outputs)[:, None]
    grad_tokens = jnp.stack(input_grads)[:, None]
    return (
        out_act,
        grad_tokens,
        big_grads[0],
        big_grads[1],
        big_grads[2],
        big_grads[3],
        small[0],
        small[1],
        small[2],
        small[3],
        small[4],
        small[5],
        small[6],
        small[7],
        small[8],
        small[9],
        small[10],
        small[11],
        small[12],
    )


F32 = jnp.float32
BF16 = jnp.bfloat16
MESH = pl.DeviceIdType.MESH
CHUNKS = (
    (1, 3072, 512, "xlyh"),
    (1, 3584, 512, "lyxh"),
    (1, 4096, 512, "yxlh"),
    (1, 1536, 512, "lyxh"),
    (1, 2048, 512, "ylhx"),
    (1, 2560, 512, "xlyh"),
    (1, 0, 768, "ylxh"),
    (1, 768, 768, "xlyh"),
    (0, 1152, 384, "xylh"),
    (0, 3072, 512, "ylhx"),
    (0, 3584, 512, "yxlh"),
    (0, 4096, 512, "xylh"),
    (0, 1536, 512, "xlyh"),
    (0, 2048, 512, "xylh"),
    (0, 2560, 512, "xylh"),
    (0, 0, 384, "xylh"),
    (0, 384, 384, "ylxh"),
    (0, 768, 384, "xylh"),
)
TICKS = 13
PLAN = {
    7: ((0, 0), (1, 0), (2, 0),),
    10: ((3, 0), (4, 0), (5, 0),),
    12: ((0, 1), (1, 1), (2, 1),),
    15: ((3, 1), (4, 1),),
    17: ((7, 0),),
    18: ((5, 1),),
    19: ((2, 2),),
    20: ((1, 2),),
    21: ((4, 2),),
    22: ((6, 0), (0, 2),),
    23: ((7, 1), (11, 0), (2, 3),),
    25: ((1, 3), (9, 0),),
    26: ((6, 1), (12, 0), (0, 3), (10, 0), (9, 1), (5, 2), (13, 0), (12, 1), (11, 1), (7, 2), (9, 2), (14, 0), (5, 3), (11, 2), (3, 2), (16, 0), (7, 3), (13, 1), (11, 3), (8, 0), (12, 2), (4, 3), (3, 3), (16, 1), (14, 1), (13, 2), (15, 0), (8, 1), (12, 3), (14, 2), (13, 3), (15, 1), (17, 0), (8, 2), (14, 3), (6, 2), (15, 2), (17, 1), (8, 3), (10, 1), (9, 3), (6, 3), (16, 2), (15, 3), (17, 2), (10, 2), (16, 3), (17, 3), (10, 3),),
}


def half_tables(count):
    odd = 2 * np.arange(count, dtype=np.int64) + 1
    angle = np.outer(odd, odd) % (8 * count) * (math.pi / (4 * count))
    twist = odd * (math.pi / (4 * count))
    return np.cos(angle), np.sin(angle), np.cos(twist)[:, None], np.sin(twist)[:, None]


def mesh_bits():
    seq, dp = lax.axis_index("seq"), lax.axis_index("dp")
    return {"x": dp, "y": lax.rem(seq, 2), "l": lax.rem(seq // 2, 2), "h": seq // 4}


def mesh_peers():
    seq, dp = lax.axis_index("seq"), lax.axis_index("dp")
    bits = mesh_bits()
    return {
        "x": {"dp": 1 - dp},
        "y": {"seq": seq + 1 - 2 * bits["y"]},
        "l": {"seq": seq + 2 - 4 * bits["l"]},
        "h": {"seq": seq + 4 - 8 * bits["h"]},
    }


def greet(devices):
    barrier = pltpu.get_barrier_semaphore()
    for device in devices:
        pl.semaphore_signal(barrier, inc=1, device_id=device, device_id_type=MESH)
    pl.semaphore_wait(barrier, len(devices))


def small_kernel(parts_ref, out_ref, recv, send_sem, recv_sem, core_sem):
    seq, dp, chan = lax.axis_index("seq"), lax.axis_index("dp"), lax.axis_index("chan")
    count = parts_ref.shape[0]
    me = seq * 2 + dp
    others = [lax.rem(me + step, count) for step in range(1, count)]
    devices = [{"seq": other // 2, "dp": lax.rem(other, 2)} for other in others]
    greet(devices + [{"chan": 1 - chan}])
    first = []
    for step in range(count - 1):
        first.append(
            pltpu.make_async_remote_copy(
                src_ref=parts_ref.at[others[step]],
                dst_ref=recv.at[step],
                send_sem=send_sem.at[0, step],
                recv_sem=recv_sem.at[0, step],
                device_id=devices[step],
                device_id_type=MESH,
            )
        )
        first[-1].start()
    total = parts_ref[me]
    for step in range(count - 1):
        first[step].wait()
        total = total + recv[step]
    out_ref[chan, me] = total
    second = []
    for step in range(count - 1):
        second.append(
            pltpu.make_async_remote_copy(
                src_ref=out_ref.at[chan, me],
                dst_ref=out_ref.at[chan, me],
                send_sem=send_sem.at[1, step],
                recv_sem=recv_sem.at[1, step],
                device_id=devices[step],
                device_id_type=MESH,
            )
        )
        second[-1].start()
    for copy in second:
        copy.wait()
    last = pltpu.make_async_remote_copy(
        src_ref=out_ref.at[chan],
        dst_ref=out_ref.at[chan],
        send_sem=core_sem.at[0],
        recv_sem=core_sem.at[1],
        device_id={"chan": 1 - chan},
        device_id_type=MESH,
    )
    last.start()
    last.wait()


def small_sum(parts):
    count, rows, lanes = parts.shape
    return pl.pallas_call(
        small_kernel,
        out_shape=jax.ShapeDtypeStruct((2, count, rows, lanes), F32),
        in_specs=[pl.BlockSpec(memory_space=pltpu.VMEM)],
        out_specs=pl.BlockSpec(memory_space=pltpu.VMEM),
        scratch_shapes=[
            pltpu.VMEM((count - 1, rows, lanes), F32),
            pltpu.SemaphoreType.DMA((2, count - 1)),
            pltpu.SemaphoreType.DMA((2, count - 1)),
            pltpu.SemaphoreType.DMA((2,)),
        ],
        compiler_params=pltpu.CompilerParams(collective_id=2, has_side_effects=True),
        name="small_sum",
    )(parts)


def mm(left, right):
    return jnp.dot(left, right, preferred_element_type=F32)


def mm_nt(left, right):
    return lax.dot_general(left, right, (((1,), (1,)), ((), ())), preferred_element_type=F32)


def chain_kernel(sizes, names, *refs):
    layers, micro, span, half, hidden = sizes
    r = types.SimpleNamespace(**dict(zip(names, refs)))
    width, rows, parts = 2 * half, micro * span, 8
    block = half // parts
    length = span * parts
    seq, chan = lax.axis_index("seq"), lax.axis_index("chan")
    pair = seq + 1 - 2 * lax.rem(seq, 2)
    step = 32

    def load(name, layer, slot):
        return pltpu.make_async_copy(getattr(r, name).at[layer], getattr(r, name + "_v"), r.w_sem.at[slot])

    weights = (("win", 0), ("wout", 1), ("wup", 2), ("wdown", 3))
    table_loads = [
        pltpu.make_async_copy(r.cos, r.cos_v, r.t_sem.at[0]),
        pltpu.make_async_copy(r.sin, r.sin_v, r.t_sem.at[1]),
    ]
    load("win", 0, 0).start()
    for copy in table_loads:
        copy.start()
    for name, slot in weights[1:]:
        load(name, 0, slot).start()
    peers, bits = mesh_peers(), mesh_bits()
    greet(
        [{"seq": lax.rem(seq + far, parts)} for far in range(1, parts)] + [{"chan": 1 - chan}, peers["x"]]
    )
    sent, done, begun, written = [], [], [], set()
    received = (r.rs1, r.rs2, r.rs3, r.rs4)

    def rs_index(chunk, stage, bit):
        order = CHUNKS[chunk][3]
        left = [axis for axis in "hlyx" if axis not in order[:stage]]
        return left, left.index(order[stage])

    def rs_held(chunk, stage, index):
        layer, start, columns = CHUNKS[chunk][:3]
        lanes = pl.ds(start, columns)
        if stage == 0:
            return r.big.at[(*index, slice(None), lanes)]
        return received[stage - 1].at[(layer, *index, slice(None), lanes)]

    def rs_copy(chunk, stage):
        layer, start, columns, order = CHUNKS[chunk][:4]
        axis = order[stage]
        left, spot = rs_index(chunk, stage, 0)
        index = tuple(1 - bits[axis] if name == axis else slice(None) for name in left)
        rest = (slice(None),) * (4 - stage)
        return pltpu.make_async_remote_copy(
            src_ref=rs_held(chunk, stage, index),
            dst_ref=received[stage].at[(layer, *rest, pl.ds(start, columns))],
            send_sem=r.rs_sem.at[0, chunk, stage],
            recv_sem=r.rs_sem.at[1, chunk, stage],
            device_id=peers[axis],
            device_id_type=MESH,
        )

    def advance(chunk, stage):
        layer, start, columns, order = CHUNKS[chunk][:4]
        lanes = pl.ds(start, columns)
        done.append((chunk, stage))
        rs_copy(chunk, stage).wait_recv()
        left, spot = rs_index(chunk, stage, 0)
        for flat in range(2 ** (3 - stage)):
            kept = [flat >> shift & 1 for shift in reversed(range(3 - stage))]
            mine = tuple(kept[:spot] + [bits[order[stage]]] + kept[spot:])
            total = rs_held(chunk, stage, mine)[...].astype(F32)
            there = received[stage].at[(layer, *kept, slice(None), lanes)]
            total = total + there[...].astype(F32)
            if stage == 3:
                r.o_big[layer, :, lanes] = total
            else:
                there[...] = total.astype(BF16)
        if stage < 3:
            rs_copy(chunk, stage + 1).start()

    def begin(layer, start, stop):
        written.update((layer, column) for column in range(start, stop, 128))
        for chunk, spec in enumerate(CHUNKS):
            need = {(spec[0], column) for column in range(spec[1], spec[1] + spec[2], 128)}
            if chunk not in begun and need <= written:
                begun.append(chunk)
                rs_copy(chunk, 0).start()

    def tick(layer, spot):
        now = TICKS * (layers - 1 - layer) + spot
        for chunk, stage in PLAN.get(now, ()):
            advance(chunk, stage)

    def short_all(layer):
        for k in range(3):
            for m in range(micro):
                short_part(layer, k, m, 0, span)

    def next_load(layer, name, slot):
        if 0 <= layer < layers:
            load(name, layer, slot).start()

    def seq_copy(send, recv, sems, other, outgoing):
        slot = seq if outgoing else other
        return pltpu.make_async_remote_copy(
            src_ref=getattr(r, send).at[other],
            dst_ref=getattr(r, recv).at[slot],
            send_sem=getattr(r, sems).at[0, other],
            recv_sem=getattr(r, sems).at[1, slot],
            device_id={"seq": other},
            device_id_type=MESH,
        )

    def all_others():
        return [lax.rem(seq + far, parts) for far in (4, 3, 5, 2, 6, 1, 7)]

    def wait_all(send, recv, sems):
        for other in all_others():
            seq_copy(send, recv, sems, other, False).wait_recv()
        for other in all_others():
            seq_copy(send, recv, sems, other, True).wait_send()

    def pair_copy(slot, m):
        return pltpu.make_async_remote_copy(
            src_ref=r.pair_send.at[slot, m],
            dst_ref=r.pair_recv.at[slot, m],
            send_sem=r.pair_sem.at[0, slot, m],
            recv_sem=r.pair_sem.at[1, slot, m],
            device_id={"chan": 1 - chan},
            device_id_type=MESH,
        )

    def rim_copy(way):
        other = lax.rem(seq + (1 if way == 0 else parts - 1), parts)
        return pltpu.make_async_remote_copy(
            src_ref=r.rim_send.at[way],
            dst_ref=r.rim_recv.at[way],
            send_sem=r.rim_sem.at[0, way],
            recv_sem=r.rim_sem.at[1, way],
            device_id={"seq": other},
            device_id_type=MESH,
        )

    def paired(slot, m, base, count):
        at = (slot, m, pl.ds(base, count), slice(None))
        return r.pair_send[at].astype(F32) + r.pair_recv[at].astype(F32)

    def row(name, index):
        return getattr(r, name)[pl.ds(index, 1), :]

    gains = [[row("vec", 2 * layer + n) for n in range(2)] for layer in range(layers)]
    biases = [[row("vec", 2 * layers + 2 * layer + n) for n in range(2)] for layer in range(layers)]
    branch_bias = [[row("vec", 4 * layers + layer), row("vec", 5 * layers + layer)] for layer in range(layers)]

    def norm_rows(at, x, layer, n):
        centred = x - jnp.mean(x, axis=1, keepdims=True)
        rstd = lax.rsqrt(jnp.mean(centred * centred, axis=1, keepdims=True) + EPS)
        scaled = centred * rstd
        r.xh[layer, n, at, :] = scaled
        r.rstd[layer, n, at, :] = rstd
        r.u[layer, n, at, :] = (scaled * gains[layer][n] + biases[layer][n]).astype(BF16)

    def forward_rows(slot, bias, layer, n):
        for m in range(micro):
            pair_copy(slot, m).wait_recv()

            @pl.loop(0, span // step)
            def _(i):
                base = pl.multiple_of(i * step, step)
                at = pl.ds(m * span + base, step)
                x = r.x[at, :] + r.mask[at, :] * (paired(slot, m, base, step) + bias)
                r.x[at, :] = x
                if layer < layers:
                    norm_rows(at, x, layer, n)

        for m in range(micro):
            pair_copy(slot, m).wait_send()

    def send_partial(slot, make):
        for m in range(micro):
            r.pair_send[slot, m] = make(m).astype(BF16)
            pair_copy(slot, m).start()

    def tap(layer, k, j):
        return r.taps[layer, k, pl.ds(j, 1), :]

    def short_part(layer, k, m, low, high):
        z = r.z
        total = r.short_b[layer, pl.ds(k, 1), :]
        for j in range(3):
            total = total + tap(layer, k, j) * z[layer, k, m, pl.ds(8 + low - j, high - low), :]
        r.s[k, m, pl.ds(low, high - low), :] = total

    def to_channels(m, value):
        turned = value.T.astype(BF16)
        for j in range(parts):
            r.a_send[j, pl.ds(m * block, block), :] = turned[j * block : (j + 1) * block]

    def start_channels():
        for other in all_others():
            seq_copy("a_send", "a_recv", "a_sem", other, True).start()
        r.a_recv[seq] = r.a_send[seq]

    def gathered():
        return jnp.concatenate([r.a_recv[j] for j in range(parts)], axis=1)

    def from_channels(m):
        stack = [r.b_recv[j, pl.ds(m * block, block), :].astype(F32) for j in range(parts)]
        return jnp.concatenate(stack, axis=0).T

    def inverse_and_send(signal):
        for far in (2, 1, 3, 0):
            at = lax.rem(seq // 2 + far, parts // 2)
            lanes = pl.ds(pl.multiple_of(at * 2 * span, 2 * span), 2 * span)
            out = mm(r.spec[0], r.cos_v[:, lanes]) + mm(r.spec[1], r.sin_v[:, lanes])
            out = (out + r.skip_v[...] * signal[:, lanes].astype(F32)).astype(BF16)
            for h in range(2):
                r.b_send[2 * at + h] = out[:, h * span : (h + 1) * span]
            if far:
                for h in range(2):
                    seq_copy("b_send", "b_recv", "b_sem", 2 * at + h, True).start()
            else:
                seq_copy("b_send", "b_recv", "b_sem", pair, True).start()
                r.b_recv[seq] = r.b_send[seq]

    for base in range(0, rows, step):
        at = pl.ds(base, step)
        x = r.x0[at, :].astype(F32)
        r.x[at, :] = x
        norm_rows(at, x, 0, 0)

    for layer in range(layers):
        load("win", layer, 0).wait()
        for k in range(3):
            z = mm(r.u[layer, 0], r.win_v[k]) + r.in_b[layer, pl.ds(k, 1), :]
            for m in range(micro):
                r.z[layer, k, m, pl.ds(8, span), :] = z[m * span : (m + 1) * span]
                r.rim_send[0, pl.ds(k * 4 + m * 2, 2), :] = z[(m + 1) * span - 2 : (m + 1) * span]
        rim_copy(0).start()
        next_load(layer + 1, "win", 0)
        for k in range(3):
            for m in range(micro):
                short_part(layer, k, m, step, span)
        rim_copy(0).wait()
        inner = (seq > 0).astype(F32)
        for k in range(3):
            for m in range(micro):
                r.z[layer, k, m, pl.ds(6, 2), :] = inner * r.rim_recv[0, pl.ds(k * 4 + m * 2, 2), :]
                short_part(layer, k, m, 0, step)
        for m in range(micro):
            to_channels(m, r.s[1, m] * r.s[2, m])
        start_channels()
        if layer == 0:
            for copy in table_loads:
                copy.wait()
        wait_all("a_send", "a_recv", "a_sem")
        signal = gathered()
        r.sig[layer] = signal
        r.skip_v[...] = r.skip[layer]
        for c in range(0, length, 256):
            lanes = pl.ds(c, 256)
            pc, ps = mm(signal, r.cos_v[:, lanes]), mm(signal, r.sin_v[:, lanes])
            fr, fi = r.fr[layer, :, lanes], r.fi[layer, :, lanes]
            r.pc[layer, :, lanes], r.ps[layer, :, lanes] = pc, ps
            r.spec[0, :, lanes] = (pc * fr + ps * fi).astype(BF16)
            r.spec[1, :, lanes] = (ps * fr - pc * fi).astype(BF16)
        inverse_and_send(r.sig.at[layer])
        load("wout", layer, 1).wait()
        wait_all("b_send", "b_recv", "b_sem")
        for m in range(micro):
            y = from_channels(m)
            r.y[layer, m] = y.astype(BF16)
            r.mixed[layer, pl.ds(m * span, span), :] = (r.s[0, m] * y).astype(BF16)
        send_partial(0, lambda m: mm(r.mixed[layer, pl.ds(m * span, span), :], r.wout_v[...]))
        next_load(layer + 1, "wout", 1)
        forward_rows(0, branch_bias[layer][0], layer, 1)

        load("wup", layer, 2).wait()
        for c in range(0, hidden, 256):
            lanes = pl.ds(c, 256)
            for m in range(micro):
                at = pl.ds(m * span, span)
                a = mm(r.u[layer, 1, at, :], r.wup_v[:, lanes]) + r.up_b[pl.ds(layer, 1), lanes]
                cdf = 0.5 + 0.5 * lax.erf(a * math.sqrt(0.5))
                pdf = jnp.exp(-0.5 * a * a) * (1.0 / math.sqrt(2.0 * math.pi))
                r.g[layer, at, lanes] = (a * cdf).astype(BF16)
                r.slope[layer, at, lanes] = (cdf + a * pdf).astype(BF16)
        next_load(layer + 1, "wup", 2)
        load("wdown", layer, 3).wait()
        send_partial(1, lambda m: mm(r.g[layer, pl.ds(m * span, span), :], r.wdown_v[...]))
        next_load(layer + 1, "wdown", 3)
        forward_rows(1, branch_bias[layer][1], layer + 1, 0)

    own_lanes = pl.ds(pl.multiple_of(chan * half, half), half)
    r.out_act[...] = r.x[:, own_lanes]

    def branch_rows(at, dx):
        branch = r.mask[at, :] * dx
        r.grad[at, :] = branch.astype(BF16)
        return jnp.sum(branch.reshape(step // 8, 8, width), axis=0)

    def put768(layer, index, value):
        r.o768[layer, pl.ds(index, 1), :] = jnp.sum(value, axis=0, keepdims=True)

    total = jnp.zeros((8, width), F32)
    for base in range(0, rows, step):
        at = pl.ds(base, step)
        dx = r.c0[at, :].astype(F32)
        r.x[at, :] = dx
        total = total + branch_rows(at, dx)
    put768(layers - 1, 5, total)

    def backward_rows(slot, layer, n):
        gain = gains[layer][n]
        sums = [jnp.zeros((8, width), F32)] * 3
        for m in range(micro):
            pair_copy(slot, m).wait_recv()

            def body(i, carry):
                base = pl.multiple_of(i * step, step)
                at = pl.ds(m * span + base, step)
                du = paired(slot, m, base, step)
                scaled = r.xh[layer, n, at, :]
                weighted = du * gain
                back = r.rstd[layer, n, at, :] * (
                    weighted
                    - jnp.mean(weighted, axis=1, keepdims=True)
                    - scaled * jnp.mean(weighted * scaled, axis=1, keepdims=True)
                )
                dx = r.x[at, :] + back
                r.x[at, :] = dx
                shape = (step // 8, 8, width)
                return [
                    carry[0] + jnp.sum((du * scaled).reshape(shape), axis=0),
                    carry[1] + jnp.sum(du.reshape(shape), axis=0),
                    carry[2] + branch_rows(at, dx),
                ]

            sums = lax.fori_loop(0, span // step, body, sums)
        for m in range(micro):
            pair_copy(slot, m).wait_send()
        put768(layer, n, sums[0])
        put768(layer, 2 + n, sums[1])
        if n == 1:
            put768(layer, 4, sums[2])
        elif layer > 0:
            put768(layer - 1, 5, sums[2])

    def transpose_into(name, value):
        getattr(r, name)[...] = value.astype(F32).T.astype(BF16)

    def weight_grad(layer, start, turned, value):
        columns = value.shape[1]
        for chunk, spec in enumerate(CHUNKS):
            if spec[0] == layer + 1 and spec[1] < start + columns and start < spec[1] + spec[2]:
                if (chunk, 0) not in done:
                    raise ValueError(chunk)
                if chunk not in sent:
                    rs_copy(chunk, 0).wait_send()
                    sent.append(chunk)
        piece = 384 if columns == 384 else 512
        for c in range(0, columns, piece):
            out = mm(getattr(r, turned)[...], value[:, c : c + piece]).astype(BF16)
            r.big[:, :, :, :, :, pl.ds(start + c, piece)] = out.reshape(2, 2, 2, 2, width // 16, piece)
            begin(layer, start + c, start + c + piece)

    for layer in reversed(range(layers)):
        last = layer == layers - 1
        if not last:
            load("wdown", layer, 3).wait()
        for c in range(0, hidden, 256):
            lanes = pl.ds(c, 256)
            da = mm_nt(r.grad[...], r.wdown_v[lanes, :]) * r.slope[layer, :, lanes].astype(F32)
            r.o_up[pl.ds(layer, 1), lanes] = jnp.sum(da, axis=0, keepdims=True)
            r.da[:, lanes] = da.astype(BF16)
        next_load(layer - 1, "wdown", 3)
        if not last:
            load("wup", layer, 2).wait()
        send_partial(0, lambda m: mm_nt(r.da[pl.ds(m * span, span), :], r.wup_v[...]))
        next_load(layer - 1, "wup", 2)
        tick(layer, 0)
        transpose_into("turned", r.grad[...])
        weight_grad(layer, 4 * half + hidden, "turned", r.g.at[layer])
        tick(layer, 1)
        transpose_into("turned", r.u[layer, 1])
        weight_grad(layer, 4 * half, "turned", r.da)
        if not last:
            short_all(layer)
        tick(layer, 2)
        backward_rows(0, layer, 1)
        tick(layer, 3)
        if not last:
            load("wout", layer, 1).wait()

        for m in range(micro):
            dmixed = mm_nt(r.grad[pl.ds(m * span, span), :], r.wout_v[...])
            to_channels(m, dmixed * r.s[0, m])
            r.ds[0, m, pl.ds(0, span), :] = dmixed * r.y[layer, m].astype(F32)
        start_channels()
        next_load(layer - 1, "wout", 1)
        tick(layer, 4)
        transpose_into("turned", r.grad[...])
        weight_grad(layer, 3 * half, "turned", r.mixed.at[layer])
        tick(layer, 5)
        wait_all("a_send", "a_recv", "a_sem")
        tick(layer, 6)
        signal = gathered()
        r.dsig[...] = signal
        r.skip_v[...] = r.skip[layer]
        for c in range(0, length, 256):
            lanes = pl.ds(c, 256)
            gc, gs = mm(signal, r.cos_v[:, lanes]), mm(signal, r.sin_v[:, lanes])
            fr, fi = r.fr[layer, :, lanes], r.fi[layer, :, lanes]
            r.gc[:, lanes], r.gs[:, lanes] = gc, gs
            r.spec[0, :, lanes] = (gc * fr - gs * fi).astype(BF16)
            r.spec[1, :, lanes] = (gs * fr + gc * fi).astype(BF16)
        inverse_and_send(r.dsig)
        tick(layer, 7)
        r.o_skip[layer] = jnp.sum(r.dsig[...].astype(F32) * r.sig[layer].astype(F32), axis=1, keepdims=True)
        for c in range(0, length, 256):
            lanes = pl.ds(c, 256)
            gc, gs, pc, ps = r.gc[:, lanes], r.gs[:, lanes], r.pc[layer, :, lanes], r.ps[layer, :, lanes]
            re, im = gc * pc + gs * ps, gc * ps - gs * pc
            re = sum(re[m * block : (m + 1) * block] for m in range(micro)) * (1.0 / length)
            im = sum(im[m * block : (m + 1) * block] for m in range(micro)) * (1.0 / length)
            tc, ts = r.turn[pl.ds(0, 1), lanes], r.turn[pl.ds(1, 1), lanes]
            for which, value in enumerate((re * tc + im * ts, re * ts - im * tc)):
                high = value.astype(BF16)
                r.corr[which, pl.ds(0, block), lanes] = high
                r.corr[which, pl.ds(block, block), lanes] = (value - high.astype(F32)).astype(BF16)
        for c in range(0, length, 256):
            lanes = pl.ds(c, 256)
            out = mm(r.corr[0], r.cos_v[:, lanes]) + mm(r.corr[1], r.sin_v[:, lanes])
            r.o_filt[layer, :, lanes] = out[:block] + out[block:]
        tick(layer, 8)
        wait_all("b_send", "b_recv", "b_sem")
        for m in range(micro):
            dp = from_channels(m)
            for k in (1, 2):
                value = dp * r.s[3 - k, m]
                r.ds[k, m, pl.ds(0, span), :] = value
            for k in range(3):
                r.rim_send[1, pl.ds(k * 4 + m * 2, 2), :] = r.ds[k, m, pl.ds(0, 2), :]
        rim_copy(1).start()
        for k in range(3):
            sums = [0.0] * 4
            for m in range(micro):
                ds = r.ds[k, m, pl.ds(0, span), :]
                sums[3] = sums[3] + jnp.sum(ds, axis=0, keepdims=True)
                for j in range(3):
                    z = r.z[layer, k, m, pl.ds(8 - j, span), :]
                    sums[j] = sums[j] + jnp.sum(ds * z, axis=0, keepdims=True)
            for j in range(3):
                r.o384[layer, pl.ds(3 + 3 * k + j, 1), :] = sums[j]
            r.o384[layer, pl.ds(12 + k, 1), :] = sums[3]
        tick(layer, 9)
        rim_copy(1).wait()
        inner = (seq < parts - 1).astype(F32)
        for k in range(3):
            total = 0.0
            for m in range(micro):
                r.ds[k, m, pl.ds(span, 2), :] = inner * r.rim_recv[1, pl.ds(k * 4 + m * 2, 2), :]
                dz = 0.0
                for j in range(3):
                    dz = dz + tap(layer, k, j) * r.ds[k, m, pl.ds(j, span), :]
                total = total + jnp.sum(dz, axis=0, keepdims=True)
                r.gz[k, pl.ds(m * span, span), :] = dz.astype(BF16)
            r.o384[layer, pl.ds(k, 1), :] = total
        if not last:
            load("win", layer, 0).wait()
        send_partial(
            1, lambda m: sum(mm_nt(r.gz[k, pl.ds(m * span, span), :], r.win_v[k]) for k in range(3))
        )
        next_load(layer - 1, "win", 0)
        tick(layer, 10)
        transpose_into("turned", r.u[layer, 0])
        for k in range(3):
            weight_grad(layer, k * half, "turned", r.gz.at[k])
        tick(layer, 11)
        backward_rows(1, layer, 0)
        tick(layer, 12)
    r.grad_tokens[...] = r.x[:, own_lanes]
    for chunk, stage in PLAN[TICKS * layers]:
        advance(chunk, stage)
    for chunk in range(len(CHUNKS)):
        for stage in range(4):
            if stage or chunk not in sent:
                rs_copy(chunk, stage).wait_send()


def chain(inputs, sizes):
    layers, micro, span, half, hidden = sizes
    width, rows, parts = 2 * half, micro * span, 8
    block, length = half // parts, span * parts
    lanes = micro * block
    columns = 4 * half + 2 * hidden
    in_any = ("win", "wout", "wup", "wdown", "cos", "sin")
    outs = dict(
        out_act=((rows, half), F32),
        grad_tokens=((rows, half), F32),
        o_big=((layers, width // 16, 4 * half + 2 * hidden), F32),
        o768=((layers, 8, width), F32),
        o384=((layers, 16, half), F32),
        o_up=((layers, hidden), F32),
        o_skip=((layers, lanes, 1), F32),
        o_filt=((layers, block, length), F32),
    )
    dma, vm = pltpu.SemaphoreType.DMA, pltpu.VMEM
    scratch = dict(
        big=vm((2, 2, 2, 2, width // 16, columns), BF16),
        rs1=vm((layers, 2, 2, 2, width // 16, columns), BF16),
        rs2=vm((layers, 2, 2, width // 16, columns), BF16),
        rs3=vm((layers, 2, width // 16, columns), BF16),
        rs4=vm((layers, width // 16, columns), BF16),
        rs_sem=dma((2, len(CHUNKS), 4)),
        win_v=vm((3, width, half), BF16),
        wout_v=vm((half, width), BF16),
        wup_v=vm((width, hidden), BF16),
        wdown_v=vm((hidden, width), BF16),
        cos_v=vm((length, length), BF16),
        sin_v=vm((length, length), BF16),
        skip_v=vm((lanes, 1), F32),
        x=vm((rows, width), F32),
        xh=vm((layers, 2, rows, width), F32),
        rstd=vm((layers, 2, rows, 1), F32),
        u=vm((layers, 2, rows, width), BF16),
        z=vm((layers, 3, micro, span + 8, half), F32),
        s=vm((3, micro, span, half), F32),
        y=vm((layers, micro, span, half), BF16),
        mixed=vm((layers, rows, half), BF16),
        sig=vm((layers, lanes, length), BF16),
        dsig=vm((lanes, length), BF16),
        pc=vm((layers, lanes, length), F32),
        ps=vm((layers, lanes, length), F32),
        gc=vm((lanes, length), F32),
        gs=vm((lanes, length), F32),
        spec=vm((2, lanes, length), BF16),
        corr=vm((2, 2 * block, length), BF16),
        slope=vm((layers, rows, hidden), BF16),
        g=vm((layers, rows, hidden), BF16),
        da=vm((rows, hidden), BF16),
        grad=vm((rows, width), BF16),
        turned=vm((width, rows), BF16),
        ds=vm((3, micro, span + 8, half), F32),
        gz=vm((3, rows, half), BF16),
        a_send=vm((parts, lanes, span), BF16),
        a_recv=vm((parts, lanes, span), BF16),
        b_send=vm((parts, lanes, span), BF16),
        b_recv=vm((parts, lanes, span), BF16),
        pair_send=vm((2, micro, span, width), BF16),
        pair_recv=vm((2, micro, span, width), BF16),
        rim_send=vm((2, 16, half), F32),
        rim_recv=vm((2, 16, half), F32),
        w_sem=dma((4,)),
        t_sem=dma((2,)),
        a_sem=dma((2, parts)),
        b_sem=dma((2, parts)),
        pair_sem=dma((2, 2, micro)),
        rim_sem=dma((2, 2)),
    )
    names = [*inputs, *outs, *scratch]
    results = pl.pallas_call(
        functools.partial(chain_kernel, sizes, names),
        out_shape=[jax.ShapeDtypeStruct(*spec) for spec in outs.values()],
        in_specs=[
            pl.BlockSpec(memory_space=pl.ANY if name in in_any else pltpu.VMEM) for name in inputs
        ],
        out_specs=[pl.BlockSpec(memory_space=pltpu.VMEM) for _ in outs],
        scratch_shapes=list(scratch.values()),
        compiler_params=pltpu.CompilerParams(
            collective_id=3, has_side_effects=True, vmem_limit_bytes=61 << 20
        ),
        name="chain",
    )(*inputs.values())
    return types.SimpleNamespace(**dict(zip(outs, results)))


def local_fast(
    tokens,
    lengths,
    cotangent,
    norm_gain,
    norm_bias,
    in_weight,
    in_bias,
    short_taps,
    short_bias,
    skip_gain,
    out_weight,
    out_bias,
    up_weight,
    up_bias,
    down_weight,
    down_bias,
    filter_in,
    filter_bias,
    filter_freq,
    filter_out,
    decay_rate,
):
    micro, rows_dev, half = tokens.shape[0], tokens.shape[2], tokens.shape[3]
    layers = norm_gain.shape[0]
    hidden = up_weight.shape[2]
    seq_parts = lax.axis_size("seq")
    seq_index, chan_index = lax.axis_index("seq"), lax.axis_index("chan")
    width = 2 * half
    rows = micro * rows_dev
    length = rows_dev * seq_parts
    block = half // seq_parts
    col_start, chan_start = seq_index * block, chan_index * half

    def both(value):
        return lax.all_gather(value, "chan", axis=value.ndim - 1, tiled=True)

    fresh = both(jnp.stack([tokens, cotangent]))[:, :, 0].reshape(2, rows, width)
    vectors = both(
        jnp.concatenate(
            [norm_gain.reshape(-1, half), norm_bias.reshape(-1, half), out_bias, down_bias], axis=0
        )
    )
    ids = seq_index * rows_dev + jnp.arange(rows_dev, dtype=jnp.int32)
    mask = (ids[None, :] < lengths[:, :1]).astype(F32).reshape(rows, 1)
    cos_np, sin_np, turn_c, turn_s = half_tables(length)
    cos_t, sin_t = jnp.asarray(cos_np, BF16), jnp.asarray(sin_np, BF16)
    turn = jnp.asarray(np.concatenate([turn_c, turn_s], axis=1).T, F32)
    table, steps_norm = positions(length, filter_in.shape[1])

    def transform_fine(value):
        high = value.astype(BF16)
        both_parts = jnp.concatenate([high, (value - high.astype(F32)).astype(BF16)], axis=0)
        pair_c, pair_s = mm(both_parts, cos_t), mm(both_parts, sin_t)
        n = value.shape[0]
        return pair_c[:n] + pair_c[n:], pair_s[:n] + pair_s[n:]

    def make_filter(w_in, w_bias, w_freq, w_out, decay):
        wave = jnp.sin(w_freq * (jnp.dot(table, w_in, precision=HIGH) + w_bias))
        raw = jnp.einsum("lf,fc->cl", wave, w_out, precision=HIGH)
        return raw * jnp.exp(-decay[:, None] * steps_norm[None, :])

    pulls, filt_re, filt_im, skips = [], [], [], []
    for layer in range(layers):
        w_out = lax.dynamic_slice_in_dim(filter_out[layer], col_start, block, 1)
        decay = lax.dynamic_slice_in_dim(decay_rate[layer], col_start, block, 0)
        skip = lax.dynamic_slice_in_dim(skip_gain[layer], col_start, block, 0)
        long_filter, pull = jax.vjp(
            lambda *leaves, decay=decay: make_filter(*leaves, decay),
            filter_in[layer],
            filter_bias[layer],
            filter_freq[layer],
            w_out,
        )
        filt_c, filt_s = transform_fine(long_filter)
        filt_re.append(jnp.tile((filt_c * turn[0] + filt_s * turn[1]) / length, (micro, 1)))
        filt_im.append(jnp.tile((filt_c * turn[1] - filt_s * turn[0]) / length, (micro, 1)))
        skips.append(jnp.tile(skip, micro)[:, None])
        pulls.append(pull)
    inputs = dict(
        x0=fresh[0],
        c0=fresh[1],
        mask=mask,
        vec=vectors,
        in_b=in_bias,
        taps=short_taps,
        short_b=short_bias,
        up_b=up_bias,
        skip=jnp.stack(skips),
        turn=turn,
        fr=jnp.stack(filt_re),
        fi=jnp.stack(filt_im),
        win=in_weight,
        wout=out_weight,
        wup=up_weight,
        wdown=down_weight,
        cos=cos_t,
        sin=sin_t,
    )
    out = chain(inputs, (layers, micro, rows_dev, half, hidden))
    out_act, grad_tokens = out.out_act, out.grad_tokens
    own768 = lax.dynamic_slice_in_dim(out.o768, chan_start, half, 2)
    small = []
    for layer in range(layers):
        g_fin, g_fbias, g_ffreq, g_fout = pulls[layer](out.o_filt[layer])
        g_skip = jnp.sum(out.o_skip[layer].reshape(micro, 1, block), axis=0)
        placed = place(jnp.concatenate([g_skip, g_fout], axis=0), col_start, half, 1)
        spread = jnp.concatenate([g_fin.reshape(-1), g_fbias, g_ffreq])
        spread_rows = -(-spread.shape[0] // half)
        spread = jnp.pad(spread, (0, spread_rows * half - spread.shape[0]))
        small.append(
            jnp.concatenate(
                [
                    own768[layer, :4],
                    out.o384[layer, :15],
                    own768[layer, 4:6],
                    out.o_up[layer].reshape(-1, half),
                    placed,
                    spread.reshape(spread_rows, half),
                ],
                axis=0,
            )
        )
    scattered = out.o_big
    flat = jnp.concatenate(small, axis=0).reshape(-1)
    lanes = 128
    piece = -(-flat.shape[0] // (16 * lanes * 8)) * 8
    flat_parts = jnp.pad(flat, (0, 16 * piece * lanes - flat.shape[0])).reshape(16, piece, lanes)
    summed = small_sum(flat_parts).reshape(2, -1)[:, : flat.shape[0]].reshape(2, layers, -1, half)

    def joined(start, stop, shape):
        value = summed[:, :, start:stop]
        value = value.transpose(1, 2, 0, 3).reshape(layers, stop - start, width)
        return value.reshape((layers, *shape, width))

    hid_rows = hidden // half
    up_value = summed[:, :, 21 : 21 + hid_rows].transpose(1, 0, 2, 3).reshape(layers, 2 * hidden)
    after = 21 + hid_rows
    bands, feat = filter_in.shape[1], filter_in.shape[2]
    spread = jnp.sum(summed[:, :, after + 1 + feat :], axis=0).reshape(layers, -1)
    in_cols, out_cols = 3 * half, 4 * half
    g_in = scattered[:, :, :in_cols].reshape(layers, width // 16, 3, half).transpose(0, 2, 1, 3)
    g_out = scattered[:, :, in_cols:out_cols].transpose(0, 2, 1)
    g_up = scattered[:, :, out_cols : out_cols + hidden]
    g_down = scattered[:, :, out_cols + hidden :].transpose(0, 2, 1)
    return (
        out_act.reshape(micro, 1, rows_dev, half),
        grad_tokens.reshape(micro, 1, rows_dev, half),
        g_in,
        g_out,
        g_up,
        g_down,
        joined(0, 2, (2,)),
        joined(2, 4, (2,)),
        joined(4, 7, (3,)),
        joined(7, 16, (3, 3)),
        joined(16, 19, (3,)),
        joined(after, after + 1, ()),
        joined(19, 20, ()),
        up_value,
        joined(20, 21, ()),
        spread[:, : bands * feat].reshape(layers, bands, feat),
        spread[:, bands * feat : bands * feat + feat],
        spread[:, bands * feat + feat : bands * feat + 2 * feat],
        joined(after + 1, after + 1 + feat, (feat,)),
    )


def solution(mesh):
    in_specs = (
        P(None, "dp", "seq", "chan"),
        P(None, "dp"),
        P(None, "dp", "seq", "chan"),
        P(None, None, "chan"),
        P(None, None, "chan"),
        P(None, None, None, "chan"),
        P(None, None, "chan"),
        P(None, None, None, "chan"),
        P(None, None, "chan"),
        P(None, "chan"),
        P(None, "chan", None),
        P(None, "chan"),
        P(None, None, "chan"),
        P(None, "chan"),
        P(None, "chan", None),
        P(None, "chan"),
        P(),
        P(),
        P(),
        P(None, None, "chan"),
        P(None, "chan"),
    )
    out_specs = (
        P(None, "dp", "seq", "chan"),
        P(None, "dp", "seq", "chan"),
        P(None, None, ("seq", "dp"), "chan"),
        P(None, "chan", ("seq", "dp")),
        P(None, ("seq", "dp"), "chan"),
        P(None, "chan", ("seq", "dp")),
        P(),
        P(),
        P(),
        P(),
        P(),
        P(),
        P(),
        P(),
        P(),
        P(),
        P(),
        P(),
        P(),
    )
    def entry(*args):
        fits = args[0].shape[2] * mesh.shape["seq"] <= 2048 and mesh.shape["seq"] == 8 and mesh.shape["dp"] == 2
        return (local_fast if fits else local)(*args)

    return jax.shard_map(entry, mesh=mesh, in_specs=in_specs, out_specs=out_specs, check_vma=False)
```

```python
import functools
import math
import types

import jax
import jax.numpy as jnp
import numpy as np
from jax import lax
from jax.experimental import pallas as pl
from jax.experimental.pallas import tpu as pltpu
from jax.sharding import PartitionSpec as P

EPS = 1e-05
HIGH = lax.Precision.HIGHEST


def shifted(value, axis, steps):
    count = lax.axis_size(axis)
    initial, last = (max(0, -steps), min(count, count - steps))
    return lax.ppermute(value, axis, [(source, source + steps) for source in range(initial, last)])


def positions(seq_length, emb_width):
    band_count = (emb_width - 1) // 2
    step_ids = jnp.arange(seq_length, dtype=jnp.float32)
    steps_norm = step_ids / seq_length
    band_freq = jnp.linspace(0.0001, band_count - 1, band_count).astype(jnp.float32)
    phases = 2.0 * math.pi * steps_norm[:, None] * band_freq[None, :]
    table = jnp.concatenate([steps_norm[:, None], jnp.cos(phases), -jnp.sin(phases)], axis=1)
    return (table, steps_norm)


def angle_table(row_count, col_count, modulus):
    product = (
        jnp.arange(row_count, dtype=jnp.int32)[:, None]
        * jnp.arange(col_count, dtype=jnp.int32)[None, :]
        % modulus
    )
    theta = product.astype(jnp.float32) * (2.0 * math.pi / modulus)
    return (jnp.cos(theta), jnp.sin(theta))


def split_length(total_length):
    lesser = 2
    for candidate in range(2, math.isqrt(total_length) + 1, 2):
        if total_length % candidate == 0:
            lesser = candidate
    return (lesser, total_length // lesser)


def dft_basis(seq_length):
    padded_len = 2 * seq_length
    lesser, greater = split_length(padded_len)
    cos_p, sin_p = angle_table(lesser, lesser, lesser)
    cos_q, sin_q = angle_table(greater, greater, greater)
    twist_c, twist_s = angle_table(lesser, greater, padded_len)
    return (cos_p, sin_p, cos_q, sin_q, twist_c, twist_s)


def right_mul(left, table):
    return jnp.einsum("ckb,bj->ckj", left, table, precision=HIGH)


def to_spectrum(signal, basis):
    cos_p, sin_p, cos_q, sin_q, twist_c, twist_s = basis
    half = cos_p.shape[0] // 2
    blocks = signal.reshape(signal.shape[0], half, cos_q.shape[0])
    first_re = jnp.einsum("ka,cab->ckb", cos_p[:, :half], blocks, precision=HIGH)
    first_im = -jnp.einsum("ka,cab->ckb", sin_p[:, :half], blocks, precision=HIGH)
    turned_re = first_re * twist_c + first_im * twist_s
    turned_im = first_im * twist_c - first_re * twist_s
    spec_re = right_mul(turned_re, cos_q) + right_mul(turned_im, sin_q)
    spec_im = right_mul(turned_im, cos_q) - right_mul(turned_re, sin_q)
    return (spec_re, spec_im)


def from_spectrum(spec_re, spec_im, basis):
    cos_p, sin_p, cos_q, sin_q, twist_c, twist_s = basis
    half = cos_p.shape[0] // 2
    back_re = right_mul(spec_re, cos_q) - right_mul(spec_im, sin_q)
    back_im = right_mul(spec_im, cos_q) + right_mul(spec_re, sin_q)
    turned_re = back_re * twist_c - back_im * twist_s
    turned_im = back_im * twist_c + back_re * twist_s
    signal = jnp.einsum("ak,ckb->cab", cos_p[:half], turned_re, precision=HIGH) - jnp.einsum(
        "ak,ckb->cab", sin_p[:half], turned_im, precision=HIGH
    )
    return signal.reshape(signal.shape[0], half * cos_q.shape[0]) / (
        cos_p.shape[0] * cos_q.shape[0]
    )


def complex_mul(left_re, left_im, right_re, right_im):
    return (left_re * right_re - left_im * right_im, left_re * right_im + left_im * right_re)


def filter_block(table, steps_norm, weight_in, bias_in, freq_in, cols_in, decay_cols):
    hidden = jnp.sin(freq_in * (jnp.dot(table, weight_in, precision=HIGH) + bias_in))
    raw = jnp.einsum("lf,fc->cl", hidden, cols_in, precision=HIGH)
    return raw * jnp.exp(-decay_cols[:, None] * steps_norm[None, :])


def to_channels(block):
    parts = lax.axis_size("seq")
    shaped = block.reshape(parts, block.shape[0] // parts, block.shape[1])
    moved = lax.all_to_all(
        shaped.astype(jnp.bfloat16), "seq", split_axis=0, concat_axis=2, tiled=True
    ).astype(shaped.dtype)
    return moved.reshape(moved.shape[1], moved.shape[2])


def to_positions(block):
    shaped = block.reshape(1, block.shape[0], block.shape[1])
    moved = lax.all_to_all(
        shaped.astype(jnp.bfloat16), "seq", split_axis=2, concat_axis=0, tiled=True
    ).astype(shaped.dtype)
    return moved.reshape(moved.shape[0] * moved.shape[1], moved.shape[2])


def branch_sum(partial_value):
    return lax.psum_scatter(
        partial_value.astype(jnp.bfloat16), "chan", scatter_dimension=1, tiled=True
    ).astype(jnp.float32)


def branch_grad(grad_low):
    return lax.all_gather(grad_low, "chan", axis=1, tiled=True)


def place(values, start, full_width, axis):
    full_shape = list(values.shape)
    full_shape[axis] = full_width
    return lax.dynamic_update_slice_in_dim(jnp.zeros(full_shape, jnp.float32), values, start, axis)


def local(
    tokens,
    lengths,
    cotangent,
    norm_gain,
    norm_bias,
    in_weight,
    in_bias,
    short_taps,
    short_bias,
    skip_gain,
    out_weight,
    out_bias,
    up_weight,
    up_bias,
    down_weight,
    down_bias,
    filter_in,
    filter_bias,
    filter_freq,
    filter_out,
    decay_rate,
):
    micro_count = tokens.shape[0]
    rows_dev = tokens.shape[2]
    chan_width = tokens.shape[3]
    layer_count = norm_gain.shape[0]
    hidden_width = up_weight.shape[2]
    seq_parts = lax.axis_size("seq")
    chan_parts = lax.axis_size("chan")
    full_width = chan_width * chan_parts
    seq_length = rows_dev * seq_parts
    seq_index = lax.axis_index("seq")
    chan_index = lax.axis_index("chan")
    block_width = chan_width // seq_parts
    col_start = seq_index * block_width
    chan_start = chan_index * chan_width
    basis = dft_basis(seq_length)
    table, steps_norm = positions(seq_length, filter_in.shape[1])
    positions_dev = seq_index * rows_dev + jnp.arange(rows_dev, dtype=jnp.int32)
    filters = []
    for layer_index in range(layer_count):
        filter_cols = lax.dynamic_slice_in_dim(filter_out[layer_index], col_start, block_width, 1)
        decay_cols = lax.dynamic_slice_in_dim(decay_rate[layer_index], col_start, block_width, 0)
        skip_cols = lax.dynamic_slice_in_dim(skip_gain[layer_index], col_start, block_width, 0)

        def make_one(weight_in, bias_in, freq_in, cols_in, decay_cols=decay_cols):
            return filter_block(table, steps_norm, weight_in, bias_in, freq_in, cols_in, decay_cols)

        long_filter, filter_pull = jax.vjp(
            make_one,
            filter_in[layer_index],
            filter_bias[layer_index],
            filter_freq[layer_index],
            filter_cols,
        )
        filt_re, filt_im = to_spectrum(long_filter, basis)
        filters.append((filt_re, filt_im, filter_pull, skip_cols))

    def norm_forward(resid, gain_bias):
        full_rows, full_gb = (
            lax.all_gather(resid, "chan", axis=1, tiled=True),
            lax.all_gather(gain_bias, "chan", axis=1, tiled=True),
        )
        mean_row = jnp.mean(full_rows, axis=1, keepdims=True)
        centred = full_rows - mean_row
        rstd = lax.rsqrt(jnp.mean(centred * centred, axis=1, keepdims=True) + EPS)
        scaled = centred * rstd
        normed = (scaled * full_gb[0] + full_gb[1]).astype(jnp.bfloat16)
        return (normed, (scaled, rstd, full_gb[0]))

    def norm_backward(grad_partial, norm_saved):
        scaled, rstd, gain_row = norm_saved
        grad_rows = lax.psum(grad_partial.astype(jnp.bfloat16), "chan").astype(jnp.float32)
        grad_scaled = grad_rows * gain_row
        grad_full = rstd * (
            grad_scaled
            - jnp.mean(grad_scaled, axis=1, keepdims=True)
            - scaled * jnp.mean(grad_scaled * scaled, axis=1, keepdims=True)
        )
        grad_own = lax.dynamic_slice_in_dim(grad_full, chan_start, chan_width, 1)
        rows_own = lax.dynamic_slice_in_dim(grad_rows, chan_start, chan_width, 1)
        scaled_own = lax.dynamic_slice_in_dim(scaled, chan_start, chan_width, 1)
        return (grad_own, jnp.sum(rows_own * scaled_own, axis=0), jnp.sum(rows_own, axis=0))

    def mixer_forward(resid, pad_mask, layer_index):
        normed, norm_saved = norm_forward(
            resid, jnp.stack([norm_gain[layer_index, 0], norm_bias[layer_index, 0]])
        )
        streams = (
            jnp.einsum(
                "sd,kdc->kcs", normed, in_weight[layer_index], preferred_element_type=jnp.float32
            )
            + in_bias[layer_index][:, :, None]
        )
        rim = shifted(streams[:, :, rows_dev - 2 :], "seq", 1)
        padded = jnp.concatenate([rim, streams], axis=2)
        taps = short_taps[layer_index]
        short_out = (
            taps[:, 0][:, :, None] * padded[:, :, 2:]
            + taps[:, 1][:, :, None] * padded[:, :, 1 : rows_dev + 1]
            + taps[:, 2][:, :, None] * padded[:, :, :rows_dev]
            + short_bias[layer_index][:, :, None]
        )
        product = short_out[1] * short_out[2]
        chan_prod = to_channels(product)
        filt_re, filt_im, filter_pull, skip_cols = filters[layer_index]
        prod_re, prod_im = to_spectrum(chan_prod, basis)
        conv_re, conv_im = complex_mul(prod_re, prod_im, filt_re, filt_im)
        chan_out = from_spectrum(conv_re, conv_im, basis) + skip_cols[:, None] * chan_prod
        long_out = to_positions(chan_out)
        mixed = (short_out[0] * long_out).astype(jnp.bfloat16)
        partial_value = jnp.einsum(
            "cs,cd->sd", mixed, out_weight[layer_index], preferred_element_type=jnp.float32
        )
        branch = branch_sum(partial_value) + out_bias[layer_index]
        saved = (
            normed,
            norm_saved,
            padded,
            short_out,
            chan_prod,
            prod_re,
            prod_im,
            long_out,
            mixed,
        )
        return (resid + pad_mask[:, None] * branch, saved)

    def mlp_forward(resid, pad_mask, layer_index):
        normed, norm_saved = norm_forward(
            resid, jnp.stack([norm_gain[layer_index, 1], norm_bias[layer_index, 1]])
        )
        pre_act = (
            jnp.dot(normed, up_weight[layer_index], preferred_element_type=jnp.float32)
            + up_bias[layer_index]
        )
        activated = jax.nn.gelu(pre_act, approximate=False).astype(jnp.bfloat16)
        partial_value = jnp.dot(
            activated, down_weight[layer_index], preferred_element_type=jnp.float32
        )
        branch = branch_sum(partial_value) + down_bias[layer_index]
        return (resid + pad_mask[:, None] * branch, (normed, norm_saved, pre_act, activated))

    def mlp_backward(grad_resid, pad_mask, layer_index, saved):
        normed, norm_saved, pre_act, activated = saved
        grad_branch = pad_mask[:, None] * grad_resid
        g_down_bias = jnp.sum(grad_branch, axis=0)
        grad_full = branch_grad(grad_branch.astype(jnp.bfloat16))
        g_down_weight = jnp.einsum(
            "sf,sd->fd", activated, grad_full, preferred_element_type=jnp.float32
        )
        grad_act = jnp.einsum(
            "sd,fd->sf", grad_full, down_weight[layer_index], preferred_element_type=jnp.float32
        )
        unused_value, gelu_pull = jax.vjp(
            lambda inner: jax.nn.gelu(inner, approximate=False), pre_act
        )
        grad_pre = gelu_pull(grad_act)[0]
        g_up_bias = jnp.sum(grad_pre, axis=0)
        pre_low = grad_pre.astype(jnp.bfloat16)
        g_up_weight = jnp.einsum("sd,sf->df", normed, pre_low, preferred_element_type=jnp.float32)
        grad_normed = jnp.einsum(
            "sf,df->sd", pre_low, up_weight[layer_index], preferred_element_type=jnp.float32
        )
        grad_own, g_gain, g_bias = norm_backward(grad_normed, norm_saved)
        return (
            grad_resid + grad_own,
            (g_up_weight, g_down_weight, g_gain, g_bias, g_up_bias, g_down_bias),
        )

    mixer_acc = [None] * layer_count
    mlp_acc = [None] * layer_count
    outputs = []
    input_grads = []
    for micro_index in range(micro_count):
        pad_mask = (positions_dev < lengths[micro_index, 0]).astype(jnp.float32)
        resid = tokens[micro_index, 0].astype(jnp.float32)
        layer_inputs = []
        layer_saved = []
        for layer_index in range(layer_count):
            layer_inputs.append(resid)
            resid, mix_saved = mixer_forward(resid, pad_mask, layer_index)
            layer_inputs.append(resid)
            resid, mlp_saved = mlp_forward(resid, pad_mask, layer_index)
            layer_saved.append((mix_saved, mlp_saved))
        outputs.append(resid)
        grad_resid = cotangent[micro_index, 0].astype(jnp.float32)
        for layer_index in reversed(range(layer_count)):
            mlp_saved = mlp_forward(layer_inputs[2 * layer_index + 1], pad_mask, layer_index)[1]
            grad_resid, mlp_grads = mlp_backward(grad_resid, pad_mask, layer_index, mlp_saved)
            mix_saved = mixer_forward(layer_inputs[2 * layer_index], pad_mask, layer_index)[1]
            (
                mixer_normed,
                mixer_norm_saved,
                mixer_padded,
                mixer_short_out,
                mixer_chan_prod,
                mixer_prod_re,
                mixer_prod_im,
                mixer_long_out,
                mixer_mixed,
            ) = mix_saved
            mixer_filt_re, mixer_filt_im, mixer_filter_pull, mixer_skip_cols = filters[layer_index]
            mixer_grad_branch = pad_mask[:, None] * grad_resid
            g_out_bias = jnp.sum(mixer_grad_branch, axis=0)
            mixer_grad_full = branch_grad(mixer_grad_branch.astype(jnp.bfloat16))
            g_out_weight = jnp.einsum(
                "cs,sd->cd", mixer_mixed, mixer_grad_full, preferred_element_type=jnp.float32
            )
            grad_mixed = jnp.einsum(
                "sd,cd->cs",
                mixer_grad_full,
                out_weight[layer_index],
                preferred_element_type=jnp.float32,
            )
            grad_long = grad_mixed * mixer_short_out[0]
            grad_gate = grad_mixed * mixer_long_out
            chan_grad = to_channels(grad_long)
            grad_re, grad_im = to_spectrum(chan_grad, basis)
            back_re, back_im = complex_mul(grad_re, grad_im, mixer_filt_re, -mixer_filt_im)
            chan_dprod = (
                from_spectrum(back_re, back_im, basis) + mixer_skip_cols[:, None] * chan_grad
            )
            corr_re, corr_im = complex_mul(grad_re, grad_im, mixer_prod_re, -mixer_prod_im)
            grad_filter = from_spectrum(corr_re, corr_im, basis)
            g_skip = jnp.sum(chan_grad * mixer_chan_prod, axis=1)
            grad_product = to_positions(chan_dprod)
            grad_short = jnp.stack(
                [grad_gate, grad_product * mixer_short_out[2], grad_product * mixer_short_out[1]]
            )
            g_short_bias = jnp.sum(grad_short, axis=2)
            g_taps = jnp.stack(
                [
                    jnp.sum(grad_short * mixer_padded[:, :, 2:], axis=2),
                    jnp.sum(grad_short * mixer_padded[:, :, 1 : rows_dev + 1], axis=2),
                    jnp.sum(grad_short * mixer_padded[:, :, :rows_dev], axis=2),
                ],
                axis=1,
            )
            next_rim = shifted(grad_short[:, :, :2], "seq", -1)
            extended = jnp.concatenate([grad_short, next_rim], axis=2)
            mixer_taps = short_taps[layer_index]
            grad_streams = (
                mixer_taps[:, 0][:, :, None] * extended[:, :, :rows_dev]
                + mixer_taps[:, 1][:, :, None] * extended[:, :, 1 : rows_dev + 1]
                + mixer_taps[:, 2][:, :, None] * extended[:, :, 2:]
            )
            g_in_bias = jnp.sum(grad_streams, axis=2)
            streams_low = grad_streams.astype(jnp.bfloat16)
            g_in_weight = jnp.einsum(
                "sd,kcs->kdc", mixer_normed, streams_low, preferred_element_type=jnp.float32
            )
            mixer_grad_normed = jnp.einsum(
                "kcs,kdc->sd",
                streams_low,
                in_weight[layer_index],
                preferred_element_type=jnp.float32,
            )
            mixer_grad_own, mixer_g_gain, mixer_g_bias = norm_backward(
                mixer_grad_normed, mixer_norm_saved
            )
            grads = (
                g_in_weight,
                g_out_weight,
                mixer_g_gain,
                mixer_g_bias,
                g_in_bias,
                g_taps,
                g_short_bias,
                g_skip,
                g_out_bias,
                grad_filter,
            )
            grad_resid, mix_grads = (grad_resid + mixer_grad_own, grads)
            if mixer_acc[layer_index] is None:
                mixer_acc[layer_index] = mix_grads
                mlp_acc[layer_index] = mlp_grads
            else:
                mixer_acc[layer_index] = jax.tree.map(jnp.add, mixer_acc[layer_index], mix_grads)
                mlp_acc[layer_index] = jax.tree.map(jnp.add, mlp_acc[layer_index], mlp_grads)
        input_grads.append(grad_resid)
    filter_grads = [
        filters[layer_index][2](mixer_acc[layer_index][9]) for layer_index in range(layer_count)
    ]
    skip_start = chan_start + col_start

    def stack_mix(member):
        return jnp.stack([mixer_acc[layer_index][member] for layer_index in range(layer_count)])

    def stack_mlp(member):
        return jnp.stack([mlp_acc[layer_index][member] for layer_index in range(layer_count)])

    def stack_filter(member):
        return jnp.stack([filter_grads[layer_index][member] for layer_index in range(layer_count)])

    big_grads = (
        lax.psum_scatter(stack_mix(0), ("seq", "dp"), scatter_dimension=2, tiled=True),
        lax.psum_scatter(stack_mix(1), ("seq", "dp"), scatter_dimension=2, tiled=True),
        lax.psum_scatter(stack_mlp(0), ("seq", "dp"), scatter_dimension=1, tiled=True),
        lax.psum_scatter(stack_mlp(1), ("seq", "dp"), scatter_dimension=2, tiled=True),
    )
    gain_grads = jnp.stack([stack_mix(2), stack_mlp(2)], axis=1)
    bias_grads = jnp.stack([stack_mix(3), stack_mlp(3)], axis=1)
    small = lax.psum(
        (
            place(gain_grads, chan_start, full_width, 2),
            place(bias_grads, chan_start, full_width, 2),
            place(stack_mix(4), chan_start, full_width, 2),
            place(stack_mix(5), chan_start, full_width, 3),
            place(stack_mix(6), chan_start, full_width, 2),
            place(stack_mix(7), skip_start, full_width, 1),
            place(stack_mix(8), chan_start, full_width, 1),
            place(stack_mlp(4), chan_index * hidden_width, hidden_width * chan_parts, 1),
            place(stack_mlp(5), chan_start, full_width, 1),
            stack_filter(0),
            stack_filter(1),
            stack_filter(2),
            place(stack_filter(3), skip_start, full_width, 2),
        ),
        ("seq", "chan", "dp"),
    )
    out_act = jnp.stack(outputs)[:, None]
    grad_tokens = jnp.stack(input_grads)[:, None]
    return (
        out_act,
        grad_tokens,
        big_grads[0],
        big_grads[1],
        big_grads[2],
        big_grads[3],
        small[0],
        small[1],
        small[2],
        small[3],
        small[4],
        small[5],
        small[6],
        small[7],
        small[8],
        small[9],
        small[10],
        small[11],
        small[12],
    )


F32 = jnp.float32
BF16 = jnp.bfloat16
MESH = pl.DeviceIdType.MESH
CHUNKS = (
    (1, 3072, 512, "xlyh"),
    (1, 3584, 512, "lyxh"),
    (1, 4096, 512, "yxlh"),
    (1, 1536, 512, "lyxh"),
    (1, 2048, 512, "ylhx"),
    (1, 2560, 512, "xlyh"),
    (1, 0, 768, "ylxh"),
    (1, 768, 768, "xlyh"),
    (0, 1152, 384, "xylh"),
    (0, 3072, 512, "ylhx"),
    (0, 3584, 512, "yxlh"),
    (0, 4096, 512, "xylh"),
    (0, 1536, 512, "xlyh"),
    (0, 2048, 512, "xylh"),
    (0, 2560, 512, "xylh"),
    (0, 0, 384, "xylh"),
    (0, 384, 384, "ylxh"),
    (0, 768, 384, "xylh"),
)
TICKS = 13
PLAN = {
    7: ((0, 0), (1, 0), (2, 0),),
    10: ((3, 0), (4, 0), (5, 0),),
    12: ((0, 1), (1, 1), (2, 1),),
    15: ((3, 1), (4, 1),),
    17: ((7, 0),),
    18: ((5, 1),),
    19: ((2, 2),),
    20: ((1, 2),),
    21: ((4, 2),),
    22: ((6, 0), (0, 2),),
    23: ((7, 1), (11, 0), (2, 3),),
    25: ((1, 3), (9, 0),),
    26: ((6, 1), (12, 0), (0, 3), (10, 0), (9, 1), (5, 2), (13, 0), (12, 1), (11, 1), (7, 2), (9, 2), (14, 0), (5, 3), (11, 2), (3, 2), (16, 0), (7, 3), (13, 1), (11, 3), (8, 0), (12, 2), (4, 3), (3, 3), (16, 1), (14, 1), (13, 2), (15, 0), (8, 1), (12, 3), (14, 2), (13, 3), (15, 1), (17, 0), (8, 2), (14, 3), (6, 2), (15, 2), (17, 1), (8, 3), (10, 1), (9, 3), (6, 3), (16, 2), (15, 3), (17, 2), (10, 2), (16, 3), (17, 3), (10, 3),),
}
SMALL = (6, 9, 22, 34)


def half_tables(count):
    odd = 2 * np.arange(count, dtype=np.int64) + 1
    angle = np.outer(odd, odd) % (8 * count) * (math.pi / (4 * count))
    twist = odd * (math.pi / (4 * count))
    return np.cos(angle), np.sin(angle), np.cos(twist)[:, None], np.sin(twist)[:, None]


def mesh_bits():
    seq, dp = lax.axis_index("seq"), lax.axis_index("dp")
    return {"x": dp, "y": lax.rem(seq, 2), "l": lax.rem(seq // 2, 2), "h": seq // 4}


def mesh_peers():
    seq, dp = lax.axis_index("seq"), lax.axis_index("dp")
    bits = mesh_bits()
    return {
        "x": {"dp": 1 - dp},
        "y": {"seq": seq + 1 - 2 * bits["y"]},
        "l": {"seq": seq + 2 - 4 * bits["l"]},
        "h": {"seq": seq + 4 - 8 * bits["h"]},
    }


def greet(devices):
    barrier = pltpu.get_barrier_semaphore()
    for device in devices:
        pl.semaphore_signal(barrier, inc=1, device_id=device, device_id_type=MESH)
    pl.semaphore_wait(barrier, len(devices))


def mm(left, right):
    return jnp.dot(left, right, preferred_element_type=F32)


def fine(left, right, dims=((1,), (0,))):
    return lax.dot_general(left, right, (dims, ((), ())), precision=HIGH, preferred_element_type=F32)


def mm_nt(left, right):
    return lax.dot_general(left, right, (((1,), (1,)), ((), ())), preferred_element_type=F32)


def chain_kernel(sizes, names, *refs):
    layers, micro, span, half, hidden, feat, freq_lane = sizes
    r = types.SimpleNamespace(**dict(zip(names, refs)))
    width, rows, parts = 2 * half, micro * span, 8
    block = half // parts
    length = span * parts
    seq, chan = lax.axis_index("seq"), lax.axis_index("chan")
    pair = seq + 1 - 2 * lax.rem(seq, 2)
    step = 32

    def load(name, layer, slot):
        return pltpu.make_async_copy(getattr(r, name).at[layer], getattr(r, name + "_v"), r.w_sem.at[slot])

    weights = (("win", 0), ("wout", 1), ("wup", 2), ("wdown", 3))
    table_loads = [
        pltpu.make_async_copy(r.cos, r.cos_v, r.t_sem.at[0]),
        pltpu.make_async_copy(r.sin, r.sin_v, r.t_sem.at[1]),
    ]
    load("win", 0, 0).start()
    for copy in table_loads:
        copy.start()
    for name, slot in weights[1:]:
        load(name, 0, slot).start()
    peers, bits = mesh_peers(), mesh_bits()
    dp = lax.axis_index("dp")
    ranks = 2 * parts
    me = 2 * seq + dp
    ranked = [lax.rem(me + far, ranks) for far in range(1, ranks)]
    greet([{"seq": other // 2, "dp": lax.rem(other, 2)} for other in ranked] + [{"chan": 1 - chan}])

    def core_copy(source, target, slot):
        return pltpu.make_async_remote_copy(
            src_ref=source,
            dst_ref=target,
            send_sem=r.core_sem.at[0, slot],
            recv_sem=r.core_sem.at[1, slot],
            device_id={"chan": 1 - chan},
            device_id_type=MESH,
        )

    for layer in range(layers):
        at = pl.ds(layer, 1)
        for n in range(2):
            r.params[pl.ds(2 * layer + n, 1), :] = r.gain[layer, pl.ds(n, 1), :]
            r.params[pl.ds(2 * layers + 2 * layer + n, 1), :] = r.bias[layer, pl.ds(n, 1), :]
        r.params[pl.ds(4 * layers + layer, 1), :] = r.out_b[at, :]
        r.params[pl.ds(5 * layers + layer, 1), :] = r.down_b[at, :]
    r.params[pl.ds(12, 4), :] = jnp.zeros((4, half), F32)
    first = [
        core_copy(r.params.at[pl.ds(0, 16)], r.vec2.at[chan], 0),
        core_copy(r.tok, r.both.at[chan, 0], 1),
        core_copy(r.cot, r.both.at[chan, 1], 2),
    ]
    for copy in first:
        copy.start()
    r.vec2[chan] = r.params[pl.ds(0, 16), :]
    r.both[chan, 0] = r.tok[...]
    r.both[chan, 1] = r.cot[...]
    r.sm[...] = jnp.zeros_like(r.sm)
    r.vecs[...] = jnp.zeros_like(r.vecs)
    r.o768[...] = jnp.zeros_like(r.o768)
    for m in range(micro):
        place_ids = seq * span + lax.broadcasted_iota(jnp.int32, (span, 1), 0)
        r.mask[pl.ds(m * span, span), :] = (place_ids < r.lens[0, m]).astype(F32)
    for layer in range(layers):
        at = pl.ds(layer, 1)
        for k in range(3):
            r.params[pl.ds(16 + 3 * layer + k, 1), :] = r.in_b[k, at, :]
            r.params[pl.ds(40 + 3 * layer + k, 1), :] = r.short_b[k, at, :]
            for j in range(3):
                r.params[pl.ds(22 + 9 * layer + 3 * k + j, 1), :] = r.taps[k, j, at, :]
    first[0].wait_recv()
    r.vec[...] = jnp.concatenate([r.vec2[0], r.vec2[1]], axis=1)

    def rank_copy(source, target, phase, other, slot):
        return pltpu.make_async_remote_copy(
            src_ref=source,
            dst_ref=target,
            send_sem=r.sm_sem.at[phase, 0, other],
            recv_sem=r.sm_sem.at[phase, 1, slot],
            device_id={"seq": other // 2, "dp": lax.rem(other, 2)},
            device_id_type=MESH,
        )

    def chan_rows(layer):
        value = r.chv[layer]
        return value[:, :feat], value[:, feat : feat + 1], value[:, feat + 1 : feat + 2]

    def filter_forward(layer):
        at = pl.ds(layer, 1)
        r.pack_t[...] = jnp.zeros_like(r.pack_t)
        for i in range(freq_lane - feat - 1):
            r.pack_t[pl.ds(feat + i, 1), :] = r.fin[i, at, :]
        r.pack_t[pl.ds(freq_lane - 1, 1), :] = r.fbias[at, :]
        r.pack_t[pl.ds(freq_lane, 1), :] = r.ffreq[at, :]
        r.pack[layer] = r.pack_t[...].T
        r.chan_t[...] = jnp.zeros_like(r.chan_t)
        r.chan_t[pl.ds(0, feat), :] = r.fout[layer]
        r.chan_t[pl.ds(feat, 1), :] = r.decay[at, :]
        r.chan_t[pl.ds(feat + 1, 1), :] = r.skip[at, :]
        r.chv_t[...] = r.chan_t[...].T
        r.chv[layer] = r.chv_t[pl.ds(pl.multiple_of(seq * block, 8), block), :]
        turned, decay, skip = chan_rows(layer)
        r.skip_l[layer] = jnp.concatenate([skip] * micro, axis=0)
        pack = r.pack[layer]
        freq = pack[:, freq_lane : freq_lane + 1]
        for c in range(0, length, 256):
            lanes = pl.ds(c, 256)
            inner = fine(pack, r.emb[:, lanes])
            wave = jnp.sin(freq * inner)
            r.inner[layer, :, lanes] = inner
            r.wave[pl.ds(layer * feat, feat), lanes] = wave
            filt = fine(turned, wave) * jnp.exp(-decay * r.emb[pl.ds(feat, 1), lanes])
            high = filt.astype(BF16)
            r.spec[0, pl.ds(0, block), lanes] = high
            r.spec[0, pl.ds(block, block), lanes] = (filt - high.astype(F32)).astype(BF16)
        for c in range(0, length, 256):
            lanes = pl.ds(c, 256)
            fc, fs = mm(r.spec[0], r.cos_v[:, lanes]), mm(r.spec[0], r.sin_v[:, lanes])
            fc, fs = fc[:block] + fc[block:], fs[:block] + fs[block:]
            tc, ts = r.turn[pl.ds(0, 1), lanes], r.turn[pl.ds(1, 1), lanes]
            r.fr[layer, :, lanes] = (fc * tc + fs * ts) * (1.0 / length)
            r.fi[layer, :, lanes] = (fc * ts - fs * tc) * (1.0 / length)

    def twice(value):
        return jnp.concatenate([value] * micro, axis=0)

    def filter_backward(layer):
        turned, decay, _ = chan_rows(layer)
        freq = r.pack[layer, :, freq_lane : freq_lane + 1]
        g_out = g_pack = g_freq = 0.0
        for c in range(0, length, 256):
            lanes = pl.ds(c, 256)
            raw = r.o_filt[layer, :, lanes] * jnp.exp(-decay * r.emb[pl.ds(feat, 1), lanes])
            g_out = g_out + fine(raw, r.wave[:, lanes], ((1,), (1,)))
            inner = r.inner[layer, :, lanes]
            slope = fine(turned, raw, ((0,), (0,))) * jnp.cos(freq * inner)
            g_freq = g_freq + jnp.sum(slope * inner, axis=1, keepdims=True)
            g_pack = g_pack + fine(slope * freq, r.emb[:, lanes], ((1,), (1,)))
        lane = lax.broadcasted_iota(jnp.int32, (block, 128), 1)
        mine = (lane >= layer * feat) & (lane < (layer + 1) * feat)
        r.sm[seq] = jnp.where(mine, g_out, r.sm[seq])
        lane = lax.broadcasted_iota(jnp.int32, (feat, 128), 1)
        r.spread[layer] = g_pack + jnp.where(lane == freq_lane, g_freq, 0.0)

    def small_begin():
        for layer in range(layers):
            r.vecs[pl.ds(32 * layer, 8), :] = r.o768[pl.ds(8 * layer, 8), own_lanes]
            for i in range(hidden // half):
                r.vecs[pl.ds(32 * layer + 24 + i, 1), :] = r.o_up[pl.ds(layer, 1), pl.ds(i * half, half)]
        spread = jnp.concatenate(
            [r.spread[layer] for layer in range(layers)] + [jnp.zeros((half - layers * feat, 128), F32)], axis=0
        )
        total = r.vecs[...].T + spread
        r.sm[pl.ds(parts, parts)] = total.reshape(parts, block, 128)
        lane = lax.broadcasted_iota(jnp.int32, (block, 128), 1)
        for layer in range(layers):
            r.sm[parts + seq] = r.sm[parts + seq] + jnp.where(lane == 112 + layer, r.gskip[layer], 0.0)
        for other in ranked:
            rank_copy(r.sm.at[other], r.sm_recv.at[me], 0, other, me).start()

    def small_middle():
        total = r.sm[me]
        for other in ranked:
            rank_copy(r.sm.at[other], r.sm_recv.at[other], 0, other, other).wait_recv()
            total = total + r.sm_recv[other]
        r.o_small[chan, me] = total
        for other in ranked:
            rank_copy(r.o_small.at[chan, me], r.o_small.at[chan, me], 1, other, me).start()

    def small_last():
        for other in ranked:
            rank_copy(r.o_small.at[chan, me], r.o_small.at[chan, other], 1, other, other).wait_recv()
        core_copy(r.o_small.at[chan], r.o_small.at[chan], 3).start()

    def small_end():
        core_copy(r.o_small.at[chan], r.o_small.at[1 - chan], 3).wait()
        for other in ranked:
            rank_copy(r.sm.at[other], r.sm_recv.at[me], 0, other, me).wait_send()
            rank_copy(r.o_small.at[chan, me], r.o_small.at[chan, me], 1, other, me).wait_send()
        for copy in first:
            copy.wait_send()

    own_lanes = pl.ds(pl.multiple_of(chan * half, half), half)
    sent, done, begun, written = [], [], [], set()
    received = (r.rs1, r.rs2, r.rs3, r.rs4)

    def rs_index(chunk, stage, bit):
        order = CHUNKS[chunk][3]
        left = [axis for axis in "hlyx" if axis not in order[:stage]]
        return left, left.index(order[stage])

    def rs_held(chunk, stage, index):
        layer, start, columns = CHUNKS[chunk][:3]
        lanes = pl.ds(start, columns)
        if stage == 0:
            return r.big.at[(*index, slice(None), lanes)]
        return received[stage - 1].at[(layer, *index, slice(None), lanes)]

    def rs_copy(chunk, stage):
        layer, start, columns, order = CHUNKS[chunk][:4]
        axis = order[stage]
        left, spot = rs_index(chunk, stage, 0)
        index = tuple(1 - bits[axis] if name == axis else slice(None) for name in left)
        rest = (slice(None),) * (4 - stage)
        return pltpu.make_async_remote_copy(
            src_ref=rs_held(chunk, stage, index),
            dst_ref=received[stage].at[(layer, *rest, pl.ds(start, columns))],
            send_sem=r.rs_sem.at[0, chunk, stage],
            recv_sem=r.rs_sem.at[1, chunk, stage],
            device_id=peers[axis],
            device_id_type=MESH,
        )

    def advance(chunk, stage):
        layer, start, columns, order = CHUNKS[chunk][:4]
        lanes = pl.ds(start, columns)
        done.append((chunk, stage))
        rs_copy(chunk, stage).wait_recv()
        left, spot = rs_index(chunk, stage, 0)
        for flat in range(2 ** (3 - stage)):
            kept = [flat >> shift & 1 for shift in reversed(range(3 - stage))]
            mine = tuple(kept[:spot] + [bits[order[stage]]] + kept[spot:])
            total = rs_held(chunk, stage, mine)[...].astype(F32)
            there = received[stage].at[(layer, *kept, slice(None), lanes)]
            total = total + there[...].astype(F32)
            if stage == 3:
                r.o_big[layer, :, lanes] = total
            else:
                there[...] = total.astype(BF16)
        if stage < 3:
            rs_copy(chunk, stage + 1).start()

    def begin(layer, start, stop):
        written.update((layer, column) for column in range(start, stop, 128))
        for chunk, spec in enumerate(CHUNKS):
            need = {(spec[0], column) for column in range(spec[1], spec[1] + spec[2], 128)}
            if chunk not in begun and need <= written:
                begun.append(chunk)
                rs_copy(chunk, 0).start()

    def tick(layer, spot):
        now = TICKS * (layers - 1 - layer) + spot
        for chunk, stage in PLAN.get(now, ()):
            advance(chunk, stage)

    def short_all(layer):
        for k in range(3):
            for m in range(micro):
                short_part(layer, k, m, 0, span)

    def next_load(layer, name, slot):
        if 0 <= layer < layers:
            load(name, layer, slot).start()

    def seq_copy(send, recv, sems, other, outgoing):
        slot = seq if outgoing else other
        return pltpu.make_async_remote_copy(
            src_ref=getattr(r, send).at[other],
            dst_ref=getattr(r, recv).at[slot],
            send_sem=getattr(r, sems).at[0, other],
            recv_sem=getattr(r, sems).at[1, slot],
            device_id={"seq": other},
            device_id_type=MESH,
        )

    def all_others():
        return [lax.rem(seq + far, parts) for far in (4, 3, 5, 2, 6, 1, 7)]

    def wait_all(send, recv, sems):
        for other in all_others():
            seq_copy(send, recv, sems, other, False).wait_recv()
        for other in all_others():
            seq_copy(send, recv, sems, other, True).wait_send()

    def pair_copy(slot, m):
        return pltpu.make_async_remote_copy(
            src_ref=r.pair_send.at[slot, m],
            dst_ref=r.pair_recv.at[slot, m],
            send_sem=r.pair_sem.at[0, slot, m],
            recv_sem=r.pair_sem.at[1, slot, m],
            device_id={"chan": 1 - chan},
            device_id_type=MESH,
        )

    def rim_copy(way):
        other = lax.rem(seq + (1 if way == 0 else parts - 1), parts)
        return pltpu.make_async_remote_copy(
            src_ref=r.rim_send.at[way],
            dst_ref=r.rim_recv.at[way],
            send_sem=r.rim_sem.at[0, way],
            recv_sem=r.rim_sem.at[1, way],
            device_id={"seq": other},
            device_id_type=MESH,
        )

    def paired(slot, m, base, count):
        at = (slot, m, pl.ds(base, count), slice(None))
        return r.pair_send[at].astype(F32) + r.pair_recv[at].astype(F32)

    def row(name, index):
        return getattr(r, name)[pl.ds(index, 1), :]

    gains = [[row("vec", 2 * layer + n) for n in range(2)] for layer in range(layers)]
    biases = [[row("vec", 2 * layers + 2 * layer + n) for n in range(2)] for layer in range(layers)]
    branch_bias = [[row("vec", 4 * layers + layer), row("vec", 5 * layers + layer)] for layer in range(layers)]

    def norm_rows(at, x, layer, n):
        centred = x - jnp.mean(x, axis=1, keepdims=True)
        rstd = lax.rsqrt(jnp.mean(centred * centred, axis=1, keepdims=True) + EPS)
        scaled = centred * rstd
        r.xh[layer, n, at, :] = scaled
        r.rstd[layer, n, at, :] = rstd
        r.u[layer, n, at, :] = (scaled * gains[layer][n] + biases[layer][n]).astype(BF16)

    def forward_rows(slot, bias, layer, n):
        for m in range(micro):
            pair_copy(slot, m).wait_recv()

            @pl.loop(0, span // step)
            def _(i):
                base = pl.multiple_of(i * step, step)
                at = pl.ds(m * span + base, step)
                x = r.x[at, :] + r.mask[at, :] * (paired(slot, m, base, step) + bias)
                r.x[at, :] = x
                if layer < layers:
                    norm_rows(at, x, layer, n)

        for m in range(micro):
            pair_copy(slot, m).wait_send()

    def send_partial(slot, make):
        for m in range(micro):
            r.pair_send[slot, m] = make(m).astype(BF16)
            pair_copy(slot, m).start()

    def tap(layer, k, j):
        return r.params[pl.ds(22 + 9 * layer + 3 * k + j, 1), :]

    def short_part(layer, k, m, low, high):
        z = r.z
        total = r.params[pl.ds(40 + 3 * layer + k, 1), :]
        for j in range(3):
            total = total + tap(layer, k, j) * z[layer, k, m, pl.ds(8 + low - j, high - low), :]
        r.s[k, m, pl.ds(low, high - low), :] = total

    def to_channels(m, value):
        turned = value.T.astype(BF16)
        for j in range(parts):
            r.a_send[j, pl.ds(m * block, block), :] = turned[j * block : (j + 1) * block]

    def start_channels():
        for other in all_others():
            seq_copy("a_send", "a_recv", "a_sem", other, True).start()
        r.a_recv[seq] = r.a_send[seq]

    def gathered():
        return jnp.concatenate([r.a_recv[j] for j in range(parts)], axis=1)

    def from_channels(m):
        stack = [r.b_recv[j, pl.ds(m * block, block), :].astype(F32) for j in range(parts)]
        return jnp.concatenate(stack, axis=0).T

    def inverse_and_send(signal):
        for far in (2, 1, 3, 0):
            at = lax.rem(seq // 2 + far, parts // 2)
            lanes = pl.ds(pl.multiple_of(at * 2 * span, 2 * span), 2 * span)
            out = mm(r.spec[0], r.cos_v[:, lanes]) + mm(r.spec[1], r.sin_v[:, lanes])
            out = (out + r.skip_v[...] * signal[:, lanes].astype(F32)).astype(BF16)
            for h in range(2):
                r.b_send[2 * at + h] = out[:, h * span : (h + 1) * span]
            if far:
                for h in range(2):
                    seq_copy("b_send", "b_recv", "b_sem", 2 * at + h, True).start()
            else:
                seq_copy("b_send", "b_recv", "b_sem", pair, True).start()
                r.b_recv[seq] = r.b_send[seq]

    first[1].wait_recv()
    for base in range(0, rows, step):
        at = pl.ds(base, step)
        x = jnp.concatenate([r.both[0, 0, at, :], r.both[1, 0, at, :]], axis=1).astype(F32)
        r.x[at, :] = x
        norm_rows(at, x, 0, 0)

    for layer in range(layers):
        load("win", layer, 0).wait()
        for k in range(3):
            z = mm(r.u[layer, 0], r.win_v[k]) + r.params[pl.ds(16 + 3 * layer + k, 1), :]
            for m in range(micro):
                r.z[layer, k, m, pl.ds(8, span), :] = z[m * span : (m + 1) * span]
                r.rim_send[0, pl.ds(k * 4 + m * 2, 2), :] = z[(m + 1) * span - 2 : (m + 1) * span]
        rim_copy(0).start()
        next_load(layer + 1, "win", 0)
        for k in range(3):
            for m in range(micro):
                short_part(layer, k, m, step, span)
        rim_copy(0).wait()
        inner = (seq > 0).astype(F32)
        for k in range(3):
            for m in range(micro):
                r.z[layer, k, m, pl.ds(6, 2), :] = inner * r.rim_recv[0, pl.ds(k * 4 + m * 2, 2), :]
                short_part(layer, k, m, 0, step)
        for m in range(micro):
            to_channels(m, r.s[1, m] * r.s[2, m])
        start_channels()
        if layer == 0:
            for copy in table_loads:
                copy.wait()
            filter_forward(0)
        wait_all("a_send", "a_recv", "a_sem")
        signal = gathered()
        r.sig[layer] = signal
        r.skip_v[...] = r.skip_l[layer]
        for c in range(0, length, 256):
            lanes = pl.ds(c, 256)
            pc, ps = mm(signal, r.cos_v[:, lanes]), mm(signal, r.sin_v[:, lanes])
            fr, fi = twice(r.fr[layer, :, lanes]), twice(r.fi[layer, :, lanes])
            r.pc[layer, :, lanes], r.ps[layer, :, lanes] = pc.astype(BF16), ps.astype(BF16)
            r.spec[0, :, lanes] = (pc * fr + ps * fi).astype(BF16)
            r.spec[1, :, lanes] = (ps * fr - pc * fi).astype(BF16)
        inverse_and_send(r.sig.at[layer])
        if layer + 1 < layers:
            filter_forward(layer + 1)
        load("wout", layer, 1).wait()
        wait_all("b_send", "b_recv", "b_sem")
        for m in range(micro):
            y = from_channels(m)
            r.y[layer, m] = y.astype(BF16)
            r.mixed[layer, pl.ds(m * span, span), :] = (r.s[0, m] * y).astype(BF16)
        send_partial(0, lambda m: mm(r.mixed[layer, pl.ds(m * span, span), :], r.wout_v[...]))
        next_load(layer + 1, "wout", 1)
        forward_rows(0, branch_bias[layer][0], layer, 1)

        load("wup", layer, 2).wait()
        for c in range(0, hidden, 256):
            lanes = pl.ds(c, 256)
            for m in range(micro):
                at = pl.ds(m * span, span)
                a = mm(r.u[layer, 1, at, :], r.wup_v[:, lanes]) + r.up_b[pl.ds(layer, 1), lanes]
                cdf = 0.5 + 0.5 * lax.erf(a * math.sqrt(0.5))
                pdf = jnp.exp(-0.5 * a * a) * (1.0 / math.sqrt(2.0 * math.pi))
                r.g[layer, at, lanes] = (a * cdf).astype(BF16)
                r.slope[layer, at, lanes] = (cdf + a * pdf).astype(BF16)
        next_load(layer + 1, "wup", 2)
        load("wdown", layer, 3).wait()
        send_partial(1, lambda m: mm(r.g[layer, pl.ds(m * span, span), :], r.wdown_v[...]))
        next_load(layer + 1, "wdown", 3)
        forward_rows(1, branch_bias[layer][1], layer + 1, 0)

    r.out_act[...] = r.x[:, own_lanes]

    def branch_rows(at, dx):
        branch = r.mask[at, :] * dx
        r.grad[at, :] = branch.astype(BF16)
        return jnp.sum(branch.reshape(step // 8, 8, width), axis=0)

    def put768(layer, index, value):
        r.o768[pl.ds(8 * layer + index, 1), :] = jnp.sum(value, axis=0, keepdims=True)

    first[2].wait_recv()
    total = jnp.zeros((8, width), F32)
    for base in range(0, rows, step):
        at = pl.ds(base, step)
        dx = jnp.concatenate([r.both[0, 1, at, :], r.both[1, 1, at, :]], axis=1).astype(F32)
        r.x[at, :] = dx
        total = total + branch_rows(at, dx)
    put768(layers - 1, 5, total)

    def backward_rows(slot, layer, n):
        gain = gains[layer][n]
        sums = [jnp.zeros((8, width), F32)] * 3
        for m in range(micro):
            pair_copy(slot, m).wait_recv()

            def body(i, carry):
                base = pl.multiple_of(i * step, step)
                at = pl.ds(m * span + base, step)
                du = paired(slot, m, base, step)
                scaled = r.xh[layer, n, at, :]
                weighted = du * gain
                back = r.rstd[layer, n, at, :] * (
                    weighted
                    - jnp.mean(weighted, axis=1, keepdims=True)
                    - scaled * jnp.mean(weighted * scaled, axis=1, keepdims=True)
                )
                dx = r.x[at, :] + back
                r.x[at, :] = dx
                shape = (step // 8, 8, width)
                return [
                    carry[0] + jnp.sum((du * scaled).reshape(shape), axis=0),
                    carry[1] + jnp.sum(du.reshape(shape), axis=0),
                    carry[2] + branch_rows(at, dx),
                ]

            sums = lax.fori_loop(0, span // step, body, sums)
        for m in range(micro):
            pair_copy(slot, m).wait_send()
        put768(layer, n, sums[0])
        put768(layer, 2 + n, sums[1])
        if n == 1:
            put768(layer, 4, sums[2])
        elif layer > 0:
            put768(layer - 1, 5, sums[2])

    def transpose_into(name, value):
        getattr(r, name)[...] = value.astype(F32).T.astype(BF16)

    def weight_grad(layer, start, turned, value):
        columns = value.shape[1]
        for chunk, spec in enumerate(CHUNKS):
            if spec[0] == layer + 1 and spec[1] < start + columns and start < spec[1] + spec[2]:
                if (chunk, 0) not in done:
                    raise ValueError(chunk)
                if chunk not in sent:
                    rs_copy(chunk, 0).wait_send()
                    sent.append(chunk)
        piece = 384 if columns == 384 else 512
        for c in range(0, columns, piece):
            out = mm(getattr(r, turned)[...], value[:, c : c + piece]).astype(BF16)
            r.big[:, :, :, :, :, pl.ds(start + c, piece)] = out.reshape(2, 2, 2, 2, width // 16, piece)
            begin(layer, start + c, start + c + piece)

    for layer in reversed(range(layers)):
        last = layer == layers - 1
        if not last:
            load("wdown", layer, 3).wait()
        for c in range(0, hidden, 256):
            lanes = pl.ds(c, 256)
            da = mm_nt(r.grad[...], r.wdown_v[lanes, :]) * r.slope[layer, :, lanes].astype(F32)
            r.o_up[pl.ds(layer, 1), lanes] = jnp.sum(da, axis=0, keepdims=True)
            r.da[:, lanes] = da.astype(BF16)
        next_load(layer - 1, "wdown", 3)
        if not last:
            load("wup", layer, 2).wait()
        send_partial(0, lambda m: mm_nt(r.da[pl.ds(m * span, span), :], r.wup_v[...]))
        next_load(layer - 1, "wup", 2)
        tick(layer, 0)
        transpose_into("turned", r.grad[...])
        weight_grad(layer, 4 * half + hidden, "turned", r.g.at[layer])
        tick(layer, 1)
        transpose_into("turned", r.u[layer, 1])
        weight_grad(layer, 4 * half, "turned", r.da)
        if not last:
            short_all(layer)
        tick(layer, 2)
        backward_rows(0, layer, 1)
        tick(layer, 3)
        if not last:
            load("wout", layer, 1).wait()

        for m in range(micro):
            dmixed = mm_nt(r.grad[pl.ds(m * span, span), :], r.wout_v[...])
            to_channels(m, dmixed * r.s[0, m])
            r.ds[0, m, pl.ds(0, span), :] = dmixed * r.y[layer, m].astype(F32)
        start_channels()
        next_load(layer - 1, "wout", 1)
        tick(layer, 4)
        transpose_into("turned", r.grad[...])
        weight_grad(layer, 3 * half, "turned", r.mixed.at[layer])
        tick(layer, 5)
        wait_all("a_send", "a_recv", "a_sem")
        tick(layer, 6)
        signal = gathered()
        r.dsig[...] = signal
        r.skip_v[...] = r.skip_l[layer]
        for c in range(0, length, 256):
            lanes = pl.ds(c, 256)
            gc, gs = mm(signal, r.cos_v[:, lanes]), mm(signal, r.sin_v[:, lanes])
            fr, fi = twice(r.fr[layer, :, lanes]), twice(r.fi[layer, :, lanes])
            r.gc[:, lanes], r.gs[:, lanes] = gc.astype(BF16), gs.astype(BF16)
            r.spec[0, :, lanes] = (gc * fr - gs * fi).astype(BF16)
            r.spec[1, :, lanes] = (gs * fr + gc * fi).astype(BF16)
        inverse_and_send(r.dsig)
        tick(layer, 7)
        both_skip = jnp.sum(r.dsig[...].astype(F32) * r.sig[layer].astype(F32), axis=1, keepdims=True)
        r.gskip[layer] = sum(both_skip[m * block : (m + 1) * block] for m in range(micro))
        for c in range(0, length, 256):
            lanes = pl.ds(c, 256)
            gc, gs = r.gc[:, lanes].astype(F32), r.gs[:, lanes].astype(F32)
            pc, ps = r.pc[layer, :, lanes].astype(F32), r.ps[layer, :, lanes].astype(F32)
            re, im = gc * pc + gs * ps, gc * ps - gs * pc
            re = sum(re[m * block : (m + 1) * block] for m in range(micro)) * (1.0 / length)
            im = sum(im[m * block : (m + 1) * block] for m in range(micro)) * (1.0 / length)
            tc, ts = r.turn[pl.ds(0, 1), lanes], r.turn[pl.ds(1, 1), lanes]
            for which, value in enumerate((re * tc + im * ts, re * ts - im * tc)):
                high = value.astype(BF16)
                r.spec[which, pl.ds(0, block), lanes] = high
                r.spec[which, pl.ds(block, block), lanes] = (value - high.astype(F32)).astype(BF16)
        for c in range(0, length, 256):
            lanes = pl.ds(c, 256)
            out = mm(r.spec[0], r.cos_v[:, lanes]) + mm(r.spec[1], r.sin_v[:, lanes])
            r.o_filt[layer, :, lanes] = out[:block] + out[block:]
        tick(layer, 8)
        wait_all("b_send", "b_recv", "b_sem")
        for m in range(micro):
            dp = from_channels(m)
            for k in (1, 2):
                value = dp * r.s[3 - k, m]
                r.ds[k, m, pl.ds(0, span), :] = value
            for k in range(3):
                r.rim_send[1, pl.ds(k * 4 + m * 2, 2), :] = r.ds[k, m, pl.ds(0, 2), :]
        rim_copy(1).start()
        for k in range(3):
            sums = [0.0] * 4
            for m in range(micro):
                ds = r.ds[k, m, pl.ds(0, span), :]
                sums[3] = sums[3] + jnp.sum(ds, axis=0, keepdims=True)
                for j in range(3):
                    z = r.z[layer, k, m, pl.ds(8 - j, span), :]
                    sums[j] = sums[j] + jnp.sum(ds * z, axis=0, keepdims=True)
            for j in range(3):
                r.vecs[pl.ds(32 * layer + 11 + 3 * k + j, 1), :] = sums[j]
            r.vecs[pl.ds(32 * layer + 20 + k, 1), :] = sums[3]
        tick(layer, 9)
        rim_copy(1).wait()
        inner = (seq < parts - 1).astype(F32)
        for k in range(3):
            total = 0.0
            for m in range(micro):
                r.ds[k, m, pl.ds(span, 2), :] = inner * r.rim_recv[1, pl.ds(k * 4 + m * 2, 2), :]
                dz = 0.0
                for j in range(3):
                    dz = dz + tap(layer, k, j) * r.ds[k, m, pl.ds(j, span), :]
                total = total + jnp.sum(dz, axis=0, keepdims=True)
                r.da[pl.ds(m * span, span), pl.ds(k * half, half)] = dz.astype(BF16)
            r.vecs[pl.ds(32 * layer + 8 + k, 1), :] = total
        if not last:
            load("win", layer, 0).wait()
        send_partial(
            1, lambda m: sum(mm_nt(r.da[pl.ds(m * span, span), pl.ds(k * half, half)], r.win_v[k]) for k in range(3))
        )
        next_load(layer - 1, "win", 0)
        tick(layer, 10)
        transpose_into("turned", r.u[layer, 0])
        for k in range(3):
            weight_grad(layer, k * half, "turned", r.da.at[:, pl.ds(k * half, half)])
        tick(layer, 11)
        backward_rows(1, layer, 0)
        tick(layer, 12)
    r.grad_tokens[...] = r.x[:, own_lanes]
    for count, (chunk, stage) in enumerate(PLAN[TICKS * layers]):
        advance(chunk, stage)
        if count == SMALL[0]:
            filter_backward(1)
        if count == SMALL[1]:
            filter_backward(0)
            small_begin()
        if count == SMALL[2]:
            small_middle()
        if count == SMALL[3]:
            small_last()
    small_end()
    for chunk in range(len(CHUNKS)):
        for stage in range(4):
            if stage or chunk not in sent:
                rs_copy(chunk, stage).wait_send()


def chain(inputs, sizes):
    layers, micro, span, half, hidden, feat, freq_lane = sizes
    width, rows, parts = 2 * half, micro * span, 8
    block, length = half // parts, span * parts
    lanes = micro * block
    columns = 4 * half + 2 * hidden
    in_any = ("win", "wout", "wup", "wdown", "cos", "sin")
    outs = dict(
        out_act=((rows, half), F32),
        grad_tokens=((rows, half), F32),
        o_big=((layers, width // 16, 4 * half + 2 * hidden), F32),
        o_small=((2, 2 * parts, block, 128), F32),
    )
    dma, vm = pltpu.SemaphoreType.DMA, pltpu.VMEM
    scratch = dict(
        big=vm((2, 2, 2, 2, width // 16, columns), BF16),
        rs1=vm((layers, 2, 2, 2, width // 16, columns), BF16),
        rs2=vm((layers, 2, 2, width // 16, columns), BF16),
        rs3=vm((layers, 2, width // 16, columns), BF16),
        rs4=vm((layers, width // 16, columns), BF16),
        rs_sem=dma((2, len(CHUNKS), 4)),
        win_v=vm((3, width, half), BF16),
        wout_v=vm((half, width), BF16),
        wup_v=vm((width, hidden), BF16),
        wdown_v=vm((hidden, width), BF16),
        cos_v=vm((length, length), BF16),
        sin_v=vm((length, length), BF16),
        skip_v=vm((lanes, 1), F32),
        skip_l=vm((layers, lanes, 1), F32),
        gskip=vm((layers, block, 1), F32),
        vec2=vm((2, 16, half), F32),
        vec=vm((16, width), F32),
        params=vm((48, half), F32),
        pack_t=vm((128, feat), F32),
        chan_t=vm((128, half), F32),
        pack=vm((layers, feat, 128), F32),
        chv=vm((layers, block, 128), F32),
        chv_t=vm((half, 128), F32),
        both=vm((2, 2, rows, half), BF16),
        mask=vm((rows, 1), F32),
        inner=vm((layers, feat, length), F32),
        wave=vm((layers * feat, length), F32),
        fr=vm((layers, block, length), F32),
        fi=vm((layers, block, length), F32),
        spread=vm((layers, feat, 128), F32),
        o_filt=vm((layers, block, length), F32),
        o768=vm((8 * layers, width), F32),
        o_up=vm((layers, hidden), F32),
        vecs=vm((128, half), F32),
        sm=vm((2 * parts, block, 128), F32),
        sm_recv=vm((2 * parts, block, 128), F32),
        sm_sem=dma((2, 2, 2 * parts)),
        core_sem=dma((2, 4)),
        x=vm((rows, width), F32),
        xh=vm((layers, 2, rows, width), F32),
        rstd=vm((layers, 2, rows, 1), F32),
        u=vm((layers, 2, rows, width), BF16),
        z=vm((layers, 3, micro, span + 8, half), F32),
        s=vm((3, micro, span, half), F32),
        y=vm((layers, micro, span, half), BF16),
        mixed=vm((layers, rows, half), BF16),
        sig=vm((layers, lanes, length), BF16),
        dsig=vm((lanes, length), BF16),
        pc=vm((layers, lanes, length), BF16),
        ps=vm((layers, lanes, length), BF16),
        gc=vm((lanes, length), BF16),
        gs=vm((lanes, length), BF16),
        spec=vm((2, lanes, length), BF16),
        slope=vm((layers, rows, hidden), BF16),
        g=vm((layers, rows, hidden), BF16),
        da=vm((rows, hidden), BF16),
        grad=vm((rows, width), BF16),
        turned=vm((width, rows), BF16),
        ds=vm((3, micro, span + 8, half), F32),
        a_send=vm((parts, lanes, span), BF16),
        a_recv=vm((parts, lanes, span), BF16),
        b_send=vm((parts, lanes, span), BF16),
        b_recv=vm((parts, lanes, span), BF16),
        pair_send=vm((2, micro, span, width), BF16),
        pair_recv=vm((2, micro, span, width), BF16),
        rim_send=vm((2, 16, half), F32),
        rim_recv=vm((2, 16, half), F32),
        w_sem=dma((4,)),
        t_sem=dma((2,)),
        a_sem=dma((2, parts)),
        b_sem=dma((2, parts)),
        pair_sem=dma((2, 2, micro)),
        rim_sem=dma((2, 2)),
    )
    names = [*inputs, *outs, *scratch]
    results = pl.pallas_call(
        functools.partial(chain_kernel, sizes, names),
        out_shape=[jax.ShapeDtypeStruct(*spec) for spec in outs.values()],
        in_specs=[
            pl.BlockSpec(memory_space=pl.ANY if name in in_any else pltpu.SMEM if name == "lens" else pltpu.VMEM)
            for name in inputs
        ],
        out_specs=[pl.BlockSpec(memory_space=pltpu.VMEM) for _ in outs],
        scratch_shapes=list(scratch.values()),
        compiler_params=pltpu.CompilerParams(
            collective_id=3, has_side_effects=True, vmem_limit_bytes=61 << 20
        ),
        name="chain",
    )(*inputs.values())
    return types.SimpleNamespace(**dict(zip(outs, results)))


def embedding(count, bands, feat):
    steps = np.arange(count, dtype=np.float32) / np.float32(count)
    number = (bands - 1) // 2
    freq = np.linspace(0.0001, number - 1, number).astype(np.float32)
    phases = (np.float32(2.0 * math.pi) * steps)[None, :] * freq[:, None]
    table = np.zeros((128, count), np.float32)
    table[feat] = steps
    table[feat + 1 : feat + 1 + number] = np.cos(phases)
    table[feat + 1 + number : feat + bands] = -np.sin(phases)
    table[feat + bands] = 1.0
    return table


def finish_kernel(sizes, names, *refs):
    layers, micro, span, half, hidden, feat, bands = sizes
    r = types.SimpleNamespace(**dict(zip(names, refs)))
    wide = hidden // half
    for m in range(micro):
        r.act[m, 0] = r.out_act[pl.ds(m * span, span), :]
        r.tokens[m, 0] = r.grad_tokens[pl.ds(m * span, span), :]
    for c in range(2):
        for piece in range(2):
            value = r.o_small[c, pl.ds(8 * piece, 8)].reshape(half, 128)
            r.turned[c, piece] = value.T
    for layer in range(layers):
        for k in range(3):
            r.g_in[layer, k] = r.o_big[layer, :, pl.ds(k * half, half)]
        r.g_out[layer] = r.o_big[layer, :, pl.ds(3 * half, half)]
        r.g_up[layer] = r.o_big[layer, :, pl.ds(4 * half, hidden)]
        r.g_down[layer] = r.o_big[layer, :, pl.ds(4 * half + hidden, hidden)]
        net = sum(r.turned[c, 1, pl.ds(feat, feat), pl.ds(layer * feat, feat)] for c in range(2))
        for i in range(bands):
            r.fin[i, pl.ds(layer, 1), :] = net[i : i + 1]
        r.fbias[pl.ds(layer, 1), :] = net[bands : bands + 1]
        r.ffreq[pl.ds(layer, 1), :] = net[bands + 1 : bands + 2]
        for c in range(2):
            lanes = pl.ds(c * half, half)
            base = 32 * layer

            def row(index, c=c):
                return r.turned[c, 1, pl.ds(index, 1), :]

            for n in range(2):
                r.gain[layer, pl.ds(n, 1), lanes] = row(base + n)
                r.bias[layer, pl.ds(n, 1), lanes] = row(base + 2 + n)
            at = pl.ds(layer, 1)
            r.out_b[at, lanes] = row(base + 4)
            r.down_b[at, lanes] = row(base + 5)
            r.skip[at, lanes] = row(112 + layer)
            for k in range(3):
                r.in_b[k, at, lanes] = row(base + 8 + k)
                r.short_b[k, at, lanes] = row(base + 20 + k)
                for j in range(3):
                    r.taps[k, j, at, lanes] = row(base + 11 + 3 * k + j)
            for i in range(wide):
                r.up_b[at, pl.ds(c * hidden + i * half, half)] = row(base + 24 + i)
            r.fout[layer, :, lanes] = r.turned[c, 0, pl.ds(layer * feat, feat), :]


def finish(out, sizes):
    layers, micro, span, half, hidden, feat, bands = sizes
    width, own = 2 * half, 2 * half // 16
    inputs = dict(out_act=out.out_act, grad_tokens=out.grad_tokens, o_big=out.o_big, o_small=out.o_small)
    outs = dict(
        act=(micro, 1, span, half),
        tokens=(micro, 1, span, half),
        g_in=(layers, 3, own, half),
        g_out=(layers, own, half),
        g_up=(layers, own, hidden),
        g_down=(layers, own, hidden),
        gain=(layers, 2, width),
        bias=(layers, 2, width),
        in_b=(3, layers, width),
        taps=(3, 3, layers, width),
        short_b=(3, layers, width),
        skip=(layers, width),
        out_b=(layers, width),
        up_b=(layers, 2 * hidden),
        down_b=(layers, width),
        fin=(bands, layers, feat),
        fbias=(layers, feat),
        ffreq=(layers, feat),
        fout=(layers, feat, width),
    )
    names = [*inputs, *outs, "turned"]
    results = pl.pallas_call(
        functools.partial(finish_kernel, sizes, names),
        out_shape=[jax.ShapeDtypeStruct(shape, F32) for shape in outs.values()],
        in_specs=[pl.BlockSpec(memory_space=pltpu.VMEM) for _ in inputs],
        out_specs=[pl.BlockSpec(memory_space=pltpu.VMEM) for _ in outs],
        scratch_shapes=[pltpu.VMEM((2, 2, 128, half), F32)],
        name="finish",
    )(*inputs.values())
    turns = dict(
        g_out=(0, 2, 1),
        g_down=(0, 2, 1),
        in_b=(1, 0, 2),
        taps=(2, 0, 1, 3),
        short_b=(1, 0, 2),
        fin=(1, 0, 2),
    )
    return tuple(
        value.transpose(turns[name]) if name in turns else value for name, value in zip(outs, results)
    )


def local_fast(
    tokens,
    lengths,
    cotangent,
    norm_gain,
    norm_bias,
    in_weight,
    in_bias,
    short_taps,
    short_bias,
    skip_gain,
    out_weight,
    out_bias,
    up_weight,
    up_bias,
    down_weight,
    down_bias,
    filter_in,
    filter_bias,
    filter_freq,
    filter_out,
    decay_rate,
):
    micro, rows_dev, half = tokens.shape[0], tokens.shape[2], tokens.shape[3]
    layers, bands, feat = filter_in.shape
    hidden = up_weight.shape[2]
    length = rows_dev * lax.axis_size("seq")
    freq_lane = feat + bands + 1
    cos_np, sin_np, turn_c, turn_s = half_tables(length)
    inputs = dict(
        tok=tokens.reshape(micro * rows_dev, half),
        cot=cotangent.reshape(micro * rows_dev, half),
        lens=lengths.T,
        gain=norm_gain,
        bias=norm_bias,
        out_b=out_bias,
        down_b=down_bias,
        in_b=in_bias.transpose(1, 0, 2),
        taps=short_taps.transpose(1, 2, 0, 3),
        short_b=short_bias.transpose(1, 0, 2),
        up_b=up_bias,
        fin=filter_in.transpose(1, 0, 2),
        fbias=filter_bias,
        ffreq=filter_freq,
        fout=filter_out,
        decay=decay_rate,
        skip=skip_gain,
        emb=jnp.asarray(embedding(length, bands, feat)),
        turn=jnp.asarray(np.concatenate([turn_c, turn_s], axis=1).T, F32),
        win=in_weight,
        wout=out_weight,
        wup=up_weight,
        wdown=down_weight,
        cos=jnp.asarray(cos_np, BF16),
        sin=jnp.asarray(sin_np, BF16),
    )
    out = chain(inputs, (layers, micro, rows_dev, half, hidden, feat, freq_lane))
    return finish(out, (layers, micro, rows_dev, half, hidden, feat, bands))


def solution(mesh):
    in_specs = (
        P(None, "dp", "seq", "chan"),
        P(None, "dp"),
        P(None, "dp", "seq", "chan"),
        P(None, None, "chan"),
        P(None, None, "chan"),
        P(None, None, None, "chan"),
        P(None, None, "chan"),
        P(None, None, None, "chan"),
        P(None, None, "chan"),
        P(None, "chan"),
        P(None, "chan", None),
        P(None, "chan"),
        P(None, None, "chan"),
        P(None, "chan"),
        P(None, "chan", None),
        P(None, "chan"),
        P(),
        P(),
        P(),
        P(None, None, "chan"),
        P(None, "chan"),
    )
    out_specs = (
        P(None, "dp", "seq", "chan"),
        P(None, "dp", "seq", "chan"),
        P(None, None, ("seq", "dp"), "chan"),
        P(None, "chan", ("seq", "dp")),
        P(None, ("seq", "dp"), "chan"),
        P(None, "chan", ("seq", "dp")),
        P(),
        P(),
        P(),
        P(),
        P(),
        P(),
        P(),
        P(),
        P(),
        P(),
        P(),
        P(),
        P(),
    )
    def entry(*args):
        fits = args[0].shape[2] * mesh.shape["seq"] <= 2048 and mesh.shape["seq"] == 8 and mesh.shape["dp"] == 2
        return (local_fast if fits else local)(*args)

    return jax.shard_map(entry, mesh=mesh, in_specs=in_specs, out_specs=out_specs, check_vma=False)
```

```python
import functools
import math
import types

import jax
import jax.numpy as jnp
import numpy as np
from jax import lax
from jax.experimental import pallas as pl
from jax.experimental.pallas import tpu as pltpu
from jax.sharding import PartitionSpec as P

EPS = 1e-05
HIGH = lax.Precision.HIGHEST


def shifted(value, axis, steps):
    count = lax.axis_size(axis)
    initial, last = (max(0, -steps), min(count, count - steps))
    return lax.ppermute(value, axis, [(source, source + steps) for source in range(initial, last)])


def positions(seq_length, emb_width):
    band_count = (emb_width - 1) // 2
    step_ids = jnp.arange(seq_length, dtype=jnp.float32)
    steps_norm = step_ids / seq_length
    band_freq = jnp.linspace(0.0001, band_count - 1, band_count).astype(jnp.float32)
    phases = 2.0 * math.pi * steps_norm[:, None] * band_freq[None, :]
    table = jnp.concatenate([steps_norm[:, None], jnp.cos(phases), -jnp.sin(phases)], axis=1)
    return (table, steps_norm)


def angle_table(row_count, col_count, modulus):
    product = (
        jnp.arange(row_count, dtype=jnp.int32)[:, None]
        * jnp.arange(col_count, dtype=jnp.int32)[None, :]
        % modulus
    )
    theta = product.astype(jnp.float32) * (2.0 * math.pi / modulus)
    return (jnp.cos(theta), jnp.sin(theta))


def split_length(total_length):
    lesser = 2
    for candidate in range(2, math.isqrt(total_length) + 1, 2):
        if total_length % candidate == 0:
            lesser = candidate
    return (lesser, total_length // lesser)


def dft_basis(seq_length):
    padded_len = 2 * seq_length
    lesser, greater = split_length(padded_len)
    cos_p, sin_p = angle_table(lesser, lesser, lesser)
    cos_q, sin_q = angle_table(greater, greater, greater)
    twist_c, twist_s = angle_table(lesser, greater, padded_len)
    return (cos_p, sin_p, cos_q, sin_q, twist_c, twist_s)


def right_mul(left, table):
    return jnp.einsum("ckb,bj->ckj", left, table, precision=HIGH)


def to_spectrum(signal, basis):
    cos_p, sin_p, cos_q, sin_q, twist_c, twist_s = basis
    half = cos_p.shape[0] // 2
    blocks = signal.reshape(signal.shape[0], half, cos_q.shape[0])
    first_re = jnp.einsum("ka,cab->ckb", cos_p[:, :half], blocks, precision=HIGH)
    first_im = -jnp.einsum("ka,cab->ckb", sin_p[:, :half], blocks, precision=HIGH)
    turned_re = first_re * twist_c + first_im * twist_s
    turned_im = first_im * twist_c - first_re * twist_s
    spec_re = right_mul(turned_re, cos_q) + right_mul(turned_im, sin_q)
    spec_im = right_mul(turned_im, cos_q) - right_mul(turned_re, sin_q)
    return (spec_re, spec_im)


def from_spectrum(spec_re, spec_im, basis):
    cos_p, sin_p, cos_q, sin_q, twist_c, twist_s = basis
    half = cos_p.shape[0] // 2
    back_re = right_mul(spec_re, cos_q) - right_mul(spec_im, sin_q)
    back_im = right_mul(spec_im, cos_q) + right_mul(spec_re, sin_q)
    turned_re = back_re * twist_c - back_im * twist_s
    turned_im = back_im * twist_c + back_re * twist_s
    signal = jnp.einsum("ak,ckb->cab", cos_p[:half], turned_re, precision=HIGH) - jnp.einsum(
        "ak,ckb->cab", sin_p[:half], turned_im, precision=HIGH
    )
    return signal.reshape(signal.shape[0], half * cos_q.shape[0]) / (
        cos_p.shape[0] * cos_q.shape[0]
    )


def complex_mul(left_re, left_im, right_re, right_im):
    return (left_re * right_re - left_im * right_im, left_re * right_im + left_im * right_re)


def filter_block(table, steps_norm, weight_in, bias_in, freq_in, cols_in, decay_cols):
    hidden = jnp.sin(freq_in * (jnp.dot(table, weight_in, precision=HIGH) + bias_in))
    raw = jnp.einsum("lf,fc->cl", hidden, cols_in, precision=HIGH)
    return raw * jnp.exp(-decay_cols[:, None] * steps_norm[None, :])


def to_channels(block):
    parts = lax.axis_size("seq")
    shaped = block.reshape(parts, block.shape[0] // parts, block.shape[1])
    moved = lax.all_to_all(
        shaped.astype(jnp.bfloat16), "seq", split_axis=0, concat_axis=2, tiled=True
    ).astype(shaped.dtype)
    return moved.reshape(moved.shape[1], moved.shape[2])


def to_positions(block):
    shaped = block.reshape(1, block.shape[0], block.shape[1])
    moved = lax.all_to_all(
        shaped.astype(jnp.bfloat16), "seq", split_axis=2, concat_axis=0, tiled=True
    ).astype(shaped.dtype)
    return moved.reshape(moved.shape[0] * moved.shape[1], moved.shape[2])


def branch_sum(partial_value):
    return lax.psum_scatter(
        partial_value.astype(jnp.bfloat16), "chan", scatter_dimension=1, tiled=True
    ).astype(jnp.float32)


def branch_grad(grad_low):
    return lax.all_gather(grad_low, "chan", axis=1, tiled=True)


def place(values, start, full_width, axis):
    full_shape = list(values.shape)
    full_shape[axis] = full_width
    return lax.dynamic_update_slice_in_dim(jnp.zeros(full_shape, jnp.float32), values, start, axis)


def local(
    tokens,
    lengths,
    cotangent,
    norm_gain,
    norm_bias,
    in_weight,
    in_bias,
    short_taps,
    short_bias,
    skip_gain,
    out_weight,
    out_bias,
    up_weight,
    up_bias,
    down_weight,
    down_bias,
    filter_in,
    filter_bias,
    filter_freq,
    filter_out,
    decay_rate,
):
    micro_count = tokens.shape[0]
    rows_dev = tokens.shape[2]
    chan_width = tokens.shape[3]
    layer_count = norm_gain.shape[0]
    hidden_width = up_weight.shape[2]
    seq_parts = lax.axis_size("seq")
    chan_parts = lax.axis_size("chan")
    full_width = chan_width * chan_parts
    seq_length = rows_dev * seq_parts
    seq_index = lax.axis_index("seq")
    chan_index = lax.axis_index("chan")
    block_width = chan_width // seq_parts
    col_start = seq_index * block_width
    chan_start = chan_index * chan_width
    basis = dft_basis(seq_length)
    table, steps_norm = positions(seq_length, filter_in.shape[1])
    positions_dev = seq_index * rows_dev + jnp.arange(rows_dev, dtype=jnp.int32)
    filters = []
    for layer_index in range(layer_count):
        filter_cols = lax.dynamic_slice_in_dim(filter_out[layer_index], col_start, block_width, 1)
        decay_cols = lax.dynamic_slice_in_dim(decay_rate[layer_index], col_start, block_width, 0)
        skip_cols = lax.dynamic_slice_in_dim(skip_gain[layer_index], col_start, block_width, 0)

        def make_one(weight_in, bias_in, freq_in, cols_in, decay_cols=decay_cols):
            return filter_block(table, steps_norm, weight_in, bias_in, freq_in, cols_in, decay_cols)

        long_filter, filter_pull = jax.vjp(
            make_one,
            filter_in[layer_index],
            filter_bias[layer_index],
            filter_freq[layer_index],
            filter_cols,
        )
        filt_re, filt_im = to_spectrum(long_filter, basis)
        filters.append((filt_re, filt_im, filter_pull, skip_cols))

    def norm_forward(resid, gain_bias):
        full_rows, full_gb = (
            lax.all_gather(resid, "chan", axis=1, tiled=True),
            lax.all_gather(gain_bias, "chan", axis=1, tiled=True),
        )
        mean_row = jnp.mean(full_rows, axis=1, keepdims=True)
        centred = full_rows - mean_row
        rstd = lax.rsqrt(jnp.mean(centred * centred, axis=1, keepdims=True) + EPS)
        scaled = centred * rstd
        normed = (scaled * full_gb[0] + full_gb[1]).astype(jnp.bfloat16)
        return (normed, (scaled, rstd, full_gb[0]))

    def norm_backward(grad_partial, norm_saved):
        scaled, rstd, gain_row = norm_saved
        grad_rows = lax.psum(grad_partial.astype(jnp.bfloat16), "chan").astype(jnp.float32)
        grad_scaled = grad_rows * gain_row
        grad_full = rstd * (
            grad_scaled
            - jnp.mean(grad_scaled, axis=1, keepdims=True)
            - scaled * jnp.mean(grad_scaled * scaled, axis=1, keepdims=True)
        )
        grad_own = lax.dynamic_slice_in_dim(grad_full, chan_start, chan_width, 1)
        rows_own = lax.dynamic_slice_in_dim(grad_rows, chan_start, chan_width, 1)
        scaled_own = lax.dynamic_slice_in_dim(scaled, chan_start, chan_width, 1)
        return (grad_own, jnp.sum(rows_own * scaled_own, axis=0), jnp.sum(rows_own, axis=0))

    def mixer_forward(resid, pad_mask, layer_index):
        normed, norm_saved = norm_forward(
            resid, jnp.stack([norm_gain[layer_index, 0], norm_bias[layer_index, 0]])
        )
        streams = (
            jnp.einsum(
                "sd,kdc->kcs", normed, in_weight[layer_index], preferred_element_type=jnp.float32
            )
            + in_bias[layer_index][:, :, None]
        )
        rim = shifted(streams[:, :, rows_dev - 2 :], "seq", 1)
        padded = jnp.concatenate([rim, streams], axis=2)
        taps = short_taps[layer_index]
        short_out = (
            taps[:, 0][:, :, None] * padded[:, :, 2:]
            + taps[:, 1][:, :, None] * padded[:, :, 1 : rows_dev + 1]
            + taps[:, 2][:, :, None] * padded[:, :, :rows_dev]
            + short_bias[layer_index][:, :, None]
        )
        product = short_out[1] * short_out[2]
        chan_prod = to_channels(product)
        filt_re, filt_im, filter_pull, skip_cols = filters[layer_index]
        prod_re, prod_im = to_spectrum(chan_prod, basis)
        conv_re, conv_im = complex_mul(prod_re, prod_im, filt_re, filt_im)
        chan_out = from_spectrum(conv_re, conv_im, basis) + skip_cols[:, None] * chan_prod
        long_out = to_positions(chan_out)
        mixed = (short_out[0] * long_out).astype(jnp.bfloat16)
        partial_value = jnp.einsum(
            "cs,cd->sd", mixed, out_weight[layer_index], preferred_element_type=jnp.float32
        )
        branch = branch_sum(partial_value) + out_bias[layer_index]
        saved = (
            normed,
            norm_saved,
            padded,
            short_out,
            chan_prod,
            prod_re,
            prod_im,
            long_out,
            mixed,
        )
        return (resid + pad_mask[:, None] * branch, saved)

    def mlp_forward(resid, pad_mask, layer_index):
        normed, norm_saved = norm_forward(
            resid, jnp.stack([norm_gain[layer_index, 1], norm_bias[layer_index, 1]])
        )
        pre_act = (
            jnp.dot(normed, up_weight[layer_index], preferred_element_type=jnp.float32)
            + up_bias[layer_index]
        )
        activated = jax.nn.gelu(pre_act, approximate=False).astype(jnp.bfloat16)
        partial_value = jnp.dot(
            activated, down_weight[layer_index], preferred_element_type=jnp.float32
        )
        branch = branch_sum(partial_value) + down_bias[layer_index]
        return (resid + pad_mask[:, None] * branch, (normed, norm_saved, pre_act, activated))

    def mlp_backward(grad_resid, pad_mask, layer_index, saved):
        normed, norm_saved, pre_act, activated = saved
        grad_branch = pad_mask[:, None] * grad_resid
        g_down_bias = jnp.sum(grad_branch, axis=0)
        grad_full = branch_grad(grad_branch.astype(jnp.bfloat16))
        g_down_weight = jnp.einsum(
            "sf,sd->fd", activated, grad_full, preferred_element_type=jnp.float32
        )
        grad_act = jnp.einsum(
            "sd,fd->sf", grad_full, down_weight[layer_index], preferred_element_type=jnp.float32
        )
        unused_value, gelu_pull = jax.vjp(
            lambda inner: jax.nn.gelu(inner, approximate=False), pre_act
        )
        grad_pre = gelu_pull(grad_act)[0]
        g_up_bias = jnp.sum(grad_pre, axis=0)
        pre_low = grad_pre.astype(jnp.bfloat16)
        g_up_weight = jnp.einsum("sd,sf->df", normed, pre_low, preferred_element_type=jnp.float32)
        grad_normed = jnp.einsum(
            "sf,df->sd", pre_low, up_weight[layer_index], preferred_element_type=jnp.float32
        )
        grad_own, g_gain, g_bias = norm_backward(grad_normed, norm_saved)
        return (
            grad_resid + grad_own,
            (g_up_weight, g_down_weight, g_gain, g_bias, g_up_bias, g_down_bias),
        )

    mixer_acc = [None] * layer_count
    mlp_acc = [None] * layer_count
    outputs = []
    input_grads = []
    for micro_index in range(micro_count):
        pad_mask = (positions_dev < lengths[micro_index, 0]).astype(jnp.float32)
        resid = tokens[micro_index, 0].astype(jnp.float32)
        layer_inputs = []
        layer_saved = []
        for layer_index in range(layer_count):
            layer_inputs.append(resid)
            resid, mix_saved = mixer_forward(resid, pad_mask, layer_index)
            layer_inputs.append(resid)
            resid, mlp_saved = mlp_forward(resid, pad_mask, layer_index)
            layer_saved.append((mix_saved, mlp_saved))
        outputs.append(resid)
        grad_resid = cotangent[micro_index, 0].astype(jnp.float32)
        for layer_index in reversed(range(layer_count)):
            mlp_saved = mlp_forward(layer_inputs[2 * layer_index + 1], pad_mask, layer_index)[1]
            grad_resid, mlp_grads = mlp_backward(grad_resid, pad_mask, layer_index, mlp_saved)
            mix_saved = mixer_forward(layer_inputs[2 * layer_index], pad_mask, layer_index)[1]
            (
                mixer_normed,
                mixer_norm_saved,
                mixer_padded,
                mixer_short_out,
                mixer_chan_prod,
                mixer_prod_re,
                mixer_prod_im,
                mixer_long_out,
                mixer_mixed,
            ) = mix_saved
            mixer_filt_re, mixer_filt_im, mixer_filter_pull, mixer_skip_cols = filters[layer_index]
            mixer_grad_branch = pad_mask[:, None] * grad_resid
            g_out_bias = jnp.sum(mixer_grad_branch, axis=0)
            mixer_grad_full = branch_grad(mixer_grad_branch.astype(jnp.bfloat16))
            g_out_weight = jnp.einsum(
                "cs,sd->cd", mixer_mixed, mixer_grad_full, preferred_element_type=jnp.float32
            )
            grad_mixed = jnp.einsum(
                "sd,cd->cs",
                mixer_grad_full,
                out_weight[layer_index],
                preferred_element_type=jnp.float32,
            )
            grad_long = grad_mixed * mixer_short_out[0]
            grad_gate = grad_mixed * mixer_long_out
            chan_grad = to_channels(grad_long)
            grad_re, grad_im = to_spectrum(chan_grad, basis)
            back_re, back_im = complex_mul(grad_re, grad_im, mixer_filt_re, -mixer_filt_im)
            chan_dprod = (
                from_spectrum(back_re, back_im, basis) + mixer_skip_cols[:, None] * chan_grad
            )
            corr_re, corr_im = complex_mul(grad_re, grad_im, mixer_prod_re, -mixer_prod_im)
            grad_filter = from_spectrum(corr_re, corr_im, basis)
            g_skip = jnp.sum(chan_grad * mixer_chan_prod, axis=1)
            grad_product = to_positions(chan_dprod)
            grad_short = jnp.stack(
                [grad_gate, grad_product * mixer_short_out[2], grad_product * mixer_short_out[1]]
            )
            g_short_bias = jnp.sum(grad_short, axis=2)
            g_taps = jnp.stack(
                [
                    jnp.sum(grad_short * mixer_padded[:, :, 2:], axis=2),
                    jnp.sum(grad_short * mixer_padded[:, :, 1 : rows_dev + 1], axis=2),
                    jnp.sum(grad_short * mixer_padded[:, :, :rows_dev], axis=2),
                ],
                axis=1,
            )
            next_rim = shifted(grad_short[:, :, :2], "seq", -1)
            extended = jnp.concatenate([grad_short, next_rim], axis=2)
            mixer_taps = short_taps[layer_index]
            grad_streams = (
                mixer_taps[:, 0][:, :, None] * extended[:, :, :rows_dev]
                + mixer_taps[:, 1][:, :, None] * extended[:, :, 1 : rows_dev + 1]
                + mixer_taps[:, 2][:, :, None] * extended[:, :, 2:]
            )
            g_in_bias = jnp.sum(grad_streams, axis=2)
            streams_low = grad_streams.astype(jnp.bfloat16)
            g_in_weight = jnp.einsum(
                "sd,kcs->kdc", mixer_normed, streams_low, preferred_element_type=jnp.float32
            )
            mixer_grad_normed = jnp.einsum(
                "kcs,kdc->sd",
                streams_low,
                in_weight[layer_index],
                preferred_element_type=jnp.float32,
            )
            mixer_grad_own, mixer_g_gain, mixer_g_bias = norm_backward(
                mixer_grad_normed, mixer_norm_saved
            )
            grads = (
                g_in_weight,
                g_out_weight,
                mixer_g_gain,
                mixer_g_bias,
                g_in_bias,
                g_taps,
                g_short_bias,
                g_skip,
                g_out_bias,
                grad_filter,
            )
            grad_resid, mix_grads = (grad_resid + mixer_grad_own, grads)
            if mixer_acc[layer_index] is None:
                mixer_acc[layer_index] = mix_grads
                mlp_acc[layer_index] = mlp_grads
            else:
                mixer_acc[layer_index] = jax.tree.map(jnp.add, mixer_acc[layer_index], mix_grads)
                mlp_acc[layer_index] = jax.tree.map(jnp.add, mlp_acc[layer_index], mlp_grads)
        input_grads.append(grad_resid)
    filter_grads = [
        filters[layer_index][2](mixer_acc[layer_index][9]) for layer_index in range(layer_count)
    ]
    skip_start = chan_start + col_start

    def stack_mix(member):
        return jnp.stack([mixer_acc[layer_index][member] for layer_index in range(layer_count)])

    def stack_mlp(member):
        return jnp.stack([mlp_acc[layer_index][member] for layer_index in range(layer_count)])

    def stack_filter(member):
        return jnp.stack([filter_grads[layer_index][member] for layer_index in range(layer_count)])

    big_grads = (
        lax.psum_scatter(stack_mix(0), ("seq", "dp"), scatter_dimension=2, tiled=True),
        lax.psum_scatter(stack_mix(1), ("seq", "dp"), scatter_dimension=2, tiled=True),
        lax.psum_scatter(stack_mlp(0), ("seq", "dp"), scatter_dimension=1, tiled=True),
        lax.psum_scatter(stack_mlp(1), ("seq", "dp"), scatter_dimension=2, tiled=True),
    )
    gain_grads = jnp.stack([stack_mix(2), stack_mlp(2)], axis=1)
    bias_grads = jnp.stack([stack_mix(3), stack_mlp(3)], axis=1)
    small = lax.psum(
        (
            place(gain_grads, chan_start, full_width, 2),
            place(bias_grads, chan_start, full_width, 2),
            place(stack_mix(4), chan_start, full_width, 2),
            place(stack_mix(5), chan_start, full_width, 3),
            place(stack_mix(6), chan_start, full_width, 2),
            place(stack_mix(7), skip_start, full_width, 1),
            place(stack_mix(8), chan_start, full_width, 1),
            place(stack_mlp(4), chan_index * hidden_width, hidden_width * chan_parts, 1),
            place(stack_mlp(5), chan_start, full_width, 1),
            stack_filter(0),
            stack_filter(1),
            stack_filter(2),
            place(stack_filter(3), skip_start, full_width, 2),
        ),
        ("seq", "chan", "dp"),
    )
    out_act = jnp.stack(outputs)[:, None]
    grad_tokens = jnp.stack(input_grads)[:, None]
    return (
        out_act,
        grad_tokens,
        big_grads[0],
        big_grads[1],
        big_grads[2],
        big_grads[3],
        small[0],
        small[1],
        small[2],
        small[3],
        small[4],
        small[5],
        small[6],
        small[7],
        small[8],
        small[9],
        small[10],
        small[11],
        small[12],
    )


F32 = jnp.float32
BF16 = jnp.bfloat16
MESH = pl.DeviceIdType.MESH
CHUNKS = (
    (1, "down", 3072, 512, "yxh"),
    (1, "down", 3584, 512, "yxh"),
    (1, "down", 4096, 512, "xyh"),
    (1, "up", 1536, 512, "xlh"),
    (1, "up", 2048, 512, "xlh"),
    (1, "up", 2560, 512, "lhx"),
    (1, "grad_out", 1152, 384, "lyh"),
    (1, "grad_in", 0, 384, "ylh"),
    (1, "grad_in", 384, 384, "yhl"),
    (1, "grad_in", 768, 384, "yhl"),
    (0, "down", 3072, 512, "ylh"),
    (0, "down", 3584, 512, "ylh"),
    (0, "down", 4096, 512, "ylh"),
    (0, "up", 1536, 512, "ylh"),
    (0, "up", 2048, 512, "ylh"),
    (0, "up", 2560, 512, "ylh"),
    (0, "grad_out", 1152, 384, "ylh"),
    (0, "grad_in", 0, 384, "ylh"),
    (0, "grad_in", 384, 384, "ylh"),
    (0, "grad_in", 768, 384, "ylh"),
)
FOLD = (
    dict(grad_in="x", grad_out="x", up="x", down="x"),
    dict(grad_in="x", grad_out="x", up="y", down="l"),
)
TICKS = 13
PLAN = {
    7: ((3, 0), (6, 0), (4, 0),),
    9: ((0, 0), (1, 0), (2, 0), (5, 0), (3, 1),),
    10: ((4, 1),),
    13: ((6, 1), (0, 1), (2, 1), (5, 1),),
    15: ((3, 2),),
    17: ((1, 1), (7, 0), (4, 2), (6, 2), (2, 2),),
    19: ((8, 0), (5, 2), (3, 3), (9, 0),),
    20: ((7, 1),),
    21: ((4, 3), (6, 3), (13, 0), (8, 1), (2, 3),),
    22: ((9, 1), (14, 0),),
    24: ((7, 2), (8, 2), (13, 1),),
    26: ((15, 0), (9, 2), (0, 2), (14, 1), (7, 3), (8, 3), (13, 2), (10, 0), (11, 0), (12, 0), (9, 3), (1, 2), (0, 3), (15, 1), (14, 2), (16, 0), (13, 3), (10, 1), (5, 3), (1, 3), (15, 2), (11, 1), (17, 0), (14, 3), (10, 2), (12, 1), (18, 0), (15, 3), (11, 2), (16, 1), (10, 3), (19, 0), (12, 2), (17, 1), (11, 3), (16, 2), (18, 1), (12, 3), (19, 1), (17, 2), (16, 3), (18, 2), (19, 2), (17, 3), (18, 3), (19, 3),),
}
SMALL = (25, 40)


def half_tables(count):
    odd = 2 * np.arange(count, dtype=np.int64) + 1
    angle = np.outer(odd, odd) % (8 * count) * (math.pi / (4 * count))
    twist = odd * (math.pi / (4 * count))
    return np.cos(angle), np.sin(angle), np.cos(twist)[:, None], np.sin(twist)[:, None]


def mesh_bits():
    seq, dp = lax.axis_index("seq"), lax.axis_index("dp")
    return {"x": dp, "y": lax.rem(seq, 2), "l": lax.rem(seq // 2, 2), "h": seq // 4}


def mesh_peers():
    seq, dp = lax.axis_index("seq"), lax.axis_index("dp")
    bits = mesh_bits()
    return {
        "x": {"dp": 1 - dp},
        "y": {"seq": seq + 1 - 2 * bits["y"]},
        "l": {"seq": seq + 2 - 4 * bits["l"]},
        "h": {"seq": seq + 4 - 8 * bits["h"]},
    }


def greet(devices):
    barrier = pltpu.get_barrier_semaphore()
    for device in devices:
        pl.semaphore_signal(barrier, inc=1, device_id=device, device_id_type=MESH)
    pl.semaphore_wait(barrier, len(devices))


def mm(left, right):
    return jnp.dot(left, right, preferred_element_type=F32)


def fine(left, right, dims=((1,), (0,))):
    return lax.dot_general(left, right, (dims, ((), ())), precision=HIGH, preferred_element_type=F32)


def mm_nt(left, right):
    return lax.dot_general(left, right, (((1,), (1,)), ((), ())), preferred_element_type=F32)


def chain_kernel(sizes, names, *refs):
    layers, micro, span, half, hidden, feat, freq_lane = sizes
    r = types.SimpleNamespace(**dict(zip(names, refs)))
    width, rows, parts = 2 * half, micro * span, 8
    block = half // parts
    length = span * parts
    seq, chan = lax.axis_index("seq"), lax.axis_index("chan")
    pair = seq + 1 - 2 * lax.rem(seq, 2)
    step = 32

    def load(name, layer, slot):
        return pltpu.make_async_copy(getattr(r, name).at[layer], getattr(r, name + "_v"), r.w_sem.at[slot])

    weights = (("win", 0), ("wout", 1), ("wup", 2), ("wdown", 3))
    table_loads = [
        pltpu.make_async_copy(r.cos, r.cos_v, r.t_sem.at[0]),
        pltpu.make_async_copy(r.sin, r.sin_v, r.t_sem.at[1]),
    ]
    load("win", 0, 0).start()
    for copy in table_loads:
        copy.start()
    for name, slot in weights[1:]:
        load(name, 0, slot).start()
    peers, bits = mesh_peers(), mesh_bits()
    dp = lax.axis_index("dp")
    ranks = 2 * parts
    me = 2 * seq + dp
    ranked = [lax.rem(me + far, ranks) for far in range(1, ranks)]
    greet([{"seq": other // 2, "dp": lax.rem(other, 2)} for other in ranked] + [{"chan": 1 - chan}])

    def core_copy(source, target, slot):
        return pltpu.make_async_remote_copy(
            src_ref=source,
            dst_ref=target,
            send_sem=r.core_sem.at[0, slot],
            recv_sem=r.core_sem.at[1, slot],
            device_id={"chan": 1 - chan},
            device_id_type=MESH,
        )

    for layer in range(layers):
        at = pl.ds(layer, 1)
        for n in range(2):
            r.params[pl.ds(2 * layer + n, 1), :] = r.gain[layer, pl.ds(n, 1), :]
            r.params[pl.ds(2 * layers + 2 * layer + n, 1), :] = r.bias[layer, pl.ds(n, 1), :]
        r.params[pl.ds(4 * layers + layer, 1), :] = r.out_b[at, :]
        r.params[pl.ds(5 * layers + layer, 1), :] = r.down_b[at, :]
    r.params[pl.ds(12, 4), :] = jnp.zeros((4, half), F32)
    first = [
        core_copy(r.params.at[pl.ds(0, 16)], r.vec2.at[chan], 0),
        core_copy(r.tok, r.both.at[chan, 0], 1),
        core_copy(r.cot, r.both.at[chan, 1], 2),
    ]
    for copy in first:
        copy.start()
    r.vec2[chan] = r.params[pl.ds(0, 16), :]
    r.both[chan, 0] = r.tok[...]
    r.both[chan, 1] = r.cot[...]
    r.sm[...] = jnp.zeros_like(r.sm)
    r.vecs[...] = jnp.zeros_like(r.vecs)
    r.o768[...] = jnp.zeros_like(r.o768)
    for m in range(micro):
        place_ids = seq * span + lax.broadcasted_iota(jnp.int32, (span, 1), 0)
        r.mask[pl.ds(m * span, span), :] = (place_ids < r.lens[0, m]).astype(F32)
    for layer in range(layers):
        at = pl.ds(layer, 1)
        for k in range(3):
            r.params[pl.ds(16 + 3 * layer + k, 1), :] = r.in_b[k, at, :]
            r.params[pl.ds(40 + 3 * layer + k, 1), :] = r.short_b[k, at, :]
            for j in range(3):
                r.params[pl.ds(22 + 9 * layer + 3 * k + j, 1), :] = r.taps[k, j, at, :]
    first[0].wait_recv()
    r.vec[...] = jnp.concatenate([r.vec2[0], r.vec2[1]], axis=1)

    def rank_copy(source, target, phase, other, slot):
        return pltpu.make_async_remote_copy(
            src_ref=source,
            dst_ref=target,
            send_sem=r.sm_sem.at[phase, 0, other],
            recv_sem=r.sm_sem.at[phase, 1, slot],
            device_id={"seq": other // 2, "dp": lax.rem(other, 2)},
            device_id_type=MESH,
        )

    def chan_rows(layer):
        value = r.chv[layer]
        return value[:, :feat], value[:, feat : feat + 1], value[:, feat + 1 : feat + 2]

    def filter_forward(layer):
        at = pl.ds(layer, 1)
        r.pack_t[...] = jnp.zeros_like(r.pack_t)
        for i in range(freq_lane - feat - 1):
            r.pack_t[pl.ds(feat + i, 1), :] = r.fin[i, at, :]
        r.pack_t[pl.ds(freq_lane - 1, 1), :] = r.fbias[at, :]
        r.pack_t[pl.ds(freq_lane, 1), :] = r.ffreq[at, :]
        r.pack[layer] = r.pack_t[...].T
        r.chan_t[...] = jnp.zeros_like(r.chan_t)
        r.chan_t[pl.ds(0, feat), :] = r.fout[layer]
        r.chan_t[pl.ds(feat, 1), :] = r.decay[at, :]
        r.chan_t[pl.ds(feat + 1, 1), :] = r.skip[at, :]
        r.chv_t[...] = r.chan_t[...].T
        r.chv[layer] = r.chv_t[pl.ds(pl.multiple_of(seq * block, 8), block), :]
        turned, decay, skip = chan_rows(layer)
        r.skip_l[layer] = jnp.concatenate([skip] * micro, axis=0)
        pack = r.pack[layer]
        freq = pack[:, freq_lane : freq_lane + 1]
        for c in range(0, length, 256):
            lanes = pl.ds(c, 256)
            inner = fine(pack, r.emb[:, lanes])
            wave = jnp.sin(freq * inner)
            r.inner[layer, :, lanes] = inner
            r.wave[pl.ds(layer * feat, feat), lanes] = wave
            filt = fine(turned, wave) * jnp.exp(-decay * r.emb[pl.ds(feat, 1), lanes])
            high = filt.astype(BF16)
            r.spec[0, pl.ds(0, block), lanes] = high
            r.spec[0, pl.ds(block, block), lanes] = (filt - high.astype(F32)).astype(BF16)
        for c in range(0, length, 256):
            lanes = pl.ds(c, 256)
            fc, fs = mm(r.spec[0], r.cos_v[:, lanes]), mm(r.spec[0], r.sin_v[:, lanes])
            fc, fs = fc[:block] + fc[block:], fs[:block] + fs[block:]
            tc, ts = r.turn[pl.ds(0, 1), lanes], r.turn[pl.ds(1, 1), lanes]
            r.fr[layer, :, lanes] = (fc * tc + fs * ts) * (1.0 / length)
            r.fi[layer, :, lanes] = (fc * ts - fs * tc) * (1.0 / length)

    def twice(value):
        return jnp.concatenate([value] * micro, axis=0)

    def filter_backward(layer):
        turned, decay, _ = chan_rows(layer)
        freq = r.pack[layer, :, freq_lane : freq_lane + 1]
        g_out = g_pack = g_freq = 0.0
        for c in range(0, length, 256):
            lanes = pl.ds(c, 256)
            raw = r.o_filt[layer, :, lanes] * jnp.exp(-decay * r.emb[pl.ds(feat, 1), lanes])
            g_out = g_out + fine(raw, r.wave[:, lanes], ((1,), (1,)))
            inner = r.inner[layer, :, lanes]
            slope = fine(turned, raw, ((0,), (0,))) * jnp.cos(freq * inner)
            g_freq = g_freq + jnp.sum(slope * inner, axis=1, keepdims=True)
            g_pack = g_pack + fine(slope * freq, r.emb[:, lanes], ((1,), (1,)))
        lane = lax.broadcasted_iota(jnp.int32, (block, 128), 1)
        mine = (lane >= layer * feat) & (lane < (layer + 1) * feat)
        r.sm[seq] = jnp.where(mine, g_out, r.sm[seq])
        lane = lax.broadcasted_iota(jnp.int32, (feat, 128), 1)
        r.spread[layer] = g_pack + jnp.where(lane == freq_lane, g_freq, 0.0)

    def small_begin():
        for layer in range(layers):
            r.vecs[pl.ds(32 * layer, 8), :] = r.o768[pl.ds(8 * layer, 8), own_lanes]
            for i in range(hidden // half):
                r.vecs[pl.ds(32 * layer + 24 + i, 1), :] = r.o_up[pl.ds(layer, 1), pl.ds(i * half, half)]
        spread = jnp.concatenate(
            [r.spread[layer] for layer in range(layers)] + [jnp.zeros((half - layers * feat, 128), F32)], axis=0
        )
        total = r.vecs[...].T + spread
        r.sm[pl.ds(parts, parts)] = total.reshape(parts, block, 128)
        lane = lax.broadcasted_iota(jnp.int32, (block, 128), 1)
        for layer in range(layers):
            r.sm[parts + seq] = r.sm[parts + seq] + jnp.where(lane == 112 + layer, r.gskip[layer], 0.0)
        for other in ranked:
            rank_copy(r.sm.at[other], r.sm_recv.at[me], 0, other, me).start()

    def small_middle():
        total = r.sm[me]
        for other in ranked:
            rank_copy(r.sm.at[other], r.sm_recv.at[other], 0, other, other).wait_recv()
            total = total + r.sm_recv[other]
        r.o_small[chan, me] = total
        for other in ranked:
            rank_copy(r.o_small.at[chan, me], r.o_small.at[chan, me], 1, other, me).start()

    def small_last():
        for other in ranked:
            rank_copy(r.o_small.at[chan, me], r.o_small.at[chan, other], 1, other, other).wait_recv()
        core_copy(r.o_small.at[chan], r.o_small.at[chan], 3).start()

    def small_end():
        core_copy(r.o_small.at[chan], r.o_small.at[1 - chan], 3).wait()
        for other in ranked:
            rank_copy(r.sm.at[other], r.sm_recv.at[me], 0, other, me).wait_send()
            rank_copy(r.o_small.at[chan, me], r.o_small.at[chan, me], 1, other, me).wait_send()
        for copy in first:
            copy.wait_send()

    own_lanes = pl.ds(pl.multiple_of(chan * half, half), half)
    sent, done, begun, written = [], [], [], set()
    received = (r.rs1, r.rs2, r.rs3)
    sent, done, arrived, pending = [], [], [], {}
    starts = dict(grad_in=0, grad_out=3 * half, up=4 * half, down=4 * half + hidden)
    slot_group = ["grad_in", "up", "grad_out", "down", "down"] + ["up"] * 3 + ["grad_out"] + ["grad_in"] * 3

    def half_of(axis, bit):
        return tuple(bit if name == axis else slice(None) for name in "hlyx")

    def fold_copy(layer, slot):
        axis = FOLD[layer][slot_group[slot]]
        theirs = half_of(axis, 1 - bits[axis])
        if slot < 2:
            source, target = r.turned.at[(slot, *theirs)], r.ut_p.at[layer, slot]
        elif slot == 2:
            source, target = r.mixed.at[layer], r.mixed_p.at[layer]
        elif slot == 3:
            source, target = r.g.at[layer], r.g_p.at[layer]
        elif slot in (4, 8):
            kind = 0 if slot == 4 else 1
            source, target = r.turned.at[(kind, *theirs)], r.gt_p.at[layer, kind]
        elif slot < 8:
            lanes = pl.ds((slot - 5) * (hidden // 3), hidden // 3)
            source, target = r.da.at[layer, :, lanes], r.da_p.at[layer, :, lanes]
        else:
            lanes = pl.ds((slot - 9) * half, half)
            source, target = r.gz.at[layer, :, lanes], r.gz_p.at[layer, :, lanes]
        return pltpu.make_async_remote_copy(
            src_ref=source,
            dst_ref=target,
            send_sem=r.fold_sem.at[0, layer, slot],
            recv_sem=r.fold_sem.at[1, layer, slot],
            device_id=peers[axis],
            device_id_type=MESH,
        )

    def turn(layer, slot, value, own):
        kind = slot if slot < 2 else (0 if slot == 4 else 1)
        if kind in pending:
            fold_copy(*pending[kind]).wait_send()
            sent.append(pending[kind])
        pending[kind] = (layer, slot)
        r.turned[kind] = value.astype(F32).T.astype(BF16).reshape(2, 2, 2, 2, width // 16, rows)
        axis = FOLD[layer][slot_group[slot]]
        own[layer, kind] = r.turned.at[(kind, *half_of(axis, bits[axis]))][...]
        fold_copy(layer, slot).start()

    def factors(chunk):
        layer, group, start, columns = CHUNKS[chunk][:4]
        lanes = pl.ds(start - starts[group], columns)
        i = (start - starts[group]) // columns
        if group == "down":
            return (3, 4), r.gt_own.at[layer, 0], r.gt_p.at[layer, 0], r.g.at[layer, :, lanes], r.g_p.at[layer, :, lanes]
        if group == "up":
            return (1, 5 + i), r.ut_own.at[layer, 1], r.ut_p.at[layer, 1], r.da.at[layer, :, lanes], r.da_p.at[layer, :, lanes]
        if group == "grad_out":
            return (2, 8), r.gt_own.at[layer, 1], r.gt_p.at[layer, 1], r.mixed.at[layer], r.mixed_p.at[layer]
        return (0, 9 + i), r.ut_own.at[layer, 0], r.ut_p.at[layer, 0], r.gz.at[layer, :, lanes], r.gz_p.at[layer, :, lanes]

    def rs_left(chunk, stage):
        layer, group, start, columns, order = CHUNKS[chunk]
        return [axis for axis in "hlyx" if axis != FOLD[layer][group] and axis not in order[:stage]]

    def rs_held(chunk, stage, index):
        layer, group, start, columns, order = CHUNKS[chunk]
        lanes = pl.ds(start, columns)
        if stage == 0:
            return r.big.at[(*index, slice(None), lanes)]
        return received[stage - 1].at[(layer, *index, slice(None), lanes)]

    def rs_copy(chunk, stage):
        layer, group, start, columns, order = CHUNKS[chunk]
        axis = order[stage]
        index = tuple(1 - bits[axis] if name == axis else slice(None) for name in rs_left(chunk, stage))
        rest = (slice(None),) * (3 - stage)
        return pltpu.make_async_remote_copy(
            src_ref=rs_held(chunk, stage, index),
            dst_ref=received[stage].at[(layer, *rest, pl.ds(start, columns))],
            send_sem=r.rs_sem.at[0, chunk, stage],
            recv_sem=r.rs_sem.at[1, chunk, stage],
            device_id=peers[axis],
            device_id_type=MESH,
        )

    def weight_grad(chunk):
        layer, group, start, columns, order = CHUNKS[chunk]
        slots, own, theirs, value, value_p = factors(chunk)
        for slot in slots:
            if (layer, slot) not in arrived:
                fold_copy(layer, slot).wait_recv()
                arrived.append((layer, slot))
        for other, spec in enumerate(CHUNKS):
            if spec[0] == layer + 1 and spec[2] == start:
                if (other, 1) not in done:
                    raise ValueError(chunk)
                rs_copy(other, 0).wait_send()
                sent.append((-1, other, 0))
        shape = (width // 2, rows)
        out = mm(own[...].reshape(shape), value[...]) + mm(theirs[...].reshape(shape), value_p[...])
        r.big[:, :, :, :, pl.ds(start, columns)] = out.astype(BF16).reshape(2, 2, 2, width // 16, columns)
        rs_copy(chunk, 0).start()

    def advance(chunk, step_of):
        layer, group, start, columns, order = CHUNKS[chunk]
        done.append((chunk, step_of))
        if step_of == 0:
            weight_grad(chunk)
            return
        stage = step_of - 1
        lanes = pl.ds(start, columns)
        rs_copy(chunk, stage).wait_recv()
        spot = rs_left(chunk, stage).index(order[stage])
        for flat in range(2 ** (2 - stage)):
            kept = [flat >> shift & 1 for shift in reversed(range(2 - stage))]
            mine = tuple(kept[:spot] + [bits[order[stage]]] + kept[spot:])
            total = rs_held(chunk, stage, mine)[...].astype(F32)
            there = received[stage].at[(layer, *kept, slice(None), lanes)]
            total = total + there[...].astype(F32)
            if stage == 2:
                r.o_big[layer, :, lanes] = total
            else:
                there[...] = total.astype(BF16)
        if stage < 2:
            rs_copy(chunk, stage + 1).start()

    def tick(layer, spot):
        now = TICKS * (layers - 1 - layer) + spot
        for chunk, stage in PLAN.get(now, ()):
            advance(chunk, stage)

    def short_all(layer):
        for k in range(3):
            for m in range(micro):
                short_part(layer, k, m, 0, span)

    def next_load(layer, name, slot):
        if 0 <= layer < layers:
            load(name, layer, slot).start()

    def seq_copy(send, recv, sems, other, outgoing):
        slot = seq if outgoing else other
        return pltpu.make_async_remote_copy(
            src_ref=getattr(r, send).at[other],
            dst_ref=getattr(r, recv).at[slot],
            send_sem=getattr(r, sems).at[0, other],
            recv_sem=getattr(r, sems).at[1, slot],
            device_id={"seq": other},
            device_id_type=MESH,
        )

    def all_others():
        return [lax.rem(seq + far, parts) for far in (4, 3, 5, 2, 6, 1, 7)]

    def wait_all(send, recv, sems):
        for other in all_others():
            seq_copy(send, recv, sems, other, False).wait_recv()
        for other in all_others():
            seq_copy(send, recv, sems, other, True).wait_send()

    def pair_copy(slot, m):
        return pltpu.make_async_remote_copy(
            src_ref=r.pair_send.at[slot, m],
            dst_ref=r.pair_recv.at[slot, m],
            send_sem=r.pair_sem.at[0, slot, m],
            recv_sem=r.pair_sem.at[1, slot, m],
            device_id={"chan": 1 - chan},
            device_id_type=MESH,
        )

    def rim_copy(way):
        other = lax.rem(seq + (1 if way == 0 else parts - 1), parts)
        return pltpu.make_async_remote_copy(
            src_ref=r.rim_send.at[way],
            dst_ref=r.rim_recv.at[way],
            send_sem=r.rim_sem.at[0, way],
            recv_sem=r.rim_sem.at[1, way],
            device_id={"seq": other},
            device_id_type=MESH,
        )

    def paired(slot, m, base, count):
        at = (slot, m, pl.ds(base, count), slice(None))
        return r.pair_send[at].astype(F32) + r.pair_recv[at].astype(F32)

    def row(name, index):
        return getattr(r, name)[pl.ds(index, 1), :]

    gains = [[row("vec", 2 * layer + n) for n in range(2)] for layer in range(layers)]
    biases = [[row("vec", 2 * layers + 2 * layer + n) for n in range(2)] for layer in range(layers)]
    branch_bias = [[row("vec", 4 * layers + layer), row("vec", 5 * layers + layer)] for layer in range(layers)]

    def norm_rows(at, x, layer, n):
        centred = x - jnp.mean(x, axis=1, keepdims=True)
        rstd = lax.rsqrt(jnp.mean(centred * centred, axis=1, keepdims=True) + EPS)
        scaled = centred * rstd
        r.xh[layer, n, at, :] = scaled
        r.rstd[layer, n, at, :] = rstd
        r.u[at, :] = (scaled * gains[layer][n] + biases[layer][n]).astype(BF16)

    def forward_rows(slot, bias, layer, n):
        for m in range(micro):
            pair_copy(slot, m).wait_recv()

            @pl.loop(0, span // step)
            def _(i):
                base = pl.multiple_of(i * step, step)
                at = pl.ds(m * span + base, step)
                x = r.x[at, :] + r.mask[at, :] * (paired(slot, m, base, step) + bias)
                r.x[at, :] = x
                if layer < layers:
                    norm_rows(at, x, layer, n)

        for m in range(micro):
            pair_copy(slot, m).wait_send()

    def send_partial(slot, make):
        for m in range(micro):
            r.pair_send[slot, m] = make(m).astype(BF16)
            pair_copy(slot, m).start()

    def tap(layer, k, j):
        return r.params[pl.ds(22 + 9 * layer + 3 * k + j, 1), :]

    def short_part(layer, k, m, low, high):
        z = r.z
        total = r.params[pl.ds(40 + 3 * layer + k, 1), :]
        for j in range(3):
            total = total + tap(layer, k, j) * z[layer, k, m, pl.ds(8 + low - j, high - low), :]
        r.s[k, m, pl.ds(low, high - low), :] = total

    def to_channels(m, value):
        turned = value.T.astype(BF16)
        for j in range(parts):
            r.a_send[j, pl.ds(m * block, block), :] = turned[j * block : (j + 1) * block]

    def start_channels():
        for other in all_others():
            seq_copy("a_send", "a_recv", "a_sem", other, True).start()
        r.a_recv[seq] = r.a_send[seq]

    def gathered():
        return jnp.concatenate([r.a_recv[j] for j in range(parts)], axis=1)

    def from_channels(m):
        stack = [r.b_recv[j, pl.ds(m * block, block), :].astype(F32) for j in range(parts)]
        return jnp.concatenate(stack, axis=0).T

    def inverse_and_send(signal):
        for far in (2, 1, 3, 0):
            at = lax.rem(seq // 2 + far, parts // 2)
            lanes = pl.ds(pl.multiple_of(at * 2 * span, 2 * span), 2 * span)
            out = mm(r.spec[0], r.cos_v[:, lanes]) + mm(r.spec[1], r.sin_v[:, lanes])
            out = (out + r.skip_v[...] * signal[:, lanes].astype(F32)).astype(BF16)
            for h in range(2):
                r.b_send[2 * at + h] = out[:, h * span : (h + 1) * span]
            if far:
                for h in range(2):
                    seq_copy("b_send", "b_recv", "b_sem", 2 * at + h, True).start()
            else:
                seq_copy("b_send", "b_recv", "b_sem", pair, True).start()
                r.b_recv[seq] = r.b_send[seq]

    first[1].wait_recv()
    for base in range(0, rows, step):
        at = pl.ds(base, step)
        x = jnp.concatenate([r.both[0, 0, at, :], r.both[1, 0, at, :]], axis=1).astype(F32)
        r.x[at, :] = x
        norm_rows(at, x, 0, 0)

    for layer in range(layers):
        load("win", layer, 0).wait()
        for k in range(3):
            z = mm(r.u[...], r.win_v[k]) + r.params[pl.ds(16 + 3 * layer + k, 1), :]
            for m in range(micro):
                r.z[layer, k, m, pl.ds(8, span), :] = z[m * span : (m + 1) * span]
                r.rim_send[0, pl.ds(k * 4 + m * 2, 2), :] = z[(m + 1) * span - 2 : (m + 1) * span]
        rim_copy(0).start()
        next_load(layer + 1, "win", 0)
        turn(layer, 0, r.u[...], r.ut_own)
        for k in range(3):
            for m in range(micro):
                short_part(layer, k, m, step, span)
        rim_copy(0).wait()
        inner = (seq > 0).astype(F32)
        for k in range(3):
            for m in range(micro):
                r.z[layer, k, m, pl.ds(6, 2), :] = inner * r.rim_recv[0, pl.ds(k * 4 + m * 2, 2), :]
                short_part(layer, k, m, 0, step)
        for m in range(micro):
            to_channels(m, r.s[1, m] * r.s[2, m])
        start_channels()
        if layer == 0:
            for copy in table_loads:
                copy.wait()
            filter_forward(0)
        wait_all("a_send", "a_recv", "a_sem")
        signal = gathered()
        r.sig[layer] = signal
        r.skip_v[...] = r.skip_l[layer]
        for c in range(0, length, 256):
            lanes = pl.ds(c, 256)
            pc, ps = mm(signal, r.cos_v[:, lanes]), mm(signal, r.sin_v[:, lanes])
            fr, fi = twice(r.fr[layer, :, lanes]), twice(r.fi[layer, :, lanes])
            r.pc[layer, :, lanes], r.ps[layer, :, lanes] = pc.astype(BF16), ps.astype(BF16)
            r.spec[0, :, lanes] = (pc * fr + ps * fi).astype(BF16)
            r.spec[1, :, lanes] = (ps * fr - pc * fi).astype(BF16)
        inverse_and_send(r.sig.at[layer])
        if layer + 1 < layers:
            filter_forward(layer + 1)
        load("wout", layer, 1).wait()
        wait_all("b_send", "b_recv", "b_sem")
        for m in range(micro):
            y = from_channels(m)
            r.y[layer, m] = y.astype(BF16)
            r.mixed[layer, pl.ds(m * span, span), :] = (r.s[0, m] * y).astype(BF16)
        send_partial(0, lambda m: mm(r.mixed[layer, pl.ds(m * span, span), :], r.wout_v[...]))
        next_load(layer + 1, "wout", 1)
        fold_copy(layer, 2).start()
        forward_rows(0, branch_bias[layer][0], layer, 1)

        load("wup", layer, 2).wait()
        for c in range(0, hidden, 256):
            lanes = pl.ds(c, 256)
            for m in range(micro):
                at = pl.ds(m * span, span)
                a = mm(r.u[at, :], r.wup_v[:, lanes]) + r.up_b[pl.ds(layer, 1), lanes]
                cdf = 0.5 + 0.5 * lax.erf(a * math.sqrt(0.5))
                pdf = jnp.exp(-0.5 * a * a) * (1.0 / math.sqrt(2.0 * math.pi))
                r.g[layer, at, lanes] = (a * cdf).astype(BF16)
                r.slope[layer, at, lanes] = (cdf + a * pdf).astype(BF16)
        next_load(layer + 1, "wup", 2)
        load("wdown", layer, 3).wait()
        send_partial(1, lambda m: mm(r.g[layer, pl.ds(m * span, span), :], r.wdown_v[...]))
        next_load(layer + 1, "wdown", 3)
        fold_copy(layer, 3).start()
        turn(layer, 1, r.u[...], r.ut_own)
        forward_rows(1, branch_bias[layer][1], layer + 1, 0)

    r.out_act[...] = r.x[:, own_lanes]

    def branch_rows(at, dx):
        branch = r.mask[at, :] * dx
        r.grad[at, :] = branch.astype(BF16)
        return jnp.sum(branch.reshape(step // 8, 8, width), axis=0)

    def put768(layer, index, value):
        r.o768[pl.ds(8 * layer + index, 1), :] = jnp.sum(value, axis=0, keepdims=True)

    first[2].wait_recv()
    total = jnp.zeros((8, width), F32)
    for base in range(0, rows, step):
        at = pl.ds(base, step)
        dx = jnp.concatenate([r.both[0, 1, at, :], r.both[1, 1, at, :]], axis=1).astype(F32)
        r.x[at, :] = dx
        total = total + branch_rows(at, dx)
    put768(layers - 1, 5, total)

    def backward_rows(slot, layer, n):
        gain = gains[layer][n]
        sums = [jnp.zeros((8, width), F32)] * 3
        for m in range(micro):
            pair_copy(slot, m).wait_recv()

            def body(i, carry):
                base = pl.multiple_of(i * step, step)
                at = pl.ds(m * span + base, step)
                du = paired(slot, m, base, step)
                scaled = r.xh[layer, n, at, :]
                weighted = du * gain
                back = r.rstd[layer, n, at, :] * (
                    weighted
                    - jnp.mean(weighted, axis=1, keepdims=True)
                    - scaled * jnp.mean(weighted * scaled, axis=1, keepdims=True)
                )
                dx = r.x[at, :] + back
                r.x[at, :] = dx
                shape = (step // 8, 8, width)
                return [
                    carry[0] + jnp.sum((du * scaled).reshape(shape), axis=0),
                    carry[1] + jnp.sum(du.reshape(shape), axis=0),
                    carry[2] + branch_rows(at, dx),
                ]

            sums = lax.fori_loop(0, span // step, body, sums)
        for m in range(micro):
            pair_copy(slot, m).wait_send()
        put768(layer, n, sums[0])
        put768(layer, 2 + n, sums[1])
        if n == 1:
            put768(layer, 4, sums[2])
        elif layer > 0:
            put768(layer - 1, 5, sums[2])

    for layer in reversed(range(layers)):
        last = layer == layers - 1
        if not last:
            load("wdown", layer, 3).wait()
        for c in range(0, hidden, 256):
            lanes = pl.ds(c, 256)
            da = mm_nt(r.grad[...], r.wdown_v[lanes, :]) * r.slope[layer, :, lanes].astype(F32)
            r.o_up[pl.ds(layer, 1), lanes] = jnp.sum(da, axis=0, keepdims=True)
            r.da[layer, :, lanes] = da.astype(BF16)
            if c % 512 == 256:
                fold_copy(layer, 5 + c // 512).start()
        next_load(layer - 1, "wdown", 3)
        if not last:
            load("wup", layer, 2).wait()
        send_partial(0, lambda m: mm_nt(r.da[layer, pl.ds(m * span, span), :], r.wup_v[...]))
        next_load(layer - 1, "wup", 2)
        tick(layer, 0)
        turn(layer, 4, r.grad[...], r.gt_own)
        tick(layer, 1)
        if not last:
            short_all(layer)
        tick(layer, 2)
        backward_rows(0, layer, 1)
        tick(layer, 3)
        if not last:
            load("wout", layer, 1).wait()

        for m in range(micro):
            dmixed = mm_nt(r.grad[pl.ds(m * span, span), :], r.wout_v[...])
            to_channels(m, dmixed * r.s[0, m])
            r.ds[0, m, pl.ds(0, span), :] = dmixed * r.y[layer, m].astype(F32)
        start_channels()
        next_load(layer - 1, "wout", 1)
        tick(layer, 4)
        turn(layer, 8, r.grad[...], r.gt_own)
        tick(layer, 5)
        wait_all("a_send", "a_recv", "a_sem")
        tick(layer, 6)
        signal = gathered()
        r.dsig[...] = signal
        r.skip_v[...] = r.skip_l[layer]
        for c in range(0, length, 256):
            lanes = pl.ds(c, 256)
            gc, gs = mm(signal, r.cos_v[:, lanes]), mm(signal, r.sin_v[:, lanes])
            fr, fi = twice(r.fr[layer, :, lanes]), twice(r.fi[layer, :, lanes])
            r.gc[:, lanes], r.gs[:, lanes] = gc.astype(BF16), gs.astype(BF16)
            r.spec[0, :, lanes] = (gc * fr - gs * fi).astype(BF16)
            r.spec[1, :, lanes] = (gs * fr + gc * fi).astype(BF16)
        inverse_and_send(r.dsig)
        tick(layer, 7)
        both_skip = jnp.sum(r.dsig[...].astype(F32) * r.sig[layer].astype(F32), axis=1, keepdims=True)
        r.gskip[layer] = sum(both_skip[m * block : (m + 1) * block] for m in range(micro))
        for c in range(0, length, 256):
            lanes = pl.ds(c, 256)
            gc, gs = r.gc[:, lanes].astype(F32), r.gs[:, lanes].astype(F32)
            pc, ps = r.pc[layer, :, lanes].astype(F32), r.ps[layer, :, lanes].astype(F32)
            re, im = gc * pc + gs * ps, gc * ps - gs * pc
            re = sum(re[m * block : (m + 1) * block] for m in range(micro)) * (1.0 / length)
            im = sum(im[m * block : (m + 1) * block] for m in range(micro)) * (1.0 / length)
            tc, ts = r.turn[pl.ds(0, 1), lanes], r.turn[pl.ds(1, 1), lanes]
            for which, value in enumerate((re * tc + im * ts, re * ts - im * tc)):
                high = value.astype(BF16)
                r.spec[which, pl.ds(0, block), lanes] = high
                r.spec[which, pl.ds(block, block), lanes] = (value - high.astype(F32)).astype(BF16)
        for c in range(0, length, 256):
            lanes = pl.ds(c, 256)
            out = mm(r.spec[0], r.cos_v[:, lanes]) + mm(r.spec[1], r.sin_v[:, lanes])
            r.o_filt[layer, :, lanes] = out[:block] + out[block:]
        filter_backward(layer)
        tick(layer, 8)
        wait_all("b_send", "b_recv", "b_sem")
        for m in range(micro):
            dp = from_channels(m)
            for k in (1, 2):
                value = dp * r.s[3 - k, m]
                r.ds[k, m, pl.ds(0, span), :] = value
            for k in range(3):
                r.rim_send[1, pl.ds(k * 4 + m * 2, 2), :] = r.ds[k, m, pl.ds(0, 2), :]
        rim_copy(1).start()
        for k in range(3):
            sums = [0.0] * 4
            for m in range(micro):
                ds = r.ds[k, m, pl.ds(0, span), :]
                sums[3] = sums[3] + jnp.sum(ds, axis=0, keepdims=True)
                for j in range(3):
                    z = r.z[layer, k, m, pl.ds(8 - j, span), :]
                    sums[j] = sums[j] + jnp.sum(ds * z, axis=0, keepdims=True)
            for j in range(3):
                r.vecs[pl.ds(32 * layer + 11 + 3 * k + j, 1), :] = sums[j]
            r.vecs[pl.ds(32 * layer + 20 + k, 1), :] = sums[3]
        tick(layer, 9)
        rim_copy(1).wait()
        inner = (seq < parts - 1).astype(F32)
        for k in range(3):
            total = 0.0
            for m in range(micro):
                r.ds[k, m, pl.ds(span, 2), :] = inner * r.rim_recv[1, pl.ds(k * 4 + m * 2, 2), :]
                dz = 0.0
                for j in range(3):
                    dz = dz + tap(layer, k, j) * r.ds[k, m, pl.ds(j, span), :]
                total = total + jnp.sum(dz, axis=0, keepdims=True)
                r.gz[layer, pl.ds(m * span, span), pl.ds(k * half, half)] = dz.astype(BF16)
            r.vecs[pl.ds(32 * layer + 8 + k, 1), :] = total
            fold_copy(layer, 9 + k).start()
        if not last:
            load("win", layer, 0).wait()
        send_partial(
            1, lambda m: sum(mm_nt(r.gz[layer, pl.ds(m * span, span), pl.ds(k * half, half)], r.win_v[k]) for k in range(3))
        )
        next_load(layer - 1, "win", 0)
        tick(layer, 10)
        tick(layer, 11)
        backward_rows(1, layer, 0)
        tick(layer, 12)
    r.grad_tokens[...] = r.x[:, own_lanes]
    small_begin()
    for count, (chunk, stage) in enumerate(PLAN[TICKS * layers]):
        advance(chunk, stage)
        if count == SMALL[0]:
            small_middle()
        if count == SMALL[1]:
            small_last()
    small_end()
    for chunk in range(len(CHUNKS)):
        for stage in range(3):
            if (-1, chunk, stage) not in sent:
                rs_copy(chunk, stage).wait_send()
    for layer in range(layers):
        for slot in range(len(slot_group)):
            if (layer, slot) not in sent:
                fold_copy(layer, slot).wait_send()


def chain(inputs, sizes):
    layers, micro, span, half, hidden, feat, freq_lane = sizes
    width, rows, parts = 2 * half, micro * span, 8
    block, length = half // parts, span * parts
    lanes = micro * block
    columns = 4 * half + 2 * hidden
    in_any = ("win", "wout", "wup", "wdown", "cos", "sin")
    outs = dict(
        out_act=((rows, half), F32),
        grad_tokens=((rows, half), F32),
        o_big=((layers, width // 16, 4 * half + 2 * hidden), F32),
        o_small=((2, 2 * parts, block, 128), F32),
    )
    dma, vm = pltpu.SemaphoreType.DMA, pltpu.VMEM
    scratch = dict(
        big=vm((2, 2, 2, width // 16, columns), BF16),
        rs1=vm((layers, 2, 2, width // 16, columns), BF16),
        rs2=vm((layers, 2, width // 16, columns), BF16),
        rs3=vm((layers, width // 16, columns), BF16),
        rs_sem=dma((2, len(CHUNKS), 3)),
        fold_sem=dma((2, layers, 12)),
        ut_own=vm((layers, 2, 2, 2, 2, width // 16, rows), BF16),
        ut_p=vm((layers, 2, 2, 2, 2, width // 16, rows), BF16),
        gt_own=vm((layers, 2, 2, 2, 2, width // 16, rows), BF16),
        gt_p=vm((layers, 2, 2, 2, 2, width // 16, rows), BF16),
        mixed_p=vm((layers, rows, half), BF16),
        g_p=vm((layers, rows, hidden), BF16),
        da_p=vm((layers, rows, hidden), BF16),
        gz=vm((layers, rows, 3 * half), BF16),
        gz_p=vm((layers, rows, 3 * half), BF16),
        win_v=vm((3, width, half), BF16),
        wout_v=vm((half, width), BF16),
        wup_v=vm((width, hidden), BF16),
        wdown_v=vm((hidden, width), BF16),
        cos_v=vm((length, length), BF16),
        sin_v=vm((length, length), BF16),
        skip_v=vm((lanes, 1), F32),
        skip_l=vm((layers, lanes, 1), F32),
        gskip=vm((layers, block, 1), F32),
        vec2=vm((2, 16, half), F32),
        vec=vm((16, width), F32),
        params=vm((48, half), F32),
        pack_t=vm((128, feat), F32),
        chan_t=vm((128, half), F32),
        pack=vm((layers, feat, 128), F32),
        chv=vm((layers, block, 128), F32),
        chv_t=vm((half, 128), F32),
        both=vm((2, 2, rows, half), BF16),
        mask=vm((rows, 1), F32),
        inner=vm((layers, feat, length), F32),
        wave=vm((layers * feat, length), F32),
        fr=vm((layers, block, length), F32),
        fi=vm((layers, block, length), F32),
        spread=vm((layers, feat, 128), F32),
        o_filt=vm((layers, block, length), F32),
        o768=vm((8 * layers, width), F32),
        o_up=vm((layers, hidden), F32),
        vecs=vm((128, half), F32),
        sm=vm((2 * parts, block, 128), F32),
        sm_recv=vm((2 * parts, block, 128), F32),
        sm_sem=dma((2, 2, 2 * parts)),
        core_sem=dma((2, 4)),
        x=vm((rows, width), F32),
        xh=vm((layers, 2, rows, width), F32),
        rstd=vm((layers, 2, rows, 1), F32),
        u=vm((rows, width), BF16),
        z=vm((layers, 3, micro, span + 8, half), F32),
        s=vm((3, micro, span, half), F32),
        y=vm((layers, micro, span, half), BF16),
        mixed=vm((layers, rows, half), BF16),
        sig=vm((layers, lanes, length), BF16),
        dsig=vm((lanes, length), BF16),
        pc=vm((layers, lanes, length), BF16),
        ps=vm((layers, lanes, length), BF16),
        gc=vm((lanes, length), BF16),
        gs=vm((lanes, length), BF16),
        spec=vm((2, lanes, length), BF16),
        slope=vm((layers, rows, hidden), BF16),
        g=vm((layers, rows, hidden), BF16),
        da=vm((layers, rows, hidden), BF16),
        grad=vm((rows, width), BF16),
        turned=vm((2, 2, 2, 2, 2, width // 16, rows), BF16),
        ds=vm((3, micro, span + 8, half), F32),
        a_send=vm((parts, lanes, span), BF16),
        a_recv=vm((parts, lanes, span), BF16),
        b_send=vm((parts, lanes, span), BF16),
        b_recv=vm((parts, lanes, span), BF16),
        pair_send=vm((2, micro, span, width), BF16),
        pair_recv=vm((2, micro, span, width), BF16),
        rim_send=vm((2, 16, half), F32),
        rim_recv=vm((2, 16, half), F32),
        w_sem=dma((4,)),
        t_sem=dma((2,)),
        a_sem=dma((2, parts)),
        b_sem=dma((2, parts)),
        pair_sem=dma((2, 2, micro)),
        rim_sem=dma((2, 2)),
    )
    names = [*inputs, *outs, *scratch]
    results = pl.pallas_call(
        functools.partial(chain_kernel, sizes, names),
        out_shape=[jax.ShapeDtypeStruct(*spec) for spec in outs.values()],
        in_specs=[
            pl.BlockSpec(memory_space=pl.ANY if name in in_any else pltpu.SMEM if name == "lens" else pltpu.VMEM)
            for name in inputs
        ],
        out_specs=[pl.BlockSpec(memory_space=pltpu.VMEM) for _ in outs],
        scratch_shapes=list(scratch.values()),
        compiler_params=pltpu.CompilerParams(
            collective_id=3, has_side_effects=True, vmem_limit_bytes=61 << 20
        ),
        name="chain",
    )(*inputs.values())
    return types.SimpleNamespace(**dict(zip(outs, results)))


def embedding(count, bands, feat):
    steps = np.arange(count, dtype=np.float32) / np.float32(count)
    number = (bands - 1) // 2
    freq = np.linspace(0.0001, number - 1, number).astype(np.float32)
    phases = (np.float32(2.0 * math.pi) * steps)[None, :] * freq[:, None]
    table = np.zeros((128, count), np.float32)
    table[feat] = steps
    table[feat + 1 : feat + 1 + number] = np.cos(phases)
    table[feat + 1 + number : feat + bands] = -np.sin(phases)
    table[feat + bands] = 1.0
    return table


def finish_kernel(sizes, names, *refs):
    layers, micro, span, half, hidden, feat, bands = sizes
    r = types.SimpleNamespace(**dict(zip(names, refs)))
    wide = hidden // half
    for m in range(micro):
        r.act[m, 0] = r.out_act[pl.ds(m * span, span), :]
        r.tokens[m, 0] = r.grad_tokens[pl.ds(m * span, span), :]
    for c in range(2):
        for piece in range(2):
            value = r.o_small[c, pl.ds(8 * piece, 8)].reshape(half, 128)
            r.turned[c, piece] = value.T
    for layer in range(layers):
        for k in range(3):
            r.g_in[layer, k] = r.o_big[layer, :, pl.ds(k * half, half)]
        r.g_out[layer] = r.o_big[layer, :, pl.ds(3 * half, half)]
        r.g_up[layer] = r.o_big[layer, :, pl.ds(4 * half, hidden)]
        r.g_down[layer] = r.o_big[layer, :, pl.ds(4 * half + hidden, hidden)]
        net = sum(r.turned[c, 1, pl.ds(feat, feat), pl.ds(layer * feat, feat)] for c in range(2))
        for i in range(bands):
            r.fin[i, pl.ds(layer, 1), :] = net[i : i + 1]
        r.fbias[pl.ds(layer, 1), :] = net[bands : bands + 1]
        r.ffreq[pl.ds(layer, 1), :] = net[bands + 1 : bands + 2]
        for c in range(2):
            lanes = pl.ds(c * half, half)
            base = 32 * layer

            def row(index, c=c):
                return r.turned[c, 1, pl.ds(index, 1), :]

            for n in range(2):
                r.gain[layer, pl.ds(n, 1), lanes] = row(base + n)
                r.bias[layer, pl.ds(n, 1), lanes] = row(base + 2 + n)
            at = pl.ds(layer, 1)
            r.out_b[at, lanes] = row(base + 4)
            r.down_b[at, lanes] = row(base + 5)
            r.skip[at, lanes] = row(112 + layer)
            for k in range(3):
                r.in_b[k, at, lanes] = row(base + 8 + k)
                r.short_b[k, at, lanes] = row(base + 20 + k)
                for j in range(3):
                    r.taps[k, j, at, lanes] = row(base + 11 + 3 * k + j)
            for i in range(wide):
                r.up_b[at, pl.ds(c * hidden + i * half, half)] = row(base + 24 + i)
            r.fout[layer, :, lanes] = r.turned[c, 0, pl.ds(layer * feat, feat), :]


def finish(out, sizes):
    layers, micro, span, half, hidden, feat, bands = sizes
    width, own = 2 * half, 2 * half // 16
    inputs = dict(out_act=out.out_act, grad_tokens=out.grad_tokens, o_big=out.o_big, o_small=out.o_small)
    outs = dict(
        act=(micro, 1, span, half),
        tokens=(micro, 1, span, half),
        g_in=(layers, 3, own, half),
        g_out=(layers, own, half),
        g_up=(layers, own, hidden),
        g_down=(layers, own, hidden),
        gain=(layers, 2, width),
        bias=(layers, 2, width),
        in_b=(3, layers, width),
        taps=(3, 3, layers, width),
        short_b=(3, layers, width),
        skip=(layers, width),
        out_b=(layers, width),
        up_b=(layers, 2 * hidden),
        down_b=(layers, width),
        fin=(bands, layers, feat),
        fbias=(layers, feat),
        ffreq=(layers, feat),
        fout=(layers, feat, width),
    )
    names = [*inputs, *outs, "turned"]
    results = pl.pallas_call(
        functools.partial(finish_kernel, sizes, names),
        out_shape=[jax.ShapeDtypeStruct(shape, F32) for shape in outs.values()],
        in_specs=[pl.BlockSpec(memory_space=pltpu.VMEM) for _ in inputs],
        out_specs=[pl.BlockSpec(memory_space=pltpu.VMEM) for _ in outs],
        scratch_shapes=[pltpu.VMEM((2, 2, 128, half), F32)],
        name="finish",
    )(*inputs.values())
    turns = dict(
        g_out=(0, 2, 1),
        g_down=(0, 2, 1),
        in_b=(1, 0, 2),
        taps=(2, 0, 1, 3),
        short_b=(1, 0, 2),
        fin=(1, 0, 2),
    )
    return tuple(
        value.transpose(turns[name]) if name in turns else value for name, value in zip(outs, results)
    )


def local_fast(
    tokens,
    lengths,
    cotangent,
    norm_gain,
    norm_bias,
    in_weight,
    in_bias,
    short_taps,
    short_bias,
    skip_gain,
    out_weight,
    out_bias,
    up_weight,
    up_bias,
    down_weight,
    down_bias,
    filter_in,
    filter_bias,
    filter_freq,
    filter_out,
    decay_rate,
):
    micro, rows_dev, half = tokens.shape[0], tokens.shape[2], tokens.shape[3]
    layers, bands, feat = filter_in.shape
    hidden = up_weight.shape[2]
    length = rows_dev * lax.axis_size("seq")
    freq_lane = feat + bands + 1
    cos_np, sin_np, turn_c, turn_s = half_tables(length)
    inputs = dict(
        tok=tokens.reshape(micro * rows_dev, half),
        cot=cotangent.reshape(micro * rows_dev, half),
        lens=lengths.T,
        gain=norm_gain,
        bias=norm_bias,
        out_b=out_bias,
        down_b=down_bias,
        in_b=in_bias.transpose(1, 0, 2),
        taps=short_taps.transpose(1, 2, 0, 3),
        short_b=short_bias.transpose(1, 0, 2),
        up_b=up_bias,
        fin=filter_in.transpose(1, 0, 2),
        fbias=filter_bias,
        ffreq=filter_freq,
        fout=filter_out,
        decay=decay_rate,
        skip=skip_gain,
        emb=jnp.asarray(embedding(length, bands, feat)),
        turn=jnp.asarray(np.concatenate([turn_c, turn_s], axis=1).T, F32),
        win=in_weight,
        wout=out_weight,
        wup=up_weight,
        wdown=down_weight,
        cos=jnp.asarray(cos_np, BF16),
        sin=jnp.asarray(sin_np, BF16),
    )
    out = chain(inputs, (layers, micro, rows_dev, half, hidden, feat, freq_lane))
    return finish(out, (layers, micro, rows_dev, half, hidden, feat, bands))


def solution(mesh):
    in_specs = (
        P(None, "dp", "seq", "chan"),
        P(None, "dp"),
        P(None, "dp", "seq", "chan"),
        P(None, None, "chan"),
        P(None, None, "chan"),
        P(None, None, None, "chan"),
        P(None, None, "chan"),
        P(None, None, None, "chan"),
        P(None, None, "chan"),
        P(None, "chan"),
        P(None, "chan", None),
        P(None, "chan"),
        P(None, None, "chan"),
        P(None, "chan"),
        P(None, "chan", None),
        P(None, "chan"),
        P(),
        P(),
        P(),
        P(None, None, "chan"),
        P(None, "chan"),
    )
    out_specs = (
        P(None, "dp", "seq", "chan"),
        P(None, "dp", "seq", "chan"),
        P(None, None, ("seq", "dp"), "chan"),
        P(None, "chan", ("seq", "dp")),
        P(None, ("seq", "dp"), "chan"),
        P(None, "chan", ("seq", "dp")),
        P(),
        P(),
        P(),
        P(),
        P(),
        P(),
        P(),
        P(),
        P(),
        P(),
        P(),
        P(),
        P(),
    )
    def entry(*args):
        fits = args[0].shape[2] * mesh.shape["seq"] <= 2048 and mesh.shape["seq"] == 8 and mesh.shape["dp"] == 2
        return (local_fast if fits else local)(*args)

    return jax.shard_map(entry, mesh=mesh, in_specs=in_specs, out_specs=out_specs, check_vma=False)
```

```python
import functools
import math
import types

import jax
import jax.numpy as jnp
import numpy as np
from jax import lax
from jax.experimental import pallas as pl
from jax.experimental.pallas import tpu as pltpu
from jax.sharding import PartitionSpec as P

EPS = 1e-05
HIGH = lax.Precision.HIGHEST


def shifted(value, axis, steps):
    count = lax.axis_size(axis)
    initial, last = (max(0, -steps), min(count, count - steps))
    return lax.ppermute(value, axis, [(source, source + steps) for source in range(initial, last)])


def positions(seq_length, emb_width):
    band_count = (emb_width - 1) // 2
    step_ids = jnp.arange(seq_length, dtype=jnp.float32)
    steps_norm = step_ids / seq_length
    band_freq = jnp.linspace(0.0001, band_count - 1, band_count).astype(jnp.float32)
    phases = 2.0 * math.pi * steps_norm[:, None] * band_freq[None, :]
    table = jnp.concatenate([steps_norm[:, None], jnp.cos(phases), -jnp.sin(phases)], axis=1)
    return (table, steps_norm)


def angle_table(row_count, col_count, modulus):
    product = (
        jnp.arange(row_count, dtype=jnp.int32)[:, None]
        * jnp.arange(col_count, dtype=jnp.int32)[None, :]
        % modulus
    )
    theta = product.astype(jnp.float32) * (2.0 * math.pi / modulus)
    return (jnp.cos(theta), jnp.sin(theta))


def split_length(total_length):
    lesser = 2
    for candidate in range(2, math.isqrt(total_length) + 1, 2):
        if total_length % candidate == 0:
            lesser = candidate
    return (lesser, total_length // lesser)


def dft_basis(seq_length):
    padded_len = 2 * seq_length
    lesser, greater = split_length(padded_len)
    cos_p, sin_p = angle_table(lesser, lesser, lesser)
    cos_q, sin_q = angle_table(greater, greater, greater)
    twist_c, twist_s = angle_table(lesser, greater, padded_len)
    return (cos_p, sin_p, cos_q, sin_q, twist_c, twist_s)


def right_mul(left, table):
    return jnp.einsum("ckb,bj->ckj", left, table, precision=HIGH)


def to_spectrum(signal, basis):
    cos_p, sin_p, cos_q, sin_q, twist_c, twist_s = basis
    half = cos_p.shape[0] // 2
    blocks = signal.reshape(signal.shape[0], half, cos_q.shape[0])
    first_re = jnp.einsum("ka,cab->ckb", cos_p[:, :half], blocks, precision=HIGH)
    first_im = -jnp.einsum("ka,cab->ckb", sin_p[:, :half], blocks, precision=HIGH)
    turned_re = first_re * twist_c + first_im * twist_s
    turned_im = first_im * twist_c - first_re * twist_s
    spec_re = right_mul(turned_re, cos_q) + right_mul(turned_im, sin_q)
    spec_im = right_mul(turned_im, cos_q) - right_mul(turned_re, sin_q)
    return (spec_re, spec_im)


def from_spectrum(spec_re, spec_im, basis):
    cos_p, sin_p, cos_q, sin_q, twist_c, twist_s = basis
    half = cos_p.shape[0] // 2
    back_re = right_mul(spec_re, cos_q) - right_mul(spec_im, sin_q)
    back_im = right_mul(spec_im, cos_q) + right_mul(spec_re, sin_q)
    turned_re = back_re * twist_c - back_im * twist_s
    turned_im = back_im * twist_c + back_re * twist_s
    signal = jnp.einsum("ak,ckb->cab", cos_p[:half], turned_re, precision=HIGH) - jnp.einsum(
        "ak,ckb->cab", sin_p[:half], turned_im, precision=HIGH
    )
    return signal.reshape(signal.shape[0], half * cos_q.shape[0]) / (
        cos_p.shape[0] * cos_q.shape[0]
    )


def complex_mul(left_re, left_im, right_re, right_im):
    return (left_re * right_re - left_im * right_im, left_re * right_im + left_im * right_re)


def filter_block(table, steps_norm, weight_in, bias_in, freq_in, cols_in, decay_cols):
    hidden = jnp.sin(freq_in * (jnp.dot(table, weight_in, precision=HIGH) + bias_in))
    raw = jnp.einsum("lf,fc->cl", hidden, cols_in, precision=HIGH)
    return raw * jnp.exp(-decay_cols[:, None] * steps_norm[None, :])


def to_channels(block):
    parts = lax.axis_size("seq")
    shaped = block.reshape(parts, block.shape[0] // parts, block.shape[1])
    moved = lax.all_to_all(
        shaped.astype(jnp.bfloat16), "seq", split_axis=0, concat_axis=2, tiled=True
    ).astype(shaped.dtype)
    return moved.reshape(moved.shape[1], moved.shape[2])


def to_positions(block):
    shaped = block.reshape(1, block.shape[0], block.shape[1])
    moved = lax.all_to_all(
        shaped.astype(jnp.bfloat16), "seq", split_axis=2, concat_axis=0, tiled=True
    ).astype(shaped.dtype)
    return moved.reshape(moved.shape[0] * moved.shape[1], moved.shape[2])


def branch_sum(partial_value):
    return lax.psum_scatter(
        partial_value.astype(jnp.bfloat16), "chan", scatter_dimension=1, tiled=True
    ).astype(jnp.float32)


def branch_grad(grad_low):
    return lax.all_gather(grad_low, "chan", axis=1, tiled=True)


def place(values, start, full_width, axis):
    full_shape = list(values.shape)
    full_shape[axis] = full_width
    return lax.dynamic_update_slice_in_dim(jnp.zeros(full_shape, jnp.float32), values, start, axis)


def local(
    tokens,
    lengths,
    cotangent,
    norm_gain,
    norm_bias,
    in_weight,
    in_bias,
    short_taps,
    short_bias,
    skip_gain,
    out_weight,
    out_bias,
    up_weight,
    up_bias,
    down_weight,
    down_bias,
    filter_in,
    filter_bias,
    filter_freq,
    filter_out,
    decay_rate,
):
    micro_count = tokens.shape[0]
    rows_dev = tokens.shape[2]
    chan_width = tokens.shape[3]
    layer_count = norm_gain.shape[0]
    hidden_width = up_weight.shape[2]
    seq_parts = lax.axis_size("seq")
    chan_parts = lax.axis_size("chan")
    full_width = chan_width * chan_parts
    seq_length = rows_dev * seq_parts
    seq_index = lax.axis_index("seq")
    chan_index = lax.axis_index("chan")
    block_width = chan_width // seq_parts
    col_start = seq_index * block_width
    chan_start = chan_index * chan_width
    basis = dft_basis(seq_length)
    table, steps_norm = positions(seq_length, filter_in.shape[1])
    positions_dev = seq_index * rows_dev + jnp.arange(rows_dev, dtype=jnp.int32)
    filters = []
    for layer_index in range(layer_count):
        filter_cols = lax.dynamic_slice_in_dim(filter_out[layer_index], col_start, block_width, 1)
        decay_cols = lax.dynamic_slice_in_dim(decay_rate[layer_index], col_start, block_width, 0)
        skip_cols = lax.dynamic_slice_in_dim(skip_gain[layer_index], col_start, block_width, 0)

        def make_one(weight_in, bias_in, freq_in, cols_in, decay_cols=decay_cols):
            return filter_block(table, steps_norm, weight_in, bias_in, freq_in, cols_in, decay_cols)

        long_filter, filter_pull = jax.vjp(
            make_one,
            filter_in[layer_index],
            filter_bias[layer_index],
            filter_freq[layer_index],
            filter_cols,
        )
        filt_re, filt_im = to_spectrum(long_filter, basis)
        filters.append((filt_re, filt_im, filter_pull, skip_cols))

    def norm_forward(resid, gain_bias):
        full_rows, full_gb = (
            lax.all_gather(resid, "chan", axis=1, tiled=True),
            lax.all_gather(gain_bias, "chan", axis=1, tiled=True),
        )
        mean_row = jnp.mean(full_rows, axis=1, keepdims=True)
        centred = full_rows - mean_row
        rstd = lax.rsqrt(jnp.mean(centred * centred, axis=1, keepdims=True) + EPS)
        scaled = centred * rstd
        normed = (scaled * full_gb[0] + full_gb[1]).astype(jnp.bfloat16)
        return (normed, (scaled, rstd, full_gb[0]))

    def norm_backward(grad_partial, norm_saved):
        scaled, rstd, gain_row = norm_saved
        grad_rows = lax.psum(grad_partial.astype(jnp.bfloat16), "chan").astype(jnp.float32)
        grad_scaled = grad_rows * gain_row
        grad_full = rstd * (
            grad_scaled
            - jnp.mean(grad_scaled, axis=1, keepdims=True)
            - scaled * jnp.mean(grad_scaled * scaled, axis=1, keepdims=True)
        )
        grad_own = lax.dynamic_slice_in_dim(grad_full, chan_start, chan_width, 1)
        rows_own = lax.dynamic_slice_in_dim(grad_rows, chan_start, chan_width, 1)
        scaled_own = lax.dynamic_slice_in_dim(scaled, chan_start, chan_width, 1)
        return (grad_own, jnp.sum(rows_own * scaled_own, axis=0), jnp.sum(rows_own, axis=0))

    def mixer_forward(resid, pad_mask, layer_index):
        normed, norm_saved = norm_forward(
            resid, jnp.stack([norm_gain[layer_index, 0], norm_bias[layer_index, 0]])
        )
        streams = (
            jnp.einsum(
                "sd,kdc->kcs", normed, in_weight[layer_index], preferred_element_type=jnp.float32
            )
            + in_bias[layer_index][:, :, None]
        )
        rim = shifted(streams[:, :, rows_dev - 2 :], "seq", 1)
        padded = jnp.concatenate([rim, streams], axis=2)
        taps = short_taps[layer_index]
        short_out = (
            taps[:, 0][:, :, None] * padded[:, :, 2:]
            + taps[:, 1][:, :, None] * padded[:, :, 1 : rows_dev + 1]
            + taps[:, 2][:, :, None] * padded[:, :, :rows_dev]
            + short_bias[layer_index][:, :, None]
        )
        product = short_out[1] * short_out[2]
        chan_prod = to_channels(product)
        filt_re, filt_im, filter_pull, skip_cols = filters[layer_index]
        prod_re, prod_im = to_spectrum(chan_prod, basis)
        conv_re, conv_im = complex_mul(prod_re, prod_im, filt_re, filt_im)
        chan_out = from_spectrum(conv_re, conv_im, basis) + skip_cols[:, None] * chan_prod
        long_out = to_positions(chan_out)
        mixed = (short_out[0] * long_out).astype(jnp.bfloat16)
        partial_value = jnp.einsum(
            "cs,cd->sd", mixed, out_weight[layer_index], preferred_element_type=jnp.float32
        )
        branch = branch_sum(partial_value) + out_bias[layer_index]
        saved = (
            normed,
            norm_saved,
            padded,
            short_out,
            chan_prod,
            prod_re,
            prod_im,
            long_out,
            mixed,
        )
        return (resid + pad_mask[:, None] * branch, saved)

    def mlp_forward(resid, pad_mask, layer_index):
        normed, norm_saved = norm_forward(
            resid, jnp.stack([norm_gain[layer_index, 1], norm_bias[layer_index, 1]])
        )
        pre_act = (
            jnp.dot(normed, up_weight[layer_index], preferred_element_type=jnp.float32)
            + up_bias[layer_index]
        )
        activated = jax.nn.gelu(pre_act, approximate=False).astype(jnp.bfloat16)
        partial_value = jnp.dot(
            activated, down_weight[layer_index], preferred_element_type=jnp.float32
        )
        branch = branch_sum(partial_value) + down_bias[layer_index]
        return (resid + pad_mask[:, None] * branch, (normed, norm_saved, pre_act, activated))

    def mlp_backward(grad_resid, pad_mask, layer_index, saved):
        normed, norm_saved, pre_act, activated = saved
        grad_branch = pad_mask[:, None] * grad_resid
        g_down_bias = jnp.sum(grad_branch, axis=0)
        grad_full = branch_grad(grad_branch.astype(jnp.bfloat16))
        g_down_weight = jnp.einsum(
            "sf,sd->fd", activated, grad_full, preferred_element_type=jnp.float32
        )
        grad_act = jnp.einsum(
            "sd,fd->sf", grad_full, down_weight[layer_index], preferred_element_type=jnp.float32
        )
        unused_value, gelu_pull = jax.vjp(
            lambda inner: jax.nn.gelu(inner, approximate=False), pre_act
        )
        grad_pre = gelu_pull(grad_act)[0]
        g_up_bias = jnp.sum(grad_pre, axis=0)
        pre_low = grad_pre.astype(jnp.bfloat16)
        g_up_weight = jnp.einsum("sd,sf->df", normed, pre_low, preferred_element_type=jnp.float32)
        grad_normed = jnp.einsum(
            "sf,df->sd", pre_low, up_weight[layer_index], preferred_element_type=jnp.float32
        )
        grad_own, g_gain, g_bias = norm_backward(grad_normed, norm_saved)
        return (
            grad_resid + grad_own,
            (g_up_weight, g_down_weight, g_gain, g_bias, g_up_bias, g_down_bias),
        )

    mixer_acc = [None] * layer_count
    mlp_acc = [None] * layer_count
    outputs = []
    input_grads = []
    for micro_index in range(micro_count):
        pad_mask = (positions_dev < lengths[micro_index, 0]).astype(jnp.float32)
        resid = tokens[micro_index, 0].astype(jnp.float32)
        layer_inputs = []
        layer_saved = []
        for layer_index in range(layer_count):
            layer_inputs.append(resid)
            resid, mix_saved = mixer_forward(resid, pad_mask, layer_index)
            layer_inputs.append(resid)
            resid, mlp_saved = mlp_forward(resid, pad_mask, layer_index)
            layer_saved.append((mix_saved, mlp_saved))
        outputs.append(resid)
        grad_resid = cotangent[micro_index, 0].astype(jnp.float32)
        for layer_index in reversed(range(layer_count)):
            mlp_saved = mlp_forward(layer_inputs[2 * layer_index + 1], pad_mask, layer_index)[1]
            grad_resid, mlp_grads = mlp_backward(grad_resid, pad_mask, layer_index, mlp_saved)
            mix_saved = mixer_forward(layer_inputs[2 * layer_index], pad_mask, layer_index)[1]
            (
                mixer_normed,
                mixer_norm_saved,
                mixer_padded,
                mixer_short_out,
                mixer_chan_prod,
                mixer_prod_re,
                mixer_prod_im,
                mixer_long_out,
                mixer_mixed,
            ) = mix_saved
            mixer_filt_re, mixer_filt_im, mixer_filter_pull, mixer_skip_cols = filters[layer_index]
            mixer_grad_branch = pad_mask[:, None] * grad_resid
            g_out_bias = jnp.sum(mixer_grad_branch, axis=0)
            mixer_grad_full = branch_grad(mixer_grad_branch.astype(jnp.bfloat16))
            g_out_weight = jnp.einsum(
                "cs,sd->cd", mixer_mixed, mixer_grad_full, preferred_element_type=jnp.float32
            )
            grad_mixed = jnp.einsum(
                "sd,cd->cs",
                mixer_grad_full,
                out_weight[layer_index],
                preferred_element_type=jnp.float32,
            )
            grad_long = grad_mixed * mixer_short_out[0]
            grad_gate = grad_mixed * mixer_long_out
            chan_grad = to_channels(grad_long)
            grad_re, grad_im = to_spectrum(chan_grad, basis)
            back_re, back_im = complex_mul(grad_re, grad_im, mixer_filt_re, -mixer_filt_im)
            chan_dprod = (
                from_spectrum(back_re, back_im, basis) + mixer_skip_cols[:, None] * chan_grad
            )
            corr_re, corr_im = complex_mul(grad_re, grad_im, mixer_prod_re, -mixer_prod_im)
            grad_filter = from_spectrum(corr_re, corr_im, basis)
            g_skip = jnp.sum(chan_grad * mixer_chan_prod, axis=1)
            grad_product = to_positions(chan_dprod)
            grad_short = jnp.stack(
                [grad_gate, grad_product * mixer_short_out[2], grad_product * mixer_short_out[1]]
            )
            g_short_bias = jnp.sum(grad_short, axis=2)
            g_taps = jnp.stack(
                [
                    jnp.sum(grad_short * mixer_padded[:, :, 2:], axis=2),
                    jnp.sum(grad_short * mixer_padded[:, :, 1 : rows_dev + 1], axis=2),
                    jnp.sum(grad_short * mixer_padded[:, :, :rows_dev], axis=2),
                ],
                axis=1,
            )
            next_rim = shifted(grad_short[:, :, :2], "seq", -1)
            extended = jnp.concatenate([grad_short, next_rim], axis=2)
            mixer_taps = short_taps[layer_index]
            grad_streams = (
                mixer_taps[:, 0][:, :, None] * extended[:, :, :rows_dev]
                + mixer_taps[:, 1][:, :, None] * extended[:, :, 1 : rows_dev + 1]
                + mixer_taps[:, 2][:, :, None] * extended[:, :, 2:]
            )
            g_in_bias = jnp.sum(grad_streams, axis=2)
            streams_low = grad_streams.astype(jnp.bfloat16)
            g_in_weight = jnp.einsum(
                "sd,kcs->kdc", mixer_normed, streams_low, preferred_element_type=jnp.float32
            )
            mixer_grad_normed = jnp.einsum(
                "kcs,kdc->sd",
                streams_low,
                in_weight[layer_index],
                preferred_element_type=jnp.float32,
            )
            mixer_grad_own, mixer_g_gain, mixer_g_bias = norm_backward(
                mixer_grad_normed, mixer_norm_saved
            )
            grads = (
                g_in_weight,
                g_out_weight,
                mixer_g_gain,
                mixer_g_bias,
                g_in_bias,
                g_taps,
                g_short_bias,
                g_skip,
                g_out_bias,
                grad_filter,
            )
            grad_resid, mix_grads = (grad_resid + mixer_grad_own, grads)
            if mixer_acc[layer_index] is None:
                mixer_acc[layer_index] = mix_grads
                mlp_acc[layer_index] = mlp_grads
            else:
                mixer_acc[layer_index] = jax.tree.map(jnp.add, mixer_acc[layer_index], mix_grads)
                mlp_acc[layer_index] = jax.tree.map(jnp.add, mlp_acc[layer_index], mlp_grads)
        input_grads.append(grad_resid)
    filter_grads = [
        filters[layer_index][2](mixer_acc[layer_index][9]) for layer_index in range(layer_count)
    ]
    skip_start = chan_start + col_start

    def stack_mix(member):
        return jnp.stack([mixer_acc[layer_index][member] for layer_index in range(layer_count)])

    def stack_mlp(member):
        return jnp.stack([mlp_acc[layer_index][member] for layer_index in range(layer_count)])

    def stack_filter(member):
        return jnp.stack([filter_grads[layer_index][member] for layer_index in range(layer_count)])

    big_grads = (
        lax.psum_scatter(stack_mix(0), ("seq", "dp"), scatter_dimension=2, tiled=True),
        lax.psum_scatter(stack_mix(1), ("seq", "dp"), scatter_dimension=2, tiled=True),
        lax.psum_scatter(stack_mlp(0), ("seq", "dp"), scatter_dimension=1, tiled=True),
        lax.psum_scatter(stack_mlp(1), ("seq", "dp"), scatter_dimension=2, tiled=True),
    )
    gain_grads = jnp.stack([stack_mix(2), stack_mlp(2)], axis=1)
    bias_grads = jnp.stack([stack_mix(3), stack_mlp(3)], axis=1)
    small = lax.psum(
        (
            place(gain_grads, chan_start, full_width, 2),
            place(bias_grads, chan_start, full_width, 2),
            place(stack_mix(4), chan_start, full_width, 2),
            place(stack_mix(5), chan_start, full_width, 3),
            place(stack_mix(6), chan_start, full_width, 2),
            place(stack_mix(7), skip_start, full_width, 1),
            place(stack_mix(8), chan_start, full_width, 1),
            place(stack_mlp(4), chan_index * hidden_width, hidden_width * chan_parts, 1),
            place(stack_mlp(5), chan_start, full_width, 1),
            stack_filter(0),
            stack_filter(1),
            stack_filter(2),
            place(stack_filter(3), skip_start, full_width, 2),
        ),
        ("seq", "chan", "dp"),
    )
    out_act = jnp.stack(outputs)[:, None]
    grad_tokens = jnp.stack(input_grads)[:, None]
    return (
        out_act,
        grad_tokens,
        big_grads[0],
        big_grads[1],
        big_grads[2],
        big_grads[3],
        small[0],
        small[1],
        small[2],
        small[3],
        small[4],
        small[5],
        small[6],
        small[7],
        small[8],
        small[9],
        small[10],
        small[11],
        small[12],
    )


F32 = jnp.float32
BF16 = jnp.bfloat16
MESH = pl.DeviceIdType.MESH
CHUNKS = (
    (1, "down", 3072, 512, "yxh"),
    (1, "down", 3584, 512, "yxh"),
    (1, "down", 4096, 512, "xyh"),
    (1, "up", 1536, 512, "xlh"),
    (1, "up", 2048, 512, "xlh"),
    (1, "up", 2560, 512, "lhx"),
    (1, "grad_out", 1152, 384, "lyh"),
    (1, "grad_in", 0, 384, "ylh"),
    (1, "grad_in", 384, 384, "yhl"),
    (1, "grad_in", 768, 384, "yhl"),
    (0, "down", 3072, 512, "ylh"),
    (0, "down", 3584, 512, "ylh"),
    (0, "down", 4096, 512, "ylh"),
    (0, "up", 1536, 512, "ylh"),
    (0, "up", 2048, 512, "ylh"),
    (0, "up", 2560, 512, "ylh"),
    (0, "grad_out", 1152, 384, "ylh"),
    (0, "grad_in", 0, 384, "ylh"),
    (0, "grad_in", 384, 384, "ylh"),
    (0, "grad_in", 768, 384, "ylh"),
)
FOLD = (
    dict(grad_in="x", grad_out="x", up="x", down="x"),
    dict(grad_in="x", grad_out="x", up="y", down="l"),
)
TICKS = 13
PLAN = {
    7: ((3, 0), (6, 0), (4, 0),),
    9: ((0, 0), (1, 0), (2, 0), (5, 0), (3, 1),),
    10: ((4, 1),),
    13: ((6, 1), (0, 1), (2, 1), (5, 1),),
    15: ((3, 2),),
    17: ((1, 1), (7, 0), (4, 2), (6, 2), (2, 2),),
    19: ((8, 0), (5, 2), (3, 3), (9, 0),),
    20: ((7, 1),),
    21: ((4, 3), (6, 3), (13, 0), (8, 1), (2, 3),),
    22: ((9, 1), (14, 0),),
    24: ((7, 2), (8, 2), (13, 1),),
    26: ((15, 0), (9, 2), (0, 2), (14, 1), (7, 3), (8, 3), (13, 2), (10, 0), (11, 0), (12, 0), (9, 3), (1, 2), (0, 3), (15, 1), (14, 2), (16, 0), (13, 3), (10, 1), (5, 3), (1, 3), (15, 2), (11, 1), (17, 0), (14, 3), (10, 2), (12, 1), (18, 0), (15, 3), (11, 2), (16, 1), (10, 3), (19, 0), (12, 2), (17, 1), (11, 3), (16, 2), (18, 1), (12, 3), (19, 1), (17, 2), (16, 3), (18, 2), (19, 2), (17, 3), (18, 3), (19, 3),),
}
SMALL = (33, 44)


def half_tables(count):
    odd = 2 * np.arange(count, dtype=np.int64) + 1
    angle = np.outer(odd, odd) % (8 * count) * (math.pi / (4 * count))
    twist = odd * (math.pi / (4 * count))
    return np.cos(angle), np.sin(angle), np.cos(twist)[:, None], np.sin(twist)[:, None]


def mesh_bits():
    seq, dp = lax.axis_index("seq"), lax.axis_index("dp")
    return {"x": dp, "y": lax.rem(seq, 2), "l": lax.rem(seq // 2, 2), "h": seq // 4}


def mesh_peers():
    seq, dp = lax.axis_index("seq"), lax.axis_index("dp")
    bits = mesh_bits()
    return {
        "x": {"dp": 1 - dp},
        "y": {"seq": seq + 1 - 2 * bits["y"]},
        "l": {"seq": seq + 2 - 4 * bits["l"]},
        "h": {"seq": seq + 4 - 8 * bits["h"]},
    }


def greet(devices):
    barrier = pltpu.get_barrier_semaphore()
    for device in devices:
        pl.semaphore_signal(barrier, inc=1, device_id=device, device_id_type=MESH)
    pl.semaphore_wait(barrier, len(devices))


def mm(left, right):
    return jnp.dot(left, right, preferred_element_type=F32)


def fine(left, right, dims=((1,), (0,))):
    return lax.dot_general(left, right, (dims, ((), ())), precision=HIGH, preferred_element_type=F32)


def mm_nt(left, right):
    return lax.dot_general(left, right, (((1,), (1,)), ((), ())), preferred_element_type=F32)


def chain_kernel(sizes, names, *refs):
    layers, micro, span, half, hidden, feat, freq_lane = sizes
    r = types.SimpleNamespace(**dict(zip(names, refs)))
    width, rows, parts = 2 * half, micro * span, 8
    block = half // parts
    length = span * parts
    seq, chan = lax.axis_index("seq"), lax.axis_index("chan")
    pair = seq + 1 - 2 * lax.rem(seq, 2)
    step = 32

    def load(name, layer, slot):
        return pltpu.make_async_copy(getattr(r, name).at[layer], getattr(r, name + "_v"), r.w_sem.at[slot])

    weights = (("win", 0), ("wout", 1), ("wup", 2), ("wdown", 3))
    table_loads = [
        pltpu.make_async_copy(r.cos, r.cos_v, r.t_sem.at[0]),
        pltpu.make_async_copy(r.sin, r.sin_v, r.t_sem.at[1]),
    ]
    load("win", 0, 0).start()
    for copy in table_loads:
        copy.start()
    for name, slot in weights[1:]:
        load(name, 0, slot).start()
    peers, bits = mesh_peers(), mesh_bits()
    dp = lax.axis_index("dp")
    ranks = 2 * parts
    me = 2 * seq + dp
    ranked = [lax.rem(me + far, ranks) for far in range(1, ranks)]
    r.sm_recv[...] = jnp.zeros_like(r.sm_recv)
    greet([{"seq": other // 2, "dp": lax.rem(other, 2)} for other in ranked] + [{"chan": 1 - chan}])

    def core_copy(source, target, slot):
        return pltpu.make_async_remote_copy(
            src_ref=source,
            dst_ref=target,
            send_sem=r.core_sem.at[0, slot],
            recv_sem=r.core_sem.at[1, slot],
            device_id={"chan": 1 - chan},
            device_id_type=MESH,
        )

    for layer in range(layers):
        at = pl.ds(layer, 1)
        for n in range(2):
            r.params[pl.ds(2 * layer + n, 1), :] = r.gain[layer, pl.ds(n, 1), :]
            r.params[pl.ds(2 * layers + 2 * layer + n, 1), :] = r.bias[layer, pl.ds(n, 1), :]
        r.params[pl.ds(4 * layers + layer, 1), :] = r.out_b[at, :]
        r.params[pl.ds(5 * layers + layer, 1), :] = r.down_b[at, :]
    r.params[pl.ds(12, 4), :] = jnp.zeros((4, half), F32)
    first = [
        core_copy(r.params.at[pl.ds(0, 16)], r.vec2.at[chan], 0),
        core_copy(r.tok, r.both.at[chan, 0], 1),
        core_copy(r.cot, r.both.at[chan, 1], 2),
    ]
    for copy in first:
        copy.start()
    r.vec2[chan] = r.params[pl.ds(0, 16), :]
    r.both[chan, 0] = r.tok[...]
    r.both[chan, 1] = r.cot[...]
    r.sm[...] = jnp.zeros_like(r.sm)
    r.vecs[...] = jnp.zeros_like(r.vecs)
    r.o768[...] = jnp.zeros_like(r.o768)
    for m in range(micro):
        place_ids = seq * span + lax.broadcasted_iota(jnp.int32, (span, 1), 0)
        r.mask[pl.ds(m * span, span), :] = (place_ids < r.lens[0, m]).astype(F32)
    for layer in range(layers):
        at = pl.ds(layer, 1)
        for k in range(3):
            r.params[pl.ds(16 + 3 * layer + k, 1), :] = r.in_b[k, at, :]
            r.params[pl.ds(40 + 3 * layer + k, 1), :] = r.short_b[k, at, :]
            for j in range(3):
                r.params[pl.ds(22 + 9 * layer + 3 * k + j, 1), :] = r.taps[k, j, at, :]
    first[0].wait_recv()
    r.vec[...] = jnp.concatenate([r.vec2[0], r.vec2[1]], axis=1)

    def rank_copy(source, target, phase, other, slot):
        return pltpu.make_async_remote_copy(
            src_ref=source,
            dst_ref=target,
            send_sem=r.sm_sem.at[phase, 0, other],
            recv_sem=r.sm_sem.at[phase, 1, slot],
            device_id={"seq": other // 2, "dp": other % 2 if isinstance(other, int) else lax.rem(other, 2)},
            device_id_type=MESH,
        )

    def small_copy(other):
        return rank_copy(r.sm_b.at[other], r.sm_recv.at[me], 0, other, me)

    def each_small(act):
        for other in range(parts, ranks):

            @pl.when(me != other)
            def _(other=other):
                act(small_copy(other))

        @pl.when(me != seq)
        def _():
            act(small_copy(seq))

    def small_wait(other):
        rank_copy(r.sm_b.at[other], r.sm_recv.at[other], 0, other, other).wait_recv()

    def chan_rows(layer):
        value = r.chv[layer]
        return value[:, :feat], value[:, feat : feat + 1], value[:, feat + 1 : feat + 2]

    def filter_forward(layer):
        at = pl.ds(layer, 1)
        r.pack_t[...] = jnp.zeros_like(r.pack_t)
        for i in range(freq_lane - feat - 1):
            r.pack_t[pl.ds(feat + i, 1), :] = r.fin[i, at, :]
        r.pack_t[pl.ds(freq_lane - 1, 1), :] = r.fbias[at, :]
        r.pack_t[pl.ds(freq_lane, 1), :] = r.ffreq[at, :]
        r.pack[layer] = r.pack_t[...].T
        r.chan_t[...] = jnp.zeros_like(r.chan_t)
        r.chan_t[pl.ds(0, feat), :] = r.fout[layer]
        r.chan_t[pl.ds(feat, 1), :] = r.decay[at, :]
        r.chan_t[pl.ds(feat + 1, 1), :] = r.skip[at, :]
        r.chv_t[...] = r.chan_t[...].T
        r.chv[layer] = r.chv_t[pl.ds(pl.multiple_of(seq * block, 8), block), :]
        turned, decay, skip = chan_rows(layer)
        r.skip_l[layer] = jnp.concatenate([skip] * micro, axis=0)
        pack = r.pack[layer]
        freq = pack[:, freq_lane : freq_lane + 1]
        for c in range(0, length, 256):
            lanes = pl.ds(c, 256)
            inner = fine(pack, r.emb[:, lanes])
            wave = jnp.sin(freq * inner)
            r.inner[layer, :, lanes] = inner
            r.wave[pl.ds(layer * feat, feat), lanes] = wave
            filt = fine(turned, wave) * jnp.exp(-decay * r.emb[pl.ds(feat, 1), lanes])
            high = filt.astype(BF16)
            r.spec[0, pl.ds(0, block), lanes] = high
            r.spec[0, pl.ds(block, block), lanes] = (filt - high.astype(F32)).astype(BF16)
        for c in range(0, length, 256):
            lanes = pl.ds(c, 256)
            fc, fs = mm(r.spec[0], r.cos_v[:, lanes]), mm(r.spec[0], r.sin_v[:, lanes])
            fc, fs = fc[:block] + fc[block:], fs[:block] + fs[block:]
            tc, ts = r.turn[pl.ds(0, 1), lanes], r.turn[pl.ds(1, 1), lanes]
            r.fr[layer, :, lanes] = (fc * tc + fs * ts) * (1.0 / length)
            r.fi[layer, :, lanes] = (fc * ts - fs * tc) * (1.0 / length)

    def twice(value):
        return jnp.concatenate([value] * micro, axis=0)

    def filter_backward(layer):
        turned, decay, _ = chan_rows(layer)
        freq = r.pack[layer, :, freq_lane : freq_lane + 1]
        g_out = g_pack = g_freq = 0.0
        for c in range(0, length, 256):
            lanes = pl.ds(c, 256)
            raw = r.o_filt[layer, :, lanes] * jnp.exp(-decay * r.emb[pl.ds(feat, 1), lanes])
            g_out = g_out + mm_nt(raw.astype(BF16), r.wave[:, lanes].astype(BF16))
            inner = r.inner[layer, :, lanes]
            slope = lax.dot_general(turned.astype(BF16), raw.astype(BF16), (((0,), (0,)), ((), ())), preferred_element_type=F32) * jnp.cos(freq * inner)
            g_freq = g_freq + jnp.sum(slope * inner, axis=1, keepdims=True)
            g_pack = g_pack + mm_nt((slope * freq).astype(BF16), r.emb[:, lanes].astype(BF16))
        lane = lax.broadcasted_iota(jnp.int32, (block, 128), 1)
        mine = (lane >= layer * feat) & (lane < (layer + 1) * feat)
        r.sm[seq] = jnp.where(mine, g_out, r.sm[seq])
        lane = lax.broadcasted_iota(jnp.int32, (feat, 128), 1)
        r.spread[layer] = g_pack + jnp.where(lane == freq_lane, g_freq, 0.0)

    def small_begin():
        for layer in range(layers):
            r.vecs[pl.ds(32 * layer, 8), :] = r.o768[pl.ds(8 * layer, 8), own_lanes]
            for i in range(hidden // half):
                r.vecs[pl.ds(32 * layer + 24 + i, 1), :] = r.o_up[pl.ds(layer, 1), pl.ds(i * half, half)]
        spread = jnp.concatenate(
            [r.spread[layer] for layer in range(layers)] + [jnp.zeros((half - layers * feat, 128), F32)], axis=0
        )
        total = r.vecs[...].T + spread
        r.sm[pl.ds(parts, parts)] = total.reshape(parts, block, 128)
        lane = lax.broadcasted_iota(jnp.int32, (block, 128), 1)
        for layer in range(layers):
            r.sm[parts + seq] = r.sm[parts + seq] + jnp.where(lane == 112 + layer, r.gskip[layer], 0.0)
        r.sm_b[...] = r.sm[...].astype(BF16)
        each_small(lambda copy: copy.start())

    def small_middle():
        total = r.sm[me]

        @pl.when(me >= parts)
        def _():
            for other in ranked:
                small_wait(other)

        for i in range(2):
            other = lax.rem(2 * me + i, ranks)

            @pl.when((me < parts) & (other != me))
            def _(other=other):
                small_wait(other)

        for other in ranked:
            total = total + r.sm_recv[other].astype(F32)
        r.o_small[chan, me] = total.astype(BF16)
        for other in ranked:
            rank_copy(r.o_small.at[chan, me], r.o_small.at[chan, me], 1, other, me).start()

    def small_last():
        for other in ranked:
            rank_copy(r.o_small.at[chan, me], r.o_small.at[chan, other], 1, other, other).wait_recv()
        core_copy(r.o_small.at[chan], r.o_small.at[chan], 3).start()

    def small_end():
        core_copy(r.o_small.at[chan], r.o_small.at[1 - chan], 3).wait()
        for other in ranked:
            rank_copy(r.o_small.at[chan, me], r.o_small.at[chan, me], 1, other, me).wait_send()
        each_small(lambda copy: copy.wait_send())
        for copy in first:
            copy.wait_send()

    own_lanes = pl.ds(pl.multiple_of(chan * half, half), half)
    sent, done, begun, written = [], [], [], set()
    received = (r.rs1, r.rs2, r.rs3)
    sent, done, arrived, pending = [], [], [], {}
    starts = dict(grad_in=0, grad_out=3 * half, up=4 * half, down=4 * half + hidden)
    slot_group = ["grad_in", "up", "grad_out", "down", "down"] + ["up"] * 3 + ["grad_out"] + ["grad_in"] * 3

    def half_of(axis, bit):
        return tuple(bit if name == axis else slice(None) for name in "hlyx")

    def fold_copy(layer, slot):
        axis = FOLD[layer][slot_group[slot]]
        theirs = half_of(axis, 1 - bits[axis])
        if slot < 2:
            source, target = r.turned.at[(slot, *theirs)], r.ut_p.at[layer, slot]
        elif slot == 2:
            source, target = r.mixed.at[layer], r.mixed_p.at[layer]
        elif slot == 3:
            source, target = r.g.at[layer], r.g_p.at[layer]
        elif slot in (4, 8):
            kind = 0 if slot == 4 else 1
            source, target = r.turned.at[(kind, *theirs)], r.gt_p.at[layer, kind]
        elif slot < 8:
            lanes = pl.ds((slot - 5) * (hidden // 3), hidden // 3)
            source, target = r.da.at[layer, :, lanes], r.da_p.at[layer, :, lanes]
        else:
            lanes = pl.ds((slot - 9) * half, half)
            source, target = r.gz.at[layer, :, lanes], r.gz_p.at[layer, :, lanes]
        return pltpu.make_async_remote_copy(
            src_ref=source,
            dst_ref=target,
            send_sem=r.fold_sem.at[0, layer, slot],
            recv_sem=r.fold_sem.at[1, layer, slot],
            device_id=peers[axis],
            device_id_type=MESH,
        )

    def turn(layer, slot, value, own):
        kind = slot if slot < 2 else (0 if slot == 4 else 1)
        if kind in pending:
            fold_copy(*pending[kind]).wait_send()
            sent.append(pending[kind])
        pending[kind] = (layer, slot)
        r.turned[kind] = value.astype(F32).T.astype(BF16).reshape(2, 2, 2, 2, width // 16, rows)
        axis = FOLD[layer][slot_group[slot]]
        own[layer, kind] = r.turned.at[(kind, *half_of(axis, bits[axis]))][...]
        fold_copy(layer, slot).start()

    def factors(chunk):
        layer, group, start, columns = CHUNKS[chunk][:4]
        lanes = pl.ds(start - starts[group], columns)
        i = (start - starts[group]) // columns
        if group == "down":
            return (3, 4), r.gt_own.at[layer, 0], r.gt_p.at[layer, 0], r.g.at[layer, :, lanes], r.g_p.at[layer, :, lanes]
        if group == "up":
            return (1, 5 + i), r.ut_own.at[layer, 1], r.ut_p.at[layer, 1], r.da.at[layer, :, lanes], r.da_p.at[layer, :, lanes]
        if group == "grad_out":
            return (2, 8), r.gt_own.at[layer, 1], r.gt_p.at[layer, 1], r.mixed.at[layer], r.mixed_p.at[layer]
        return (0, 9 + i), r.ut_own.at[layer, 0], r.ut_p.at[layer, 0], r.gz.at[layer, :, lanes], r.gz_p.at[layer, :, lanes]

    def rs_left(chunk, stage):
        layer, group, start, columns, order = CHUNKS[chunk]
        return [axis for axis in "hlyx" if axis != FOLD[layer][group] and axis not in order[:stage]]

    def rs_held(chunk, stage, index):
        layer, group, start, columns, order = CHUNKS[chunk]
        lanes = pl.ds(start, columns)
        if stage == 0:
            return r.big.at[(*index, slice(None), lanes)]
        return received[stage - 1].at[(layer, *index, slice(None), lanes)]

    def rs_copy(chunk, stage):
        layer, group, start, columns, order = CHUNKS[chunk]
        axis = order[stage]
        index = tuple(1 - bits[axis] if name == axis else slice(None) for name in rs_left(chunk, stage))
        rest = (slice(None),) * (3 - stage)
        return pltpu.make_async_remote_copy(
            src_ref=rs_held(chunk, stage, index),
            dst_ref=received[stage].at[(layer, *rest, pl.ds(start, columns))],
            send_sem=r.rs_sem.at[0, chunk, stage],
            recv_sem=r.rs_sem.at[1, chunk, stage],
            device_id=peers[axis],
            device_id_type=MESH,
        )

    def weight_grad(chunk):
        layer, group, start, columns, order = CHUNKS[chunk]
        slots, own, theirs, value, value_p = factors(chunk)
        for slot in slots:
            if (layer, slot) not in arrived:
                fold_copy(layer, slot).wait_recv()
                arrived.append((layer, slot))
        for other, spec in enumerate(CHUNKS):
            if spec[0] == layer + 1 and spec[2] == start:
                if (other, 1) not in done:
                    raise ValueError(chunk)
                rs_copy(other, 0).wait_send()
                sent.append((-1, other, 0))
        shape = (width // 2, rows)
        out = mm(own[...].reshape(shape), value[...]) + mm(theirs[...].reshape(shape), value_p[...])
        r.big[:, :, :, :, pl.ds(start, columns)] = out.astype(BF16).reshape(2, 2, 2, width // 16, columns)
        rs_copy(chunk, 0).start()

    def advance(chunk, step_of):
        layer, group, start, columns, order = CHUNKS[chunk]
        done.append((chunk, step_of))
        if step_of == 0:
            weight_grad(chunk)
            return
        stage = step_of - 1
        lanes = pl.ds(start, columns)
        rs_copy(chunk, stage).wait_recv()
        spot = rs_left(chunk, stage).index(order[stage])
        for flat in range(2 ** (2 - stage)):
            kept = [flat >> shift & 1 for shift in reversed(range(2 - stage))]
            mine = tuple(kept[:spot] + [bits[order[stage]]] + kept[spot:])
            total = rs_held(chunk, stage, mine)[...].astype(F32)
            there = received[stage].at[(layer, *kept, slice(None), lanes)]
            total = total + there[...].astype(F32)
            if stage == 2:
                r.o_big[layer, :, lanes] = total
            else:
                there[...] = total.astype(BF16)
        if stage < 2:
            rs_copy(chunk, stage + 1).start()

    def tick(layer, spot):
        now = TICKS * (layers - 1 - layer) + spot
        for chunk, stage in PLAN.get(now, ()):
            advance(chunk, stage)

    def short_all(layer):
        for k in range(3):
            for m in range(micro):
                short_part(layer, k, m, 0, span)

    def next_load(layer, name, slot):
        if 0 <= layer < layers:
            load(name, layer, slot).start()

    def seq_copy(send, recv, sems, other, outgoing):
        slot = seq if outgoing else other
        return pltpu.make_async_remote_copy(
            src_ref=getattr(r, send).at[other],
            dst_ref=getattr(r, recv).at[slot],
            send_sem=getattr(r, sems).at[0, other],
            recv_sem=getattr(r, sems).at[1, slot],
            device_id={"seq": other},
            device_id_type=MESH,
        )

    def all_others():
        return [lax.rem(seq + far, parts) for far in (4, 3, 5, 2, 6, 1, 7)]

    def wait_all(send, recv, sems):
        for other in all_others():
            seq_copy(send, recv, sems, other, False).wait_recv()
        for other in all_others():
            seq_copy(send, recv, sems, other, True).wait_send()

    def pair_copy(slot, m):
        return pltpu.make_async_remote_copy(
            src_ref=r.pair_send.at[slot, m],
            dst_ref=r.pair_recv.at[slot, m],
            send_sem=r.pair_sem.at[0, slot, m],
            recv_sem=r.pair_sem.at[1, slot, m],
            device_id={"chan": 1 - chan},
            device_id_type=MESH,
        )

    def rim_copy(way):
        other = lax.rem(seq + (1 if way == 0 else parts - 1), parts)
        return pltpu.make_async_remote_copy(
            src_ref=r.rim_send.at[way],
            dst_ref=r.rim_recv.at[way],
            send_sem=r.rim_sem.at[0, way],
            recv_sem=r.rim_sem.at[1, way],
            device_id={"seq": other},
            device_id_type=MESH,
        )

    def paired(slot, m, base, count):
        at = (slot, m, pl.ds(base, count), slice(None))
        return r.pair_send[at].astype(F32) + r.pair_recv[at].astype(F32)

    def row(name, index):
        return getattr(r, name)[pl.ds(index, 1), :]

    gains = [[row("vec", 2 * layer + n) for n in range(2)] for layer in range(layers)]
    biases = [[row("vec", 2 * layers + 2 * layer + n) for n in range(2)] for layer in range(layers)]
    branch_bias = [[row("vec", 4 * layers + layer), row("vec", 5 * layers + layer)] for layer in range(layers)]

    def norm_rows(at, x, layer, n):
        centred = x - jnp.mean(x, axis=1, keepdims=True)
        rstd = lax.rsqrt(jnp.mean(centred * centred, axis=1, keepdims=True) + EPS)
        scaled = centred * rstd
        r.xh[layer, n, at, :] = scaled
        r.rstd[layer, n, at, :] = rstd
        r.u[at, :] = (scaled * gains[layer][n] + biases[layer][n]).astype(BF16)

    def forward_rows(slot, bias, layer, n):
        for m in range(micro):
            pair_copy(slot, m).wait_recv()

            @pl.loop(0, span // step)
            def _(i):
                base = pl.multiple_of(i * step, step)
                at = pl.ds(m * span + base, step)
                x = r.x[at, :] + r.mask[at, :] * (paired(slot, m, base, step) + bias)
                r.x[at, :] = x
                if layer < layers:
                    norm_rows(at, x, layer, n)

        for m in range(micro):
            pair_copy(slot, m).wait_send()

    def send_partial(slot, make):
        for m in range(micro):
            r.pair_send[slot, m] = make(m).astype(BF16)
            pair_copy(slot, m).start()

    def tap(layer, k, j):
        return r.params[pl.ds(22 + 9 * layer + 3 * k + j, 1), :]

    def short_part(layer, k, m, low, high):
        z = r.z
        total = r.params[pl.ds(40 + 3 * layer + k, 1), :]
        for j in range(3):
            total = total + tap(layer, k, j) * z[layer, k, m, pl.ds(8 + low - j, high - low), :]
        r.s[k, m, pl.ds(low, high - low), :] = total

    def to_channels(m, value):
        turned = value.T.astype(BF16)
        for j in range(parts):
            r.a_send[j, pl.ds(m * block, block), :] = turned[j * block : (j + 1) * block]

    def start_channels():
        for other in all_others():
            seq_copy("a_send", "a_recv", "a_sem", other, True).start()
        r.a_recv[seq] = r.a_send[seq]

    def gathered():
        return jnp.concatenate([r.a_recv[j] for j in range(parts)], axis=1)

    def from_channels(m):
        stack = [r.b_recv[j, pl.ds(m * block, block), :].astype(F32) for j in range(parts)]
        return jnp.concatenate(stack, axis=0).T

    def inverse_and_send(signal):
        for far in (2, 1, 3, 0):
            at = lax.rem(seq // 2 + far, parts // 2)
            lanes = pl.ds(pl.multiple_of(at * 2 * span, 2 * span), 2 * span)
            out = mm(r.spec[0], r.cos_v[:, lanes]) + mm(r.spec[1], r.sin_v[:, lanes])
            out = (out + r.skip_v[...] * signal[:, lanes].astype(F32)).astype(BF16)
            for h in range(2):
                r.b_send[2 * at + h] = out[:, h * span : (h + 1) * span]
            if far:
                for h in range(2):
                    seq_copy("b_send", "b_recv", "b_sem", 2 * at + h, True).start()
            else:
                seq_copy("b_send", "b_recv", "b_sem", pair, True).start()
                r.b_recv[seq] = r.b_send[seq]

    first[1].wait_recv()
    for base in range(0, rows, step):
        at = pl.ds(base, step)
        x = jnp.concatenate([r.both[0, 0, at, :], r.both[1, 0, at, :]], axis=1).astype(F32)
        r.x[at, :] = x
        norm_rows(at, x, 0, 0)

    for layer in range(layers):
        load("win", layer, 0).wait()
        for k in range(3):
            z = mm(r.u[...], r.win_v[k]) + r.params[pl.ds(16 + 3 * layer + k, 1), :]
            for m in range(micro):
                r.z[layer, k, m, pl.ds(8, span), :] = z[m * span : (m + 1) * span]
                r.rim_send[0, pl.ds(k * 4 + m * 2, 2), :] = z[(m + 1) * span - 2 : (m + 1) * span]
        rim_copy(0).start()
        next_load(layer + 1, "win", 0)
        turn(layer, 0, r.u[...], r.ut_own)
        for k in range(3):
            for m in range(micro):
                short_part(layer, k, m, step, span)
        rim_copy(0).wait()
        inner = (seq > 0).astype(F32)
        for k in range(3):
            for m in range(micro):
                r.z[layer, k, m, pl.ds(6, 2), :] = inner * r.rim_recv[0, pl.ds(k * 4 + m * 2, 2), :]
                short_part(layer, k, m, 0, step)
        for m in range(micro):
            to_channels(m, r.s[1, m] * r.s[2, m])
        start_channels()
        if layer == 0:
            for copy in table_loads:
                copy.wait()
            filter_forward(0)
        wait_all("a_send", "a_recv", "a_sem")
        signal = gathered()
        r.sig[layer] = signal
        r.skip_v[...] = r.skip_l[layer]
        for c in range(0, length, 256):
            lanes = pl.ds(c, 256)
            pc, ps = mm(signal, r.cos_v[:, lanes]), mm(signal, r.sin_v[:, lanes])
            fr, fi = twice(r.fr[layer, :, lanes]), twice(r.fi[layer, :, lanes])
            r.pc[layer, :, lanes], r.ps[layer, :, lanes] = pc.astype(BF16), ps.astype(BF16)
            r.spec[0, :, lanes] = (pc * fr + ps * fi).astype(BF16)
            r.spec[1, :, lanes] = (ps * fr - pc * fi).astype(BF16)
        inverse_and_send(r.sig.at[layer])
        if layer + 1 < layers:
            filter_forward(layer + 1)
        load("wout", layer, 1).wait()
        wait_all("b_send", "b_recv", "b_sem")
        for m in range(micro):
            y = from_channels(m)
            r.y[layer, m] = y.astype(BF16)
            r.mixed[layer, pl.ds(m * span, span), :] = (r.s[0, m] * y).astype(BF16)
        send_partial(0, lambda m: mm(r.mixed[layer, pl.ds(m * span, span), :], r.wout_v[...]))
        next_load(layer + 1, "wout", 1)
        fold_copy(layer, 2).start()
        forward_rows(0, branch_bias[layer][0], layer, 1)

        load("wup", layer, 2).wait()
        for c in range(0, hidden, 256):
            lanes = pl.ds(c, 256)
            for m in range(micro):
                at = pl.ds(m * span, span)
                a = mm(r.u[at, :], r.wup_v[:, lanes]) + r.up_b[pl.ds(layer, 1), lanes]
                cdf = 0.5 + 0.5 * lax.erf(a * math.sqrt(0.5))
                pdf = jnp.exp(-0.5 * a * a) * (1.0 / math.sqrt(2.0 * math.pi))
                r.g[layer, at, lanes] = (a * cdf).astype(BF16)
                r.slope[layer, at, lanes] = (cdf + a * pdf).astype(BF16)
        next_load(layer + 1, "wup", 2)
        load("wdown", layer, 3).wait()
        send_partial(1, lambda m: mm(r.g[layer, pl.ds(m * span, span), :], r.wdown_v[...]))
        next_load(layer + 1, "wdown", 3)
        fold_copy(layer, 3).start()
        turn(layer, 1, r.u[...], r.ut_own)
        forward_rows(1, branch_bias[layer][1], layer + 1, 0)

    r.out_act[...] = r.x[:, own_lanes]

    def branch_rows(at, dx):
        branch = r.mask[at, :] * dx
        r.grad[at, :] = branch.astype(BF16)
        return jnp.sum(branch.reshape(step // 8, 8, width), axis=0)

    def put768(layer, index, value):
        r.o768[pl.ds(8 * layer + index, 1), :] = jnp.sum(value, axis=0, keepdims=True)

    first[2].wait_recv()
    total = jnp.zeros((8, width), F32)
    for base in range(0, rows, step):
        at = pl.ds(base, step)
        dx = jnp.concatenate([r.both[0, 1, at, :], r.both[1, 1, at, :]], axis=1).astype(F32)
        r.x[at, :] = dx
        total = total + branch_rows(at, dx)
    put768(layers - 1, 5, total)

    def backward_rows(slot, layer, n):
        gain = gains[layer][n]
        sums = [jnp.zeros((8, width), F32)] * 3
        for m in range(micro):
            pair_copy(slot, m).wait_recv()

            def body(i, carry):
                base = pl.multiple_of(i * step, step)
                at = pl.ds(m * span + base, step)
                du = paired(slot, m, base, step)
                scaled = r.xh[layer, n, at, :]
                weighted = du * gain
                back = r.rstd[layer, n, at, :] * (
                    weighted
                    - jnp.mean(weighted, axis=1, keepdims=True)
                    - scaled * jnp.mean(weighted * scaled, axis=1, keepdims=True)
                )
                dx = r.x[at, :] + back
                r.x[at, :] = dx
                shape = (step // 8, 8, width)
                return [
                    carry[0] + jnp.sum((du * scaled).reshape(shape), axis=0),
                    carry[1] + jnp.sum(du.reshape(shape), axis=0),
                    carry[2] + branch_rows(at, dx),
                ]

            sums = lax.fori_loop(0, span // step, body, sums)
        for m in range(micro):
            pair_copy(slot, m).wait_send()
        put768(layer, n, sums[0])
        put768(layer, 2 + n, sums[1])
        if n == 1:
            put768(layer, 4, sums[2])
        elif layer > 0:
            put768(layer - 1, 5, sums[2])

    for layer in reversed(range(layers)):
        last = layer == layers - 1
        if not last:
            load("wdown", layer, 3).wait()
        for c in range(0, hidden, 256):
            lanes = pl.ds(c, 256)
            da = mm_nt(r.grad[...], r.wdown_v[lanes, :]) * r.slope[layer, :, lanes].astype(F32)
            r.o_up[pl.ds(layer, 1), lanes] = jnp.sum(da, axis=0, keepdims=True)
            r.da[layer, :, lanes] = da.astype(BF16)
            if c % 512 == 256:
                fold_copy(layer, 5 + c // 512).start()
        next_load(layer - 1, "wdown", 3)
        if not last:
            load("wup", layer, 2).wait()
        send_partial(0, lambda m: mm_nt(r.da[layer, pl.ds(m * span, span), :], r.wup_v[...]))
        next_load(layer - 1, "wup", 2)
        tick(layer, 0)
        turn(layer, 4, r.grad[...], r.gt_own)
        tick(layer, 1)
        if not last:
            short_all(layer)
        tick(layer, 2)
        backward_rows(0, layer, 1)
        tick(layer, 3)
        if not last:
            load("wout", layer, 1).wait()

        for m in range(micro):
            dmixed = mm_nt(r.grad[pl.ds(m * span, span), :], r.wout_v[...])
            to_channels(m, dmixed * r.s[0, m])
            r.ds[0, m, pl.ds(0, span), :] = dmixed * r.y[layer, m].astype(F32)
        start_channels()
        next_load(layer - 1, "wout", 1)
        tick(layer, 4)
        turn(layer, 8, r.grad[...], r.gt_own)
        tick(layer, 5)
        wait_all("a_send", "a_recv", "a_sem")
        tick(layer, 6)
        signal = gathered()
        r.dsig[...] = signal
        r.skip_v[...] = r.skip_l[layer]
        for c in range(0, length, 256):
            lanes = pl.ds(c, 256)
            gc, gs = mm(signal, r.cos_v[:, lanes]), mm(signal, r.sin_v[:, lanes])
            fr, fi = twice(r.fr[layer, :, lanes]), twice(r.fi[layer, :, lanes])
            r.gc[:, lanes], r.gs[:, lanes] = gc.astype(BF16), gs.astype(BF16)
            r.spec[0, :, lanes] = (gc * fr - gs * fi).astype(BF16)
            r.spec[1, :, lanes] = (gs * fr + gc * fi).astype(BF16)
        inverse_and_send(r.dsig)
        tick(layer, 7)
        both_skip = jnp.sum(r.dsig[...].astype(F32) * r.sig[layer].astype(F32), axis=1, keepdims=True)
        r.gskip[layer] = sum(both_skip[m * block : (m + 1) * block] for m in range(micro))
        for c in range(0, length, 256):
            lanes = pl.ds(c, 256)
            gc, gs = r.gc[:, lanes].astype(F32), r.gs[:, lanes].astype(F32)
            pc, ps = r.pc[layer, :, lanes].astype(F32), r.ps[layer, :, lanes].astype(F32)
            re, im = gc * pc + gs * ps, gc * ps - gs * pc
            re = sum(re[m * block : (m + 1) * block] for m in range(micro)) * (1.0 / length)
            im = sum(im[m * block : (m + 1) * block] for m in range(micro)) * (1.0 / length)
            tc, ts = r.turn[pl.ds(0, 1), lanes], r.turn[pl.ds(1, 1), lanes]
            for which, value in enumerate((re * tc + im * ts, re * ts - im * tc)):
                high = value.astype(BF16)
                r.spec[which, pl.ds(0, block), lanes] = high
                r.spec[which, pl.ds(block, block), lanes] = (value - high.astype(F32)).astype(BF16)
        for c in range(0, length, 256):
            lanes = pl.ds(c, 256)
            out = mm(r.spec[0], r.cos_v[:, lanes]) + mm(r.spec[1], r.sin_v[:, lanes])
            r.o_filt[layer, :, lanes] = out[:block] + out[block:]
        filter_backward(layer)
        tick(layer, 8)
        wait_all("b_send", "b_recv", "b_sem")
        for m in range(micro):
            dp = from_channels(m)
            for k in (1, 2):
                value = dp * r.s[3 - k, m]
                r.ds[k, m, pl.ds(0, span), :] = value
            for k in range(3):
                r.rim_send[1, pl.ds(k * 4 + m * 2, 2), :] = r.ds[k, m, pl.ds(0, 2), :]
        rim_copy(1).start()
        for k in range(3):
            sums = [0.0] * 4
            for m in range(micro):
                ds = r.ds[k, m, pl.ds(0, span), :]
                sums[3] = sums[3] + jnp.sum(ds, axis=0, keepdims=True)
                for j in range(3):
                    z = r.z[layer, k, m, pl.ds(8 - j, span), :]
                    sums[j] = sums[j] + jnp.sum(ds * z, axis=0, keepdims=True)
            for j in range(3):
                r.vecs[pl.ds(32 * layer + 11 + 3 * k + j, 1), :] = sums[j]
            r.vecs[pl.ds(32 * layer + 20 + k, 1), :] = sums[3]
        tick(layer, 9)
        rim_copy(1).wait()
        inner = (seq < parts - 1).astype(F32)
        for k in range(3):
            total = 0.0
            for m in range(micro):
                r.ds[k, m, pl.ds(span, 2), :] = inner * r.rim_recv[1, pl.ds(k * 4 + m * 2, 2), :]
                dz = 0.0
                for j in range(3):
                    dz = dz + tap(layer, k, j) * r.ds[k, m, pl.ds(j, span), :]
                total = total + jnp.sum(dz, axis=0, keepdims=True)
                r.gz[layer, pl.ds(m * span, span), pl.ds(k * half, half)] = dz.astype(BF16)
            r.vecs[pl.ds(32 * layer + 8 + k, 1), :] = total
            fold_copy(layer, 9 + k).start()
        if not last:
            load("win", layer, 0).wait()
        send_partial(
            1, lambda m: sum(mm_nt(r.gz[layer, pl.ds(m * span, span), pl.ds(k * half, half)], r.win_v[k]) for k in range(3))
        )
        next_load(layer - 1, "win", 0)
        tick(layer, 10)
        tick(layer, 11)
        backward_rows(1, layer, 0)
        tick(layer, 12)
    r.grad_tokens[...] = r.x[:, own_lanes]
    small_begin()
    for count, (chunk, stage) in enumerate(PLAN[TICKS * layers]):
        advance(chunk, stage)
        if count == SMALL[0]:
            small_middle()
        if count == SMALL[1]:
            small_last()
    small_end()
    for chunk in range(len(CHUNKS)):
        for stage in range(3):
            if (-1, chunk, stage) not in sent:
                rs_copy(chunk, stage).wait_send()
    for layer in range(layers):
        for slot in range(len(slot_group)):
            if (layer, slot) not in sent:
                fold_copy(layer, slot).wait_send()


def chain(inputs, sizes):
    layers, micro, span, half, hidden, feat, freq_lane = sizes
    width, rows, parts = 2 * half, micro * span, 8
    block, length = half // parts, span * parts
    lanes = micro * block
    columns = 4 * half + 2 * hidden
    in_any = ("win", "wout", "wup", "wdown", "cos", "sin")
    outs = dict(
        out_act=((rows, half), F32),
        grad_tokens=((rows, half), F32),
        o_big=((layers, width // 16, 4 * half + 2 * hidden), F32),
        o_small=((2, 2 * parts, block, 128), BF16),
    )
    dma, vm = pltpu.SemaphoreType.DMA, pltpu.VMEM
    scratch = dict(
        big=vm((2, 2, 2, width // 16, columns), BF16),
        rs1=vm((layers, 2, 2, width // 16, columns), BF16),
        rs2=vm((layers, 2, width // 16, columns), BF16),
        rs3=vm((layers, width // 16, columns), BF16),
        rs_sem=dma((2, len(CHUNKS), 3)),
        fold_sem=dma((2, layers, 12)),
        ut_own=vm((layers, 2, 2, 2, 2, width // 16, rows), BF16),
        ut_p=vm((layers, 2, 2, 2, 2, width // 16, rows), BF16),
        gt_own=vm((layers, 2, 2, 2, 2, width // 16, rows), BF16),
        gt_p=vm((layers, 2, 2, 2, 2, width // 16, rows), BF16),
        mixed_p=vm((layers, rows, half), BF16),
        g_p=vm((layers, rows, hidden), BF16),
        da_p=vm((layers, rows, hidden), BF16),
        gz=vm((layers, rows, 3 * half), BF16),
        gz_p=vm((layers, rows, 3 * half), BF16),
        win_v=vm((3, width, half), BF16),
        wout_v=vm((half, width), BF16),
        wup_v=vm((width, hidden), BF16),
        wdown_v=vm((hidden, width), BF16),
        cos_v=vm((length, length), BF16),
        sin_v=vm((length, length), BF16),
        skip_v=vm((lanes, 1), F32),
        skip_l=vm((layers, lanes, 1), F32),
        gskip=vm((layers, block, 1), F32),
        vec2=vm((2, 16, half), F32),
        vec=vm((16, width), F32),
        params=vm((48, half), F32),
        pack_t=vm((128, feat), F32),
        chan_t=vm((128, half), F32),
        pack=vm((layers, feat, 128), F32),
        chv=vm((layers, block, 128), F32),
        chv_t=vm((half, 128), F32),
        both=vm((2, 2, rows, half), BF16),
        mask=vm((rows, 1), F32),
        inner=vm((layers, feat, length), F32),
        wave=vm((layers * feat, length), F32),
        fr=vm((layers, block, length), F32),
        fi=vm((layers, block, length), F32),
        spread=vm((layers, feat, 128), F32),
        o_filt=vm((layers, block, length), F32),
        o768=vm((8 * layers, width), F32),
        o_up=vm((layers, hidden), F32),
        vecs=vm((128, half), F32),
        sm=vm((2 * parts, block, 128), F32),
        sm_b=vm((2 * parts, block, 128), BF16),
        sm_recv=vm((2 * parts, block, 128), BF16),
        sm_sem=dma((2, 2, 2 * parts)),
        core_sem=dma((2, 4)),
        x=vm((rows, width), F32),
        xh=vm((layers, 2, rows, width), F32),
        rstd=vm((layers, 2, rows, 1), F32),
        u=vm((rows, width), BF16),
        z=vm((layers, 3, micro, span + 8, half), F32),
        s=vm((3, micro, span, half), F32),
        y=vm((layers, micro, span, half), BF16),
        mixed=vm((layers, rows, half), BF16),
        sig=vm((layers, lanes, length), BF16),
        dsig=vm((lanes, length), BF16),
        pc=vm((layers, lanes, length), BF16),
        ps=vm((layers, lanes, length), BF16),
        gc=vm((lanes, length), BF16),
        gs=vm((lanes, length), BF16),
        spec=vm((2, lanes, length), BF16),
        slope=vm((layers, rows, hidden), BF16),
        g=vm((layers, rows, hidden), BF16),
        da=vm((layers, rows, hidden), BF16),
        grad=vm((rows, width), BF16),
        turned=vm((2, 2, 2, 2, 2, width // 16, rows), BF16),
        ds=vm((3, micro, span + 8, half), F32),
        a_send=vm((parts, lanes, span), BF16),
        a_recv=vm((parts, lanes, span), BF16),
        b_send=vm((parts, lanes, span), BF16),
        b_recv=vm((parts, lanes, span), BF16),
        pair_send=vm((2, micro, span, width), BF16),
        pair_recv=vm((2, micro, span, width), BF16),
        rim_send=vm((2, 16, half), F32),
        rim_recv=vm((2, 16, half), F32),
        w_sem=dma((4,)),
        t_sem=dma((2,)),
        a_sem=dma((2, parts)),
        b_sem=dma((2, parts)),
        pair_sem=dma((2, 2, micro)),
        rim_sem=dma((2, 2)),
    )
    names = [*inputs, *outs, *scratch]
    results = pl.pallas_call(
        functools.partial(chain_kernel, sizes, names),
        out_shape=[jax.ShapeDtypeStruct(*spec) for spec in outs.values()],
        in_specs=[
            pl.BlockSpec(memory_space=pl.ANY if name in in_any else pltpu.SMEM if name == "lens" else pltpu.VMEM)
            for name in inputs
        ],
        out_specs=[pl.BlockSpec(memory_space=pltpu.VMEM) for _ in outs],
        scratch_shapes=list(scratch.values()),
        compiler_params=pltpu.CompilerParams(
            collective_id=3, has_side_effects=True, vmem_limit_bytes=61 << 20
        ),
        name="chain",
    )(*inputs.values())
    return types.SimpleNamespace(**dict(zip(outs, results)))


def embedding(count, bands, feat):
    steps = np.arange(count, dtype=np.float32) / np.float32(count)
    number = (bands - 1) // 2
    freq = np.linspace(0.0001, number - 1, number).astype(np.float32)
    phases = (np.float32(2.0 * math.pi) * steps)[None, :] * freq[:, None]
    table = np.zeros((128, count), np.float32)
    table[feat] = steps
    table[feat + 1 : feat + 1 + number] = np.cos(phases)
    table[feat + 1 + number : feat + bands] = -np.sin(phases)
    table[feat + bands] = 1.0
    return table


def finish_kernel(sizes, names, *refs):
    layers, micro, span, half, hidden, feat, bands = sizes
    r = types.SimpleNamespace(**dict(zip(names, refs)))
    wide = hidden // half
    for m in range(micro):
        r.act[m, 0] = r.out_act[pl.ds(m * span, span), :]
        r.tokens[m, 0] = r.grad_tokens[pl.ds(m * span, span), :]
    for c in range(2):
        for piece in range(2):
            value = r.o_small[c, pl.ds(8 * piece, 8)].astype(F32).reshape(half, 128)
            r.turned[c, piece] = value.T
    for layer in range(layers):
        for k in range(3):
            r.g_in[layer, k] = r.o_big[layer, :, pl.ds(k * half, half)]
        r.g_out[layer] = r.o_big[layer, :, pl.ds(3 * half, half)]
        r.g_up[layer] = r.o_big[layer, :, pl.ds(4 * half, hidden)]
        r.g_down[layer] = r.o_big[layer, :, pl.ds(4 * half + hidden, hidden)]
        net = sum(r.turned[c, 1, pl.ds(feat, feat), pl.ds(layer * feat, feat)] for c in range(2))
        for i in range(bands):
            r.fin[i, pl.ds(layer, 1), :] = net[i : i + 1]
        r.fbias[pl.ds(layer, 1), :] = net[bands : bands + 1]
        r.ffreq[pl.ds(layer, 1), :] = net[bands + 1 : bands + 2]
        for c in range(2):
            lanes = pl.ds(c * half, half)
            base = 32 * layer

            def row(index, c=c):
                return r.turned[c, 1, pl.ds(index, 1), :]

            for n in range(2):
                r.gain[layer, pl.ds(n, 1), lanes] = row(base + n)
                r.bias[layer, pl.ds(n, 1), lanes] = row(base + 2 + n)
            at = pl.ds(layer, 1)
            r.out_b[at, lanes] = row(base + 4)
            r.down_b[at, lanes] = row(base + 5)
            r.skip[at, lanes] = row(112 + layer)
            for k in range(3):
                r.in_b[k, at, lanes] = row(base + 8 + k)
                r.short_b[k, at, lanes] = row(base + 20 + k)
                for j in range(3):
                    r.taps[k, j, at, lanes] = row(base + 11 + 3 * k + j)
            for i in range(wide):
                r.up_b[at, pl.ds(c * hidden + i * half, half)] = row(base + 24 + i)
            r.fout[layer, :, lanes] = r.turned[c, 0, pl.ds(layer * feat, feat), :]


def finish(out, sizes):
    layers, micro, span, half, hidden, feat, bands = sizes
    width, own = 2 * half, 2 * half // 16
    inputs = dict(out_act=out.out_act, grad_tokens=out.grad_tokens, o_big=out.o_big, o_small=out.o_small)
    outs = dict(
        act=(micro, 1, span, half),
        tokens=(micro, 1, span, half),
        g_in=(layers, 3, own, half),
        g_out=(layers, own, half),
        g_up=(layers, own, hidden),
        g_down=(layers, own, hidden),
        gain=(layers, 2, width),
        bias=(layers, 2, width),
        in_b=(3, layers, width),
        taps=(3, 3, layers, width),
        short_b=(3, layers, width),
        skip=(layers, width),
        out_b=(layers, width),
        up_b=(layers, 2 * hidden),
        down_b=(layers, width),
        fin=(bands, layers, feat),
        fbias=(layers, feat),
        ffreq=(layers, feat),
        fout=(layers, feat, width),
    )
    names = [*inputs, *outs, "turned"]
    results = pl.pallas_call(
        functools.partial(finish_kernel, sizes, names),
        out_shape=[jax.ShapeDtypeStruct(shape, F32) for shape in outs.values()],
        in_specs=[pl.BlockSpec(memory_space=pltpu.VMEM) for _ in inputs],
        out_specs=[pl.BlockSpec(memory_space=pltpu.VMEM) for _ in outs],
        scratch_shapes=[pltpu.VMEM((2, 2, 128, half), F32)],
        name="finish",
    )(*inputs.values())
    turns = dict(
        g_out=(0, 2, 1),
        g_down=(0, 2, 1),
        in_b=(1, 0, 2),
        taps=(2, 0, 1, 3),
        short_b=(1, 0, 2),
        fin=(1, 0, 2),
    )
    return tuple(
        value.transpose(turns[name]) if name in turns else value for name, value in zip(outs, results)
    )


def local_fast(
    tokens,
    lengths,
    cotangent,
    norm_gain,
    norm_bias,
    in_weight,
    in_bias,
    short_taps,
    short_bias,
    skip_gain,
    out_weight,
    out_bias,
    up_weight,
    up_bias,
    down_weight,
    down_bias,
    filter_in,
    filter_bias,
    filter_freq,
    filter_out,
    decay_rate,
):
    micro, rows_dev, half = tokens.shape[0], tokens.shape[2], tokens.shape[3]
    layers, bands, feat = filter_in.shape
    hidden = up_weight.shape[2]
    length = rows_dev * lax.axis_size("seq")
    freq_lane = feat + bands + 1
    cos_np, sin_np, turn_c, turn_s = half_tables(length)
    inputs = dict(
        tok=tokens.reshape(micro * rows_dev, half),
        cot=cotangent.reshape(micro * rows_dev, half),
        lens=lengths.T,
        gain=norm_gain,
        bias=norm_bias,
        out_b=out_bias,
        down_b=down_bias,
        in_b=in_bias.transpose(1, 0, 2),
        taps=short_taps.transpose(1, 2, 0, 3),
        short_b=short_bias.transpose(1, 0, 2),
        up_b=up_bias,
        fin=filter_in.transpose(1, 0, 2),
        fbias=filter_bias,
        ffreq=filter_freq,
        fout=filter_out,
        decay=decay_rate,
        skip=skip_gain,
        emb=jnp.asarray(embedding(length, bands, feat)),
        turn=jnp.asarray(np.concatenate([turn_c, turn_s], axis=1).T, F32),
        win=in_weight,
        wout=out_weight,
        wup=up_weight,
        wdown=down_weight,
        cos=jnp.asarray(cos_np, BF16),
        sin=jnp.asarray(sin_np, BF16),
    )
    out = chain(inputs, (layers, micro, rows_dev, half, hidden, feat, freq_lane))
    return finish(out, (layers, micro, rows_dev, half, hidden, feat, bands))


def solution(mesh):
    in_specs = (
        P(None, "dp", "seq", "chan"),
        P(None, "dp"),
        P(None, "dp", "seq", "chan"),
        P(None, None, "chan"),
        P(None, None, "chan"),
        P(None, None, None, "chan"),
        P(None, None, "chan"),
        P(None, None, None, "chan"),
        P(None, None, "chan"),
        P(None, "chan"),
        P(None, "chan", None),
        P(None, "chan"),
        P(None, None, "chan"),
        P(None, "chan"),
        P(None, "chan", None),
        P(None, "chan"),
        P(),
        P(),
        P(),
        P(None, None, "chan"),
        P(None, "chan"),
    )
    out_specs = (
        P(None, "dp", "seq", "chan"),
        P(None, "dp", "seq", "chan"),
        P(None, None, ("seq", "dp"), "chan"),
        P(None, "chan", ("seq", "dp")),
        P(None, ("seq", "dp"), "chan"),
        P(None, "chan", ("seq", "dp")),
        P(),
        P(),
        P(),
        P(),
        P(),
        P(),
        P(),
        P(),
        P(),
        P(),
        P(),
        P(),
        P(),
    )
    def entry(*args):
        fits = args[0].shape[2] * mesh.shape["seq"] <= 2048 and mesh.shape["seq"] == 8 and mesh.shape["dp"] == 2
        return (local_fast if fits else local)(*args)

    return jax.shard_map(entry, mesh=mesh, in_specs=in_specs, out_specs=out_specs, check_vma=False)
```

```python
import functools
import math
import types

import jax
import jax.numpy as jnp
import numpy as np
from jax import lax
from jax.experimental import pallas as pl
from jax.experimental.pallas import tpu as pltpu
from jax.sharding import PartitionSpec as P

EPS = 1e-05
HIGH = lax.Precision.HIGHEST


def shifted(value, axis, steps):
    count = lax.axis_size(axis)
    initial, last = (max(0, -steps), min(count, count - steps))
    return lax.ppermute(value, axis, [(source, source + steps) for source in range(initial, last)])


def positions(seq_length, emb_width):
    band_count = (emb_width - 1) // 2
    step_ids = jnp.arange(seq_length, dtype=jnp.float32)
    steps_norm = step_ids / seq_length
    band_freq = jnp.linspace(0.0001, band_count - 1, band_count).astype(jnp.float32)
    phases = 2.0 * math.pi * steps_norm[:, None] * band_freq[None, :]
    table = jnp.concatenate([steps_norm[:, None], jnp.cos(phases), -jnp.sin(phases)], axis=1)
    return (table, steps_norm)


def angle_table(row_count, col_count, modulus):
    product = (
        jnp.arange(row_count, dtype=jnp.int32)[:, None]
        * jnp.arange(col_count, dtype=jnp.int32)[None, :]
        % modulus
    )
    theta = product.astype(jnp.float32) * (2.0 * math.pi / modulus)
    return (jnp.cos(theta), jnp.sin(theta))


def split_length(total_length):
    lesser = 2
    for candidate in range(2, math.isqrt(total_length) + 1, 2):
        if total_length % candidate == 0:
            lesser = candidate
    return (lesser, total_length // lesser)


def dft_basis(seq_length):
    padded_len = 2 * seq_length
    lesser, greater = split_length(padded_len)
    cos_p, sin_p = angle_table(lesser, lesser, lesser)
    cos_q, sin_q = angle_table(greater, greater, greater)
    twist_c, twist_s = angle_table(lesser, greater, padded_len)
    return (cos_p, sin_p, cos_q, sin_q, twist_c, twist_s)


def right_mul(left, table):
    return jnp.einsum("ckb,bj->ckj", left, table, precision=HIGH)


def to_spectrum(signal, basis):
    cos_p, sin_p, cos_q, sin_q, twist_c, twist_s = basis
    half = cos_p.shape[0] // 2
    blocks = signal.reshape(signal.shape[0], half, cos_q.shape[0])
    first_re = jnp.einsum("ka,cab->ckb", cos_p[:, :half], blocks, precision=HIGH)
    first_im = -jnp.einsum("ka,cab->ckb", sin_p[:, :half], blocks, precision=HIGH)
    turned_re = first_re * twist_c + first_im * twist_s
    turned_im = first_im * twist_c - first_re * twist_s
    spec_re = right_mul(turned_re, cos_q) + right_mul(turned_im, sin_q)
    spec_im = right_mul(turned_im, cos_q) - right_mul(turned_re, sin_q)
    return (spec_re, spec_im)


def from_spectrum(spec_re, spec_im, basis):
    cos_p, sin_p, cos_q, sin_q, twist_c, twist_s = basis
    half = cos_p.shape[0] // 2
    back_re = right_mul(spec_re, cos_q) - right_mul(spec_im, sin_q)
    back_im = right_mul(spec_im, cos_q) + right_mul(spec_re, sin_q)
    turned_re = back_re * twist_c - back_im * twist_s
    turned_im = back_im * twist_c + back_re * twist_s
    signal = jnp.einsum("ak,ckb->cab", cos_p[:half], turned_re, precision=HIGH) - jnp.einsum(
        "ak,ckb->cab", sin_p[:half], turned_im, precision=HIGH
    )
    return signal.reshape(signal.shape[0], half * cos_q.shape[0]) / (
        cos_p.shape[0] * cos_q.shape[0]
    )


def complex_mul(left_re, left_im, right_re, right_im):
    return (left_re * right_re - left_im * right_im, left_re * right_im + left_im * right_re)


def filter_block(table, steps_norm, weight_in, bias_in, freq_in, cols_in, decay_cols):
    hidden = jnp.sin(freq_in * (jnp.dot(table, weight_in, precision=HIGH) + bias_in))
    raw = jnp.einsum("lf,fc->cl", hidden, cols_in, precision=HIGH)
    return raw * jnp.exp(-decay_cols[:, None] * steps_norm[None, :])


def to_channels(block):
    parts = lax.axis_size("seq")
    shaped = block.reshape(parts, block.shape[0] // parts, block.shape[1])
    moved = lax.all_to_all(
        shaped.astype(jnp.bfloat16), "seq", split_axis=0, concat_axis=2, tiled=True
    ).astype(shaped.dtype)
    return moved.reshape(moved.shape[1], moved.shape[2])


def to_positions(block):
    shaped = block.reshape(1, block.shape[0], block.shape[1])
    moved = lax.all_to_all(
        shaped.astype(jnp.bfloat16), "seq", split_axis=2, concat_axis=0, tiled=True
    ).astype(shaped.dtype)
    return moved.reshape(moved.shape[0] * moved.shape[1], moved.shape[2])


def branch_sum(partial_value):
    return lax.psum_scatter(
        partial_value.astype(jnp.bfloat16), "chan", scatter_dimension=1, tiled=True
    ).astype(jnp.float32)


def branch_grad(grad_low):
    return lax.all_gather(grad_low, "chan", axis=1, tiled=True)


def place(values, start, full_width, axis):
    full_shape = list(values.shape)
    full_shape[axis] = full_width
    return lax.dynamic_update_slice_in_dim(jnp.zeros(full_shape, jnp.float32), values, start, axis)


def local(
    tokens,
    lengths,
    cotangent,
    norm_gain,
    norm_bias,
    in_weight,
    in_bias,
    short_taps,
    short_bias,
    skip_gain,
    out_weight,
    out_bias,
    up_weight,
    up_bias,
    down_weight,
    down_bias,
    filter_in,
    filter_bias,
    filter_freq,
    filter_out,
    decay_rate,
):
    micro_count = tokens.shape[0]
    rows_dev = tokens.shape[2]
    chan_width = tokens.shape[3]
    layer_count = norm_gain.shape[0]
    hidden_width = up_weight.shape[2]
    seq_parts = lax.axis_size("seq")
    chan_parts = lax.axis_size("chan")
    full_width = chan_width * chan_parts
    seq_length = rows_dev * seq_parts
    seq_index = lax.axis_index("seq")
    chan_index = lax.axis_index("chan")
    block_width = chan_width // seq_parts
    col_start = seq_index * block_width
    chan_start = chan_index * chan_width
    basis = dft_basis(seq_length)
    table, steps_norm = positions(seq_length, filter_in.shape[1])
    positions_dev = seq_index * rows_dev + jnp.arange(rows_dev, dtype=jnp.int32)
    filters = []
    for layer_index in range(layer_count):
        filter_cols = lax.dynamic_slice_in_dim(filter_out[layer_index], col_start, block_width, 1)
        decay_cols = lax.dynamic_slice_in_dim(decay_rate[layer_index], col_start, block_width, 0)
        skip_cols = lax.dynamic_slice_in_dim(skip_gain[layer_index], col_start, block_width, 0)

        def make_one(weight_in, bias_in, freq_in, cols_in, decay_cols=decay_cols):
            return filter_block(table, steps_norm, weight_in, bias_in, freq_in, cols_in, decay_cols)

        long_filter, filter_pull = jax.vjp(
            make_one,
            filter_in[layer_index],
            filter_bias[layer_index],
            filter_freq[layer_index],
            filter_cols,
        )
        filt_re, filt_im = to_spectrum(long_filter, basis)
        filters.append((filt_re, filt_im, filter_pull, skip_cols))

    def norm_forward(resid, gain_bias):
        full_rows, full_gb = (
            lax.all_gather(resid, "chan", axis=1, tiled=True),
            lax.all_gather(gain_bias, "chan", axis=1, tiled=True),
        )
        mean_row = jnp.mean(full_rows, axis=1, keepdims=True)
        centred = full_rows - mean_row
        rstd = lax.rsqrt(jnp.mean(centred * centred, axis=1, keepdims=True) + EPS)
        scaled = centred * rstd
        normed = (scaled * full_gb[0] + full_gb[1]).astype(jnp.bfloat16)
        return (normed, (scaled, rstd, full_gb[0]))

    def norm_backward(grad_partial, norm_saved):
        scaled, rstd, gain_row = norm_saved
        grad_rows = lax.psum(grad_partial.astype(jnp.bfloat16), "chan").astype(jnp.float32)
        grad_scaled = grad_rows * gain_row
        grad_full = rstd * (
            grad_scaled
            - jnp.mean(grad_scaled, axis=1, keepdims=True)
            - scaled * jnp.mean(grad_scaled * scaled, axis=1, keepdims=True)
        )
        grad_own = lax.dynamic_slice_in_dim(grad_full, chan_start, chan_width, 1)
        rows_own = lax.dynamic_slice_in_dim(grad_rows, chan_start, chan_width, 1)
        scaled_own = lax.dynamic_slice_in_dim(scaled, chan_start, chan_width, 1)
        return (grad_own, jnp.sum(rows_own * scaled_own, axis=0), jnp.sum(rows_own, axis=0))

    def mixer_forward(resid, pad_mask, layer_index):
        normed, norm_saved = norm_forward(
            resid, jnp.stack([norm_gain[layer_index, 0], norm_bias[layer_index, 0]])
        )
        streams = (
            jnp.einsum(
                "sd,kdc->kcs", normed, in_weight[layer_index], preferred_element_type=jnp.float32
            )
            + in_bias[layer_index][:, :, None]
        )
        rim = shifted(streams[:, :, rows_dev - 2 :], "seq", 1)
        padded = jnp.concatenate([rim, streams], axis=2)
        taps = short_taps[layer_index]
        short_out = (
            taps[:, 0][:, :, None] * padded[:, :, 2:]
            + taps[:, 1][:, :, None] * padded[:, :, 1 : rows_dev + 1]
            + taps[:, 2][:, :, None] * padded[:, :, :rows_dev]
            + short_bias[layer_index][:, :, None]
        )
        product = short_out[1] * short_out[2]
        chan_prod = to_channels(product)
        filt_re, filt_im, filter_pull, skip_cols = filters[layer_index]
        prod_re, prod_im = to_spectrum(chan_prod, basis)
        conv_re, conv_im = complex_mul(prod_re, prod_im, filt_re, filt_im)
        chan_out = from_spectrum(conv_re, conv_im, basis) + skip_cols[:, None] * chan_prod
        long_out = to_positions(chan_out)
        mixed = (short_out[0] * long_out).astype(jnp.bfloat16)
        partial_value = jnp.einsum(
            "cs,cd->sd", mixed, out_weight[layer_index], preferred_element_type=jnp.float32
        )
        branch = branch_sum(partial_value) + out_bias[layer_index]
        saved = (
            normed,
            norm_saved,
            padded,
            short_out,
            chan_prod,
            prod_re,
            prod_im,
            long_out,
            mixed,
        )
        return (resid + pad_mask[:, None] * branch, saved)

    def mlp_forward(resid, pad_mask, layer_index):
        normed, norm_saved = norm_forward(
            resid, jnp.stack([norm_gain[layer_index, 1], norm_bias[layer_index, 1]])
        )
        pre_act = (
            jnp.dot(normed, up_weight[layer_index], preferred_element_type=jnp.float32)
            + up_bias[layer_index]
        )
        activated = jax.nn.gelu(pre_act, approximate=False).astype(jnp.bfloat16)
        partial_value = jnp.dot(
            activated, down_weight[layer_index], preferred_element_type=jnp.float32
        )
        branch = branch_sum(partial_value) + down_bias[layer_index]
        return (resid + pad_mask[:, None] * branch, (normed, norm_saved, pre_act, activated))

    def mlp_backward(grad_resid, pad_mask, layer_index, saved):
        normed, norm_saved, pre_act, activated = saved
        grad_branch = pad_mask[:, None] * grad_resid
        g_down_bias = jnp.sum(grad_branch, axis=0)
        grad_full = branch_grad(grad_branch.astype(jnp.bfloat16))
        g_down_weight = jnp.einsum(
            "sf,sd->fd", activated, grad_full, preferred_element_type=jnp.float32
        )
        grad_act = jnp.einsum(
            "sd,fd->sf", grad_full, down_weight[layer_index], preferred_element_type=jnp.float32
        )
        unused_value, gelu_pull = jax.vjp(
            lambda inner: jax.nn.gelu(inner, approximate=False), pre_act
        )
        grad_pre = gelu_pull(grad_act)[0]
        g_up_bias = jnp.sum(grad_pre, axis=0)
        pre_low = grad_pre.astype(jnp.bfloat16)
        g_up_weight = jnp.einsum("sd,sf->df", normed, pre_low, preferred_element_type=jnp.float32)
        grad_normed = jnp.einsum(
            "sf,df->sd", pre_low, up_weight[layer_index], preferred_element_type=jnp.float32
        )
        grad_own, g_gain, g_bias = norm_backward(grad_normed, norm_saved)
        return (
            grad_resid + grad_own,
            (g_up_weight, g_down_weight, g_gain, g_bias, g_up_bias, g_down_bias),
        )

    mixer_acc = [None] * layer_count
    mlp_acc = [None] * layer_count
    outputs = []
    input_grads = []
    for micro_index in range(micro_count):
        pad_mask = (positions_dev < lengths[micro_index, 0]).astype(jnp.float32)
        resid = tokens[micro_index, 0].astype(jnp.float32)
        layer_inputs = []
        layer_saved = []
        for layer_index in range(layer_count):
            layer_inputs.append(resid)
            resid, mix_saved = mixer_forward(resid, pad_mask, layer_index)
            layer_inputs.append(resid)
            resid, mlp_saved = mlp_forward(resid, pad_mask, layer_index)
            layer_saved.append((mix_saved, mlp_saved))
        outputs.append(resid)
        grad_resid = cotangent[micro_index, 0].astype(jnp.float32)
        for layer_index in reversed(range(layer_count)):
            mlp_saved = mlp_forward(layer_inputs[2 * layer_index + 1], pad_mask, layer_index)[1]
            grad_resid, mlp_grads = mlp_backward(grad_resid, pad_mask, layer_index, mlp_saved)
            mix_saved = mixer_forward(layer_inputs[2 * layer_index], pad_mask, layer_index)[1]
            (
                mixer_normed,
                mixer_norm_saved,
                mixer_padded,
                mixer_short_out,
                mixer_chan_prod,
                mixer_prod_re,
                mixer_prod_im,
                mixer_long_out,
                mixer_mixed,
            ) = mix_saved
            mixer_filt_re, mixer_filt_im, mixer_filter_pull, mixer_skip_cols = filters[layer_index]
            mixer_grad_branch = pad_mask[:, None] * grad_resid
            g_out_bias = jnp.sum(mixer_grad_branch, axis=0)
            mixer_grad_full = branch_grad(mixer_grad_branch.astype(jnp.bfloat16))
            g_out_weight = jnp.einsum(
                "cs,sd->cd", mixer_mixed, mixer_grad_full, preferred_element_type=jnp.float32
            )
            grad_mixed = jnp.einsum(
                "sd,cd->cs",
                mixer_grad_full,
                out_weight[layer_index],
                preferred_element_type=jnp.float32,
            )
            grad_long = grad_mixed * mixer_short_out[0]
            grad_gate = grad_mixed * mixer_long_out
            chan_grad = to_channels(grad_long)
            grad_re, grad_im = to_spectrum(chan_grad, basis)
            back_re, back_im = complex_mul(grad_re, grad_im, mixer_filt_re, -mixer_filt_im)
            chan_dprod = (
                from_spectrum(back_re, back_im, basis) + mixer_skip_cols[:, None] * chan_grad
            )
            corr_re, corr_im = complex_mul(grad_re, grad_im, mixer_prod_re, -mixer_prod_im)
            grad_filter = from_spectrum(corr_re, corr_im, basis)
            g_skip = jnp.sum(chan_grad * mixer_chan_prod, axis=1)
            grad_product = to_positions(chan_dprod)
            grad_short = jnp.stack(
                [grad_gate, grad_product * mixer_short_out[2], grad_product * mixer_short_out[1]]
            )
            g_short_bias = jnp.sum(grad_short, axis=2)
            g_taps = jnp.stack(
                [
                    jnp.sum(grad_short * mixer_padded[:, :, 2:], axis=2),
                    jnp.sum(grad_short * mixer_padded[:, :, 1 : rows_dev + 1], axis=2),
                    jnp.sum(grad_short * mixer_padded[:, :, :rows_dev], axis=2),
                ],
                axis=1,
            )
            next_rim = shifted(grad_short[:, :, :2], "seq", -1)
            extended = jnp.concatenate([grad_short, next_rim], axis=2)
            mixer_taps = short_taps[layer_index]
            grad_streams = (
                mixer_taps[:, 0][:, :, None] * extended[:, :, :rows_dev]
                + mixer_taps[:, 1][:, :, None] * extended[:, :, 1 : rows_dev + 1]
                + mixer_taps[:, 2][:, :, None] * extended[:, :, 2:]
            )
            g_in_bias = jnp.sum(grad_streams, axis=2)
            streams_low = grad_streams.astype(jnp.bfloat16)
            g_in_weight = jnp.einsum(
                "sd,kcs->kdc", mixer_normed, streams_low, preferred_element_type=jnp.float32
            )
            mixer_grad_normed = jnp.einsum(
                "kcs,kdc->sd",
                streams_low,
                in_weight[layer_index],
                preferred_element_type=jnp.float32,
            )
            mixer_grad_own, mixer_g_gain, mixer_g_bias = norm_backward(
                mixer_grad_normed, mixer_norm_saved
            )
            grads = (
                g_in_weight,
                g_out_weight,
                mixer_g_gain,
                mixer_g_bias,
                g_in_bias,
                g_taps,
                g_short_bias,
                g_skip,
                g_out_bias,
                grad_filter,
            )
            grad_resid, mix_grads = (grad_resid + mixer_grad_own, grads)
            if mixer_acc[layer_index] is None:
                mixer_acc[layer_index] = mix_grads
                mlp_acc[layer_index] = mlp_grads
            else:
                mixer_acc[layer_index] = jax.tree.map(jnp.add, mixer_acc[layer_index], mix_grads)
                mlp_acc[layer_index] = jax.tree.map(jnp.add, mlp_acc[layer_index], mlp_grads)
        input_grads.append(grad_resid)
    filter_grads = [
        filters[layer_index][2](mixer_acc[layer_index][9]) for layer_index in range(layer_count)
    ]
    skip_start = chan_start + col_start

    def stack_mix(member):
        return jnp.stack([mixer_acc[layer_index][member] for layer_index in range(layer_count)])

    def stack_mlp(member):
        return jnp.stack([mlp_acc[layer_index][member] for layer_index in range(layer_count)])

    def stack_filter(member):
        return jnp.stack([filter_grads[layer_index][member] for layer_index in range(layer_count)])

    big_grads = (
        lax.psum_scatter(stack_mix(0), ("seq", "dp"), scatter_dimension=2, tiled=True),
        lax.psum_scatter(stack_mix(1), ("seq", "dp"), scatter_dimension=2, tiled=True),
        lax.psum_scatter(stack_mlp(0), ("seq", "dp"), scatter_dimension=1, tiled=True),
        lax.psum_scatter(stack_mlp(1), ("seq", "dp"), scatter_dimension=2, tiled=True),
    )
    gain_grads = jnp.stack([stack_mix(2), stack_mlp(2)], axis=1)
    bias_grads = jnp.stack([stack_mix(3), stack_mlp(3)], axis=1)
    small = lax.psum(
        (
            place(gain_grads, chan_start, full_width, 2),
            place(bias_grads, chan_start, full_width, 2),
            place(stack_mix(4), chan_start, full_width, 2),
            place(stack_mix(5), chan_start, full_width, 3),
            place(stack_mix(6), chan_start, full_width, 2),
            place(stack_mix(7), skip_start, full_width, 1),
            place(stack_mix(8), chan_start, full_width, 1),
            place(stack_mlp(4), chan_index * hidden_width, hidden_width * chan_parts, 1),
            place(stack_mlp(5), chan_start, full_width, 1),
            stack_filter(0),
            stack_filter(1),
            stack_filter(2),
            place(stack_filter(3), skip_start, full_width, 2),
        ),
        ("seq", "chan", "dp"),
    )
    out_act = jnp.stack(outputs)[:, None]
    grad_tokens = jnp.stack(input_grads)[:, None]
    return (
        out_act,
        grad_tokens,
        big_grads[0],
        big_grads[1],
        big_grads[2],
        big_grads[3],
        small[0],
        small[1],
        small[2],
        small[3],
        small[4],
        small[5],
        small[6],
        small[7],
        small[8],
        small[9],
        small[10],
        small[11],
        small[12],
    )


F32 = jnp.float32
BF16 = jnp.bfloat16
MESH = pl.DeviceIdType.MESH
CHUNKS = (
    (1, "down", 3072, 512, "yxh"),
    (1, "down", 3584, 512, "yxh"),
    (1, "down", 4096, 512, "xyh"),
    (1, "up", 1536, 512, "xlh"),
    (1, "up", 2048, 512, "xlh"),
    (1, "up", 2560, 512, "lhx"),
    (1, "grad_out", 1152, 384, "lyh"),
    (1, "grad_in", 0, 384, "ylh"),
    (1, "grad_in", 384, 384, "yhl"),
    (1, "grad_in", 768, 384, "yhl"),
    (0, "down", 3072, 512, "ylh"),
    (0, "down", 3584, 512, "ylh"),
    (0, "down", 4096, 512, "ylh"),
    (0, "up", 1536, 512, "ylh"),
    (0, "up", 2048, 512, "ylh"),
    (0, "up", 2560, 512, "ylh"),
    (0, "grad_out", 1152, 384, "ylh"),
    (0, "grad_in", 0, 384, "ylh"),
    (0, "grad_in", 384, 384, "ylh"),
    (0, "grad_in", 768, 384, "ylh"),
)
FOLD = (
    dict(grad_in="x", grad_out="x", up="x", down="x"),
    dict(grad_in="x", grad_out="x", up="y", down="l"),
)
TICKS = 13
PLAN = {
    7: ((3, 0), (6, 0), (4, 0),),
    9: ((0, 0), (1, 0), (2, 0), (5, 0), (3, 1),),
    10: ((4, 1),),
    13: ((6, 1), (0, 1), (2, 1), (5, 1),),
    15: ((3, 2),),
    17: ((1, 1), (7, 0), (4, 2), (6, 2), (2, 2),),
    19: ((8, 0), (5, 2), (3, 3), (9, 0),),
    20: ((7, 1),),
    21: ((4, 3), (6, 3), (13, 0), (8, 1), (2, 3),),
    22: ((9, 1), (14, 0),),
    24: ((7, 2), (8, 2), (13, 1),),
    26: ((15, 0), (9, 2), (0, 2), (14, 1), (7, 3), (8, 3), (13, 2), (10, 0), (11, 0), (12, 0), (9, 3), (1, 2), (0, 3), (15, 1), (14, 2), (16, 0), (13, 3), (10, 1), (5, 3), (1, 3), (15, 2), (11, 1), (17, 0), (14, 3), (10, 2), (12, 1), (18, 0), (15, 3), (11, 2), (16, 1), (10, 3), (19, 0), (12, 2), (17, 1), (11, 3), (16, 2), (18, 1), (12, 3), (19, 1), (17, 2), (16, 3), (18, 2), (19, 2), (17, 3), (18, 3), (19, 3),),
}
SMALL = (33, 44)


def half_tables(count):
    odd = 2 * np.arange(count, dtype=np.int64) + 1
    angle = np.outer(odd, odd) % (8 * count) * (math.pi / (4 * count))
    twist = odd * (math.pi / (4 * count))
    return np.cos(angle), np.sin(angle), np.cos(twist)[:, None], np.sin(twist)[:, None]


def mesh_bits():
    seq, dp = lax.axis_index("seq"), lax.axis_index("dp")
    return {"x": dp, "y": lax.rem(seq, 2), "l": lax.rem(seq // 2, 2), "h": seq // 4}


def mesh_peers():
    seq, dp = lax.axis_index("seq"), lax.axis_index("dp")
    bits = mesh_bits()
    return {
        "x": {"dp": 1 - dp},
        "y": {"seq": seq + 1 - 2 * bits["y"]},
        "l": {"seq": seq + 2 - 4 * bits["l"]},
        "h": {"seq": seq + 4 - 8 * bits["h"]},
    }


def greet(devices):
    barrier = pltpu.get_barrier_semaphore()
    for device in devices:
        pl.semaphore_signal(barrier, inc=1, device_id=device, device_id_type=MESH)
    pl.semaphore_wait(barrier, len(devices))


def mm(left, right):
    return jnp.dot(left, right, preferred_element_type=F32)


def fine(left, right, dims=((1,), (0,))):
    return lax.dot_general(left, right, (dims, ((), ())), precision=HIGH, preferred_element_type=F32)


def mm_nt(left, right):
    return lax.dot_general(left, right, (((1,), (1,)), ((), ())), preferred_element_type=F32)


def chain_kernel(sizes, names, *refs):
    layers, micro, span, half, hidden, feat, freq_lane = sizes
    r = types.SimpleNamespace(**dict(zip(names, refs)))
    width, rows, parts = 2 * half, micro * span, 8
    block = half // parts
    length = span * parts
    seq, chan = lax.axis_index("seq"), lax.axis_index("chan")
    pair = seq + 1 - 2 * lax.rem(seq, 2)
    step = 32

    def load(name, layer, slot):
        return pltpu.make_async_copy(getattr(r, name).at[layer], getattr(r, name + "_v"), r.w_sem.at[slot])

    weights = (("win", 0), ("wout", 1), ("wup", 2), ("wdown", 3))
    table_loads = [
        pltpu.make_async_copy(r.cos, r.cos_v, r.t_sem.at[0]),
        pltpu.make_async_copy(r.sin, r.sin_v, r.t_sem.at[1]),
    ]
    load("win", 0, 0).start()
    for copy in table_loads:
        copy.start()
    for name, slot in weights[1:]:
        load(name, 0, slot).start()
    peers, bits = mesh_peers(), mesh_bits()
    dp = lax.axis_index("dp")
    ranks = 2 * parts
    me = 2 * seq + dp
    ranked = [lax.rem(me + far, ranks) for far in range(1, ranks)]
    r.sm_recv[...] = jnp.zeros_like(r.sm_recv)
    greet([{"seq": other // 2, "dp": lax.rem(other, 2)} for other in ranked] + [{"chan": 1 - chan}])

    def core_copy(source, target, slot):
        return pltpu.make_async_remote_copy(
            src_ref=source,
            dst_ref=target,
            send_sem=r.core_sem.at[0, slot],
            recv_sem=r.core_sem.at[1, slot],
            device_id={"chan": 1 - chan},
            device_id_type=MESH,
        )

    for layer in range(layers):
        at = pl.ds(layer, 1)
        for n in range(2):
            r.params[pl.ds(2 * layer + n, 1), :] = r.gain[layer, pl.ds(n, 1), :]
            r.params[pl.ds(2 * layers + 2 * layer + n, 1), :] = r.bias[layer, pl.ds(n, 1), :]
        r.params[pl.ds(4 * layers + layer, 1), :] = r.out_b[at, :]
        r.params[pl.ds(5 * layers + layer, 1), :] = r.down_b[at, :]
    r.params[pl.ds(12, 4), :] = jnp.zeros((4, half), F32)
    first = [
        core_copy(r.params.at[pl.ds(0, 16)], r.vec2.at[chan], 0),
        core_copy(r.tok, r.both.at[chan, 0], 1),
        core_copy(r.cot, r.both.at[chan, 1], 2),
    ]
    for copy in first:
        copy.start()
    r.vec2[chan] = r.params[pl.ds(0, 16), :]
    r.both[chan, 0] = r.tok[...]
    r.both[chan, 1] = r.cot[...]
    r.sm[...] = jnp.zeros_like(r.sm)
    r.vecs[...] = jnp.zeros_like(r.vecs)
    r.o768[...] = jnp.zeros_like(r.o768)
    for m in range(micro):
        place_ids = seq * span + lax.broadcasted_iota(jnp.int32, (span, 1), 0)
        r.mask[pl.ds(m * span, span), :] = (place_ids < r.lens[0, m]).astype(F32)
    for layer in range(layers):
        at = pl.ds(layer, 1)
        for k in range(3):
            r.params[pl.ds(16 + 3 * layer + k, 1), :] = r.in_b[k, at, :]
            r.params[pl.ds(40 + 3 * layer + k, 1), :] = r.short_b[k, at, :]
            for j in range(3):
                r.params[pl.ds(22 + 9 * layer + 3 * k + j, 1), :] = r.taps[k, j, at, :]
    first[0].wait_recv()
    r.vec[...] = jnp.concatenate([r.vec2[0], r.vec2[1]], axis=1)

    def rank_copy(source, target, phase, other, slot):
        return pltpu.make_async_remote_copy(
            src_ref=source,
            dst_ref=target,
            send_sem=r.sm_sem.at[phase, 0, other],
            recv_sem=r.sm_sem.at[phase, 1, slot],
            device_id={"seq": other // 2, "dp": other % 2 if isinstance(other, int) else lax.rem(other, 2)},
            device_id_type=MESH,
        )

    def small_copy(other):
        return rank_copy(r.sm_b.at[other], r.sm_recv.at[me], 0, other, me)

    def each_small(act):
        for other in range(parts, ranks):

            @pl.when(me != other)
            def _(other=other):
                act(small_copy(other))

        @pl.when(me != seq)
        def _():
            act(small_copy(seq))

    def small_wait(other):
        rank_copy(r.sm_b.at[other], r.sm_recv.at[other], 0, other, other).wait_recv()

    def chan_rows(layer):
        value = r.chv[layer]
        return value[:, :feat], value[:, feat : feat + 1], value[:, feat + 1 : feat + 2]

    def filter_forward(layer):
        at = pl.ds(layer, 1)
        r.pack_t[...] = jnp.zeros_like(r.pack_t)
        for i in range(freq_lane - feat - 1):
            r.pack_t[pl.ds(feat + i, 1), :] = r.fin[i, at, :]
        r.pack_t[pl.ds(freq_lane - 1, 1), :] = r.fbias[at, :]
        r.pack_t[pl.ds(freq_lane, 1), :] = r.ffreq[at, :]
        r.pack[layer] = r.pack_t[...].T
        r.chan_t[...] = jnp.zeros_like(r.chan_t)
        r.chan_t[pl.ds(0, feat), :] = r.fout[layer]
        r.chan_t[pl.ds(feat, 1), :] = r.decay[at, :]
        r.chan_t[pl.ds(feat + 1, 1), :] = r.skip[at, :]
        r.chv_t[...] = r.chan_t[...].T
        r.chv[layer] = r.chv_t[pl.ds(pl.multiple_of(seq * block, 8), block), :]
        turned, decay, skip = chan_rows(layer)
        r.skip_l[layer] = jnp.concatenate([skip] * micro, axis=0)
        pack = r.pack[layer]
        freq = pack[:, freq_lane : freq_lane + 1]
        for c in range(0, length, 256):
            lanes = pl.ds(c, 256)
            inner = fine(pack, r.emb[:, lanes])
            wave = jnp.sin(freq * inner)
            r.inner[layer, :, lanes] = inner
            r.wave[pl.ds(layer * feat, feat), lanes] = wave
            filt = fine(turned, wave) * jnp.exp(-decay * r.emb[pl.ds(feat, 1), lanes])
            high = filt.astype(BF16)
            r.spec[0, pl.ds(0, block), lanes] = high
            r.spec[0, pl.ds(block, block), lanes] = (filt - high.astype(F32)).astype(BF16)
        for c in range(0, length, 256):
            lanes = pl.ds(c, 256)
            fc, fs = mm(r.spec[0], r.cos_v[:, lanes]), mm(r.spec[0], r.sin_v[:, lanes])
            fc, fs = fc[:block] + fc[block:], fs[:block] + fs[block:]
            tc, ts = r.turn[pl.ds(0, 1), lanes], r.turn[pl.ds(1, 1), lanes]
            r.fr[layer, :, lanes] = (fc * tc + fs * ts) * (1.0 / length)
            r.fi[layer, :, lanes] = (fc * ts - fs * tc) * (1.0 / length)

    def twice(value):
        return jnp.concatenate([value] * micro, axis=0)

    def filter_backward(layer):
        turned, decay, _ = chan_rows(layer)
        freq = r.pack[layer, :, freq_lane : freq_lane + 1]
        g_out = g_pack = g_freq = 0.0
        for c in range(0, length, 256):
            lanes = pl.ds(c, 256)
            raw = r.o_filt[layer, :, lanes] * jnp.exp(-decay * r.emb[pl.ds(feat, 1), lanes])
            g_out = g_out + mm_nt(raw.astype(BF16), r.wave[:, lanes].astype(BF16))
            inner = r.inner[layer, :, lanes]
            slope = lax.dot_general(turned.astype(BF16), raw.astype(BF16), (((0,), (0,)), ((), ())), preferred_element_type=F32) * jnp.cos(freq * inner)
            g_freq = g_freq + jnp.sum(slope * inner, axis=1, keepdims=True)
            g_pack = g_pack + mm_nt((slope * freq).astype(BF16), r.emb[:, lanes].astype(BF16))
        lane = lax.broadcasted_iota(jnp.int32, (block, 128), 1)
        mine = (lane >= layer * feat) & (lane < (layer + 1) * feat)
        r.sm[seq] = jnp.where(mine, g_out, r.sm[seq])
        lane = lax.broadcasted_iota(jnp.int32, (feat, 128), 1)
        r.spread[layer] = g_pack + jnp.where(lane == freq_lane, g_freq, 0.0)

    def small_begin():
        for layer in range(layers):
            r.vecs[pl.ds(32 * layer, 8), :] = r.o768[pl.ds(8 * layer, 8), own_lanes]
            for i in range(hidden // half):
                r.vecs[pl.ds(32 * layer + 24 + i, 1), :] = r.o_up[pl.ds(layer, 1), pl.ds(i * half, half)]
        spread = jnp.concatenate(
            [r.spread[layer] for layer in range(layers)] + [jnp.zeros((half - layers * feat, 128), F32)], axis=0
        )
        total = r.vecs[...].T + spread
        r.sm[pl.ds(parts, parts)] = total.reshape(parts, block, 128)
        lane = lax.broadcasted_iota(jnp.int32, (block, 128), 1)
        for layer in range(layers):
            r.sm[parts + seq] = r.sm[parts + seq] + jnp.where(lane == 112 + layer, r.gskip[layer], 0.0)
        r.sm_b[...] = r.sm[...].astype(BF16)
        each_small(lambda copy: copy.start())

    def small_middle():
        total = r.sm[me]

        @pl.when(me >= parts)
        def _():
            for other in ranked:
                small_wait(other)

        for i in range(2):
            other = lax.rem(2 * me + i, ranks)

            @pl.when((me < parts) & (other != me))
            def _(other=other):
                small_wait(other)

        for other in ranked:
            total = total + r.sm_recv[other].astype(F32)
        r.o_small[chan, me] = total.astype(BF16)
        for other in ranked:
            rank_copy(r.o_small.at[chan, me], r.o_small.at[chan, me], 1, other, me).start()

    def small_last():
        for other in ranked:
            rank_copy(r.o_small.at[chan, me], r.o_small.at[chan, other], 1, other, other).wait_recv()
        core_copy(r.o_small.at[chan], r.o_small.at[chan], 3).start()

    def small_end():
        core_copy(r.o_small.at[chan], r.o_small.at[1 - chan], 3).wait()
        for other in ranked:
            rank_copy(r.o_small.at[chan, me], r.o_small.at[chan, me], 1, other, me).wait_send()
        each_small(lambda copy: copy.wait_send())
        for copy in first:
            copy.wait_send()

    own_lanes = pl.ds(pl.multiple_of(chan * half, half), half)
    sent, done, begun, written = [], [], [], set()
    received = (r.rs1, r.rs2, r.rs3)
    sent, done, arrived, pending = [], [], [], {}
    starts = dict(grad_in=0, grad_out=3 * half, up=4 * half, down=4 * half + hidden)
    slot_group = ["grad_in", "up", "grad_out", "down", "down"] + ["up"] * 3 + ["grad_out"] + ["grad_in"] * 3

    def half_of(axis, bit):
        return tuple(bit if name == axis else slice(None) for name in "hlyx")

    def fold_copy(layer, slot):
        axis = FOLD[layer][slot_group[slot]]
        theirs = half_of(axis, 1 - bits[axis])
        if slot < 2:
            source, target = r.turned.at[(slot, *theirs)], r.ut_p.at[layer, slot]
        elif slot == 2:
            source, target = r.mixed.at[layer], r.mixed_p.at[layer]
        elif slot == 3:
            source, target = r.g.at[layer], r.g_p.at[layer]
        elif slot in (4, 8):
            kind = 0 if slot == 4 else 1
            source, target = r.turned.at[(kind, *theirs)], r.gt_p.at[layer, kind]
        elif slot < 8:
            lanes = pl.ds((slot - 5) * (hidden // 3), hidden // 3)
            source, target = r.da.at[layer, :, lanes], r.da_p.at[layer, :, lanes]
        else:
            lanes = pl.ds((slot - 9) * half, half)
            source, target = r.gz.at[layer, :, lanes], r.gz_p.at[layer, :, lanes]
        return pltpu.make_async_remote_copy(
            src_ref=source,
            dst_ref=target,
            send_sem=r.fold_sem.at[0, layer, slot],
            recv_sem=r.fold_sem.at[1, layer, slot],
            device_id=peers[axis],
            device_id_type=MESH,
        )

    def turn(layer, slot, value, own):
        kind = slot if slot < 2 else (0 if slot == 4 else 1)
        if kind in pending:
            fold_copy(*pending[kind]).wait_send()
            sent.append(pending[kind])
        pending[kind] = (layer, slot)
        r.turned[kind] = value.astype(F32).T.astype(BF16).reshape(2, 2, 2, 2, width // 16, rows)
        axis = FOLD[layer][slot_group[slot]]
        own[layer, kind] = r.turned.at[(kind, *half_of(axis, bits[axis]))][...]
        fold_copy(layer, slot).start()

    def factors(chunk):
        layer, group, start, columns = CHUNKS[chunk][:4]
        lanes = pl.ds(start - starts[group], columns)
        i = (start - starts[group]) // columns
        if group == "down":
            return (3, 4), r.gt_own.at[layer, 0], r.gt_p.at[layer, 0], r.g.at[layer, :, lanes], r.g_p.at[layer, :, lanes]
        if group == "up":
            return (1, 5 + i), r.ut_own.at[layer, 1], r.ut_p.at[layer, 1], r.da.at[layer, :, lanes], r.da_p.at[layer, :, lanes]
        if group == "grad_out":
            return (2, 8), r.gt_own.at[layer, 1], r.gt_p.at[layer, 1], r.mixed.at[layer], r.mixed_p.at[layer]
        return (0, 9 + i), r.ut_own.at[layer, 0], r.ut_p.at[layer, 0], r.gz.at[layer, :, lanes], r.gz_p.at[layer, :, lanes]

    def rs_left(chunk, stage):
        layer, group, start, columns, order = CHUNKS[chunk]
        return [axis for axis in "hlyx" if axis != FOLD[layer][group] and axis not in order[:stage]]

    def rs_held(chunk, stage, index):
        layer, group, start, columns, order = CHUNKS[chunk]
        lanes = pl.ds(start, columns)
        if stage == 0:
            return r.big.at[(*index, slice(None), lanes)]
        return received[stage - 1].at[(layer, *index, slice(None), lanes)]

    def rs_copy(chunk, stage):
        layer, group, start, columns, order = CHUNKS[chunk]
        axis = order[stage]
        index = tuple(1 - bits[axis] if name == axis else slice(None) for name in rs_left(chunk, stage))
        rest = (slice(None),) * (3 - stage)
        return pltpu.make_async_remote_copy(
            src_ref=rs_held(chunk, stage, index),
            dst_ref=received[stage].at[(layer, *rest, pl.ds(start, columns))],
            send_sem=r.rs_sem.at[0, chunk, stage],
            recv_sem=r.rs_sem.at[1, chunk, stage],
            device_id=peers[axis],
            device_id_type=MESH,
        )

    def weight_grad(chunk):
        layer, group, start, columns, order = CHUNKS[chunk]
        slots, own, theirs, value, value_p = factors(chunk)
        for slot in slots:
            if (layer, slot) not in arrived:
                fold_copy(layer, slot).wait_recv()
                arrived.append((layer, slot))
        for other, spec in enumerate(CHUNKS):
            if spec[0] == layer + 1 and spec[2] == start:
                if (other, 1) not in done:
                    raise ValueError(chunk)
                rs_copy(other, 0).wait_send()
                sent.append((-1, other, 0))
        shape = (width // 2, rows)
        out = mm(own[...].reshape(shape), value[...]) + mm(theirs[...].reshape(shape), value_p[...])
        r.big[:, :, :, :, pl.ds(start, columns)] = out.astype(BF16).reshape(2, 2, 2, width // 16, columns)
        rs_copy(chunk, 0).start()

    def advance(chunk, step_of):
        layer, group, start, columns, order = CHUNKS[chunk]
        done.append((chunk, step_of))
        if step_of == 0:
            weight_grad(chunk)
            return
        stage = step_of - 1
        lanes = pl.ds(start, columns)
        rs_copy(chunk, stage).wait_recv()
        spot = rs_left(chunk, stage).index(order[stage])
        for flat in range(2 ** (2 - stage)):
            kept = [flat >> shift & 1 for shift in reversed(range(2 - stage))]
            mine = tuple(kept[:spot] + [bits[order[stage]]] + kept[spot:])
            total = rs_held(chunk, stage, mine)[...].astype(F32)
            there = received[stage].at[(layer, *kept, slice(None), lanes)]
            total = total + there[...].astype(F32)
            if stage == 2:
                r.o_big[layer, :, lanes] = total
            else:
                there[...] = total.astype(BF16)
        if stage < 2:
            rs_copy(chunk, stage + 1).start()

    def tick(layer, spot):
        now = TICKS * (layers - 1 - layer) + spot
        for chunk, stage in PLAN.get(now, ()):
            advance(chunk, stage)

    def short_all(layer):
        for k in range(3):
            for m in range(micro):
                short_part(layer, k, m, 0, span)

    def next_load(layer, name, slot):
        if 0 <= layer < layers:
            load(name, layer, slot).start()

    def seq_copy(send, recv, sems, other, outgoing):
        slot = seq if outgoing else other
        return pltpu.make_async_remote_copy(
            src_ref=getattr(r, send).at[other],
            dst_ref=getattr(r, recv).at[slot],
            send_sem=getattr(r, sems).at[0, other],
            recv_sem=getattr(r, sems).at[1, slot],
            device_id={"seq": other},
            device_id_type=MESH,
        )

    def all_others():
        return [lax.rem(seq + far, parts) for far in (4, 3, 5, 2, 6, 1, 7)]

    def wait_all(send, recv, sems):
        for other in all_others():
            seq_copy(send, recv, sems, other, False).wait_recv()
        for other in all_others():
            seq_copy(send, recv, sems, other, True).wait_send()

    def pair_copy(slot, m):
        return pltpu.make_async_remote_copy(
            src_ref=r.pair_send.at[slot, m],
            dst_ref=r.pair_recv.at[slot, m],
            send_sem=r.pair_sem.at[0, slot, m],
            recv_sem=r.pair_sem.at[1, slot, m],
            device_id={"chan": 1 - chan},
            device_id_type=MESH,
        )

    def rim_copy(way):
        other = lax.rem(seq + (1 if way == 0 else parts - 1), parts)
        return pltpu.make_async_remote_copy(
            src_ref=r.rim_send.at[way],
            dst_ref=r.rim_recv.at[way],
            send_sem=r.rim_sem.at[0, way],
            recv_sem=r.rim_sem.at[1, way],
            device_id={"seq": other},
            device_id_type=MESH,
        )

    def paired(slot, m, base, count):
        at = (slot, m, pl.ds(base, count), slice(None))
        return r.pair_send[at].astype(F32) + r.pair_recv[at].astype(F32)

    def row(name, index):
        return getattr(r, name)[pl.ds(index, 1), :]

    gains = [[row("vec", 2 * layer + n) for n in range(2)] for layer in range(layers)]
    biases = [[row("vec", 2 * layers + 2 * layer + n) for n in range(2)] for layer in range(layers)]
    branch_bias = [[row("vec", 4 * layers + layer), row("vec", 5 * layers + layer)] for layer in range(layers)]

    def norm_rows(at, x, layer, n):
        centred = x - jnp.mean(x, axis=1, keepdims=True)
        rstd = lax.rsqrt(jnp.mean(centred * centred, axis=1, keepdims=True) + EPS)
        scaled = centred * rstd
        r.xh[layer, n, at, :] = scaled
        r.rstd[layer, n, at, :] = rstd
        r.u[at, :] = (scaled * gains[layer][n] + biases[layer][n]).astype(BF16)

    def forward_rows(slot, bias, layer, n):
        for m in range(micro):
            pair_copy(slot, m).wait_recv()

            @pl.loop(0, span // step)
            def _(i):
                base = pl.multiple_of(i * step, step)
                at = pl.ds(m * span + base, step)
                x = r.x[at, :] + r.mask[at, :] * (paired(slot, m, base, step) + bias)
                r.x[at, :] = x
                if layer < layers:
                    norm_rows(at, x, layer, n)

        for m in range(micro):
            pair_copy(slot, m).wait_send()

    def send_partial(slot, make):
        for m in range(micro):
            r.pair_send[slot, m] = make(m).astype(BF16)
            pair_copy(slot, m).start()

    def tap(layer, k, j):
        return r.params[pl.ds(22 + 9 * layer + 3 * k + j, 1), :]

    def short_part(layer, k, m, low, high):
        z = r.z
        total = r.params[pl.ds(40 + 3 * layer + k, 1), :]
        for j in range(3):
            total = total + tap(layer, k, j) * z[layer, k, m, pl.ds(8 + low - j, high - low), :]
        r.s[k, m, pl.ds(low, high - low), :] = total

    def to_channels(m, value):
        turned = value.T.astype(BF16)
        for j in range(parts):
            r.a_send[j, pl.ds(m * block, block), :] = turned[j * block : (j + 1) * block]

    def start_channels():
        for other in all_others():
            seq_copy("a_send", "a_recv", "a_sem", other, True).start()
        r.a_recv[seq] = r.a_send[seq]

    def gathered():
        return jnp.concatenate([r.a_recv[j] for j in range(parts)], axis=1)

    def from_channels(m):
        stack = [r.b_recv[j, pl.ds(m * block, block), :].astype(F32) for j in range(parts)]
        return jnp.concatenate(stack, axis=0).T

    def inverse_and_send(signal):
        for far in (2, 1, 3, 0):
            at = lax.rem(seq // 2 + far, parts // 2)
            lanes = pl.ds(pl.multiple_of(at * 2 * span, 2 * span), 2 * span)
            out = mm(r.spec[0], r.cos_v[:, lanes]) + mm(r.spec[1], r.sin_v[:, lanes])
            out = (out + r.skip_v[...] * signal[:, lanes].astype(F32)).astype(BF16)
            for h in range(2):
                r.b_send[2 * at + h] = out[:, h * span : (h + 1) * span]
            if far:
                for h in range(2):
                    seq_copy("b_send", "b_recv", "b_sem", 2 * at + h, True).start()
            else:
                seq_copy("b_send", "b_recv", "b_sem", pair, True).start()
                r.b_recv[seq] = r.b_send[seq]

    first[1].wait_recv()
    for base in range(0, rows, step):
        at = pl.ds(base, step)
        x = jnp.concatenate([r.both[0, 0, at, :], r.both[1, 0, at, :]], axis=1).astype(F32)
        r.x[at, :] = x
        norm_rows(at, x, 0, 0)

    for layer in range(layers):
        load("win", layer, 0).wait()
        for k in range(3):
            z = mm(r.u[...], r.win_v[k]) + r.params[pl.ds(16 + 3 * layer + k, 1), :]
            for m in range(micro):
                r.z[layer, k, m, pl.ds(8, span), :] = z[m * span : (m + 1) * span]
                r.rim_send[0, pl.ds(k * 4 + m * 2, 2), :] = z[(m + 1) * span - 2 : (m + 1) * span]
        rim_copy(0).start()
        next_load(layer + 1, "win", 0)
        turn(layer, 0, r.u[...], r.ut_own)
        for k in range(3):
            for m in range(micro):
                short_part(layer, k, m, step, span)
        rim_copy(0).wait()
        inner = (seq > 0).astype(F32)
        for k in range(3):
            for m in range(micro):
                r.z[layer, k, m, pl.ds(6, 2), :] = inner * r.rim_recv[0, pl.ds(k * 4 + m * 2, 2), :]
                short_part(layer, k, m, 0, step)
        for m in range(micro):
            to_channels(m, r.s[1, m] * r.s[2, m])
        start_channels()
        if layer == 0:
            for copy in table_loads:
                copy.wait()
            filter_forward(0)
        wait_all("a_send", "a_recv", "a_sem")
        signal = gathered()
        r.sig[layer] = signal
        r.skip_v[...] = r.skip_l[layer]
        for c in range(0, length, 256):
            lanes = pl.ds(c, 256)
            pc, ps = mm(signal, r.cos_v[:, lanes]), mm(signal, r.sin_v[:, lanes])
            fr, fi = twice(r.fr[layer, :, lanes]), twice(r.fi[layer, :, lanes])
            r.pc[layer, :, lanes], r.ps[layer, :, lanes] = pc.astype(BF16), ps.astype(BF16)
            r.spec[0, :, lanes] = (pc * fr + ps * fi).astype(BF16)
            r.spec[1, :, lanes] = (ps * fr - pc * fi).astype(BF16)
        inverse_and_send(r.sig.at[layer])
        if layer + 1 < layers:
            filter_forward(layer + 1)
        load("wout", layer, 1).wait()
        wait_all("b_send", "b_recv", "b_sem")
        for m in range(micro):
            y = from_channels(m)
            r.y[layer, m] = y.astype(BF16)
            r.mixed[layer, pl.ds(m * span, span), :] = (r.s[0, m] * y).astype(BF16)
        send_partial(0, lambda m: mm(r.mixed[layer, pl.ds(m * span, span), :], r.wout_v[...]))
        next_load(layer + 1, "wout", 1)
        fold_copy(layer, 2).start()
        forward_rows(0, branch_bias[layer][0], layer, 1)

        load("wup", layer, 2).wait()
        for c in range(0, hidden, 256):
            lanes = pl.ds(c, 256)
            for m in range(micro):
                at = pl.ds(m * span, span)
                a = mm(r.u[at, :], r.wup_v[:, lanes]) + r.up_b[pl.ds(layer, 1), lanes]
                cdf = 0.5 + 0.5 * lax.erf(a * math.sqrt(0.5))
                pdf = jnp.exp(-0.5 * a * a) * (1.0 / math.sqrt(2.0 * math.pi))
                r.g[layer, at, lanes] = (a * cdf).astype(BF16)
                r.slope[layer, at, lanes] = (cdf + a * pdf).astype(BF16)
        next_load(layer + 1, "wup", 2)
        load("wdown", layer, 3).wait()
        send_partial(1, lambda m: mm(r.g[layer, pl.ds(m * span, span), :], r.wdown_v[...]))
        next_load(layer + 1, "wdown", 3)
        fold_copy(layer, 3).start()
        turn(layer, 1, r.u[...], r.ut_own)
        forward_rows(1, branch_bias[layer][1], layer + 1, 0)

    r.out_act[...] = r.x[:, own_lanes]

    def branch_rows(at, dx):
        branch = r.mask[at, :] * dx
        r.grad[at, :] = branch.astype(BF16)
        return jnp.sum(branch.reshape(step // 8, 8, width), axis=0)

    def put768(layer, index, value):
        r.o768[pl.ds(8 * layer + index, 1), :] = jnp.sum(value, axis=0, keepdims=True)

    first[2].wait_recv()
    total = jnp.zeros((8, width), F32)
    for base in range(0, rows, step):
        at = pl.ds(base, step)
        dx = jnp.concatenate([r.both[0, 1, at, :], r.both[1, 1, at, :]], axis=1).astype(F32)
        r.x[at, :] = dx
        total = total + branch_rows(at, dx)
    put768(layers - 1, 5, total)

    def backward_rows(slot, layer, n):
        gain = gains[layer][n]
        sums = [jnp.zeros((8, width), F32)] * 3
        for m in range(micro):
            pair_copy(slot, m).wait_recv()

            def body(i, carry):
                base = pl.multiple_of(i * step, step)
                at = pl.ds(m * span + base, step)
                du = paired(slot, m, base, step)
                scaled = r.xh[layer, n, at, :]
                weighted = du * gain
                back = r.rstd[layer, n, at, :] * (
                    weighted
                    - jnp.mean(weighted, axis=1, keepdims=True)
                    - scaled * jnp.mean(weighted * scaled, axis=1, keepdims=True)
                )
                dx = r.x[at, :] + back
                r.x[at, :] = dx
                shape = (step // 8, 8, width)
                return [
                    carry[0] + jnp.sum((du * scaled).reshape(shape), axis=0),
                    carry[1] + jnp.sum(du.reshape(shape), axis=0),
                    carry[2] + branch_rows(at, dx),
                ]

            sums = lax.fori_loop(0, span // step, body, sums)
        for m in range(micro):
            pair_copy(slot, m).wait_send()
        put768(layer, n, sums[0])
        put768(layer, 2 + n, sums[1])
        if n == 1:
            put768(layer, 4, sums[2])
        elif layer > 0:
            put768(layer - 1, 5, sums[2])

    for layer in reversed(range(layers)):
        last = layer == layers - 1
        if not last:
            load("wdown", layer, 3).wait()
        for c in range(0, hidden, 256):
            lanes = pl.ds(c, 256)
            da = mm_nt(r.grad[...], r.wdown_v[lanes, :]) * r.slope[layer, :, lanes].astype(F32)
            r.o_up[pl.ds(layer, 1), lanes] = jnp.sum(da, axis=0, keepdims=True)
            r.da[layer, :, lanes] = da.astype(BF16)
            if c % 512 == 256:
                fold_copy(layer, 5 + c // 512).start()
        next_load(layer - 1, "wdown", 3)
        if not last:
            load("wup", layer, 2).wait()
        send_partial(0, lambda m: mm_nt(r.da[layer, pl.ds(m * span, span), :], r.wup_v[...]))
        next_load(layer - 1, "wup", 2)
        tick(layer, 0)
        turn(layer, 4, r.grad[...], r.gt_own)
        tick(layer, 1)
        if not last:
            short_all(layer)
        tick(layer, 2)
        backward_rows(0, layer, 1)
        tick(layer, 3)
        if not last:
            load("wout", layer, 1).wait()

        for m in range(micro):
            dmixed = mm_nt(r.grad[pl.ds(m * span, span), :], r.wout_v[...])
            to_channels(m, dmixed * r.s[0, m])
            r.ds[0, m, pl.ds(0, span), :] = dmixed * r.y[layer, m].astype(F32)
        start_channels()
        next_load(layer - 1, "wout", 1)
        tick(layer, 4)
        turn(layer, 8, r.grad[...], r.gt_own)
        tick(layer, 5)
        if not last:
            filter_backward(layer + 1)
        wait_all("a_send", "a_recv", "a_sem")
        tick(layer, 6)
        signal = gathered()
        r.dsig[...] = signal
        r.skip_v[...] = r.skip_l[layer]
        for c in range(0, length, 256):
            lanes = pl.ds(c, 256)
            gc, gs = mm(signal, r.cos_v[:, lanes]), mm(signal, r.sin_v[:, lanes])
            fr, fi = twice(r.fr[layer, :, lanes]), twice(r.fi[layer, :, lanes])
            r.gc[:, lanes], r.gs[:, lanes] = gc.astype(BF16), gs.astype(BF16)
            r.spec[0, :, lanes] = (gc * fr - gs * fi).astype(BF16)
            r.spec[1, :, lanes] = (gs * fr + gc * fi).astype(BF16)
        inverse_and_send(r.dsig)
        tick(layer, 7)
        both_skip = jnp.sum(r.dsig[...].astype(F32) * r.sig[layer].astype(F32), axis=1, keepdims=True)
        r.gskip[layer] = sum(both_skip[m * block : (m + 1) * block] for m in range(micro))
        for c in range(0, length, 256):
            lanes = pl.ds(c, 256)
            gc, gs = r.gc[:, lanes].astype(F32), r.gs[:, lanes].astype(F32)
            pc, ps = r.pc[layer, :, lanes].astype(F32), r.ps[layer, :, lanes].astype(F32)
            re, im = gc * pc + gs * ps, gc * ps - gs * pc
            re = sum(re[m * block : (m + 1) * block] for m in range(micro)) * (1.0 / length)
            im = sum(im[m * block : (m + 1) * block] for m in range(micro)) * (1.0 / length)
            tc, ts = r.turn[pl.ds(0, 1), lanes], r.turn[pl.ds(1, 1), lanes]
            for which, value in enumerate((re * tc + im * ts, re * ts - im * tc)):
                high = value.astype(BF16)
                r.spec[which, pl.ds(0, block), lanes] = high
                r.spec[which, pl.ds(block, block), lanes] = (value - high.astype(F32)).astype(BF16)
        for c in range(0, length, 256):
            lanes = pl.ds(c, 256)
            out = mm(r.spec[0], r.cos_v[:, lanes]) + mm(r.spec[1], r.sin_v[:, lanes])
            r.o_filt[layer, :, lanes] = out[:block] + out[block:]
        tick(layer, 8)
        wait_all("b_send", "b_recv", "b_sem")
        for m in range(micro):
            dp = from_channels(m)
            for k in (1, 2):
                value = dp * r.s[3 - k, m]
                r.ds[k, m, pl.ds(0, span), :] = value
            for k in range(3):
                r.rim_send[1, pl.ds(k * 4 + m * 2, 2), :] = r.ds[k, m, pl.ds(0, 2), :]
        rim_copy(1).start()
        for k in range(3):
            sums = [0.0] * 4
            for m in range(micro):
                ds = r.ds[k, m, pl.ds(0, span), :]
                sums[3] = sums[3] + jnp.sum(ds, axis=0, keepdims=True)
                for j in range(3):
                    z = r.z[layer, k, m, pl.ds(8 - j, span), :]
                    sums[j] = sums[j] + jnp.sum(ds * z, axis=0, keepdims=True)
            for j in range(3):
                r.vecs[pl.ds(32 * layer + 11 + 3 * k + j, 1), :] = sums[j]
            r.vecs[pl.ds(32 * layer + 20 + k, 1), :] = sums[3]
        tick(layer, 9)
        rim_copy(1).wait()
        inner = (seq < parts - 1).astype(F32)
        for k in range(3):
            total = 0.0
            for m in range(micro):
                r.ds[k, m, pl.ds(span, 2), :] = inner * r.rim_recv[1, pl.ds(k * 4 + m * 2, 2), :]
                dz = 0.0
                for j in range(3):
                    dz = dz + tap(layer, k, j) * r.ds[k, m, pl.ds(j, span), :]
                total = total + jnp.sum(dz, axis=0, keepdims=True)
                r.gz[layer, pl.ds(m * span, span), pl.ds(k * half, half)] = dz.astype(BF16)
            r.vecs[pl.ds(32 * layer + 8 + k, 1), :] = total
            fold_copy(layer, 9 + k).start()
        if not last:
            load("win", layer, 0).wait()
        send_partial(
            1, lambda m: sum(mm_nt(r.gz[layer, pl.ds(m * span, span), pl.ds(k * half, half)], r.win_v[k]) for k in range(3))
        )
        next_load(layer - 1, "win", 0)
        tick(layer, 10)
        tick(layer, 11)
        backward_rows(1, layer, 0)
        tick(layer, 12)
    r.grad_tokens[...] = r.x[:, own_lanes]
    for count, (chunk, stage) in enumerate(PLAN[TICKS * layers]):
        advance(chunk, stage)
        if count == 3:
            filter_backward(0)
            small_begin()
        if count == SMALL[0]:
            small_middle()
        if count == SMALL[1]:
            small_last()
    small_end()
    for chunk in range(len(CHUNKS)):
        for stage in range(3):
            if (-1, chunk, stage) not in sent:
                rs_copy(chunk, stage).wait_send()
    for layer in range(layers):
        for slot in range(len(slot_group)):
            if (layer, slot) not in sent:
                fold_copy(layer, slot).wait_send()


def chain(inputs, sizes):
    layers, micro, span, half, hidden, feat, freq_lane = sizes
    width, rows, parts = 2 * half, micro * span, 8
    block, length = half // parts, span * parts
    lanes = micro * block
    columns = 4 * half + 2 * hidden
    in_any = ("win", "wout", "wup", "wdown", "cos", "sin")
    outs = dict(
        out_act=((rows, half), F32),
        grad_tokens=((rows, half), F32),
        o_big=((layers, width // 16, 4 * half + 2 * hidden), F32),
        o_small=((2, 2 * parts, block, 128), BF16),
    )
    dma, vm = pltpu.SemaphoreType.DMA, pltpu.VMEM
    scratch = dict(
        big=vm((2, 2, 2, width // 16, columns), BF16),
        rs1=vm((layers, 2, 2, width // 16, columns), BF16),
        rs2=vm((layers, 2, width // 16, columns), BF16),
        rs3=vm((layers, width // 16, columns), BF16),
        rs_sem=dma((2, len(CHUNKS), 3)),
        fold_sem=dma((2, layers, 12)),
        ut_own=vm((layers, 2, 2, 2, 2, width // 16, rows), BF16),
        ut_p=vm((layers, 2, 2, 2, 2, width // 16, rows), BF16),
        gt_own=vm((layers, 2, 2, 2, 2, width // 16, rows), BF16),
        gt_p=vm((layers, 2, 2, 2, 2, width // 16, rows), BF16),
        mixed_p=vm((layers, rows, half), BF16),
        g_p=vm((layers, rows, hidden), BF16),
        da_p=vm((layers, rows, hidden), BF16),
        gz=vm((layers, rows, 3 * half), BF16),
        gz_p=vm((layers, rows, 3 * half), BF16),
        win_v=vm((3, width, half), BF16),
        wout_v=vm((half, width), BF16),
        wup_v=vm((width, hidden), BF16),
        wdown_v=vm((hidden, width), BF16),
        cos_v=vm((length, length), BF16),
        sin_v=vm((length, length), BF16),
        skip_v=vm((lanes, 1), F32),
        skip_l=vm((layers, lanes, 1), F32),
        gskip=vm((layers, block, 1), F32),
        vec2=vm((2, 16, half), F32),
        vec=vm((16, width), F32),
        params=vm((48, half), F32),
        pack_t=vm((128, feat), F32),
        chan_t=vm((128, half), F32),
        pack=vm((layers, feat, 128), F32),
        chv=vm((layers, block, 128), F32),
        chv_t=vm((half, 128), F32),
        both=vm((2, 2, rows, half), BF16),
        mask=vm((rows, 1), F32),
        inner=vm((layers, feat, length), F32),
        wave=vm((layers * feat, length), F32),
        fr=vm((layers, block, length), F32),
        fi=vm((layers, block, length), F32),
        spread=vm((layers, feat, 128), F32),
        o_filt=vm((layers, block, length), F32),
        o768=vm((8 * layers, width), F32),
        o_up=vm((layers, hidden), F32),
        vecs=vm((128, half), F32),
        sm=vm((2 * parts, block, 128), F32),
        sm_b=vm((2 * parts, block, 128), BF16),
        sm_recv=vm((2 * parts, block, 128), BF16),
        sm_sem=dma((2, 2, 2 * parts)),
        core_sem=dma((2, 4)),
        x=vm((rows, width), F32),
        xh=vm((layers, 2, rows, width), F32),
        rstd=vm((layers, 2, rows, 1), F32),
        u=vm((rows, width), BF16),
        z=vm((layers, 3, micro, span + 8, half), F32),
        s=vm((3, micro, span, half), F32),
        y=vm((layers, micro, span, half), BF16),
        mixed=vm((layers, rows, half), BF16),
        sig=vm((layers, lanes, length), BF16),
        dsig=vm((lanes, length), BF16),
        pc=vm((layers, lanes, length), BF16),
        ps=vm((layers, lanes, length), BF16),
        gc=vm((lanes, length), BF16),
        gs=vm((lanes, length), BF16),
        spec=vm((2, lanes, length), BF16),
        slope=vm((layers, rows, hidden), BF16),
        g=vm((layers, rows, hidden), BF16),
        da=vm((layers, rows, hidden), BF16),
        grad=vm((rows, width), BF16),
        turned=vm((2, 2, 2, 2, 2, width // 16, rows), BF16),
        ds=vm((3, micro, span + 8, half), F32),
        a_send=vm((parts, lanes, span), BF16),
        a_recv=vm((parts, lanes, span), BF16),
        b_send=vm((parts, lanes, span), BF16),
        b_recv=vm((parts, lanes, span), BF16),
        pair_send=vm((2, micro, span, width), BF16),
        pair_recv=vm((2, micro, span, width), BF16),
        rim_send=vm((2, 16, half), F32),
        rim_recv=vm((2, 16, half), F32),
        w_sem=dma((4,)),
        t_sem=dma((2,)),
        a_sem=dma((2, parts)),
        b_sem=dma((2, parts)),
        pair_sem=dma((2, 2, micro)),
        rim_sem=dma((2, 2)),
    )
    names = [*inputs, *outs, *scratch]
    results = pl.pallas_call(
        functools.partial(chain_kernel, sizes, names),
        out_shape=[jax.ShapeDtypeStruct(*spec) for spec in outs.values()],
        in_specs=[
            pl.BlockSpec(memory_space=pl.ANY if name in in_any else pltpu.SMEM if name == "lens" else pltpu.VMEM)
            for name in inputs
        ],
        out_specs=[pl.BlockSpec(memory_space=pltpu.VMEM) for _ in outs],
        scratch_shapes=list(scratch.values()),
        compiler_params=pltpu.CompilerParams(
            collective_id=3, has_side_effects=True, vmem_limit_bytes=61 << 20
        ),
        name="chain",
    )(*inputs.values())
    return types.SimpleNamespace(**dict(zip(outs, results)))


def embedding(count, bands, feat):
    steps = np.arange(count, dtype=np.float32) / np.float32(count)
    number = (bands - 1) // 2
    freq = np.linspace(0.0001, number - 1, number).astype(np.float32)
    phases = (np.float32(2.0 * math.pi) * steps)[None, :] * freq[:, None]
    table = np.zeros((128, count), np.float32)
    table[feat] = steps
    table[feat + 1 : feat + 1 + number] = np.cos(phases)
    table[feat + 1 + number : feat + bands] = -np.sin(phases)
    table[feat + bands] = 1.0
    return table


def finish_kernel(sizes, names, *refs):
    layers, micro, span, half, hidden, feat, bands = sizes
    r = types.SimpleNamespace(**dict(zip(names, refs)))
    wide = hidden // half
    for m in range(micro):
        r.act[m, 0] = r.out_act[pl.ds(m * span, span), :]
        r.tokens[m, 0] = r.grad_tokens[pl.ds(m * span, span), :]
    for c in range(2):
        for piece in range(2):
            value = r.o_small[c, pl.ds(8 * piece, 8)].astype(F32).reshape(half, 128)
            r.turned[c, piece] = value.T
    for layer in range(layers):
        for k in range(3):
            r.g_in[layer, k] = r.o_big[layer, :, pl.ds(k * half, half)]
        r.g_out[layer] = r.o_big[layer, :, pl.ds(3 * half, half)]
        r.g_up[layer] = r.o_big[layer, :, pl.ds(4 * half, hidden)]
        r.g_down[layer] = r.o_big[layer, :, pl.ds(4 * half + hidden, hidden)]
        net = sum(r.turned[c, 1, pl.ds(feat, feat), pl.ds(layer * feat, feat)] for c in range(2))
        for i in range(bands):
            r.fin[i, pl.ds(layer, 1), :] = net[i : i + 1]
        r.fbias[pl.ds(layer, 1), :] = net[bands : bands + 1]
        r.ffreq[pl.ds(layer, 1), :] = net[bands + 1 : bands + 2]
        for c in range(2):
            lanes = pl.ds(c * half, half)
            base = 32 * layer

            def row(index, c=c):
                return r.turned[c, 1, pl.ds(index, 1), :]

            for n in range(2):
                r.gain[layer, pl.ds(n, 1), lanes] = row(base + n)
                r.bias[layer, pl.ds(n, 1), lanes] = row(base + 2 + n)
            at = pl.ds(layer, 1)
            r.out_b[at, lanes] = row(base + 4)
            r.down_b[at, lanes] = row(base + 5)
            r.skip[at, lanes] = row(112 + layer)
            for k in range(3):
                r.in_b[k, at, lanes] = row(base + 8 + k)
                r.short_b[k, at, lanes] = row(base + 20 + k)
                for j in range(3):
                    r.taps[k, j, at, lanes] = row(base + 11 + 3 * k + j)
            for i in range(wide):
                r.up_b[at, pl.ds(c * hidden + i * half, half)] = row(base + 24 + i)
            r.fout[layer, :, lanes] = r.turned[c, 0, pl.ds(layer * feat, feat), :]


def finish(out, sizes):
    layers, micro, span, half, hidden, feat, bands = sizes
    width, own = 2 * half, 2 * half // 16
    inputs = dict(out_act=out.out_act, grad_tokens=out.grad_tokens, o_big=out.o_big, o_small=out.o_small)
    outs = dict(
        act=(micro, 1, span, half),
        tokens=(micro, 1, span, half),
        g_in=(layers, 3, own, half),
        g_out=(layers, own, half),
        g_up=(layers, own, hidden),
        g_down=(layers, own, hidden),
        gain=(layers, 2, width),
        bias=(layers, 2, width),
        in_b=(3, layers, width),
        taps=(3, 3, layers, width),
        short_b=(3, layers, width),
        skip=(layers, width),
        out_b=(layers, width),
        up_b=(layers, 2 * hidden),
        down_b=(layers, width),
        fin=(bands, layers, feat),
        fbias=(layers, feat),
        ffreq=(layers, feat),
        fout=(layers, feat, width),
    )
    names = [*inputs, *outs, "turned"]
    results = pl.pallas_call(
        functools.partial(finish_kernel, sizes, names),
        out_shape=[jax.ShapeDtypeStruct(shape, F32) for shape in outs.values()],
        in_specs=[pl.BlockSpec(memory_space=pltpu.VMEM) for _ in inputs],
        out_specs=[pl.BlockSpec(memory_space=pltpu.VMEM) for _ in outs],
        scratch_shapes=[pltpu.VMEM((2, 2, 128, half), F32)],
        name="finish",
    )(*inputs.values())
    turns = dict(
        g_out=(0, 2, 1),
        g_down=(0, 2, 1),
        in_b=(1, 0, 2),
        taps=(2, 0, 1, 3),
        short_b=(1, 0, 2),
        fin=(1, 0, 2),
    )
    return tuple(
        value.transpose(turns[name]) if name in turns else value for name, value in zip(outs, results)
    )


def local_fast(
    tokens,
    lengths,
    cotangent,
    norm_gain,
    norm_bias,
    in_weight,
    in_bias,
    short_taps,
    short_bias,
    skip_gain,
    out_weight,
    out_bias,
    up_weight,
    up_bias,
    down_weight,
    down_bias,
    filter_in,
    filter_bias,
    filter_freq,
    filter_out,
    decay_rate,
):
    micro, rows_dev, half = tokens.shape[0], tokens.shape[2], tokens.shape[3]
    layers, bands, feat = filter_in.shape
    hidden = up_weight.shape[2]
    length = rows_dev * lax.axis_size("seq")
    freq_lane = feat + bands + 1
    cos_np, sin_np, turn_c, turn_s = half_tables(length)
    inputs = dict(
        tok=tokens.reshape(micro * rows_dev, half),
        cot=cotangent.reshape(micro * rows_dev, half),
        lens=lengths.T,
        gain=norm_gain,
        bias=norm_bias,
        out_b=out_bias,
        down_b=down_bias,
        in_b=in_bias.transpose(1, 0, 2),
        taps=short_taps.transpose(1, 2, 0, 3),
        short_b=short_bias.transpose(1, 0, 2),
        up_b=up_bias,
        fin=filter_in.transpose(1, 0, 2),
        fbias=filter_bias,
        ffreq=filter_freq,
        fout=filter_out,
        decay=decay_rate,
        skip=skip_gain,
        emb=jnp.asarray(embedding(length, bands, feat)),
        turn=jnp.asarray(np.concatenate([turn_c, turn_s], axis=1).T, F32),
        win=in_weight,
        wout=out_weight,
        wup=up_weight,
        wdown=down_weight,
        cos=jnp.asarray(cos_np, BF16),
        sin=jnp.asarray(sin_np, BF16),
    )
    out = chain(inputs, (layers, micro, rows_dev, half, hidden, feat, freq_lane))
    return finish(out, (layers, micro, rows_dev, half, hidden, feat, bands))


def solution(mesh):
    in_specs = (
        P(None, "dp", "seq", "chan"),
        P(None, "dp"),
        P(None, "dp", "seq", "chan"),
        P(None, None, "chan"),
        P(None, None, "chan"),
        P(None, None, None, "chan"),
        P(None, None, "chan"),
        P(None, None, None, "chan"),
        P(None, None, "chan"),
        P(None, "chan"),
        P(None, "chan", None),
        P(None, "chan"),
        P(None, None, "chan"),
        P(None, "chan"),
        P(None, "chan", None),
        P(None, "chan"),
        P(),
        P(),
        P(),
        P(None, None, "chan"),
        P(None, "chan"),
    )
    out_specs = (
        P(None, "dp", "seq", "chan"),
        P(None, "dp", "seq", "chan"),
        P(None, None, ("seq", "dp"), "chan"),
        P(None, "chan", ("seq", "dp")),
        P(None, ("seq", "dp"), "chan"),
        P(None, "chan", ("seq", "dp")),
        P(),
        P(),
        P(),
        P(),
        P(),
        P(),
        P(),
        P(),
        P(),
        P(),
        P(),
        P(),
        P(),
    )
    def entry(*args):
        fits = args[0].shape[2] * mesh.shape["seq"] <= 2048 and mesh.shape["seq"] == 8 and mesh.shape["dp"] == 2
        return (local_fast if fits else local)(*args)

    return jax.shard_map(entry, mesh=mesh, in_specs=in_specs, out_specs=out_specs, check_vma=False)
```
